128 devices in a mesh: dp: 4 (over z), seq: 4 (over y), tensor: 8 (over x, core).
Axes of the slice: x: 4, y: 4, z: 4, core: 2. Of those that a mesh axis runs over, the one named last changes fastest.
Arguments:
- activations: bfloat16 [12, 352, 8192], P('dp', 'seq', 'tensor'), may hold values from -6 to 6
- cotangents: bfloat16 [12, 352, 14336], P('dp', 'seq', 'tensor'), may hold values from -0.59765625 to 0.59765625
- row_ids: int32 [4, 3], P('dp'), may hold values from 0 to 2, each once within a row
- row_counts: int32 [4, 3], P('dp'), may hold values from 88 to 352
Outputs:
- weighted_grad: float32 [8192, 14336], P(('dp', 'seq'), 'tensor')
- example_weights: float32 [4, 2], P('dp')
The draws below stay inside these ranges and needn't reach their ends.
All inputs are finite; a program needn't handle non-finite values.
Results may differ from the reference program's by a relative error of at most 0.004.
Values may be sent and summed in bfloat16 or wider, within the bound.
A program may use at most 128 MiB of HBM per device.

```python
import jax
import jax.numpy as jnp
from jax import lax

D = 8192
FF = 14336
LEN = 352
ROWS = 3
CLEAN = 1
NOISY = 2
ALL_ROWS = 12
N_DP = 4
N_SEQ = 4


def with_ends(drawn, stream_key, smallest, largest):
    dims = drawn.shape
    place = [jax.random.randint(jax.random.fold_in(stream_key, axis), (), 0, dims[axis]) for axis in range(len(dims))]
    drawn = drawn.at[tuple(place)].set(smallest)
    longest = dims.index(max(dims))
    place[longest] = (place[longest] + 1) % dims[longest]
    return drawn.at[tuple(place)].set(largest)


def levels(stream_key, dims, shards, low, high):
    gain, own = 1.0, jax.random.fold_in(stream_key, 6)
    for dim, blocks in shards:
        heights = jnp.exp(jax.random.uniform(jax.random.fold_in(own, dim), (blocks,), jnp.float32, low / len(shards), high / len(shards)))
        gain = gain * jnp.repeat(heights, dims[dim] // blocks).reshape([-1 if axis == dim else 1 for axis in range(len(dims))])
    return gain


def normal_values(rng, shape, deviation, most, cuts=(), held_as=jnp.bfloat16):
    result = deviation * jax.random.normal(rng, shape, jnp.float32)
    if cuts:
        result = result * levels(rng, shape, cuts, -0.22, 0.18)
    return jnp.clip(result, -most, most).astype(held_as)


def setup_inputs(seed: int = 0) -> dict:
    keys = jax.random.split(jax.random.key(seed), 5)
    return {
        "activations": normal_values(keys[0], (ALL_ROWS, LEN, D), 1.0, 6.0, ((0, 4), (1, 4), (2, 8))),
        "cotangents": normal_values(keys[1], (ALL_ROWS, LEN, FF), 0.1, 0.59765625, ((0, 4), (1, 4), (2, 8))),
        "row_ids": jax.vmap(lambda own: jax.random.permutation(own, ROWS))(jax.random.split(keys[2], N_DP)).reshape((N_DP, ROWS)).astype(jnp.int32),
        "row_counts": with_ends(jax.random.randint(keys[3], (N_DP, ROWS), LEN // 4, LEN + 1), jax.random.fold_in(keys[3], 1), LEN // 4, LEN).astype(jnp.int32),
    }


def reference(activations, cotangents, row_ids, row_counts):
    positions = jnp.arange(LEN, dtype=jnp.int32)
    live_mask = (positions[None, :] < row_counts.reshape(-1)[:, None]).astype(jnp.bfloat16)
    masked = cotangents * live_mask[:, :, None]
    global_ids = (jnp.arange(N_DP, dtype=jnp.int32)[:, None] * ROWS + row_ids).astype(jnp.int32)
    clean_rows = global_ids[:, :CLEAN].reshape(-1)
    noisy_rows = global_ids[:, CLEAN:].reshape(-1)
    noisy_acts = jnp.take(activations, noisy_rows, axis=0)
    noisy_grads = jnp.take(masked, noisy_rows, axis=0)
    clean_acts = jnp.take(activations, clean_rows, axis=0).reshape(-1, D)
    clean_grads = jnp.take(masked, clean_rows, axis=0).reshape(-1, FF)
    acts_gram = jnp.dot(noisy_acts.reshape(-1, D), clean_acts.T, preferred_element_type=jnp.float32)
    grad_gram = jnp.dot(noisy_grads.reshape(-1, FF), clean_grads.T, preferred_element_type=jnp.float32)
    row_dots = jnp.sum((acts_gram * grad_gram).reshape(N_DP * NOISY, -1), axis=1)
    dot_mass = jnp.sum(jnp.abs(row_dots))
    weights = jnp.maximum(-row_dots, 0.0) / dot_mass
    scaled = (noisy_grads.astype(jnp.float32) * weights[:, None, None]).astype(jnp.bfloat16)
    seg_len = LEN // N_SEQ
    group_acts = noisy_acts.reshape(N_DP, NOISY, N_SEQ, seg_len, D).transpose(0, 2, 1, 3, 4).reshape(N_DP * N_SEQ, NOISY * seg_len, D)
    group_grads = scaled.reshape(N_DP, NOISY, N_SEQ, seg_len, FF).transpose(0, 2, 1, 3, 4).reshape(N_DP * N_SEQ, NOISY * seg_len, FF)

    def add_group(running, paired):
        partial_value = lax.dot_general(paired[0], paired[1], (((0,), (0,)), ((), ())), preferred_element_type=jnp.float32)
        partial_value = lax.optimization_barrier(partial_value.astype(jnp.bfloat16)).astype(jnp.float32)
        return running + partial_value, None

    weighted, unused = lax.scan(add_group, jnp.zeros((D, FF), jnp.float32), (group_acts, group_grads))
    return weighted, weights.reshape(N_DP, NOISY)
```

```python
import jax
import jax.numpy as jnp
from jax import lax
from jax.sharding import PartitionSpec as P

CLEAN = 1
NOISY = 2


def body(activations, cotangents, row_ids, row_counts):
    rows_here, seg_len, width_part = activations.shape
    ff_part = cotangents.shape[2]
    n_dp, n_seq = lax.axis_size("dp"), lax.axis_size("seq")
    spread = n_dp * n_seq
    block = width_part * lax.axis_size("tensor") // spread
    offset = lax.axis_index("seq") * seg_len
    positions = offset + jnp.arange(seg_len, dtype=jnp.int32)
    ids = row_ids[0]
    counts = jnp.take(row_counts[0], ids)
    live_mask = (positions[None, :] < counts[:, None]).astype(jnp.bfloat16)
    grads = jnp.take(cotangents, ids, axis=0) * live_mask[:, :, None]
    acts = jnp.take(activations, ids, axis=0)
    all_grads = lax.all_gather(grads, ("dp", "seq"), axis=0, tiled=False)
    full_acts = lax.all_gather(acts, "tensor", axis=2, tiled=True)
    split = full_acts.reshape(rows_here, seg_len, spread, block).transpose(2, 0, 1, 3)
    all_acts = lax.all_to_all(split, ("dp", "seq"), split_axis=0, concat_axis=0, tiled=True)
    g = all_grads.reshape(n_dp, n_seq, rows_here, seg_len, ff_part).transpose(0, 2, 1, 3, 4)
    a = all_acts.reshape(n_dp, n_seq, rows_here, seg_len, block).transpose(0, 2, 1, 3, 4)

    def product(a_part, g_part):
        return lax.dot_general(
            a_part, g_part, (((0,), (0,)), ((), ())), preferred_element_type=jnp.float32
        )

    clean = product(a[:, :CLEAN].reshape(-1, block), g[:, :CLEAN].reshape(-1, ff_part))
    noisy = [
        product(a[k, j].reshape(-1, block), g[k, j].reshape(-1, ff_part))
        for k in range(n_dp)
        for j in range(CLEAN, rows_here)
    ]
    dots = lax.psum(jnp.stack([jnp.sum(w * clean) for w in noisy]), ("dp", "seq", "tensor"))
    weights = jnp.maximum(-dots, 0.0) / jnp.sum(jnp.abs(dots))
    weighted = sum(weights[n] * noisy[n] for n in range(len(noisy)))
    own = lax.dynamic_slice_in_dim(weights, lax.axis_index("dp") * NOISY, NOISY, 0)
    return weighted, own[None, :]


def solution(mesh):
    placed = (P("dp", "seq", "tensor"), P("dp", "seq", "tensor"), P("dp", None), P("dp", None))
    return jax.shard_map(
        body,
        mesh=mesh,
        in_specs=placed,
        out_specs=(P(("dp", "seq"), "tensor"), P("dp", None)),
        check_vma=False,
    )
```

```python
import jax
import jax.numpy as jnp
from jax import lax
from jax.experimental import pallas as pl
from jax.experimental.pallas import tpu as pltpu
from jax.sharding import PartitionSpec as P

MESH = pl.DeviceIdType.MESH
F32 = jnp.float32
BF16 = jnp.bfloat16

SEG = 88
NOISE = 176
CLEAN_ROWS = 96
WA = 768
WB = 1024
LANES = 128


def body_kernel(ids_ref, counts_ref, acts_ref, cot_ref, out_ref, wout_ref,
                na, ca, cg, ga, gb, ao, ata, atb, acc, gr, d2, sm, x3,
                sv1, sv2, sv3, wts, scale,
                ring_s, ring_r, p_s, p_r, p_l, x_s, x_r, k_s, k_r,
                d_s, d_r, m_s, m_r, v_s, v_r, o_s):
    z = lax.axis_index("dp")
    y = lax.axis_index("seq")
    t = lax.axis_index("tensor")
    x = t // 2
    c = lax.rem(t, 2)

    def mod4(v):
        return lax.rem(v, 4)

    def copy(src, dst, s, r, dev):
        return pltpu.make_async_remote_copy(
            src_ref=src, dst_ref=dst, send_sem=s, recv_sem=r, device_id=dev, device_id_type=MESH)

    barrier = pltpu.get_barrier_semaphore()

    def greet(dev):
        pl.semaphore_signal(barrier, inc=1, device_id=dev, device_id_type=MESH)

    for r in range(1, 4):
        greet((mod4(z + r), y, t))
        greet((z, mod4(y + r), t))
    for r in range(1, 8):
        greet((z, y, lax.rem(t + r, 8)))

    targets = [(h, q, (x, 2 * c + h, 2 * q + z // 2)) for h in range(2) for q in range(4)]
    target_self = [(x == z) & (y == 2 * c + h) & (q == x) & (c == z // 2) for h, q, _ in targets]
    sources = [(2 * c + i // 4, i % 4) for i in range(8)]
    source_self = [(zs == z) & (ys == y) & (x == z) & (c == y // 2) for zs, ys in sources]
    for (_, _, dev), same in zip(targets, target_self):
        @pl.when(jnp.logical_not(same))
        def _():
            greet(dev)
    for (zs, ys), same in zip(sources, source_self):
        @pl.when(jnp.logical_not(same))
        def _():
            greet((zs, ys, 2 * z + y // 2))
    has_self = ((x == z) & (c == y // 2) & (c == z // 2)).astype(jnp.int32)

    rid = [ids_ref[0, j] for j in range(3)]
    live = [counts_ref[0, rid[j]] - y * SEG for j in range(3)]
    rows = lax.broadcasted_iota(jnp.int32, (SEG, LANES), 0)
    pad = jnp.zeros((CLEAN_ROWS - SEG, LANES), F32)

    def stage_acts(i, carry):
        cols = pl.ds(pl.multiple_of(i * LANES, LANES), LANES)
        part = [acts_ref[rid[j], :, cols].astype(F32) for j in range(3)]
        na[y, :, cols] = jnp.concatenate([part[1], part[2]], axis=0).astype(BF16)
        ca[z, :, cols] = jnp.concatenate([part[0], pad], axis=0).astype(BF16)
        return carry

    lax.fori_loop(0, 1024 // LANES, stage_acts, 0)

    def masked(j, cols):
        return jnp.where(rows < live[j], cot_ref[rid[j], :, cols].astype(F32), 0.0)

    pl.semaphore_wait(barrier, 29 - 2 * has_self)

    pieces = []
    for i, ((h, q, dev), same) in enumerate(zip(targets, target_self)):
        src = na.at[y, :, pl.ds(h * 512 + q * LANES, LANES)]
        dst = ao.at[q, z, y]
        far_copy = copy(src, dst, p_s.at[i], p_r.at[lax.rem(z, 2) * 4 + y], dev)
        near_copy = pltpu.make_async_copy(src, dst, p_l)

        @pl.when(same)
        def _():
            near_copy.start()

        @pl.when(jnp.logical_not(same))
        def _():
            far_copy.start()
        pieces.append((far_copy, near_copy, same))

    rings = []

    class Ring:
        def __init__(self, at, axis, width):
            n = len(rings)
            rings.append(self)
            me = y if axis == "y" else z

            def dev(v):
                return (z, v, t) if axis == "y" else (v, y, t)

            up, down, far = mod4(me + 1), mod4(me + 3), mod4(me + 2)
            half = width // 2
            first, second = pl.ds(0, half), pl.ds(half, half)
            own, low, high, opp = at(me), at(down), at(up), at(far)
            self.go = [copy(own, own, ring_s.at[n, 0], ring_r.at[n, 0], dev(up)),
                       copy(own, own, ring_s.at[n, 1], ring_r.at[n, 1], dev(down))]
            self.got = [copy(low, low, ring_s.at[n, 0], ring_r.at[n, 0], dev(up)),
                        copy(high, high, ring_s.at[n, 1], ring_r.at[n, 1], dev(down))]
            self.pass_on = [
                copy(low.at[:, first], low.at[:, first], ring_s.at[n, 2], ring_r.at[n, 2], dev(up)),
                copy(high.at[:, second], high.at[:, second], ring_s.at[n, 3], ring_r.at[n, 3], dev(down))]
            self.got_far = [
                copy(opp.at[:, first], opp.at[:, first], ring_s.at[n, 2], ring_r.at[n, 2], dev(up)),
                copy(opp.at[:, second], opp.at[:, second], ring_s.at[n, 3], ring_r.at[n, 3], dev(down))]

        def start(self):
            for k in self.go:
                k.start()

        def forward(self):
            for k in range(2):
                self.got[k].wait_recv()
                self.pass_on[k].start()

        def finish(self):
            for k in self.got_far:
                k.wait_recv()

        def drain(self):
            for k in self.go + self.pass_on:
                k.wait_send()

    def az_ring(k):
        item = mod4(y + k)
        return Ring(lambda v: ga.at[v, item], "z", WA)

    def by_ring(k):
        item = mod4(z + k)
        return Ring(lambda v: gb.at[v, item], "y", WB)

    r_na = Ring(lambda v: na.at[v], "y", 1024)
    r_ca = Ring(lambda v: ca.at[v], "z", 1024)
    r_cg = Ring(lambda v: cg.at[v], "z", WA + WB)
    r_ay = Ring(lambda v: ga.at[z, v], "y", WA)
    r_bz = Ring(lambda v: gb.at[y, v], "z", WB)
    r_az = {k: az_ring(k) for k in (0, 3, 1, 2)}
    r_by = {k: by_ring(k) for k in (0, 3, 1, 2)}

    r_na.start()
    r_ca.start()

    def stage_clean(i, carry):
        cols = pl.ds(pl.multiple_of(i * LANES, LANES), LANES)
        cg[z, :, cols] = jnp.concatenate([masked(0, cols), pad], axis=0).astype(BF16)
        return carry

    lax.fori_loop(0, (WA + WB) // LANES, stage_clean, 0)
    r_cg.start()

    def stage_a(i, carry):
        cols = pl.ds(pl.multiple_of(i * LANES, LANES), LANES)
        ga[z, y, :, cols] = jnp.concatenate([masked(1, cols), masked(2, cols)], axis=0).astype(BF16)
        return carry

    lax.fori_loop(0, WA // LANES, stage_a, 0)
    r_ay.start()

    def stage_b(i, carry):
        cols = pl.ds(pl.multiple_of(i * LANES, LANES), LANES)
        from_cols = pl.ds(pl.multiple_of(WA + i * LANES, LANES), LANES)
        gb[y, z, :, cols] = jnp.concatenate(
            [masked(1, from_cols), masked(2, from_cols)], axis=0).astype(BF16)
        return carry

    lax.fori_loop(0, WB // LANES, stage_b, 0)
    r_bz.start()
    r_by[0].start()
    r_az[0].start()

    r_na.forward()
    here = pl.ds(2 * c, 2)
    there = pl.ds(2 * (1 - c), 2)
    for i, ((zs, ys), same) in enumerate(zip(sources, source_self)):
        dst = ao.at[x, zs, ys]
        far_copy = copy(dst, dst, p_s.at[i], p_r.at[i], (z, y, lax.rem(t + 1, 8)))
        near_copy = pltpu.make_async_copy(dst, dst, p_l)

        @pl.when(same)
        def _():
            near_copy.wait()

        @pl.when(jnp.logical_not(same))
        def _():
            far_copy.wait_recv()
    mine = ao.at[x, here]
    partner = (z, y, 2 * x + 1 - c)
    spread = [copy(mine, mine, x_s.at[r - 1], x_r.at[r - 1], (z, y, 2 * mod4(x + r) + c)) for r in range(1, 4)]
    for k in spread:
        k.start()
    core = [copy(mine, mine, k_s.at[0], k_r.at[0], partner)]
    core[0].start()

    r_ca.forward()
    r_cg.forward()
    r_ay.forward()
    r_az[3].start()
    r_az[1].start()
    r_bz.forward()
    r_by[3].start()
    r_by[1].start()
    r_by[0].forward()
    r_az[0].forward()

    for r in range(1, 4):
        block = ao.at[mod4(x + 4 - r), here]
        copy(block, block, x_s.at[r - 1], x_r.at[r - 1], partner).wait_recv()
        relay = copy(block, block, k_s.at[r], k_r.at[r], partner)
        relay.start()
        core.append(relay)

    contract = (((1,), (1,)), ((), ()))

    def gram(left, right):
        return lax.dot_general(left, right, contract, preferred_element_type=F32)

    r_na.finish()
    r_ca.finish()
    gr[0] = gram(na[...].reshape(4 * NOISE, 1024), ca[...].reshape(4 * CLEAN_ROWS, 1024))
    r_cg.finish()
    r_ay.finish()
    r_az[2].start()
    r_bz.finish()
    r_by[2].start()
    r_by[0].finish()
    gr[1] = gram(ga[z].reshape(4 * NOISE, WA), cg[:, :, :WA].reshape(4 * CLEAN_ROWS, WA)) + gram(
        gb[:, z].reshape(4 * NOISE, WB), cg[:, :, WA:].reshape(4 * CLEAN_ROWS, WB))
    away = gr.at[:, pl.ds(pl.multiple_of((1 - c) * 352, 8), 352)]
    swap = copy(away, d2, d_s, d_r, partner)
    swap.start()

    for r in range(4):
        block = ao.at[mod4(x + 4 - r), there]
        copy(block, block, k_s.at[r], k_r.at[r], partner).wait_recv()

    def turn(k, carry):
        for q in range(4):
            span = pl.ds(q * LANES, LANES)
            ata[k, span, :] = ao[q, k].reshape(4 * NOISE, LANES).T
            atb[k, span, :] = ao[q, :, k].reshape(4 * NOISE, LANES).T
        return carry

    lax.fori_loop(0, 4, turn, 0)

    swap.wait_recv()
    sm[...] = gr[:, pl.ds(pl.multiple_of(c * 352, 8), 352)] + d2[...]
    share = []
    for r in range(1, 4):
        to = mod4(x + r)
        share.append(copy(sm.at[:, pl.ds(pl.multiple_of(to * SEG, 8), SEG)], x3.at[r - 1],
                          m_s.at[r - 1], m_r.at[r - 1], (z, y, 2 * to + c)))
    for k in share:
        k.start()

    for k in (3, 1):
        r_az[k].forward()
        r_by[k].forward()

    for k in share:
        k.wait_recv()
    total = sm[:, pl.ds(pl.multiple_of(x * SEG, 8), SEG)] + x3[0] + x3[1] + x3[2]
    dot = jnp.sum(jnp.sum(total[0] * total[1], axis=0, keepdims=True), axis=1, keepdims=True)
    slot = 2 * z + lax.rem(x, 2)
    place = lax.broadcasted_iota(jnp.int32, (8, LANES), 0)
    tile = jnp.where(place == slot, jnp.broadcast_to(dot, (8, LANES)), 0.0)

    sends = []

    def exchange(buf, value, me, n, dev, base):
        buf[me] = value
        out = [copy(buf.at[me], buf.at[me], v_s.at[base + r], v_r.at[base + r], dev(lax.rem(me + r, n)))
               for r in range(1, n)]
        for k in out:
            k.start()
        sends.extend(out)
        for r in range(1, n):
            origin = lax.rem(me + n - r, n)
            copy(buf.at[origin], buf.at[origin], v_s.at[base + r], v_r.at[base + r], dev(origin)).wait_recv()
        return jnp.sum(buf[...], axis=0)

    tile = exchange(sv1, tile, t, 8, lambda v: (z, y, v), 0)
    tile = exchange(sv2, tile, y, 4, lambda v: (z, v, t), 8)
    tile = exchange(sv3, tile, z, 4, lambda v: (v, y, t), 12)
    weights = jnp.maximum(-tile, 0.0) / jnp.sum(jnp.abs(tile), axis=0, keepdims=True)
    wts[...] = weights
    for k in range(4):
        scale[k, :SEG] = jnp.broadcast_to(wts[2 * k:2 * k + 1, :], (SEG, LANES))
        scale[k, SEG:] = jnp.broadcast_to(wts[2 * k + 1:2 * k + 2, :], (SEG, LANES))
    lane = lax.broadcasted_iota(jnp.int32, (1, LANES), 1)
    wout_ref[...] = jnp.where(lane == 0, wts[pl.ds(2 * z, 1), :], wts[pl.ds(2 * z + 1, 1), :])[:, :2]

    r_az[2].forward()
    r_by[2].forward()

    def scaled(raw, s):
        full = jnp.concatenate([s, s], axis=1)
        return (raw.astype(F32) * full).astype(BF16)

    def product(at, pieces_of, width, base, first):
        def step(i, carry):
            cols = pl.ds(pl.multiple_of(i * 256, 256), 256)
            dest = pl.ds(pl.multiple_of(base + i * 256, 256), 256)
            right = jnp.concatenate([scaled(raw, s) for raw, s in pieces_of(cols)], axis=0)
            value = jnp.dot(at[...], right, preferred_element_type=F32)
            if first:
                acc[:, dest] = value
            else:
                acc[:, dest] += value
            return carry

        lax.fori_loop(0, width // 256, step, 0)

    def add_a(k, first=False):
        v = mod4(z + k)
        product(ata.at[v], lambda cols: [(ga[v, i, :, cols], scale[v]) for i in range(4)], WA, 0, first)

    def add_b(k, first=False):
        v = mod4(y + k)
        product(atb.at[v], lambda cols: [(gb[v, i, :, cols], scale[i]) for i in range(4)], WB, WA, first)

    add_a(0, True)
    add_b(0, True)
    for k in (3, 1):
        add_a(k)
        add_b(k)
    for k in (0, 3, 1, 2):
        r_az[k].finish()
    add_a(2)
    out_a = pltpu.make_async_copy(acc.at[:, pl.ds(0, WA)], out_ref.at[:, pl.ds(0, WA)], o_s.at[0])
    out_a.start()
    for k in (3, 1, 2):
        r_by[k].finish()
    add_b(2)
    out_b = pltpu.make_async_copy(acc.at[:, pl.ds(WA, WB)], out_ref.at[:, pl.ds(WA, WB)], o_s.at[1])
    out_b.start()

    for far_copy, _, same in pieces:
        @pl.when(jnp.logical_not(same))
        def _():
            far_copy.wait_send()
    for ring in rings:
        ring.drain()
    for k in spread + core + [swap] + share + sends:
        k.wait_send()
    out_a.wait()
    out_b.wait()


def body(activations, cotangents, row_ids, row_counts):
    dma = pltpu.SemaphoreType.DMA
    vmem = pltpu.VMEM
    return pl.pallas_call(
        body_kernel,
        out_shape=(jax.ShapeDtypeStruct((512, WA + WB), F32), jax.ShapeDtypeStruct((1, 2), F32)),
        in_specs=[pl.BlockSpec(memory_space=pltpu.SMEM)] * 2 + [pl.BlockSpec(memory_space=pltpu.VMEM)] * 2,
        out_specs=(pl.BlockSpec(memory_space=pl.ANY), pl.BlockSpec(memory_space=pltpu.VMEM)),
        scratch_shapes=[
            vmem((4, NOISE, 1024), BF16),
            vmem((4, CLEAN_ROWS, 1024), BF16),
            vmem((4, CLEAN_ROWS, WA + WB), BF16),
            vmem((4, 4, NOISE, WA), BF16),
            vmem((4, 4, NOISE, WB), BF16),
            vmem((4, 4, 4, NOISE, LANES), BF16),
            vmem((4, 512, 4 * NOISE), BF16),
            vmem((4, 512, 4 * NOISE), BF16),
            vmem((512, WA + WB), F32),
            vmem((2, 4 * NOISE, 4 * CLEAN_ROWS), F32),
            vmem((2, 2 * NOISE, 4 * CLEAN_ROWS), F32),
            vmem((2, 2 * NOISE, 4 * CLEAN_ROWS), F32),
            vmem((3, 2, SEG, 4 * CLEAN_ROWS), F32),
            vmem((8, 8, LANES), F32),
            vmem((4, 8, LANES), F32),
            vmem((4, 8, LANES), F32),
            vmem((8, LANES), F32),
            vmem((4, NOISE, LANES), F32),
            dma((13, 4)), dma((13, 4)),
            dma((8,)), dma((8,)), dma,
            dma((3,)), dma((3,)),
            dma((4,)), dma((4,)),
            dma, dma,
            dma((3,)), dma((3,)),
            dma((16,)), dma((16,)),
            dma((2,)),
        ],
        compiler_params=pltpu.CompilerParams(
            collective_id=0, has_side_effects=True, vmem_limit_bytes=60 * 1024 * 1024),
        cost_estimate=pl.CostEstimate(flops=8_000_000_000, bytes_accessed=8_000_000, transcendentals=0),
        name="reweight",
    )(row_ids, row_counts, activations, cotangents)


def solution(mesh):
    placed = (P("dp", "seq", "tensor"), P("dp", "seq", "tensor"), P("dp", None), P("dp", None))
    return jax.shard_map(
        body,
        mesh=mesh,
        in_specs=placed,
        out_specs=(P(("dp", "seq"), "tensor"), P("dp", None)),
        check_vma=False,
    )
```

```python
import jax
import jax.numpy as jnp
from jax import lax
from jax.experimental import pallas as pl
from jax.experimental.pallas import tpu as pltpu
from jax.sharding import PartitionSpec as P

MESH = pl.DeviceIdType.MESH
F32 = jnp.float32
BF16 = jnp.bfloat16

SEG = 88
NOISE = 176
CLEAN_ROWS = 96
WA = 768
WB = 1024
LANES = 128


def body_kernel(ids_ref, counts_ref, acts_ref, cot_ref, out_ref, wout_ref,
                na, ca, cg, ga, gb, ao, ata, atb, acc, part_gram, grad_gram, full, d2, sm,
                near_a, near_b, x3, sv1, sv2, wts, scale,
                ring_s, ring_r, p_s, p_r, p_l, x_s, x_r, k_s, k_r,
                d_s, d_r, m_s, m_r, v_s, v_r, o_s):
    z = lax.axis_index("dp")
    y = lax.axis_index("seq")
    t = lax.axis_index("tensor")
    x = t // 2
    c = lax.rem(t, 2)

    def mod4(v):
        return lax.rem(v, 4)

    def copy(src, dst, s, r, dev):
        return pltpu.make_async_remote_copy(
            src_ref=src, dst_ref=dst, send_sem=s, recv_sem=r, device_id=dev, device_id_type=MESH)

    barrier = pltpu.get_barrier_semaphore()

    def greet(dev):
        pl.semaphore_signal(barrier, inc=1, device_id=dev, device_id_type=MESH)

    def cell(r):
        other = lax.rem(4 * z + y + r, 16)
        return other // 4, lax.rem(other, 4), t

    for r in range(1, 16):
        greet(cell(r))
    for r in range(1, 8):
        greet((z, y, lax.rem(t + r, 8)))

    targets = [(h, q, (x, 2 * c + h, 2 * q + z // 2)) for h in range(2) for q in range(4)]
    target_self = [(x == z) & (y == 2 * c + h) & (q == x) & (c == z // 2) for h, q, _ in targets]
    sources = [(2 * c + i // 4, i % 4) for i in range(8)]
    source_self = [(zs == z) & (ys == y) & (x == z) & (c == y // 2) for zs, ys in sources]
    for (_, _, dev), same in zip(targets, target_self):
        @pl.when(jnp.logical_not(same))
        def _():
            greet(dev)
    for (zs, ys), same in zip(sources, source_self):
        @pl.when(jnp.logical_not(same))
        def _():
            greet((zs, ys, 2 * z + y // 2))
    has_self = ((x == z) & (c == y // 2) & (c == z // 2)).astype(jnp.int32)

    rid = [ids_ref[0, j] for j in range(3)]
    live = [counts_ref[0, rid[j]] - y * SEG for j in range(3)]
    rows = lax.broadcasted_iota(jnp.int32, (SEG, LANES), 0)
    pad = jnp.zeros((CLEAN_ROWS - SEG, LANES), F32)

    def stage_acts(i, carry):
        cols = pl.ds(pl.multiple_of(i * LANES, LANES), LANES)
        part = [acts_ref[rid[j], :, cols].astype(F32) for j in range(3)]
        na[y, :, cols] = jnp.concatenate([part[1], part[2]], axis=0).astype(BF16)
        ca[z, :, cols] = jnp.concatenate([part[0], pad], axis=0).astype(BF16)
        return carry

    lax.fori_loop(0, 1024 // LANES, stage_acts, 0)

    def masked(j, cols):
        return jnp.where(rows < live[j], cot_ref[rid[j], :, cols].astype(F32), 0.0)

    def stage_clean(i, carry):
        cols = pl.ds(pl.multiple_of(i * LANES, LANES), LANES)
        cg[z, :, cols] = jnp.concatenate([masked(0, cols), pad], axis=0).astype(BF16)
        return carry

    def stage_a(i, carry):
        cols = pl.ds(pl.multiple_of(i * LANES, LANES), LANES)
        ga[z, y, :, cols] = jnp.concatenate([masked(1, cols), masked(2, cols)], axis=0).astype(BF16)
        return carry

    def stage_b(i, carry):
        cols = pl.ds(pl.multiple_of(i * LANES, LANES), LANES)
        from_cols = pl.ds(pl.multiple_of(WA + i * LANES, LANES), LANES)
        gb[y, z, :, cols] = jnp.concatenate(
            [masked(1, from_cols), masked(2, from_cols)], axis=0).astype(BF16)
        return carry

    lax.fori_loop(0, WA // LANES, stage_a, 0)
    lax.fori_loop(0, (WA + WB) // LANES, stage_clean, 0)
    lax.fori_loop(0, WB // LANES, stage_b, 0)
    pl.semaphore_wait(barrier, 38 - 2 * has_self)

    pieces = []
    for i, ((h, q, dev), same) in enumerate(zip(targets, target_self)):
        src = na.at[y, :, pl.ds(h * 512 + q * LANES, LANES)]
        dst = ao.at[q, z, y]
        far_copy = copy(src, dst, p_s.at[i], p_r.at[lax.rem(z, 2) * 4 + y], dev)
        near_copy = pltpu.make_async_copy(src, dst, p_l)

        @pl.when(same)
        def _():
            near_copy.start()

        @pl.when(jnp.logical_not(same))
        def _():
            far_copy.start()
        pieces.append((far_copy, near_copy, same))

    rings = []

    class Ring:
        def __init__(self, at, axis, first, second):
            n = len(rings)
            rings.append(self)
            me = {"x": x, "y": y, "z": z}[axis]

            def dev(v):
                return {"x": (z, y, 2 * v + c), "y": (z, v, t), "z": (v, y, t)}[axis]

            up, down, far = mod4(me + 1), mod4(me + 3), mod4(me + 2)
            own, low, high, opp = at(me), at(down), at(up), at(far)
            self.go = [copy(own, own, ring_s.at[n, 0], ring_r.at[n, 0], dev(up)),
                       copy(own, own, ring_s.at[n, 1], ring_r.at[n, 1], dev(down))]
            self.got = [copy(low, low, ring_s.at[n, 0], ring_r.at[n, 0], dev(up)),
                        copy(high, high, ring_s.at[n, 1], ring_r.at[n, 1], dev(down))]
            self.pass_on = [
                copy(low.at[first], low.at[first], ring_s.at[n, 2], ring_r.at[n, 2], dev(up)),
                copy(high.at[second], high.at[second], ring_s.at[n, 3], ring_r.at[n, 3], dev(down))]
            self.got_far = [
                copy(opp.at[first], opp.at[first], ring_s.at[n, 2], ring_r.at[n, 2], dev(up)),
                copy(opp.at[second], opp.at[second], ring_s.at[n, 3], ring_r.at[n, 3], dev(down))]

        def start(self):
            for k in self.go:
                k.start()

        def forward(self):
            for k in range(2):
                self.got[k].wait_recv()
                self.pass_on[k].start()

        def finish(self):
            for k in self.got_far:
                k.wait_recv()

        def drain(self):
            for k in self.go + self.pass_on:
                k.wait_send()

    def halves(width):
        half = width // 2
        return (slice(None), pl.ds(0, half)), (slice(None), pl.ds(half, half))

    def az_ring(k):
        item = mod4(y + k)
        return Ring(lambda v: ga.at[v, item], "z", *halves(WA))

    def by_ring(k):
        item = mod4(z + k)
        return Ring(lambda v: gb.at[v, item], "y", *halves(WB))

    def rows_of(chunk):
        return pl.ds(pl.multiple_of(chunk * SEG, 8), SEG)

    r_na = Ring(lambda v: na.at[v], "y", *halves(1024))
    r_ca = Ring(lambda v: ca.at[v], "z", *halves(1024))
    r_cg = Ring(lambda v: cg.at[v], "z", *halves(WA + WB))
    r_ay = Ring(lambda v: ga.at[z, v], "y", *halves(WA))
    r_bz = Ring(lambda v: gb.at[y, v], "z", *halves(WB))
    r_az = {k: az_ring(k) for k in (0, 3, 1, 2)}
    r_by = {k: by_ring(k) for k in (0, 3, 1, 2)}
    r_full = Ring(lambda v: full.at[rows_of(4 * c + v)], "x", (pl.ds(0, 48),), (pl.ds(48, 40),))

    r_na.start()
    r_ca.start()
    r_ay.start()
    r_cg.start()
    r_bz.start()

    r_na.forward()
    r_by[0].start()
    here = pl.ds(2 * c, 2)
    there = pl.ds(2 * (1 - c), 2)
    for i, ((zs, ys), same) in enumerate(zip(sources, source_self)):
        dst = ao.at[x, zs, ys]
        far_copy = copy(dst, dst, p_s.at[i], p_r.at[i], (z, y, lax.rem(t + 1, 8)))
        near_copy = pltpu.make_async_copy(dst, dst, p_l)

        @pl.when(same)
        def _():
            near_copy.wait()

        @pl.when(jnp.logical_not(same))
        def _():
            far_copy.wait_recv()
    mine = ao.at[x, here]
    partner = (z, y, 2 * x + 1 - c)
    spread = [copy(mine, mine, x_s.at[r - 1], x_r.at[r - 1], (z, y, 2 * mod4(x + r) + c)) for r in range(1, 4)]
    for k in spread:
        k.start()
    core = [copy(mine, mine, k_s.at[0], k_r.at[0], partner)]
    core[0].start()

    r_ca.forward()
    r_cg.forward()
    r_az[0].start()
    r_ay.forward()
    r_az[3].start()
    r_az[1].start()
    r_bz.forward()

    contract = (((1,), (1,)), ((), ()))

    def gram(left, right):
        return lax.dot_general(left, right, contract, preferred_element_type=F32)

    r_na.finish()
    r_ca.finish()
    part_gram[...] = gram(na[...].reshape(4 * NOISE, 1024), ca[...].reshape(4 * CLEAN_ROWS, 1024))
    own_half = pl.ds(pl.multiple_of(c * 352, 8), 352)
    other_half = pl.ds(pl.multiple_of((1 - c) * 352, 8), 352)
    swap = copy(part_gram.at[other_half], d2, d_s.at[0], d_r.at[0], partner)
    swap.start()

    r_by[0].forward()
    r_by[3].start()
    r_by[1].start()
    for r in range(1, 4):
        block = ao.at[mod4(x + 4 - r), here]
        copy(block, block, x_s.at[r - 1], x_r.at[r - 1], partner).wait_recv()
        relay = copy(block, block, k_s.at[r], k_r.at[r], partner)
        relay.start()
        core.append(relay)

    swap.wait_recv()
    sm[...] = part_gram[own_half] + d2[...]
    up, down, across = mod4(x + 1), mod4(x + 3), mod4(x + 2)
    dev_up, dev_down = (z, y, 2 * up + c), (z, y, 2 * down + c)
    first = pl.ds(pl.multiple_of(across * SEG, 8), 48)
    second = pl.ds(pl.multiple_of(across * SEG + 48, 8), 40)
    share = [copy(sm.at[first], near_a, m_s.at[0], m_r.at[0], dev_up),
             copy(sm.at[second], near_b, m_s.at[1], m_r.at[1], dev_down),
             copy(sm.at[rows_of(up)], x3.at[0], m_s.at[2], m_r.at[2], dev_up),
             copy(sm.at[rows_of(down)], x3.at[1], m_s.at[3], m_r.at[3], dev_down)]
    share[0].start()
    share[1].start()
    r_az[0].forward()
    share[0].wait_recv()
    sm[pl.ds(pl.multiple_of(up * SEG, 8), 48)] += near_a[...]
    share[2].start()
    share[1].wait_recv()
    sm[pl.ds(pl.multiple_of(down * SEG + 48, 8), 40)] += near_b[...]
    share[3].start()

    r_cg.finish()
    r_ay.finish()
    r_az[2].start()
    grad_gram[...] = gram(ga[z].reshape(4 * NOISE, WA), cg[:, :, :WA].reshape(4 * CLEAN_ROWS, WA))

    share[2].wait_recv()
    share[3].wait_recv()
    full[rows_of(4 * c + x)] = sm[rows_of(x)] + x3[0] + x3[1]
    r_full.start()
    r_bz.finish()
    r_by[2].start()
    r_full.forward()
    r_full.finish()
    give = copy(full.at[own_half], full.at[own_half], d_s.at[1], d_r.at[1], partner)
    give.start()

    r_by[0].finish()
    grad_gram[...] += gram(gb[:, z].reshape(4 * NOISE, WB), cg[:, :, WA:].reshape(4 * CLEAN_ROWS, WB))
    copy(full.at[other_half], full.at[other_half], d_s.at[1], d_r.at[1], partner).wait_recv()

    def row_dot(j):
        terms = [grad_gram[g * SEG:(g + 1) * SEG] * full[g * SEG:(g + 1) * SEG] for g in range(j, 8, 2)]
        rows_sum = jnp.sum(terms[0] + terms[1] + terms[2] + terms[3], axis=0, keepdims=True)
        return jnp.broadcast_to(jnp.sum(rows_sum, axis=1, keepdims=True), (8, LANES))

    place = lax.broadcasted_iota(jnp.int32, (8, LANES), 0)
    tile = jnp.where(place == 2 * z, row_dot(0), jnp.where(place == 2 * z + 1, row_dot(1), 0.0))

    sends = []

    def send_tile(buf, value, me, n, dev, base):
        buf[me] = value
        for r in range(1, n):
            out = copy(buf.at[me], buf.at[me], v_s.at[base + r], v_r.at[base + r], dev(r))
            out.start()
            sends.append(out)

    def sum_tiles(buf, me, n, base):
        for r in range(1, n):
            origin = buf.at[lax.rem(me + n - r, n)]
            copy(origin, origin, v_s.at[base + r], v_r.at[base + r], partner).wait_recv()
        return jnp.sum(buf[...], axis=0)

    send_tile(sv1, tile, t, 8, lambda r: (z, y, lax.rem(t + r, 8)), 0)

    for r in range(4):
        block = ao.at[mod4(x + 4 - r), there]
        copy(block, block, k_s.at[r], k_r.at[r], partner).wait_recv()

    def turn(k, carry):
        for q in range(4):
            span = pl.ds(q * LANES, LANES)
            ata[k, span, :] = ao[q, k].reshape(4 * NOISE, LANES).T
            atb[k, span, :] = ao[q, :, k].reshape(4 * NOISE, LANES).T
        return carry

    lax.fori_loop(0, 4, turn, 0)

    tile = sum_tiles(sv1, t, 8, 0)
    send_tile(sv2, tile, 4 * z + y, 16, cell, 8)
    for k in (3, 1):
        r_az[k].forward()
        r_by[k].forward()
    tile = sum_tiles(sv2, 4 * z + y, 16, 8)
    weights = jnp.maximum(-tile, 0.0) / jnp.sum(jnp.abs(tile), axis=0, keepdims=True)
    wts[...] = weights
    for k in range(4):
        scale[k, :SEG] = jnp.broadcast_to(wts[2 * k:2 * k + 1, :], (SEG, LANES))
        scale[k, SEG:] = jnp.broadcast_to(wts[2 * k + 1:2 * k + 2, :], (SEG, LANES))
    lane = lax.broadcasted_iota(jnp.int32, (1, LANES), 1)
    wout_ref[...] = jnp.where(lane == 0, wts[pl.ds(2 * z, 1), :], wts[pl.ds(2 * z + 1, 1), :])[:, :2]

    def scaled(raw, s):
        full = jnp.concatenate([s, s], axis=1)
        return (raw.astype(F32) * full).astype(BF16)

    def product(at, pieces_of, width, base, first):
        def step(i, carry):
            cols = pl.ds(pl.multiple_of(i * 256, 256), 256)
            dest = pl.ds(pl.multiple_of(base + i * 256, 256), 256)
            right = jnp.concatenate([scaled(raw, s) for raw, s in pieces_of(cols)], axis=0)
            value = jnp.dot(at[...], right, preferred_element_type=F32)
            if first:
                acc[:, dest] = value
            else:
                acc[:, dest] += value
            return carry

        lax.fori_loop(0, width // 256, step, 0)

    def add_a(k, first=False):
        v = mod4(z + k)
        product(ata.at[v], lambda cols: [(ga[v, i, :, cols], scale[v]) for i in range(4)], WA, 0, first)

    def add_b(k, first=False):
        v = mod4(y + k)
        product(atb.at[v], lambda cols: [(gb[v, i, :, cols], scale[i]) for i in range(4)], WB, WA, first)

    add_a(0, True)
    add_b(0, True)
    r_az[2].forward()
    r_by[2].forward()
    for k in (3, 1):
        add_a(k)
        add_b(k)
    for k in (0, 3, 1, 2):
        r_az[k].finish()
    add_a(2)
    out_a = pltpu.make_async_copy(acc.at[:, pl.ds(0, WA)], out_ref.at[:, pl.ds(0, WA)], o_s.at[0])
    out_a.start()
    for k in (3, 1, 2):
        r_by[k].finish()
    add_b(2)
    out_b = pltpu.make_async_copy(acc.at[:, pl.ds(WA, WB)], out_ref.at[:, pl.ds(WA, WB)], o_s.at[1])
    out_b.start()

    for far_copy, _, same in pieces:
        @pl.when(jnp.logical_not(same))
        def _():
            far_copy.wait_send()
    for ring in rings:
        ring.drain()
    for k in spread + core + [swap, give] + share + sends:
        k.wait_send()
    out_a.wait()
    out_b.wait()


def body(activations, cotangents, row_ids, row_counts):
    dma = pltpu.SemaphoreType.DMA
    vmem = pltpu.VMEM
    return pl.pallas_call(
        body_kernel,
        out_shape=(jax.ShapeDtypeStruct((512, WA + WB), F32), jax.ShapeDtypeStruct((1, 2), F32)),
        in_specs=[pl.BlockSpec(memory_space=pltpu.SMEM)] * 2 + [pl.BlockSpec(memory_space=pltpu.VMEM)] * 2,
        out_specs=(pl.BlockSpec(memory_space=pl.ANY), pl.BlockSpec(memory_space=pltpu.VMEM)),
        scratch_shapes=[
            vmem((4, NOISE, 1024), BF16),
            vmem((4, CLEAN_ROWS, 1024), BF16),
            vmem((4, CLEAN_ROWS, WA + WB), BF16),
            vmem((4, 4, NOISE, WA), BF16),
            vmem((4, 4, NOISE, WB), BF16),
            vmem((4, 4, 4, NOISE, LANES), BF16),
            vmem((4, 512, 4 * NOISE), BF16),
            vmem((4, 512, 4 * NOISE), BF16),
            vmem((512, WA + WB), F32),
            vmem((4 * NOISE, 4 * CLEAN_ROWS), F32),
            vmem((4 * NOISE, 4 * CLEAN_ROWS), F32),
            vmem((4 * NOISE, 4 * CLEAN_ROWS), F32),
            vmem((2 * NOISE, 4 * CLEAN_ROWS), F32),
            vmem((2 * NOISE, 4 * CLEAN_ROWS), F32),
            vmem((48, 4 * CLEAN_ROWS), F32),
            vmem((40, 4 * CLEAN_ROWS), F32),
            vmem((2, SEG, 4 * CLEAN_ROWS), F32),
            vmem((8, 8, LANES), F32),
            vmem((16, 8, LANES), F32),
            vmem((8, LANES), F32),
            vmem((4, NOISE, LANES), F32),
            dma((14, 4)), dma((14, 4)),
            dma((8,)), dma((8,)), dma,
            dma((3,)), dma((3,)),
            dma((4,)), dma((4,)),
            dma((2,)), dma((2,)),
            dma((4,)), dma((4,)),
            dma((24,)), dma((24,)),
            dma((2,)),
        ],
        compiler_params=pltpu.CompilerParams(
            collective_id=0, has_side_effects=True, vmem_limit_bytes=60 * 1024 * 1024),
        cost_estimate=pl.CostEstimate(flops=8_000_000_000, bytes_accessed=8_000_000, transcendentals=0),
        name="reweight",
    )(row_ids, row_counts, activations, cotangents)


def solution(mesh):
    placed = (P("dp", "seq", "tensor"), P("dp", "seq", "tensor"), P("dp", None), P("dp", None))
    return jax.shard_map(
        body,
        mesh=mesh,
        in_specs=placed,
        out_specs=(P(("dp", "seq"), "tensor"), P("dp", None)),
        check_vma=False,
    )
```

```python
import jax
import jax.numpy as jnp
from jax import lax
from jax.experimental import pallas as pl
from jax.experimental.pallas import tpu as pltpu
from jax.sharding import PartitionSpec as P

MESH = pl.DeviceIdType.MESH
F32 = jnp.float32
BF16 = jnp.bfloat16

SEG = 88
NOISE = 176
CLEAN_ROWS = 96
WA = 768
WB = 1024
LANES = 128


def body_kernel(ids_ref, counts_ref, acts_ref, cot_ref, out_ref, wout_ref,
                na, ca, cg, ga, gb, ao, ata, atb, acc, part_gram, grad_gram, full, d2, sm,
                near_a, near_b, x3, sv1, sv2, wts, scale,
                ring_s, ring_r, p_s, p_r, p_l, k_s, k_r,
                d_s, d_r, m_s, m_r, v_s, v_r, o_s):
    z = lax.axis_index("dp")
    y = lax.axis_index("seq")
    t = lax.axis_index("tensor")
    x = t // 2
    c = lax.rem(t, 2)

    def mod4(v):
        return lax.rem(v, 4)

    def copy(src, dst, s, r, dev):
        return pltpu.make_async_remote_copy(
            src_ref=src, dst_ref=dst, send_sem=s, recv_sem=r, device_id=dev, device_id_type=MESH)

    barrier = pltpu.get_barrier_semaphore()

    def greet(dev):
        pl.semaphore_signal(barrier, inc=1, device_id=dev, device_id_type=MESH)

    def cell(r):
        other = lax.rem(4 * z + y + r, 16)
        return other // 4, lax.rem(other, 4), t

    for r in range(1, 16):
        greet(cell(r))
    for r in range(1, 8):
        greet((z, y, lax.rem(t + r, 8)))

    targets = [(h, q, (x, 2 * c + h, 2 * q + z // 2)) for h in range(2) for q in range(4)]
    target_self = [(x == z) & (y == 2 * c + h) & (q == x) & (c == z // 2) for h, q, _ in targets]
    sources = [(2 * c + i // 4, i % 4) for i in range(8)]
    source_self = [(zs == z) & (ys == y) & (x == z) & (c == y // 2) for zs, ys in sources]
    for (_, _, dev), same in zip(targets, target_self):
        @pl.when(jnp.logical_not(same))
        def _():
            greet(dev)
    for (zs, ys), same in zip(sources, source_self):
        @pl.when(jnp.logical_not(same))
        def _():
            greet((zs, ys, 2 * z + y // 2))
    has_self = ((x == z) & (c == y // 2) & (c == z // 2)).astype(jnp.int32)

    rid = [ids_ref[0, j] for j in range(3)]
    live = [counts_ref[0, rid[j]] - y * SEG for j in range(3)]
    rows = lax.broadcasted_iota(jnp.int32, (SEG, LANES), 0)
    pad = jnp.zeros((CLEAN_ROWS - SEG, LANES), F32)

    def stage_acts(i, carry):
        cols = pl.ds(pl.multiple_of(i * LANES, LANES), LANES)
        part = [acts_ref[rid[j], :, cols].astype(F32) for j in range(3)]
        na[y, :, cols] = jnp.concatenate([part[1], part[2]], axis=0).astype(BF16)
        ca[z, :, cols] = jnp.concatenate([part[0], pad], axis=0).astype(BF16)
        return carry

    lax.fori_loop(0, 1024 // LANES, stage_acts, 0)

    def masked(j, cols):
        return jnp.where(rows < live[j], cot_ref[rid[j], :, cols].astype(F32), 0.0)

    def stage_clean(i, carry):
        cols = pl.ds(pl.multiple_of(i * LANES, LANES), LANES)
        cg[z, :, cols] = jnp.concatenate([masked(0, cols), pad], axis=0).astype(BF16)
        return carry

    def stage_a(i, carry):
        cols = pl.ds(pl.multiple_of(i * LANES, LANES), LANES)
        ga[z, y, :, cols] = jnp.concatenate([masked(1, cols), masked(2, cols)], axis=0).astype(BF16)
        return carry

    def stage_b(i, carry):
        cols = pl.ds(pl.multiple_of(i * LANES, LANES), LANES)
        from_cols = pl.ds(pl.multiple_of(WA + i * LANES, LANES), LANES)
        gb[y, z, :, cols] = jnp.concatenate(
            [masked(1, from_cols), masked(2, from_cols)], axis=0).astype(BF16)
        return carry

    lax.fori_loop(0, WA // LANES, stage_a, 0)
    lax.fori_loop(0, (WA + WB) // LANES, stage_clean, 0)
    lax.fori_loop(0, WB // LANES, stage_b, 0)
    pl.semaphore_wait(barrier, 38 - 2 * has_self)

    pieces = []
    for i, ((h, q, dev), same) in enumerate(zip(targets, target_self)):
        src = na.at[y, :, pl.ds(h * 512 + q * LANES, LANES)]
        dst = ao.at[q, z, y]
        far_copy = copy(src, dst, p_s.at[i], p_r.at[lax.rem(z, 2) * 4 + y], dev)
        near_copy = pltpu.make_async_copy(src, dst, p_l)

        @pl.when(same)
        def _():
            near_copy.start()

        @pl.when(jnp.logical_not(same))
        def _():
            far_copy.start()
        pieces.append((far_copy, near_copy, same))

    rings = []

    class Ring:
        def __init__(self, at, axis, first, second):
            n = len(rings)
            rings.append(self)
            me = {"x": x, "y": y, "z": z}[axis]

            def dev(v):
                return {"x": (z, y, 2 * v + c), "y": (z, v, t), "z": (v, y, t)}[axis]

            up, down, far = mod4(me + 1), mod4(me + 3), mod4(me + 2)
            own, low, high, opp = at(me), at(down), at(up), at(far)
            self.go = [copy(own, own, ring_s.at[n, 0], ring_r.at[n, 0], dev(up)),
                       copy(own, own, ring_s.at[n, 1], ring_r.at[n, 1], dev(down))]
            self.got = [copy(low, low, ring_s.at[n, 0], ring_r.at[n, 0], dev(up)),
                        copy(high, high, ring_s.at[n, 1], ring_r.at[n, 1], dev(down))]
            self.pass_on = [
                copy(low.at[first], low.at[first], ring_s.at[n, 2], ring_r.at[n, 2], dev(up)),
                copy(high.at[second], high.at[second], ring_s.at[n, 3], ring_r.at[n, 3], dev(down))]
            self.got_far = [
                copy(opp.at[first], opp.at[first], ring_s.at[n, 2], ring_r.at[n, 2], dev(up)),
                copy(opp.at[second], opp.at[second], ring_s.at[n, 3], ring_r.at[n, 3], dev(down))]

        def start(self):
            for k in self.go:
                k.start()

        def forward(self):
            for k in range(2):
                self.got[k].wait_recv()
                self.pass_on[k].start()

        def finish(self):
            for k in self.got_far:
                k.wait_recv()

        def drain(self):
            for k in self.go + self.pass_on:
                k.wait_send()

    def halves(width):
        half = width // 2
        return (slice(None), pl.ds(0, half)), (slice(None), pl.ds(half, half))

    def az_ring(k):
        item = mod4(y + k)
        return Ring(lambda v: ga.at[v, item], "z", *halves(WA))

    def by_ring(k):
        item = mod4(z + k)
        return Ring(lambda v: gb.at[v, item], "y", *halves(WB))

    def rows_of(chunk):
        return pl.ds(pl.multiple_of(chunk * SEG, 8), SEG)

    r_na = Ring(lambda v: na.at[v], "y", *halves(1024))
    r_ca = Ring(lambda v: ca.at[v], "z", *halves(1024))
    r_cg = Ring(lambda v: cg.at[v], "z", *halves(WA + WB))
    r_ay = Ring(lambda v: ga.at[z, v], "y", *halves(WA))
    r_bz = Ring(lambda v: gb.at[y, v], "z", *halves(WB))
    r_az = {k: az_ring(k) for k in (0, 3, 1, 2)}
    r_by = {k: by_ring(k) for k in (0, 3, 1, 2)}
    here = pl.ds(2 * c, 2)
    there = pl.ds(2 * (1 - c), 2)
    r_ao = Ring(lambda v: ao.at[v, here], "x", (pl.ds(0, 1),), (pl.ds(1, 1),))
    r_full = Ring(lambda v: full.at[rows_of(4 * c + v)], "x", (pl.ds(0, 48),), (pl.ds(48, 40),))

    r_na.start()
    r_ca.start()
    r_ay.start()
    r_cg.start()
    r_bz.start()

    r_na.forward()
    r_by[0].start()
    for i, ((zs, ys), same) in enumerate(zip(sources, source_self)):
        dst = ao.at[x, zs, ys]
        far_copy = copy(dst, dst, p_s.at[i], p_r.at[i], (z, y, lax.rem(t + 1, 8)))
        near_copy = pltpu.make_async_copy(dst, dst, p_l)

        @pl.when(same)
        def _():
            near_copy.wait()

        @pl.when(jnp.logical_not(same))
        def _():
            far_copy.wait_recv()
    mine = ao.at[x, here]
    partner = (z, y, 2 * x + 1 - c)
    r_ao.start()
    core = [copy(mine, mine, k_s.at[0], k_r.at[0], partner)]
    core[0].start()

    r_ca.forward()
    r_cg.forward()
    r_az[0].start()
    r_ay.forward()
    r_az[3].start()
    r_az[1].start()
    r_bz.forward()

    def relay(r):
        block = ao.at[mod4(x + 4 - r), here]
        core.append(copy(block, block, k_s.at[r], k_r.at[r], partner))
        core[-1].start()

    r_ao.forward()
    relay(1)
    relay(3)

    contract = (((1,), (1,)), ((), ()))

    def gram(left, right):
        return lax.dot_general(left, right, contract, preferred_element_type=F32)

    r_na.finish()
    r_ca.finish()
    part_gram[...] = gram(na[...].reshape(4 * NOISE, 1024), ca[...].reshape(4 * CLEAN_ROWS, 1024))
    own_half = pl.ds(pl.multiple_of(c * 352, 8), 352)
    other_half = pl.ds(pl.multiple_of((1 - c) * 352, 8), 352)
    swap = copy(part_gram.at[other_half], d2, d_s.at[0], d_r.at[0], partner)
    swap.start()

    r_by[0].forward()
    r_by[3].start()
    r_by[1].start()
    r_ao.finish()
    relay(2)

    swap.wait_recv()
    sm[...] = part_gram[own_half] + d2[...]
    up, down, across = mod4(x + 1), mod4(x + 3), mod4(x + 2)
    dev_up, dev_down = (z, y, 2 * up + c), (z, y, 2 * down + c)
    first = pl.ds(pl.multiple_of(across * SEG, 8), 48)
    second = pl.ds(pl.multiple_of(across * SEG + 48, 8), 40)
    share = [copy(sm.at[first], near_a, m_s.at[0], m_r.at[0], dev_up),
             copy(sm.at[second], near_b, m_s.at[1], m_r.at[1], dev_down),
             copy(sm.at[rows_of(up)], x3.at[0], m_s.at[2], m_r.at[2], dev_up),
             copy(sm.at[rows_of(down)], x3.at[1], m_s.at[3], m_r.at[3], dev_down)]
    share[0].start()
    share[1].start()
    r_az[0].forward()
    share[0].wait_recv()
    sm[pl.ds(pl.multiple_of(up * SEG, 8), 48)] += near_a[...]
    share[2].start()
    share[1].wait_recv()
    sm[pl.ds(pl.multiple_of(down * SEG + 48, 8), 40)] += near_b[...]
    share[3].start()

    r_cg.finish()
    r_ay.finish()
    r_az[2].start()
    grad_gram[...] = gram(ga[z].reshape(4 * NOISE, WA), cg[:, :, :WA].reshape(4 * CLEAN_ROWS, WA))

    share[2].wait_recv()
    share[3].wait_recv()
    full[rows_of(4 * c + x)] = sm[rows_of(x)] + x3[0] + x3[1]
    r_full.start()
    r_bz.finish()
    r_by[2].start()
    r_full.forward()
    r_full.finish()
    give = copy(full.at[own_half], full.at[own_half], d_s.at[1], d_r.at[1], partner)
    give.start()

    r_by[0].finish()
    grad_gram[...] += gram(gb[:, z].reshape(4 * NOISE, WB), cg[:, :, WA:].reshape(4 * CLEAN_ROWS, WB))
    copy(full.at[other_half], full.at[other_half], d_s.at[1], d_r.at[1], partner).wait_recv()

    def row_dot(j):
        terms = [grad_gram[g * SEG:(g + 1) * SEG] * full[g * SEG:(g + 1) * SEG] for g in range(j, 8, 2)]
        rows_sum = jnp.sum(terms[0] + terms[1] + terms[2] + terms[3], axis=0, keepdims=True)
        return jnp.broadcast_to(jnp.sum(rows_sum, axis=1, keepdims=True), (8, LANES))

    place = lax.broadcasted_iota(jnp.int32, (8, LANES), 0)
    tile = jnp.where(place == 2 * z, row_dot(0), jnp.where(place == 2 * z + 1, row_dot(1), 0.0))

    sends = []

    def send_tile(buf, value, me, n, dev, base):
        buf[me] = value
        for r in range(1, n):
            out = copy(buf.at[me], buf.at[me], v_s.at[base + r], v_r.at[base + r], dev(r))
            out.start()
            sends.append(out)

    def sum_tiles(buf, me, n, base):
        for r in range(1, n):
            origin = buf.at[lax.rem(me + n - r, n)]
            copy(origin, origin, v_s.at[base + r], v_r.at[base + r], partner).wait_recv()
        return jnp.sum(buf[...], axis=0)

    send_tile(sv1, tile, t, 8, lambda r: (z, y, lax.rem(t + r, 8)), 0)

    for r in range(4):
        block = ao.at[mod4(x + 4 - r), there]
        copy(block, block, k_s.at[r], k_r.at[r], partner).wait_recv()

    def turn(k, carry):
        for q in range(4):
            span = pl.ds(q * LANES, LANES)
            ata[k, span, :] = ao[q, k].reshape(4 * NOISE, LANES).T
            atb[k, span, :] = ao[q, :, k].reshape(4 * NOISE, LANES).T
        return carry

    lax.fori_loop(0, 4, turn, 0)

    tile = sum_tiles(sv1, t, 8, 0)
    send_tile(sv2, tile, 4 * z + y, 16, cell, 8)
    for k in (3, 1):
        r_az[k].forward()
        r_by[k].forward()
    r_az[2].forward()
    r_by[2].forward()
    tile = sum_tiles(sv2, 4 * z + y, 16, 8)
    weights = jnp.maximum(-tile, 0.0) / jnp.sum(jnp.abs(tile), axis=0, keepdims=True)
    wts[...] = weights
    for k in range(4):
        scale[k, :SEG] = jnp.broadcast_to(wts[2 * k:2 * k + 1, :], (SEG, LANES))
        scale[k, SEG:] = jnp.broadcast_to(wts[2 * k + 1:2 * k + 2, :], (SEG, LANES))
    lane = lax.broadcasted_iota(jnp.int32, (1, LANES), 1)
    wout_ref[...] = jnp.where(lane == 0, wts[pl.ds(2 * z, 1), :], wts[pl.ds(2 * z + 1, 1), :])[:, :2]

    def scaled(raw, s):
        full = jnp.concatenate([s, s], axis=1)
        return (raw.astype(F32) * full).astype(BF16)

    def product(at, pieces_of, width, base, first):
        def step(i, carry):
            cols = pl.ds(pl.multiple_of(i * 256, 256), 256)
            dest = pl.ds(pl.multiple_of(base + i * 256, 256), 256)
            right = jnp.concatenate([scaled(raw, s) for raw, s in pieces_of(cols)], axis=0)
            value = jnp.dot(at[...], right, preferred_element_type=F32)
            if first:
                acc[:, dest] = value
            else:
                acc[:, dest] += value
            return carry

        lax.fori_loop(0, width // 256, step, 0)

    def add_a(k, first=False):
        v = mod4(z + k)
        product(ata.at[v], lambda cols: [(ga[v, i, :, cols], scale[v]) for i in range(4)], WA, 0, first)

    def add_b(k, first=False):
        v = mod4(y + k)
        product(atb.at[v], lambda cols: [(gb[v, i, :, cols], scale[i]) for i in range(4)], WB, WA, first)

    add_a(0, True)
    add_b(0, True)
    for k in (3, 1):
        add_a(k)
        add_b(k)
    for k in (0, 3, 1, 2):
        r_az[k].finish()
    add_a(2)
    out_a = pltpu.make_async_copy(acc.at[:, pl.ds(0, WA)], out_ref.at[:, pl.ds(0, WA)], o_s.at[0])
    out_a.start()
    for k in (3, 1, 2):
        r_by[k].finish()
    add_b(2)
    out_b = pltpu.make_async_copy(acc.at[:, pl.ds(WA, WB)], out_ref.at[:, pl.ds(WA, WB)], o_s.at[1])
    out_b.start()

    for far_copy, _, same in pieces:
        @pl.when(jnp.logical_not(same))
        def _():
            far_copy.wait_send()
    for ring in rings:
        ring.drain()
    for k in core + [swap, give] + share + sends:
        k.wait_send()
    out_a.wait()
    out_b.wait()


def body(activations, cotangents, row_ids, row_counts):
    dma = pltpu.SemaphoreType.DMA
    vmem = pltpu.VMEM
    return pl.pallas_call(
        body_kernel,
        out_shape=(jax.ShapeDtypeStruct((512, WA + WB), F32), jax.ShapeDtypeStruct((1, 2), F32)),
        in_specs=[pl.BlockSpec(memory_space=pltpu.SMEM)] * 2 + [pl.BlockSpec(memory_space=pltpu.VMEM)] * 2,
        out_specs=(pl.BlockSpec(memory_space=pl.ANY), pl.BlockSpec(memory_space=pltpu.VMEM)),
        scratch_shapes=[
            vmem((4, NOISE, 1024), BF16),
            vmem((4, CLEAN_ROWS, 1024), BF16),
            vmem((4, CLEAN_ROWS, WA + WB), BF16),
            vmem((4, 4, NOISE, WA), BF16),
            vmem((4, 4, NOISE, WB), BF16),
            vmem((4, 4, 4, NOISE, LANES), BF16),
            vmem((4, 512, 4 * NOISE), BF16),
            vmem((4, 512, 4 * NOISE), BF16),
            vmem((512, WA + WB), F32),
            vmem((4 * NOISE, 4 * CLEAN_ROWS), F32),
            vmem((4 * NOISE, 4 * CLEAN_ROWS), F32),
            vmem((4 * NOISE, 4 * CLEAN_ROWS), F32),
            vmem((2 * NOISE, 4 * CLEAN_ROWS), F32),
            vmem((2 * NOISE, 4 * CLEAN_ROWS), F32),
            vmem((48, 4 * CLEAN_ROWS), F32),
            vmem((40, 4 * CLEAN_ROWS), F32),
            vmem((2, SEG, 4 * CLEAN_ROWS), F32),
            vmem((8, 8, LANES), F32),
            vmem((16, 8, LANES), F32),
            vmem((8, LANES), F32),
            vmem((4, NOISE, LANES), F32),
            dma((15, 4)), dma((15, 4)),
            dma((8,)), dma((8,)), dma,
            dma((4,)), dma((4,)),
            dma((2,)), dma((2,)),
            dma((4,)), dma((4,)),
            dma((24,)), dma((24,)),
            dma((2,)),
        ],
        compiler_params=pltpu.CompilerParams(
            collective_id=0, has_side_effects=True, vmem_limit_bytes=60 * 1024 * 1024),
        cost_estimate=pl.CostEstimate(flops=8_000_000_000, bytes_accessed=8_000_000, transcendentals=0),
        name="reweight",
    )(row_ids, row_counts, activations, cotangents)


def solution(mesh):
    placed = (P("dp", "seq", "tensor"), P("dp", "seq", "tensor"), P("dp", None), P("dp", None))
    return jax.shard_map(
        body,
        mesh=mesh,
        in_specs=placed,
        out_specs=(P(("dp", "seq"), "tensor"), P("dp", None)),
        check_vma=False,
    )
```

```python
import jax
import jax.numpy as jnp
from jax import lax
from jax.experimental import pallas as pl
from jax.experimental.pallas import tpu as pltpu
from jax.sharding import PartitionSpec as P

MESH = pl.DeviceIdType.MESH
F32 = jnp.float32
BF16 = jnp.bfloat16

SEG = 88
NOISE = 176
CLEAN_ROWS = 96
WA = 768
WB = 1024
LANES = 128


def body_kernel(ids_ref, counts_ref, acts_ref, cot_ref, out_ref, wout_ref,
                na, ca, cg, ga, gb, hop, ao, ata, atb, acc, part_gram, grad_gram, full, d2, sm,
                near_a, near_b, x3, sv1, sv2, wts, scale,
                ring_s, ring_r, h_s, h_r, p_s, p_r, p_l, k_s, k_r,
                d_s, d_r, m_s, m_r, v_s, v_r, o_s):
    z = lax.axis_index("dp")
    y = lax.axis_index("seq")
    t = lax.axis_index("tensor")
    x = t // 2
    c = lax.rem(t, 2)

    def mod4(v):
        return lax.rem(v, 4)

    def copy(src, dst, s, r, dev):
        return pltpu.make_async_remote_copy(
            src_ref=src, dst_ref=dst, send_sem=s, recv_sem=r, device_id=dev, device_id_type=MESH)

    barrier = pltpu.get_barrier_semaphore()

    def greet(dev):
        pl.semaphore_signal(barrier, inc=1, device_id=dev, device_id_type=MESH)

    def cell(r):
        other = lax.rem(4 * z + y + r, 16)
        return other // 4, lax.rem(other, 4), t

    for r in range(1, 16):
        greet(cell(r))
    for r in range(1, 8):
        greet((z, y, lax.rem(t + r, 8)))

    targets = [(r, h, (mod4(x + r), 2 * c + h, 2 * x + z // 2)) for r in range(4) for h in range(2)]
    target_self = [(dev[0] == z) & (dev[1] == y) & (c == z // 2) for _, _, dev in targets]
    sources = [(2 * c + i // 4, i % 4) for i in range(8)]
    source_self = [(zs == z) & (ys == y) & (c == y // 2) for zs, ys in sources]
    for (_, _, dev), same in zip(targets, target_self):
        @pl.when(jnp.logical_not(same))
        def _():
            greet(dev)
    for (zs, ys), same in zip(sources, source_self):
        @pl.when(jnp.logical_not(same))
        def _():
            greet((zs, ys, 2 * x + y // 2))
    has_self = ((c == y // 2) & (c == z // 2)).astype(jnp.int32)

    rid = [ids_ref[0, j] for j in range(3)]
    live = [counts_ref[0, rid[j]] - y * SEG for j in range(3)]
    rows = lax.broadcasted_iota(jnp.int32, (SEG, LANES), 0)
    pad = jnp.zeros((CLEAN_ROWS - SEG, LANES), F32)

    def stage_acts(i, carry):
        cols = pl.ds(pl.multiple_of(i * LANES, LANES), LANES)
        part = [acts_ref[rid[j], :, cols].astype(F32) for j in range(3)]
        na[y, :, cols] = jnp.concatenate([part[1], part[2]], axis=0).astype(BF16)
        ca[z, :, cols] = jnp.concatenate([part[0], pad], axis=0).astype(BF16)
        return carry

    lax.fori_loop(0, 1024 // LANES, stage_acts, 0)

    def masked(j, cols):
        return jnp.where(rows < live[j], cot_ref[rid[j], :, cols].astype(F32), 0.0)

    def stage_clean(i, carry):
        cols = pl.ds(pl.multiple_of(i * LANES, LANES), LANES)
        cg[z, :, cols] = jnp.concatenate([masked(0, cols), pad], axis=0).astype(BF16)
        return carry

    def stage_a(i, carry):
        cols = pl.ds(pl.multiple_of(i * LANES, LANES), LANES)
        ga[z, y, :, cols] = jnp.concatenate([masked(1, cols), masked(2, cols)], axis=0).astype(BF16)
        return carry

    def stage_b(i, carry):
        cols = pl.ds(pl.multiple_of(i * LANES, LANES), LANES)
        from_cols = pl.ds(pl.multiple_of(WA + i * LANES, LANES), LANES)
        gb[y, z, :, cols] = jnp.concatenate(
            [masked(1, from_cols), masked(2, from_cols)], axis=0).astype(BF16)
        return carry

    lax.fori_loop(0, WA // LANES, stage_a, 0)
    lax.fori_loop(0, (WA + WB) // LANES, stage_clean, 0)
    lax.fori_loop(0, WB // LANES, stage_b, 0)
    pl.semaphore_wait(barrier, 38 - 2 * has_self)

    hops = []
    for r in range(1, 4):
        q = mod4(x + r)
        for h in range(2):
            src = na.at[y, :, pl.ds(pl.multiple_of(h * 512 + q * LANES, LANES), LANES)]
            hops.append(copy(src, hop.at[r, h], h_s.at[r, h], h_r.at[r, h], (z, y, 2 * q + c)))
    for k in hops:
        k.start()

    pieces = []

    def send_piece(i):
        r, h, dev = targets[i]
        same = target_self[i]
        if r:
            src = hop.at[4 - r, h]
            copy(src, src, h_s.at[4 - r, h], h_r.at[4 - r, h], (z, y, lax.rem(t + 1, 8))).wait_recv()
        else:
            src = na.at[y, :, pl.ds(pl.multiple_of(h * 512 + x * LANES, LANES), LANES)]
        dst = ao.at[x, z, y]
        far_copy = copy(src, dst, p_s.at[i], p_r.at[lax.rem(z, 2) * 4 + y], dev)
        near_copy = pltpu.make_async_copy(src, dst, p_l)

        @pl.when(same)
        def _():
            near_copy.start()

        @pl.when(jnp.logical_not(same))
        def _():
            far_copy.start()
        pieces.append((far_copy, same))

    send_piece(0)
    send_piece(1)

    rings = []

    class Ring:
        def __init__(self, at, axis, first, second):
            n = len(rings)
            rings.append(self)
            me = {"x": x, "y": y, "z": z}[axis]

            def dev(v):
                return {"x": (z, y, 2 * v + c), "y": (z, v, t), "z": (v, y, t)}[axis]

            up, down, far = mod4(me + 1), mod4(me + 3), mod4(me + 2)
            own, low, high, opp = at(me), at(down), at(up), at(far)
            self.go = [copy(own, own, ring_s.at[n, 0], ring_r.at[n, 0], dev(up)),
                       copy(own, own, ring_s.at[n, 1], ring_r.at[n, 1], dev(down))]
            self.got = [copy(low, low, ring_s.at[n, 0], ring_r.at[n, 0], dev(up)),
                        copy(high, high, ring_s.at[n, 1], ring_r.at[n, 1], dev(down))]
            self.pass_on = [
                copy(low.at[first], low.at[first], ring_s.at[n, 2], ring_r.at[n, 2], dev(up)),
                copy(high.at[second], high.at[second], ring_s.at[n, 3], ring_r.at[n, 3], dev(down))]
            self.got_far = [
                copy(opp.at[first], opp.at[first], ring_s.at[n, 2], ring_r.at[n, 2], dev(up)),
                copy(opp.at[second], opp.at[second], ring_s.at[n, 3], ring_r.at[n, 3], dev(down))]

        def start(self):
            for k in self.go:
                k.start()

        def forward(self):
            for k in range(2):
                self.got[k].wait_recv()
                self.pass_on[k].start()

        def finish(self):
            for k in self.got_far:
                k.wait_recv()

        def drain(self):
            for k in self.go + self.pass_on:
                k.wait_send()

    def halves(width):
        half = width // 2
        return (slice(None), pl.ds(0, half)), (slice(None), pl.ds(half, half))

    def az_ring(k):
        item = mod4(y + k)
        return Ring(lambda v: ga.at[v, item], "z", *halves(WA))

    def by_ring(k):
        item = mod4(z + k)
        return Ring(lambda v: gb.at[v, item], "y", *halves(WB))

    def rows_of(chunk):
        return pl.ds(pl.multiple_of(chunk * SEG, 8), SEG)

    r_na = Ring(lambda v: na.at[v], "y", *halves(1024))
    r_ca = Ring(lambda v: ca.at[v], "z", *halves(1024))
    r_cg = Ring(lambda v: cg.at[v], "z", *halves(WA + WB))
    r_ay = Ring(lambda v: ga.at[z, v], "y", *halves(WA))
    r_bz = Ring(lambda v: gb.at[y, v], "z", *halves(WB))
    r_az = {k: az_ring(k) for k in (0, 3, 1, 2)}
    r_by = {k: by_ring(k) for k in (0, 3, 1, 2)}
    here = pl.ds(2 * c, 2)
    there = pl.ds(2 * (1 - c), 2)
    r_ao = Ring(lambda v: ao.at[v, here], "x", (pl.ds(0, 1),), (pl.ds(1, 1),))
    r_full = Ring(lambda v: full.at[rows_of(4 * c + v)], "x", (pl.ds(0, 48),), (pl.ds(48, 40),))

    r_na.start()
    r_ca.start()
    r_ay.start()
    r_cg.start()
    r_bz.start()
    for i in range(2, 8):
        send_piece(i)

    r_na.forward()
    r_by[0].start()
    for i, ((zs, ys), same) in enumerate(zip(sources, source_self)):
        dst = ao.at[x, zs, ys]
        far_copy = copy(dst, dst, p_s.at[i], p_r.at[i], (z, y, lax.rem(t + 1, 8)))
        near_copy = pltpu.make_async_copy(dst, dst, p_l)

        @pl.when(same)
        def _():
            near_copy.wait()

        @pl.when(jnp.logical_not(same))
        def _():
            far_copy.wait_recv()
    mine = ao.at[x, here]
    partner = (z, y, 2 * x + 1 - c)
    r_ao.start()
    core = [copy(mine, mine, k_s.at[0], k_r.at[0], partner)]
    core[0].start()

    r_ca.forward()
    r_cg.forward()
    r_az[0].start()
    r_ay.forward()
    r_az[3].start()
    r_az[1].start()
    r_bz.forward()

    def relay(r):
        block = ao.at[mod4(x + 4 - r), here]
        core.append(copy(block, block, k_s.at[r], k_r.at[r], partner))
        core[-1].start()

    r_ao.forward()
    relay(1)
    relay(3)

    contract = (((1,), (1,)), ((), ()))

    def gram(left, right):
        return lax.dot_general(left, right, contract, preferred_element_type=F32)

    r_na.finish()
    r_ca.finish()
    part_gram[...] = gram(na[...].reshape(4 * NOISE, 1024), ca[...].reshape(4 * CLEAN_ROWS, 1024))
    own_half = pl.ds(pl.multiple_of(c * 352, 8), 352)
    other_half = pl.ds(pl.multiple_of((1 - c) * 352, 8), 352)
    swap = copy(part_gram.at[other_half], d2, d_s.at[0], d_r.at[0], partner)
    swap.start()

    r_by[0].forward()
    r_by[3].start()
    r_by[1].start()
    r_ao.finish()
    relay(2)

    swap.wait_recv()
    sm[...] = part_gram[own_half] + d2[...]
    up, down, across = mod4(x + 1), mod4(x + 3), mod4(x + 2)
    dev_up, dev_down = (z, y, 2 * up + c), (z, y, 2 * down + c)
    first = pl.ds(pl.multiple_of(across * SEG, 8), 48)
    second = pl.ds(pl.multiple_of(across * SEG + 48, 8), 40)
    share = [copy(sm.at[first], near_a, m_s.at[0], m_r.at[0], dev_up),
             copy(sm.at[second], near_b, m_s.at[1], m_r.at[1], dev_down),
             copy(sm.at[rows_of(up)], x3.at[0], m_s.at[2], m_r.at[2], dev_up),
             copy(sm.at[rows_of(down)], x3.at[1], m_s.at[3], m_r.at[3], dev_down)]
    share[0].start()
    share[1].start()
    r_az[0].forward()
    share[0].wait_recv()
    sm[pl.ds(pl.multiple_of(up * SEG, 8), 48)] += near_a[...]
    share[2].start()
    share[1].wait_recv()
    sm[pl.ds(pl.multiple_of(down * SEG + 48, 8), 40)] += near_b[...]
    share[3].start()

    r_cg.finish()
    r_ay.finish()
    r_az[2].start()
    grad_gram[...] = gram(ga[z].reshape(4 * NOISE, WA), cg[:, :, :WA].reshape(4 * CLEAN_ROWS, WA))

    share[2].wait_recv()
    share[3].wait_recv()
    full[rows_of(4 * c + x)] = sm[rows_of(x)] + x3[0] + x3[1]
    r_full.start()
    r_bz.finish()
    r_by[2].start()
    r_full.forward()
    r_full.finish()
    give = copy(full.at[own_half], full.at[own_half], d_s.at[1], d_r.at[1], partner)
    give.start()

    r_by[0].finish()
    grad_gram[...] += gram(gb[:, z].reshape(4 * NOISE, WB), cg[:, :, WA:].reshape(4 * CLEAN_ROWS, WB))
    copy(full.at[other_half], full.at[other_half], d_s.at[1], d_r.at[1], partner).wait_recv()

    def row_dot(j):
        terms = [grad_gram[g * SEG:(g + 1) * SEG] * full[g * SEG:(g + 1) * SEG] for g in range(j, 8, 2)]
        rows_sum = jnp.sum(terms[0] + terms[1] + terms[2] + terms[3], axis=0, keepdims=True)
        return jnp.broadcast_to(jnp.sum(rows_sum, axis=1, keepdims=True), (8, LANES))

    place = lax.broadcasted_iota(jnp.int32, (8, LANES), 0)
    tile = jnp.where(place == 2 * z, row_dot(0), jnp.where(place == 2 * z + 1, row_dot(1), 0.0))

    sends = []

    def send_tile(buf, value, me, n, dev, base):
        buf[me] = value
        for r in range(1, n):
            out = copy(buf.at[me], buf.at[me], v_s.at[base + r], v_r.at[base + r], dev(r))
            out.start()
            sends.append(out)

    def sum_tiles(buf, me, n, base):
        for r in range(1, n):
            origin = buf.at[lax.rem(me + n - r, n)]
            copy(origin, origin, v_s.at[base + r], v_r.at[base + r], partner).wait_recv()
        return jnp.sum(buf[...], axis=0)

    send_tile(sv1, tile, t, 8, lambda r: (z, y, lax.rem(t + r, 8)), 0)

    for r in range(4):
        block = ao.at[mod4(x + 4 - r), there]
        copy(block, block, k_s.at[r], k_r.at[r], partner).wait_recv()

    def turn(k, carry):
        for q in range(4):
            span = pl.ds(q * LANES, LANES)
            ata[k, span, :] = ao[q, k].reshape(4 * NOISE, LANES).T
            atb[k, span, :] = ao[q, :, k].reshape(4 * NOISE, LANES).T
        return carry

    lax.fori_loop(0, 4, turn, 0)

    tile = sum_tiles(sv1, t, 8, 0)
    send_tile(sv2, tile, 4 * z + y, 16, cell, 8)
    for k in (3, 1):
        r_az[k].forward()
        r_by[k].forward()
    r_az[2].forward()
    r_by[2].forward()
    tile = sum_tiles(sv2, 4 * z + y, 16, 8)
    weights = jnp.maximum(-tile, 0.0) / jnp.sum(jnp.abs(tile), axis=0, keepdims=True)
    wts[...] = weights
    for k in range(4):
        scale[k, :SEG] = jnp.broadcast_to(wts[2 * k:2 * k + 1, :], (SEG, LANES))
        scale[k, SEG:] = jnp.broadcast_to(wts[2 * k + 1:2 * k + 2, :], (SEG, LANES))
    lane = lax.broadcasted_iota(jnp.int32, (1, LANES), 1)
    wout_ref[...] = jnp.where(lane == 0, wts[pl.ds(2 * z, 1), :], wts[pl.ds(2 * z + 1, 1), :])[:, :2]

    def scaled(raw, s):
        full = jnp.concatenate([s, s], axis=1)
        return (raw.astype(F32) * full).astype(BF16)

    def product(at, pieces_of, width, base, first):
        def step(i, carry):
            cols = pl.ds(pl.multiple_of(i * 256, 256), 256)
            dest = pl.ds(pl.multiple_of(base + i * 256, 256), 256)
            right = jnp.concatenate([scaled(raw, s) for raw, s in pieces_of(cols)], axis=0)
            value = jnp.dot(at[...], right, preferred_element_type=F32)
            if first:
                acc[:, dest] = value
            else:
                acc[:, dest] += value
            return carry

        lax.fori_loop(0, width // 256, step, 0)

    def add_a(k, first=False):
        v = mod4(z + k)
        product(ata.at[v], lambda cols: [(ga[v, i, :, cols], scale[v]) for i in range(4)], WA, 0, first)

    def add_b(k, first=False):
        v = mod4(y + k)
        product(atb.at[v], lambda cols: [(gb[v, i, :, cols], scale[i]) for i in range(4)], WB, WA, first)

    add_a(0, True)
    add_b(0, True)
    for k in (3, 1):
        add_a(k)
        add_b(k)
    for k in (0, 3, 1, 2):
        r_az[k].finish()
    add_a(2)
    out_a = pltpu.make_async_copy(acc.at[:, pl.ds(0, WA)], out_ref.at[:, pl.ds(0, WA)], o_s.at[0])
    out_a.start()
    for k in (3, 1, 2):
        r_by[k].finish()
    add_b(2)
    out_b = pltpu.make_async_copy(acc.at[:, pl.ds(WA, WB)], out_ref.at[:, pl.ds(WA, WB)], o_s.at[1])
    out_b.start()

    for far_copy, same in pieces:
        @pl.when(jnp.logical_not(same))
        def _():
            far_copy.wait_send()
    for ring in rings:
        ring.drain()
    for k in hops + core + [swap, give] + share + sends:
        k.wait_send()
    out_a.wait()
    out_b.wait()


def body(activations, cotangents, row_ids, row_counts):
    dma = pltpu.SemaphoreType.DMA
    vmem = pltpu.VMEM
    return pl.pallas_call(
        body_kernel,
        out_shape=(jax.ShapeDtypeStruct((512, WA + WB), F32), jax.ShapeDtypeStruct((1, 2), F32)),
        in_specs=[pl.BlockSpec(memory_space=pltpu.SMEM)] * 2 + [pl.BlockSpec(memory_space=pltpu.VMEM)] * 2,
        out_specs=(pl.BlockSpec(memory_space=pl.ANY), pl.BlockSpec(memory_space=pltpu.VMEM)),
        scratch_shapes=[
            vmem((4, NOISE, 1024), BF16),
            vmem((4, CLEAN_ROWS, 1024), BF16),
            vmem((4, CLEAN_ROWS, WA + WB), BF16),
            vmem((4, 4, NOISE, WA), BF16),
            vmem((4, 4, NOISE, WB), BF16),
            vmem((4, 2, NOISE, LANES), BF16),
            vmem((4, 4, 4, NOISE, LANES), BF16),
            vmem((4, 512, 4 * NOISE), BF16),
            vmem((4, 512, 4 * NOISE), BF16),
            vmem((512, WA + WB), F32),
            vmem((4 * NOISE, 4 * CLEAN_ROWS), F32),
            vmem((4 * NOISE, 4 * CLEAN_ROWS), F32),
            vmem((4 * NOISE, 4 * CLEAN_ROWS), F32),
            vmem((2 * NOISE, 4 * CLEAN_ROWS), F32),
            vmem((2 * NOISE, 4 * CLEAN_ROWS), F32),
            vmem((48, 4 * CLEAN_ROWS), F32),
            vmem((40, 4 * CLEAN_ROWS), F32),
            vmem((2, SEG, 4 * CLEAN_ROWS), F32),
            vmem((8, 8, LANES), F32),
            vmem((16, 8, LANES), F32),
            vmem((8, LANES), F32),
            vmem((4, NOISE, LANES), F32),
            dma((15, 4)), dma((15, 4)),
            dma((4, 2)), dma((4, 2)),
            dma((8,)), dma((8,)), dma,
            dma((4,)), dma((4,)),
            dma((2,)), dma((2,)),
            dma((4,)), dma((4,)),
            dma((24,)), dma((24,)),
            dma((2,)),
        ],
        compiler_params=pltpu.CompilerParams(
            collective_id=0, has_side_effects=True, vmem_limit_bytes=60 * 1024 * 1024),
        cost_estimate=pl.CostEstimate(flops=8_000_000_000, bytes_accessed=8_000_000, transcendentals=0),
        name="reweight",
    )(row_ids, row_counts, activations, cotangents)


def solution(mesh):
    placed = (P("dp", "seq", "tensor"), P("dp", "seq", "tensor"), P("dp", None), P("dp", None))
    return jax.shard_map(
        body,
        mesh=mesh,
        in_specs=placed,
        out_specs=(P(("dp", "seq"), "tensor"), P("dp", None)),
        check_vma=False,
    )
```

```python
import jax
import jax.numpy as jnp
from jax import lax
from jax.experimental import pallas as pl
from jax.experimental.pallas import tpu as pltpu
from jax.sharding import PartitionSpec as P

MESH = pl.DeviceIdType.MESH
F32 = jnp.float32
BF16 = jnp.bfloat16

SEG = 88
NOISE = 176
CLEAN_ROWS = 96
WA = 768
WB = 1024
LANES = 128


def body_kernel(ids_ref, counts_ref, acts_ref, cot_ref, out_ref, wout_ref,
                na, ca, cg, ga, gb, ao, ata, atb, part_gram, grad_gram, full, d2, sm,
                near_a, near_b, x3, sv1, sv2, wts, scale,
                ring_s, ring_r, p_s, p_r, p_l, k_s, k_r,
                d_s, d_r, m_s, m_r, v_s, v_r):
    z = lax.axis_index("dp")
    y = lax.axis_index("seq")
    t = lax.axis_index("tensor")
    x = t // 2
    c = lax.rem(t, 2)

    def mod4(v):
        return lax.rem(v, 4)

    def copy(src, dst, s, r, dev):
        return pltpu.make_async_remote_copy(
            src_ref=src, dst_ref=dst, send_sem=s, recv_sem=r, device_id=dev, device_id_type=MESH)

    barrier = pltpu.get_barrier_semaphore()

    def greet(dev):
        pl.semaphore_signal(barrier, inc=1, device_id=dev, device_id_type=MESH)

    def cell(r):
        other = lax.rem(4 * z + y + r, 16)
        return other // 4, lax.rem(other, 4), t

    for r in range(1, 16):
        greet(cell(r))
    for r in range(1, 8):
        greet((z, y, lax.rem(t + r, 8)))

    targets = [(h, q, (x, 2 * c + h, 2 * q + z // 2)) for h in range(2) for q in range(4)]
    target_self = [(x == z) & (y == 2 * c + h) & (q == x) & (c == z // 2) for h, q, _ in targets]
    sources = [(2 * c + i // 4, i % 4) for i in range(8)]
    source_self = [(zs == z) & (ys == y) & (x == z) & (c == y // 2) for zs, ys in sources]
    for (_, _, dev), same in zip(targets, target_self):
        @pl.when(jnp.logical_not(same))
        def _():
            greet(dev)
    for (zs, ys), same in zip(sources, source_self):
        @pl.when(jnp.logical_not(same))
        def _():
            greet((zs, ys, 2 * z + y // 2))
    has_self = ((x == z) & (c == y // 2) & (c == z // 2)).astype(jnp.int32)

    rid = [ids_ref[0, j] for j in range(3)]
    live = [counts_ref[0, rid[j]] - y * SEG for j in range(3)]
    rows = lax.broadcasted_iota(jnp.int32, (SEG, LANES), 0)
    pad = jnp.zeros((CLEAN_ROWS - SEG, LANES), F32)

    def stage_acts(i, carry):
        cols = pl.ds(pl.multiple_of(i * LANES, LANES), LANES)
        part = [acts_ref[rid[j], :, cols].astype(F32) for j in range(3)]
        na[y, :, cols] = jnp.concatenate([part[1], part[2]], axis=0).astype(BF16)
        ca[z, :, cols] = jnp.concatenate([part[0], pad], axis=0).astype(BF16)
        return carry

    lax.fori_loop(0, 1024 // LANES, stage_acts, 0)

    def masked(j, cols):
        return jnp.where(rows < live[j], cot_ref[rid[j], :, cols].astype(F32), 0.0)

    def stage_clean(i, carry):
        cols = pl.ds(pl.multiple_of(i * LANES, LANES), LANES)
        cg[z, :, cols] = jnp.concatenate([masked(0, cols), pad], axis=0).astype(BF16)
        return carry

    def stage_a(i, carry):
        cols = pl.ds(pl.multiple_of(i * LANES, LANES), LANES)
        ga[z, y, :, cols] = jnp.concatenate([masked(1, cols), masked(2, cols)], axis=0).astype(BF16)
        return carry

    def stage_b(i, carry):
        cols = pl.ds(pl.multiple_of(i * LANES, LANES), LANES)
        from_cols = pl.ds(pl.multiple_of(WA + i * LANES, LANES), LANES)
        gb[y, z, :, cols] = jnp.concatenate(
            [masked(1, from_cols), masked(2, from_cols)], axis=0).astype(BF16)
        return carry

    pl.semaphore_wait(barrier, 38 - 2 * has_self)

    pieces = []
    for i, ((h, q, dev), same) in enumerate(zip(targets, target_self)):
        src = na.at[y, :, pl.ds(h * 512 + q * LANES, LANES)]
        dst = ao.at[q, z, y]
        far_copy = copy(src, dst, p_s.at[i], p_r.at[lax.rem(z, 2) * 4 + y], dev)
        near_copy = pltpu.make_async_copy(src, dst, p_l)

        @pl.when(same)
        def _():
            near_copy.start()

        @pl.when(jnp.logical_not(same))
        def _():
            far_copy.start()
        pieces.append((far_copy, near_copy, same))

    rings = []

    class Ring:
        def __init__(self, at, axis, first, second):
            n = len(rings)
            rings.append(self)
            me = {"x": x, "y": y, "z": z}[axis]

            def dev(v):
                return {"x": (z, y, 2 * v + c), "y": (z, v, t), "z": (v, y, t)}[axis]

            up, down, far = mod4(me + 1), mod4(me + 3), mod4(me + 2)
            own, low, high, opp = at(me), at(down), at(up), at(far)
            self.go = [copy(own, own, ring_s.at[n, 0], ring_r.at[n, 0], dev(up)),
                       copy(own, own, ring_s.at[n, 1], ring_r.at[n, 1], dev(down))]
            self.got = [copy(low, low, ring_s.at[n, 0], ring_r.at[n, 0], dev(up)),
                        copy(high, high, ring_s.at[n, 1], ring_r.at[n, 1], dev(down))]
            self.pass_on = [
                copy(low.at[first], low.at[first], ring_s.at[n, 2], ring_r.at[n, 2], dev(up)),
                copy(high.at[second], high.at[second], ring_s.at[n, 3], ring_r.at[n, 3], dev(down))]
            self.got_far = [
                copy(opp.at[first], opp.at[first], ring_s.at[n, 2], ring_r.at[n, 2], dev(up)),
                copy(opp.at[second], opp.at[second], ring_s.at[n, 3], ring_r.at[n, 3], dev(down))]

        def start(self):
            for k in self.go:
                k.start()

        def forward(self):
            for k in range(2):
                self.got[k].wait_recv()
                self.pass_on[k].start()

        def finish(self):
            for k in self.got_far:
                k.wait_recv()

        def drain(self):
            for k in self.go + self.pass_on:
                k.wait_send()

    def halves(width):
        half = width // 2
        return (slice(None), pl.ds(0, half)), (slice(None), pl.ds(half, half))

    def az_ring(k):
        item = mod4(y + k)
        return Ring(lambda v: ga.at[v, item], "z", *halves(WA))

    def by_ring(k):
        item = mod4(z + k)
        return Ring(lambda v: gb.at[v, item], "y", *halves(WB))

    def rows_of(chunk):
        return pl.ds(pl.multiple_of(chunk * SEG, 8), SEG)

    r_na = Ring(lambda v: na.at[v], "y", *halves(1024))
    r_ca = Ring(lambda v: ca.at[v], "z", *halves(1024))
    r_cg = Ring(lambda v: cg.at[v], "z", *halves(WA + WB))
    r_ay = Ring(lambda v: ga.at[z, v], "y", *halves(WA))
    r_bz = Ring(lambda v: gb.at[y, v], "z", *halves(WB))
    r_az = {k: az_ring(k) for k in (0, 3, 1, 2)}
    r_by = {k: by_ring(k) for k in (0, 3, 1, 2)}
    here = pl.ds(2 * c, 2)
    there = pl.ds(2 * (1 - c), 2)
    r_ao = Ring(lambda v: ao.at[v, here], "x", (pl.ds(0, 1),), (pl.ds(1, 1),))
    r_full = Ring(lambda v: full.at[rows_of(4 * c + v)], "x", (pl.ds(0, 48),), (pl.ds(48, 40),))

    r_na.start()
    r_ca.start()
    lax.fori_loop(0, WA // LANES, stage_a, 0)
    r_ay.start()
    lax.fori_loop(0, (WA + WB) // LANES, stage_clean, 0)
    r_cg.start()
    lax.fori_loop(0, WB // LANES, stage_b, 0)
    r_bz.start()

    r_na.forward()
    r_by[0].start()
    for i, ((zs, ys), same) in enumerate(zip(sources, source_self)):
        dst = ao.at[x, zs, ys]
        far_copy = copy(dst, dst, p_s.at[i], p_r.at[i], (z, y, lax.rem(t + 1, 8)))
        near_copy = pltpu.make_async_copy(dst, dst, p_l)

        @pl.when(same)
        def _():
            near_copy.wait()

        @pl.when(jnp.logical_not(same))
        def _():
            far_copy.wait_recv()
    mine = ao.at[x, here]
    partner = (z, y, 2 * x + 1 - c)
    r_ao.start()
    core = [copy(mine, mine, k_s.at[0], k_r.at[0], partner)]
    core[0].start()

    r_ca.forward()
    r_cg.forward()
    r_az[0].start()
    r_ay.forward()
    r_az[3].start()
    r_az[1].start()
    r_bz.forward()

    def relay(r):
        block = ao.at[mod4(x + 4 - r), here]
        core.append(copy(block, block, k_s.at[r], k_r.at[r], partner))
        core[-1].start()

    r_ao.forward()
    relay(1)
    relay(3)

    contract = (((1,), (1,)), ((), ()))

    def gram(left, right):
        return lax.dot_general(left, right, contract, preferred_element_type=F32)

    r_na.finish()
    r_ca.finish()
    part_gram[...] = gram(na[...].reshape(4 * NOISE, 1024), ca[...].reshape(4 * CLEAN_ROWS, 1024))
    own_half = pl.ds(pl.multiple_of(c * 352, 8), 352)
    other_half = pl.ds(pl.multiple_of((1 - c) * 352, 8), 352)
    swap = copy(part_gram.at[other_half], d2, d_s.at[0], d_r.at[0], partner)
    swap.start()

    r_by[0].forward()
    r_by[3].start()
    r_by[1].start()
    r_ao.finish()
    relay(2)

    swap.wait_recv()
    sm[...] = part_gram[own_half] + d2[...]
    up, down, across = mod4(x + 1), mod4(x + 3), mod4(x + 2)
    dev_up, dev_down = (z, y, 2 * up + c), (z, y, 2 * down + c)
    first = pl.ds(pl.multiple_of(across * SEG, 8), 48)
    second = pl.ds(pl.multiple_of(across * SEG + 48, 8), 40)
    share = [copy(sm.at[first], near_a, m_s.at[0], m_r.at[0], dev_up),
             copy(sm.at[second], near_b, m_s.at[1], m_r.at[1], dev_down),
             copy(sm.at[rows_of(up)], x3.at[0], m_s.at[2], m_r.at[2], dev_up),
             copy(sm.at[rows_of(down)], x3.at[1], m_s.at[3], m_r.at[3], dev_down)]
    share[0].start()
    share[1].start()
    r_az[0].forward()
    share[0].wait_recv()
    sm[pl.ds(pl.multiple_of(up * SEG, 8), 48)] += near_a[...]
    share[2].start()
    share[1].wait_recv()
    sm[pl.ds(pl.multiple_of(down * SEG + 48, 8), 40)] += near_b[...]
    share[3].start()

    r_cg.finish()
    r_ay.finish()
    r_az[2].start()
    grad_gram[...] = gram(ga[z].reshape(4 * NOISE, WA), cg[:, :, :WA].reshape(4 * CLEAN_ROWS, WA))

    share[2].wait_recv()
    share[3].wait_recv()
    full[rows_of(4 * c + x)] = sm[rows_of(x)] + x3[0] + x3[1]
    r_full.start()
    r_bz.finish()
    r_by[2].start()
    r_full.forward()
    r_full.finish()
    give = copy(full.at[own_half], full.at[own_half], d_s.at[1], d_r.at[1], partner)
    give.start()

    r_by[0].finish()
    grad_gram[...] += gram(gb[:, z].reshape(4 * NOISE, WB), cg[:, :, WA:].reshape(4 * CLEAN_ROWS, WB))
    copy(full.at[other_half], full.at[other_half], d_s.at[1], d_r.at[1], partner).wait_recv()

    def row_dot(j):
        terms = [grad_gram[g * SEG:(g + 1) * SEG] * full[g * SEG:(g + 1) * SEG] for g in range(j, 8, 2)]
        rows_sum = jnp.sum(terms[0] + terms[1] + terms[2] + terms[3], axis=0, keepdims=True)
        return jnp.broadcast_to(jnp.sum(rows_sum, axis=1, keepdims=True), (8, LANES))

    place = lax.broadcasted_iota(jnp.int32, (8, LANES), 0)
    tile = jnp.where(place == 2 * z, row_dot(0), jnp.where(place == 2 * z + 1, row_dot(1), 0.0))

    sends = []

    def send_tile(buf, value, me, n, dev, base):
        buf[me] = value
        for r in range(1, n):
            out = copy(buf.at[me], buf.at[me], v_s.at[base + r], v_r.at[base + r], dev(r))
            out.start()
            sends.append(out)

    def sum_tiles(buf, me, n, base):
        for r in range(1, n):
            origin = buf.at[lax.rem(me + n - r, n)]
            copy(origin, origin, v_s.at[base + r], v_r.at[base + r], partner).wait_recv()
        return jnp.sum(buf[...], axis=0)

    send_tile(sv1, tile, t, 8, lambda r: (z, y, lax.rem(t + r, 8)), 0)

    for r in range(4):
        block = ao.at[mod4(x + 4 - r), there]
        copy(block, block, k_s.at[r], k_r.at[r], partner).wait_recv()

    def turn(k, carry):
        for q in range(4):
            span = pl.ds(q * LANES, LANES)
            ata[k, span, :] = ao[q, k].reshape(4 * NOISE, LANES).T
            atb[k, span, :] = ao[q, :, k].reshape(4 * NOISE, LANES).T
        return carry

    lax.fori_loop(0, 4, turn, 0)

    tile = sum_tiles(sv1, t, 8, 0)
    send_tile(sv2, tile, 4 * z + y, 16, cell, 8)
    for k in (3, 1):
        r_az[k].forward()
        r_by[k].forward()
    r_az[2].forward()
    r_by[2].forward()
    tile = sum_tiles(sv2, 4 * z + y, 16, 8)
    weights = jnp.maximum(-tile, 0.0) / jnp.sum(jnp.abs(tile), axis=0, keepdims=True)
    wts[...] = weights
    for k in range(4):
        scale[k, :SEG] = jnp.broadcast_to(wts[2 * k:2 * k + 1, :], (SEG, LANES))
        scale[k, SEG:] = jnp.broadcast_to(wts[2 * k + 1:2 * k + 2, :], (SEG, LANES))
    lane = lax.broadcasted_iota(jnp.int32, (1, LANES), 1)
    wout_ref[...] = jnp.where(lane == 0, wts[pl.ds(2 * z, 1), :], wts[pl.ds(2 * z + 1, 1), :])[:, :2]

    def scaled(raw, s):
        full = jnp.concatenate([s, s], axis=1)
        return (raw.astype(F32) * full).astype(BF16)

    def product(at, pieces_of, width, base, first):
        def step(i, carry):
            cols = pl.ds(pl.multiple_of(i * 256, 256), 256)
            dest = pl.ds(pl.multiple_of(base + i * 256, 256), 256)
            right = jnp.concatenate([scaled(raw, s) for raw, s in pieces_of(cols)], axis=0)
            value = jnp.dot(at[...], right, preferred_element_type=F32)
            if first:
                out_ref[:, dest] = value
            else:
                out_ref[:, dest] += value
            return carry

        lax.fori_loop(0, width // 256, step, 0)

    def add_a(k, first=False):
        v = mod4(z + k)
        product(ata.at[v], lambda cols: [(ga[v, i, :, cols], scale[v]) for i in range(4)], WA, 0, first)

    def add_b(k, first=False):
        v = mod4(y + k)
        product(atb.at[v], lambda cols: [(gb[v, i, :, cols], scale[i]) for i in range(4)], WB, WA, first)

    add_a(0, True)
    add_b(0, True)
    for k in (3, 1):
        add_a(k)
        add_b(k)
    for k in (0, 3, 1, 2):
        r_az[k].finish()
    add_a(2)
    for k in (3, 1, 2):
        r_by[k].finish()
    add_b(2)

    for far_copy, _, same in pieces:
        @pl.when(jnp.logical_not(same))
        def _():
            far_copy.wait_send()
    for ring in rings:
        ring.drain()
    for k in core + [swap, give] + share + sends:
        k.wait_send()


def body(activations, cotangents, row_ids, row_counts):
    dma = pltpu.SemaphoreType.DMA
    vmem = pltpu.VMEM
    return pl.pallas_call(
        body_kernel,
        out_shape=(pltpu.VMEM((512, WA + WB), F32), pltpu.VMEM((1, 2), F32)),
        in_specs=[pl.BlockSpec(memory_space=pltpu.SMEM)] * 2 + [pl.BlockSpec(memory_space=pltpu.VMEM)] * 2,
        out_specs=(pl.BlockSpec(memory_space=pltpu.VMEM), pl.BlockSpec(memory_space=pltpu.VMEM)),
        scratch_shapes=[
            vmem((4, NOISE, 1024), BF16),
            vmem((4, CLEAN_ROWS, 1024), BF16),
            vmem((4, CLEAN_ROWS, WA + WB), BF16),
            vmem((4, 4, NOISE, WA), BF16),
            vmem((4, 4, NOISE, WB), BF16),
            vmem((4, 4, 4, NOISE, LANES), BF16),
            vmem((4, 512, 4 * NOISE), BF16),
            vmem((4, 512, 4 * NOISE), BF16),
            vmem((4 * NOISE, 4 * CLEAN_ROWS), F32),
            vmem((4 * NOISE, 4 * CLEAN_ROWS), F32),
            vmem((4 * NOISE, 4 * CLEAN_ROWS), F32),
            vmem((2 * NOISE, 4 * CLEAN_ROWS), F32),
            vmem((2 * NOISE, 4 * CLEAN_ROWS), F32),
            vmem((48, 4 * CLEAN_ROWS), F32),
            vmem((40, 4 * CLEAN_ROWS), F32),
            vmem((2, SEG, 4 * CLEAN_ROWS), F32),
            vmem((8, 8, LANES), F32),
            vmem((16, 8, LANES), F32),
            vmem((8, LANES), F32),
            vmem((4, NOISE, LANES), F32),
            dma((15, 4)), dma((15, 4)),
            dma((8,)), dma((8,)), dma,
            dma((4,)), dma((4,)),
            dma((2,)), dma((2,)),
            dma((4,)), dma((4,)),
            dma((24,)), dma((24,)),
        ],
        compiler_params=pltpu.CompilerParams(
            collective_id=0, has_side_effects=True, vmem_limit_bytes=60 * 1024 * 1024),
        cost_estimate=pl.CostEstimate(flops=8_000_000_000, bytes_accessed=8_000_000, transcendentals=0),
        name="reweight",
    )(row_ids, row_counts, activations, cotangents)


def solution(mesh):
    placed = (P("dp", "seq", "tensor"), P("dp", "seq", "tensor"), P("dp", None), P("dp", None))
    return jax.shard_map(
        body,
        mesh=mesh,
        in_specs=placed,
        out_specs=(P(("dp", "seq"), "tensor"), P("dp", None)),
        check_vma=False,
    )
```

```python
import jax
import jax.numpy as jnp
from jax import lax
from jax.experimental import pallas as pl
from jax.experimental.pallas import tpu as pltpu
from jax.sharding import PartitionSpec as P

MESH = pl.DeviceIdType.MESH
F32 = jnp.float32
BF16 = jnp.bfloat16

SEG = 88
NOISE = 176
CLEAN_ROWS = 96
WA = 768
WB = 1024
LANES = 128


def body_kernel(ids_ref, counts_ref, acts_ref, cot_ref, out_ref, wout_ref,
                na, ca, cg, ga, gb, ao, ata, atb, part_gram, grad_gram, full, d2, sm,
                near_a, near_b, x3, sv1, sv2, wts, scale,
                ring_s, ring_r, p_s, p_r, p_l, k_s, k_r,
                d_s, d_r, m_s, m_r, v_s, v_r):
    z = lax.axis_index("dp")
    y = lax.axis_index("seq")
    t = lax.axis_index("tensor")
    x = t // 2
    c = lax.rem(t, 2)

    def mod4(v):
        return lax.rem(v, 4)

    def copy(src, dst, s, r, dev):
        return pltpu.make_async_remote_copy(
            src_ref=src, dst_ref=dst, send_sem=s, recv_sem=r, device_id=dev, device_id_type=MESH)

    barrier = pltpu.get_barrier_semaphore()

    def greet(dev):
        pl.semaphore_signal(barrier, inc=1, device_id=dev, device_id_type=MESH)

    def cell(r):
        other = lax.rem(4 * z + y + r, 16)
        return other // 4, lax.rem(other, 4), t

    for r in range(1, 16):
        greet(cell(r))
    for r in range(1, 8):
        greet((z, y, lax.rem(t + r, 8)))

    targets = [(h, q, (x, 2 * c + h, 2 * q + z // 2)) for h in range(2) for q in range(4)]
    target_self = [(x == z) & (y == 2 * c + h) & (q == x) & (c == z // 2) for h, q, _ in targets]
    sources = [(2 * c + i // 4, i % 4) for i in range(8)]
    source_self = [(zs == z) & (ys == y) & (x == z) & (c == y // 2) for zs, ys in sources]
    for (_, _, dev), same in zip(targets, target_self):
        @pl.when(jnp.logical_not(same))
        def _():
            greet(dev)
    for (zs, ys), same in zip(sources, source_self):
        @pl.when(jnp.logical_not(same))
        def _():
            greet((zs, ys, 2 * z + y // 2))
    has_self = ((x == z) & (c == y // 2) & (c == z // 2)).astype(jnp.int32)

    rid = [ids_ref[0, j] for j in range(3)]
    live = [counts_ref[0, rid[j]] - y * SEG for j in range(3)]
    rows = lax.broadcasted_iota(jnp.int32, (SEG, LANES), 0)
    pad = jnp.zeros((CLEAN_ROWS - SEG, LANES), F32)

    def stage_acts(i, carry):
        cols = pl.ds(pl.multiple_of(i * LANES, LANES), LANES)
        part = [acts_ref[rid[j], :, cols].astype(F32) for j in range(3)]
        na[y, :, cols] = jnp.concatenate([part[1], part[2]], axis=0).astype(BF16)
        ca[z, :, cols] = jnp.concatenate([part[0], pad], axis=0).astype(BF16)
        return carry

    lax.fori_loop(0, 1024 // LANES, stage_acts, 0)

    def masked(j, cols):
        return jnp.where(rows < live[j], cot_ref[rid[j], :, cols].astype(F32), 0.0)

    def stage_clean(i, carry):
        cols = pl.ds(pl.multiple_of(i * LANES, LANES), LANES)
        cg[z, :, cols] = jnp.concatenate([masked(0, cols), pad], axis=0).astype(BF16)
        return carry

    def stage_a(i, carry):
        cols = pl.ds(pl.multiple_of(i * LANES, LANES), LANES)
        ga[z, y, :, cols] = jnp.concatenate([masked(1, cols), masked(2, cols)], axis=0).astype(BF16)
        return carry

    def stage_b(i, carry):
        cols = pl.ds(pl.multiple_of(i * LANES, LANES), LANES)
        from_cols = pl.ds(pl.multiple_of(WA + i * LANES, LANES), LANES)
        gb[y, z, :, cols] = jnp.concatenate(
            [masked(1, from_cols), masked(2, from_cols)], axis=0).astype(BF16)
        return carry

    pl.semaphore_wait(barrier, 38 - 2 * has_self)

    pieces = []
    for i, ((h, q, dev), same) in enumerate(zip(targets, target_self)):
        src = na.at[y, :, pl.ds(h * 512 + q * LANES, LANES)]
        dst = ao.at[q, z, y]
        far_copy = copy(src, dst, p_s.at[i], p_r.at[lax.rem(z, 2) * 4 + y], dev)
        near_copy = pltpu.make_async_copy(src, dst, p_l)

        @pl.when(same)
        def _():
            near_copy.start()

        @pl.when(jnp.logical_not(same))
        def _():
            far_copy.start()
        pieces.append((far_copy, near_copy, same))

    rings = []

    class Ring:
        def __init__(self, at, axis, first, second):
            n = len(rings)
            rings.append(self)
            me = {"x": x, "y": y, "z": z}[axis]

            def dev(v):
                return {"x": (z, y, 2 * v + c), "y": (z, v, t), "z": (v, y, t)}[axis]

            up, down, far = mod4(me + 1), mod4(me + 3), mod4(me + 2)
            own, low, high, opp = at(me), at(down), at(up), at(far)
            self.go = [copy(own, own, ring_s.at[n, 0], ring_r.at[n, 0], dev(up)),
                       copy(own, own, ring_s.at[n, 1], ring_r.at[n, 1], dev(down))]
            self.got = [copy(low, low, ring_s.at[n, 0], ring_r.at[n, 0], dev(up)),
                        copy(high, high, ring_s.at[n, 1], ring_r.at[n, 1], dev(down))]
            self.pass_on = [
                copy(low.at[first], low.at[first], ring_s.at[n, 2], ring_r.at[n, 2], dev(up)),
                copy(high.at[second], high.at[second], ring_s.at[n, 3], ring_r.at[n, 3], dev(down))]
            self.got_far = [
                copy(opp.at[first], opp.at[first], ring_s.at[n, 2], ring_r.at[n, 2], dev(up)),
                copy(opp.at[second], opp.at[second], ring_s.at[n, 3], ring_r.at[n, 3], dev(down))]

        def start(self):
            for k in self.go:
                k.start()

        def forward(self):
            for k in range(2):
                self.got[k].wait_recv()
                self.pass_on[k].start()

        def finish(self):
            for k in self.got_far:
                k.wait_recv()

        def drain(self):
            for k in self.go + self.pass_on:
                k.wait_send()

    def halves(width):
        half = width // 2
        return (slice(None), pl.ds(0, half)), (slice(None), pl.ds(half, half))

    def az_ring(k):
        item = mod4(y + k)
        return Ring(lambda v: ga.at[v, item], "z", *halves(WA))

    def by_ring(k):
        item = mod4(z + k)
        return Ring(lambda v: gb.at[v, item], "y", *halves(WB))

    def rows_of(chunk):
        return pl.ds(pl.multiple_of(chunk * SEG, 8), SEG)

    r_na = Ring(lambda v: na.at[v], "y", *halves(1024))
    r_ca = Ring(lambda v: ca.at[v], "z", *halves(1024))
    r_cg = Ring(lambda v: cg.at[v], "z", *halves(WA + WB))
    r_ay = Ring(lambda v: ga.at[z, v], "y", *halves(WA))
    r_bz = Ring(lambda v: gb.at[y, v], "z", *halves(WB))
    r_az = {k: az_ring(k) for k in (0, 3, 1, 2)}
    r_by = {k: by_ring(k) for k in (0, 3, 1, 2)}
    here = pl.ds(2 * c, 2)
    there = pl.ds(2 * (1 - c), 2)
    r_ao = Ring(lambda v: ao.at[v, here], "x", (pl.ds(0, 1),), (pl.ds(1, 1),))
    r_full = Ring(lambda v: full.at[rows_of(4 * c + v)], "x", (pl.ds(0, 48),), (pl.ds(48, 40),))

    r_na.start()
    r_ca.start()
    lax.fori_loop(0, WA // LANES, stage_a, 0)
    r_ay.start()
    lax.fori_loop(0, (WA + WB) // LANES, stage_clean, 0)
    r_cg.start()
    lax.fori_loop(0, WB // LANES, stage_b, 0)

    r_ca.forward()
    r_bz.start()
    r_na.forward()
    r_by[0].start()
    for i, ((zs, ys), same) in enumerate(zip(sources, source_self)):
        dst = ao.at[x, zs, ys]
        far_copy = copy(dst, dst, p_s.at[i], p_r.at[i], (z, y, lax.rem(t + 1, 8)))
        near_copy = pltpu.make_async_copy(dst, dst, p_l)

        @pl.when(same)
        def _():
            near_copy.wait()

        @pl.when(jnp.logical_not(same))
        def _():
            far_copy.wait_recv()
    mine = ao.at[x, here]
    partner = (z, y, 2 * x + 1 - c)
    r_ao.start()
    core = [copy(mine, mine, k_s.at[0], k_r.at[0], partner)]
    core[0].start()

    def relay(r):
        block = ao.at[mod4(x + 4 - r), here]
        core.append(copy(block, block, k_s.at[r], k_r.at[r], partner))
        core[-1].start()

    r_cg.forward()
    r_az[0].start()
    r_ay.forward()

    contract = (((1,), (1,)), ((), ()))

    def gram(left, right):
        return lax.dot_general(left, right, contract, preferred_element_type=F32)

    r_na.finish()
    r_ca.finish()
    part_gram[...] = gram(na[...].reshape(4 * NOISE, 1024), ca[...].reshape(4 * CLEAN_ROWS, 1024))
    own_half = pl.ds(pl.multiple_of(c * 352, 8), 352)
    other_half = pl.ds(pl.multiple_of((1 - c) * 352, 8), 352)
    swap = copy(part_gram.at[other_half], d2, d_s.at[0], d_r.at[0], partner)
    swap.start()

    r_ao.forward()
    relay(1)
    relay(3)
    r_bz.forward()
    r_az[3].start()
    r_az[1].start()

    swap.wait_recv()
    sm[...] = part_gram[own_half] + d2[...]
    up, down, across = mod4(x + 1), mod4(x + 3), mod4(x + 2)
    dev_up, dev_down = (z, y, 2 * up + c), (z, y, 2 * down + c)
    first = pl.ds(pl.multiple_of(across * SEG, 8), 48)
    second = pl.ds(pl.multiple_of(across * SEG + 48, 8), 40)
    share = [copy(sm.at[first], near_a, m_s.at[0], m_r.at[0], dev_up),
             copy(sm.at[second], near_b, m_s.at[1], m_r.at[1], dev_down),
             copy(sm.at[rows_of(up)], x3.at[0], m_s.at[2], m_r.at[2], dev_up),
             copy(sm.at[rows_of(down)], x3.at[1], m_s.at[3], m_r.at[3], dev_down)]
    share[0].start()
    share[1].start()
    r_ao.finish()
    relay(2)
    r_by[0].forward()
    r_by[3].start()
    r_by[1].start()
    share[0].wait_recv()
    sm[pl.ds(pl.multiple_of(up * SEG, 8), 48)] += near_a[...]
    share[2].start()
    share[1].wait_recv()
    sm[pl.ds(pl.multiple_of(down * SEG + 48, 8), 40)] += near_b[...]
    share[3].start()

    r_cg.finish()
    r_ay.finish()
    r_az[2].start()
    grad_gram[...] = gram(ga[z].reshape(4 * NOISE, WA), cg[:, :, :WA].reshape(4 * CLEAN_ROWS, WA))

    share[2].wait_recv()
    share[3].wait_recv()
    full[rows_of(4 * c + x)] = sm[rows_of(x)] + x3[0] + x3[1]
    r_full.start()
    r_az[0].forward()
    r_full.forward()
    r_full.finish()
    give = copy(full.at[own_half], full.at[own_half], d_s.at[1], d_r.at[1], partner)
    give.start()

    r_bz.finish()
    r_by[2].start()
    r_by[0].finish()
    grad_gram[...] += gram(gb[:, z].reshape(4 * NOISE, WB), cg[:, :, WA:].reshape(4 * CLEAN_ROWS, WB))
    copy(full.at[other_half], full.at[other_half], d_s.at[1], d_r.at[1], partner).wait_recv()

    def row_dot(j):
        terms = [grad_gram[g * SEG:(g + 1) * SEG] * full[g * SEG:(g + 1) * SEG] for g in range(j, 8, 2)]
        rows_sum = jnp.sum(terms[0] + terms[1] + terms[2] + terms[3], axis=0, keepdims=True)
        return jnp.broadcast_to(jnp.sum(rows_sum, axis=1, keepdims=True), (8, LANES))

    place = lax.broadcasted_iota(jnp.int32, (8, LANES), 0)
    tile = jnp.where(place == 2 * z, row_dot(0), jnp.where(place == 2 * z + 1, row_dot(1), 0.0))

    sends = []

    def send_tile(buf, value, me, n, dev, base):
        buf[me] = value
        for r in range(1, n):
            out = copy(buf.at[me], buf.at[me], v_s.at[base + r], v_r.at[base + r], dev(r))
            out.start()
            sends.append(out)

    def sum_tiles(buf, me, n, base):
        for r in range(1, n):
            origin = buf.at[lax.rem(me + n - r, n)]
            copy(origin, origin, v_s.at[base + r], v_r.at[base + r], partner).wait_recv()
        return jnp.sum(buf[...], axis=0)

    send_tile(sv1, tile, t, 8, lambda r: (z, y, lax.rem(t + r, 8)), 0)

    for r in range(4):
        block = ao.at[mod4(x + 4 - r), there]
        copy(block, block, k_s.at[r], k_r.at[r], partner).wait_recv()

    def turn(k, carry):
        for q in range(4):
            span = pl.ds(q * LANES, LANES)
            ata[k, span, :] = ao[q, k].reshape(4 * NOISE, LANES).T
            atb[k, span, :] = ao[q, :, k].reshape(4 * NOISE, LANES).T
        return carry

    lax.fori_loop(0, 4, turn, 0)

    tile = sum_tiles(sv1, t, 8, 0)
    send_tile(sv2, tile, 4 * z + y, 16, cell, 8)
    r_az[3].forward()
    r_by[3].forward()
    tile = sum_tiles(sv2, 4 * z + y, 16, 8)
    weights = jnp.maximum(-tile, 0.0) / jnp.sum(jnp.abs(tile), axis=0, keepdims=True)
    wts[...] = weights
    for k in range(4):
        scale[k, :SEG] = jnp.broadcast_to(wts[2 * k:2 * k + 1, :], (SEG, LANES))
        scale[k, SEG:] = jnp.broadcast_to(wts[2 * k + 1:2 * k + 2, :], (SEG, LANES))
    lane = lax.broadcasted_iota(jnp.int32, (1, LANES), 1)
    wout_ref[...] = jnp.where(lane == 0, wts[pl.ds(2 * z, 1), :], wts[pl.ds(2 * z + 1, 1), :])[:, :2]

    def scaled(raw, s):
        full = jnp.concatenate([s, s], axis=1)
        return (raw.astype(F32) * full).astype(BF16)

    def product(at, pieces_of, width, base, first):
        def step(i, carry):
            cols = pl.ds(pl.multiple_of(i * 256, 256), 256)
            dest = pl.ds(pl.multiple_of(base + i * 256, 256), 256)
            right = jnp.concatenate([scaled(raw, s) for raw, s in pieces_of(cols)], axis=0)
            value = jnp.dot(at[...], right, preferred_element_type=F32)
            if first:
                out_ref[:, dest] = value
            else:
                out_ref[:, dest] += value
            return carry

        lax.fori_loop(0, width // 256, step, 0)

    def add_a(k, first=False):
        v = mod4(z + k)
        product(ata.at[v], lambda cols: [(ga[v, i, :, cols], scale[v]) for i in range(4)], WA, 0, first)

    def add_b(k, first=False):
        v = mod4(y + k)
        product(atb.at[v], lambda cols: [(gb[v, i, :, cols], scale[i]) for i in range(4)], WB, WA, first)

    add_a(0, True)
    r_az[1].forward()
    r_by[1].forward()
    add_b(0, True)
    r_az[2].forward()
    add_a(3)
    r_by[2].forward()
    add_a(1)
    add_b(3)
    add_b(1)
    for k in (0, 3, 1, 2):
        r_az[k].finish()
    add_a(2)
    for k in (3, 1, 2):
        r_by[k].finish()
    add_b(2)

    for far_copy, _, same in pieces:
        @pl.when(jnp.logical_not(same))
        def _():
            far_copy.wait_send()
    for ring in rings:
        ring.drain()
    for k in core + [swap, give] + share + sends:
        k.wait_send()


def body(activations, cotangents, row_ids, row_counts):
    dma = pltpu.SemaphoreType.DMA
    vmem = pltpu.VMEM
    return pl.pallas_call(
        body_kernel,
        out_shape=(pltpu.VMEM((512, WA + WB), F32), pltpu.VMEM((1, 2), F32)),
        in_specs=[pl.BlockSpec(memory_space=pltpu.SMEM)] * 2 + [pl.BlockSpec(memory_space=pltpu.VMEM)] * 2,
        out_specs=(pl.BlockSpec(memory_space=pltpu.VMEM), pl.BlockSpec(memory_space=pltpu.VMEM)),
        scratch_shapes=[
            vmem((4, NOISE, 1024), BF16),
            vmem((4, CLEAN_ROWS, 1024), BF16),
            vmem((4, CLEAN_ROWS, WA + WB), BF16),
            vmem((4, 4, NOISE, WA), BF16),
            vmem((4, 4, NOISE, WB), BF16),
            vmem((4, 4, 4, NOISE, LANES), BF16),
            vmem((4, 512, 4 * NOISE), BF16),
            vmem((4, 512, 4 * NOISE), BF16),
            vmem((4 * NOISE, 4 * CLEAN_ROWS), F32),
            vmem((4 * NOISE, 4 * CLEAN_ROWS), F32),
            vmem((4 * NOISE, 4 * CLEAN_ROWS), F32),
            vmem((2 * NOISE, 4 * CLEAN_ROWS), F32),
            vmem((2 * NOISE, 4 * CLEAN_ROWS), F32),
            vmem((48, 4 * CLEAN_ROWS), F32),
            vmem((40, 4 * CLEAN_ROWS), F32),
            vmem((2, SEG, 4 * CLEAN_ROWS), F32),
            vmem((8, 8, LANES), F32),
            vmem((16, 8, LANES), F32),
            vmem((8, LANES), F32),
            vmem((4, NOISE, LANES), F32),
            dma((15, 4)), dma((15, 4)),
            dma((8,)), dma((8,)), dma,
            dma((4,)), dma((4,)),
            dma((2,)), dma((2,)),
            dma((4,)), dma((4,)),
            dma((24,)), dma((24,)),
        ],
        compiler_params=pltpu.CompilerParams(
            collective_id=0, has_side_effects=True, vmem_limit_bytes=60 * 1024 * 1024),
        cost_estimate=pl.CostEstimate(flops=8_000_000_000, bytes_accessed=8_000_000, transcendentals=0),
        name="reweight",
    )(row_ids, row_counts, activations, cotangents)


def solution(mesh):
    placed = (P("dp", "seq", "tensor"), P("dp", "seq", "tensor"), P("dp", None), P("dp", None))
    return jax.shard_map(
        body,
        mesh=mesh,
        in_specs=placed,
        out_specs=(P(("dp", "seq"), "tensor"), P("dp", None)),
        check_vma=False,
    )
```

```python
import jax
import jax.numpy as jnp
from jax import lax
from jax.experimental import pallas as pl
from jax.experimental.pallas import tpu as pltpu
from jax.sharding import PartitionSpec as P

MESH = pl.DeviceIdType.MESH
F32 = jnp.float32
BF16 = jnp.bfloat16

SEG = 88
NOISE = 176
CLEAN_ROWS = 96
WA = 768
WB = 1024
LANES = 128


def body_kernel(ids_ref, counts_ref, acts_ref, cot_ref, out_ref, wout_ref,
                na, ca, cg, ga, gb, ao, ata, atb, part_gram, grad_gram, full, d2, sm,
                near_a, near_b, x3, sv1, sv2, wts, scale,
                ring_s, ring_r, p_s, p_r, p_l, k_s, k_r,
                d_s, d_r, m_s, m_r, v_s, v_r):
    z = lax.axis_index("dp")
    y = lax.axis_index("seq")
    t = lax.axis_index("tensor")
    x = t // 2
    c = lax.rem(t, 2)

    def mod4(v):
        return lax.rem(v, 4)

    def copy(src, dst, s, r, dev):
        return pltpu.make_async_remote_copy(
            src_ref=src, dst_ref=dst, send_sem=s, recv_sem=r, device_id=dev, device_id_type=MESH)

    barrier = pltpu.get_barrier_semaphore()

    def greet(dev):
        pl.semaphore_signal(barrier, inc=1, device_id=dev, device_id_type=MESH)

    def cell(r):
        other = lax.rem(4 * z + y + r, 16)
        return other // 4, lax.rem(other, 4), t

    for r in range(1, 16):
        greet(cell(r))
    for r in range(1, 8):
        greet((z, y, lax.rem(t + r, 8)))

    targets = [(h, q, (x, 2 * c + h, 2 * q + z // 2)) for h in range(2) for q in range(4)]
    target_self = [(x == z) & (y == 2 * c + h) & (q == x) & (c == z // 2) for h, q, _ in targets]
    sources = [(2 * c + i // 4, i % 4) for i in range(8)]
    source_self = [(zs == z) & (ys == y) & (x == z) & (c == y // 2) for zs, ys in sources]
    for (_, _, dev), same in zip(targets, target_self):
        @pl.when(jnp.logical_not(same))
        def _():
            greet(dev)
    for (zs, ys), same in zip(sources, source_self):
        @pl.when(jnp.logical_not(same))
        def _():
            greet((zs, ys, 2 * z + y // 2))
    has_self = ((x == z) & (c == y // 2) & (c == z // 2)).astype(jnp.int32)

    rid = [ids_ref[0, j] for j in range(3)]
    live = [counts_ref[0, rid[j]] - y * SEG for j in range(3)]
    rows = lax.broadcasted_iota(jnp.int32, (SEG, LANES), 0)
    pad = jnp.zeros((CLEAN_ROWS - SEG, LANES), F32)

    def stage_acts(i, carry):
        cols = pl.ds(pl.multiple_of(i * LANES, LANES), LANES)
        part = [acts_ref[rid[j], :, cols].astype(F32) for j in range(3)]
        na[y, :, cols] = jnp.concatenate([part[1], part[2]], axis=0).astype(BF16)
        ca[z, :, cols] = jnp.concatenate([part[0], pad], axis=0).astype(BF16)
        return carry

    lax.fori_loop(0, 1024 // LANES, stage_acts, 0)

    def masked(j, cols):
        return jnp.where(rows < live[j], cot_ref[rid[j], :, cols].astype(F32), 0.0)

    def stage_clean(i, carry):
        cols = pl.ds(pl.multiple_of(i * LANES, LANES), LANES)
        cg[z, :, cols] = jnp.concatenate([masked(0, cols), pad], axis=0).astype(BF16)
        return carry

    def stage_a(i, carry):
        cols = pl.ds(pl.multiple_of(i * LANES, LANES), LANES)
        ga[z, y, :, cols] = jnp.concatenate([masked(1, cols), masked(2, cols)], axis=0).astype(BF16)
        return carry

    def stage_b(i, carry):
        cols = pl.ds(pl.multiple_of(i * LANES, LANES), LANES)
        from_cols = pl.ds(pl.multiple_of(WA + i * LANES, LANES), LANES)
        gb[y, z, :, cols] = jnp.concatenate(
            [masked(1, from_cols), masked(2, from_cols)], axis=0).astype(BF16)
        return carry

    pl.semaphore_wait(barrier, 38 - 2 * has_self)

    pieces = []
    for i, ((h, q, dev), same) in enumerate(zip(targets, target_self)):
        src = na.at[y, :, pl.ds(h * 512 + q * LANES, LANES)]
        dst = ao.at[q, z, y]
        far_copy = copy(src, dst, p_s.at[i], p_r.at[lax.rem(z, 2) * 4 + y], dev)
        near_copy = pltpu.make_async_copy(src, dst, p_l)

        @pl.when(same)
        def _():
            near_copy.start()

        @pl.when(jnp.logical_not(same))
        def _():
            far_copy.start()
        pieces.append((far_copy, near_copy, same))

    rings = []

    class Ring:
        def __init__(self, at, axis, first, second):
            n = len(rings)
            rings.append(self)
            me = {"x": x, "y": y, "z": z}[axis]

            def dev(v):
                return {"x": (z, y, 2 * v + c), "y": (z, v, t), "z": (v, y, t)}[axis]

            up, down, far = mod4(me + 1), mod4(me + 3), mod4(me + 2)
            own, low, high, opp = at(me), at(down), at(up), at(far)
            self.go = [copy(own, own, ring_s.at[n, 0], ring_r.at[n, 0], dev(up)),
                       copy(own, own, ring_s.at[n, 1], ring_r.at[n, 1], dev(down))]
            self.got = [copy(low, low, ring_s.at[n, 0], ring_r.at[n, 0], dev(up)),
                        copy(high, high, ring_s.at[n, 1], ring_r.at[n, 1], dev(down))]
            self.pass_on = [
                copy(low.at[first], low.at[first], ring_s.at[n, 2], ring_r.at[n, 2], dev(up)),
                copy(high.at[second], high.at[second], ring_s.at[n, 3], ring_r.at[n, 3], dev(down))]
            self.got_far = [
                copy(opp.at[first], opp.at[first], ring_s.at[n, 2], ring_r.at[n, 2], dev(up)),
                copy(opp.at[second], opp.at[second], ring_s.at[n, 3], ring_r.at[n, 3], dev(down))]

        def start(self):
            for k in self.go:
                k.start()

        def forward(self):
            for k in range(2):
                self.got[k].wait_recv()
                self.pass_on[k].start()

        def finish(self):
            for k in self.got_far:
                k.wait_recv()

        def drain(self):
            for k in self.go + self.pass_on:
                k.wait_send()

    even = (pl.ds(0, 96),), (pl.ds(96, 80),)
    odd = (pl.ds(80, 96),), (pl.ds(0, 80),)
    equal = (pl.ds(0, 48),), (pl.ds(48, 48),)

    def az_ring(k):
        item = mod4(y + k)
        return Ring(lambda v: ga.at[v, item], "z", *(even if k in (0, 1) else odd))

    def by_ring(k):
        item = mod4(z + k)
        return Ring(lambda v: gb.at[v, item], "y", *(even if k in (0, 1) else odd))

    def rows_of(chunk):
        return pl.ds(pl.multiple_of(chunk * SEG, 8), SEG)

    r_na = Ring(lambda v: na.at[v], "y", *even)
    r_ca = Ring(lambda v: ca.at[v], "z", *equal)
    r_cg = Ring(lambda v: cg.at[v], "z", *equal)
    r_ay = Ring(lambda v: ga.at[z, v], "y", *odd)
    r_bz = Ring(lambda v: gb.at[y, v], "z", *odd)
    r_az = {k: az_ring(k) for k in (0, 3, 1, 2)}
    r_by = {k: by_ring(k) for k in (0, 3, 1, 2)}
    here = pl.ds(2 * c, 2)
    there = pl.ds(2 * (1 - c), 2)
    r_ao = Ring(lambda v: ao.at[v, here], "x", (pl.ds(0, 1),), (pl.ds(1, 1),))
    r_full = Ring(lambda v: full.at[rows_of(4 * c + v)], "x", (pl.ds(0, 48),), (pl.ds(48, 40),))

    r_na.start()
    r_ca.start()
    lax.fori_loop(0, WA // LANES, stage_a, 0)
    r_ay.start()
    lax.fori_loop(0, (WA + WB) // LANES, stage_clean, 0)
    r_cg.start()
    lax.fori_loop(0, WB // LANES, stage_b, 0)

    r_ca.forward()
    r_bz.start()
    r_na.forward()
    r_by[0].start()
    for i, ((zs, ys), same) in enumerate(zip(sources, source_self)):
        dst = ao.at[x, zs, ys]
        far_copy = copy(dst, dst, p_s.at[i], p_r.at[i], (z, y, lax.rem(t + 1, 8)))
        near_copy = pltpu.make_async_copy(dst, dst, p_l)

        @pl.when(same)
        def _():
            near_copy.wait()

        @pl.when(jnp.logical_not(same))
        def _():
            far_copy.wait_recv()
    mine = ao.at[x, here]
    partner = (z, y, 2 * x + 1 - c)
    r_ao.start()
    core = [copy(mine, mine, k_s.at[0], k_r.at[0], partner)]
    core[0].start()

    def relay(r):
        block = ao.at[mod4(x + 4 - r), here]
        core.append(copy(block, block, k_s.at[r], k_r.at[r], partner))
        core[-1].start()

    r_cg.forward()
    r_az[0].start()
    r_ay.forward()

    contract = (((1,), (1,)), ((), ()))

    def gram(left, right):
        return lax.dot_general(left, right, contract, preferred_element_type=F32)

    r_na.finish()
    r_ca.finish()
    part_gram[...] = gram(na[...].reshape(4 * NOISE, 1024), ca[...].reshape(4 * CLEAN_ROWS, 1024))
    own_half = pl.ds(pl.multiple_of(c * 352, 8), 352)
    other_half = pl.ds(pl.multiple_of((1 - c) * 352, 8), 352)
    swap = copy(part_gram.at[other_half], d2, d_s.at[0], d_r.at[0], partner)
    swap.start()

    r_ao.forward()
    relay(1)
    relay(3)
    r_bz.forward()
    r_az[3].start()
    r_az[1].start()

    swap.wait_recv()
    sm[...] = part_gram[own_half] + d2[...]
    up, down, across = mod4(x + 1), mod4(x + 3), mod4(x + 2)
    dev_up, dev_down = (z, y, 2 * up + c), (z, y, 2 * down + c)
    first = pl.ds(pl.multiple_of(across * SEG, 8), 48)
    second = pl.ds(pl.multiple_of(across * SEG + 48, 8), 40)
    share = [copy(sm.at[first], near_a, m_s.at[0], m_r.at[0], dev_up),
             copy(sm.at[second], near_b, m_s.at[1], m_r.at[1], dev_down),
             copy(sm.at[rows_of(up)], x3.at[0], m_s.at[2], m_r.at[2], dev_up),
             copy(sm.at[rows_of(down)], x3.at[1], m_s.at[3], m_r.at[3], dev_down)]
    share[0].start()
    share[1].start()
    r_ao.finish()
    relay(2)
    r_by[0].forward()
    r_by[3].start()
    r_by[1].start()
    share[0].wait_recv()
    sm[pl.ds(pl.multiple_of(up * SEG, 8), 48)] += near_a[...]
    share[2].start()
    share[1].wait_recv()
    sm[pl.ds(pl.multiple_of(down * SEG + 48, 8), 40)] += near_b[...]
    share[3].start()

    r_cg.finish()
    r_ay.finish()
    r_az[2].start()
    grad_gram[...] = gram(ga[z].reshape(4 * NOISE, WA), cg[:, :, :WA].reshape(4 * CLEAN_ROWS, WA))

    share[2].wait_recv()
    share[3].wait_recv()
    full[rows_of(4 * c + x)] = sm[rows_of(x)] + x3[0] + x3[1]
    r_full.start()
    r_az[0].forward()
    r_full.forward()
    r_full.finish()
    give = copy(full.at[own_half], full.at[own_half], d_s.at[1], d_r.at[1], partner)
    give.start()

    r_bz.finish()
    r_by[2].start()
    r_by[0].finish()
    grad_gram[...] += gram(gb[:, z].reshape(4 * NOISE, WB), cg[:, :, WA:].reshape(4 * CLEAN_ROWS, WB))
    copy(full.at[other_half], full.at[other_half], d_s.at[1], d_r.at[1], partner).wait_recv()

    def row_dot(j):
        terms = [grad_gram[g * SEG:(g + 1) * SEG] * full[g * SEG:(g + 1) * SEG] for g in range(j, 8, 2)]
        rows_sum = jnp.sum(terms[0] + terms[1] + terms[2] + terms[3], axis=0, keepdims=True)
        return jnp.broadcast_to(jnp.sum(rows_sum, axis=1, keepdims=True), (8, LANES))

    place = lax.broadcasted_iota(jnp.int32, (8, LANES), 0)
    tile = jnp.where(place == 2 * z, row_dot(0), jnp.where(place == 2 * z + 1, row_dot(1), 0.0))

    sends = []

    def send_tile(buf, value, me, n, dev, base):
        buf[me] = value
        for r in range(1, n):
            out = copy(buf.at[me], buf.at[me], v_s.at[base + r], v_r.at[base + r], dev(r))
            out.start()
            sends.append(out)

    def sum_tiles(buf, me, n, base):
        for r in range(1, n):
            origin = buf.at[lax.rem(me + n - r, n)]
            copy(origin, origin, v_s.at[base + r], v_r.at[base + r], partner).wait_recv()
        return jnp.sum(buf[...], axis=0)

    send_tile(sv1, tile, t, 8, lambda r: (z, y, lax.rem(t + r, 8)), 0)

    for r in range(4):
        block = ao.at[mod4(x + 4 - r), there]
        copy(block, block, k_s.at[r], k_r.at[r], partner).wait_recv()

    def turn(k, carry):
        for q in range(4):
            span = pl.ds(q * LANES, LANES)
            ata[k, span, :] = ao[q, k].reshape(4 * NOISE, LANES).T
            atb[k, span, :] = ao[q, :, k].reshape(4 * NOISE, LANES).T
        return carry

    lax.fori_loop(0, 4, turn, 0)

    tile = sum_tiles(sv1, t, 8, 0)
    send_tile(sv2, tile, 4 * z + y, 16, cell, 8)
    r_az[3].forward()
    r_by[3].forward()
    tile = sum_tiles(sv2, 4 * z + y, 16, 8)
    weights = jnp.maximum(-tile, 0.0) / jnp.sum(jnp.abs(tile), axis=0, keepdims=True)
    wts[...] = weights
    for k in range(4):
        scale[k, :SEG] = jnp.broadcast_to(wts[2 * k:2 * k + 1, :], (SEG, LANES))
        scale[k, SEG:] = jnp.broadcast_to(wts[2 * k + 1:2 * k + 2, :], (SEG, LANES))
    lane = lax.broadcasted_iota(jnp.int32, (1, LANES), 1)
    wout_ref[...] = jnp.where(lane == 0, wts[pl.ds(2 * z, 1), :], wts[pl.ds(2 * z + 1, 1), :])[:, :2]

    def scaled(raw, s):
        full = jnp.concatenate([s, s], axis=1)
        return (raw.astype(F32) * full).astype(BF16)

    def product(at, pieces_of, width, base, first):
        def step(i, carry):
            cols = pl.ds(pl.multiple_of(i * 256, 256), 256)
            dest = pl.ds(pl.multiple_of(base + i * 256, 256), 256)
            right = jnp.concatenate([scaled(raw, s) for raw, s in pieces_of(cols)], axis=0)
            value = jnp.dot(at[...], right, preferred_element_type=F32)
            if first:
                out_ref[:, dest] = value
            else:
                out_ref[:, dest] += value
            return carry

        lax.fori_loop(0, width // 256, step, 0)

    def add_a(k, first=False):
        v = mod4(z + k)
        product(ata.at[v], lambda cols: [(ga[v, i, :, cols], scale[v]) for i in range(4)], WA, 0, first)

    def add_b(k, first=False):
        v = mod4(y + k)
        product(atb.at[v], lambda cols: [(gb[v, i, :, cols], scale[i]) for i in range(4)], WB, WA, first)

    add_a(0, True)
    r_az[1].forward()
    r_by[1].forward()
    add_b(0, True)
    r_az[2].forward()
    add_a(3)
    r_by[2].forward()
    add_a(1)
    add_b(3)
    add_b(1)
    for k in (0, 3, 1, 2):
        r_az[k].finish()
    add_a(2)
    for k in (3, 1, 2):
        r_by[k].finish()
    add_b(2)

    for far_copy, _, same in pieces:
        @pl.when(jnp.logical_not(same))
        def _():
            far_copy.wait_send()
    for ring in rings:
        ring.drain()
    for k in core + [swap, give] + share + sends:
        k.wait_send()


def body(activations, cotangents, row_ids, row_counts):
    dma = pltpu.SemaphoreType.DMA
    vmem = pltpu.VMEM
    return pl.pallas_call(
        body_kernel,
        out_shape=(pltpu.VMEM((512, WA + WB), F32), pltpu.VMEM((1, 2), F32)),
        in_specs=[pl.BlockSpec(memory_space=pltpu.SMEM)] * 2 + [pl.BlockSpec(memory_space=pltpu.VMEM)] * 2,
        out_specs=(pl.BlockSpec(memory_space=pltpu.VMEM), pl.BlockSpec(memory_space=pltpu.VMEM)),
        scratch_shapes=[
            vmem((4, NOISE, 1024), BF16),
            vmem((4, CLEAN_ROWS, 1024), BF16),
            vmem((4, CLEAN_ROWS, WA + WB), BF16),
            vmem((4, 4, NOISE, WA), BF16),
            vmem((4, 4, NOISE, WB), BF16),
            vmem((4, 4, 4, NOISE, LANES), BF16),
            vmem((4, 512, 4 * NOISE), BF16),
            vmem((4, 512, 4 * NOISE), BF16),
            vmem((4 * NOISE, 4 * CLEAN_ROWS), F32),
            vmem((4 * NOISE, 4 * CLEAN_ROWS), F32),
            vmem((4 * NOISE, 4 * CLEAN_ROWS), F32),
            vmem((2 * NOISE, 4 * CLEAN_ROWS), F32),
            vmem((2 * NOISE, 4 * CLEAN_ROWS), F32),
            vmem((48, 4 * CLEAN_ROWS), F32),
            vmem((40, 4 * CLEAN_ROWS), F32),
            vmem((2, SEG, 4 * CLEAN_ROWS), F32),
            vmem((8, 8, LANES), F32),
            vmem((16, 8, LANES), F32),
            vmem((8, LANES), F32),
            vmem((4, NOISE, LANES), F32),
            dma((15, 4)), dma((15, 4)),
            dma((8,)), dma((8,)), dma,
            dma((4,)), dma((4,)),
            dma((2,)), dma((2,)),
            dma((4,)), dma((4,)),
            dma((24,)), dma((24,)),
        ],
        compiler_params=pltpu.CompilerParams(
            collective_id=0, has_side_effects=True, vmem_limit_bytes=60 * 1024 * 1024),
        cost_estimate=pl.CostEstimate(flops=8_000_000_000, bytes_accessed=8_000_000, transcendentals=0),
        name="reweight",
    )(row_ids, row_counts, activations, cotangents)


def solution(mesh):
    placed = (P("dp", "seq", "tensor"), P("dp", "seq", "tensor"), P("dp", None), P("dp", None))
    return jax.shard_map(
        body,
        mesh=mesh,
        in_specs=placed,
        out_specs=(P(("dp", "seq"), "tensor"), P("dp", None)),
        check_vma=False,
    )
```

```python
import jax
import jax.numpy as jnp
from jax import lax
from jax.experimental import pallas as pl
from jax.experimental.pallas import tpu as pltpu
from jax.sharding import PartitionSpec as P

MESH = pl.DeviceIdType.MESH
F32 = jnp.float32
BF16 = jnp.bfloat16

SEG = 88
NOISE = 176
CLEAN_ROWS = 96
WA = 768
WB = 1024
LANES = 128


def body_kernel(ids_ref, counts_ref, acts_ref, cot_ref, out_ref, wout_ref,
                na, ca, cg, ga, gb, hop, ao, ata, atb, part_gram, grad_gram, full, d2, sm,
                near_a, near_b, x3, sv1, sv2, wts, scale,
                ring_s, ring_r, h_s, h_r, p_s, p_r, p_l, k_s, k_r,
                d_s, d_r, m_s, m_r, v_s, v_r):
    z = lax.axis_index("dp")
    y = lax.axis_index("seq")
    t = lax.axis_index("tensor")
    x = t // 2
    c = lax.rem(t, 2)

    def mod4(v):
        return lax.rem(v, 4)

    def copy(src, dst, s, r, dev):
        return pltpu.make_async_remote_copy(
            src_ref=src, dst_ref=dst, send_sem=s, recv_sem=r, device_id=dev, device_id_type=MESH)

    barrier = pltpu.get_barrier_semaphore()

    def greet(dev):
        pl.semaphore_signal(barrier, inc=1, device_id=dev, device_id_type=MESH)

    def cell(r):
        other = lax.rem(4 * z + y + r, 16)
        return other // 4, lax.rem(other, 4), t

    for r in range(1, 16):
        greet(cell(r))
    for r in range(1, 8):
        greet((z, y, lax.rem(t + r, 8)))

    targets = [(r, h, (mod4(x + r), 2 * c + h, 2 * x + z // 2)) for r in range(4) for h in range(2)]
    target_self = [(dev[0] == z) & (dev[1] == y) & (c == z // 2) for _, _, dev in targets]
    sources = [(2 * c + i // 4, i % 4) for i in range(8)]
    source_self = [(zs == z) & (ys == y) & (c == y // 2) for zs, ys in sources]
    for (_, _, dev), same in zip(targets, target_self):
        @pl.when(jnp.logical_not(same))
        def _():
            greet(dev)
    for (zs, ys), same in zip(sources, source_self):
        @pl.when(jnp.logical_not(same))
        def _():
            greet((zs, ys, 2 * x + y // 2))
    has_self = ((c == y // 2) & (c == z // 2)).astype(jnp.int32)

    rid = [ids_ref[0, j] for j in range(3)]
    live = [counts_ref[0, rid[j]] - y * SEG for j in range(3)]
    rows = lax.broadcasted_iota(jnp.int32, (SEG, LANES), 0)
    pad = jnp.zeros((CLEAN_ROWS - SEG, LANES), F32)

    def stage_acts(i, carry):
        cols = pl.ds(pl.multiple_of(i * LANES, LANES), LANES)
        part = [acts_ref[rid[j], :, cols].astype(F32) for j in range(3)]
        na[y, :, cols] = jnp.concatenate([part[1], part[2]], axis=0).astype(BF16)
        ca[z, :, cols] = jnp.concatenate([part[0], pad], axis=0).astype(BF16)
        return carry

    lax.fori_loop(0, 1024 // LANES, stage_acts, 0)

    def masked(j, cols):
        return jnp.where(rows < live[j], cot_ref[rid[j], :, cols].astype(F32), 0.0)

    def stage_clean(i, carry):
        cols = pl.ds(pl.multiple_of(i * LANES, LANES), LANES)
        cg[z, :, cols] = jnp.concatenate([masked(0, cols), pad], axis=0).astype(BF16)
        return carry

    def stage_a(i, carry):
        cols = pl.ds(pl.multiple_of(i * LANES, LANES), LANES)
        ga[z, y, :, cols] = jnp.concatenate([masked(1, cols), masked(2, cols)], axis=0).astype(BF16)
        return carry

    def stage_b(i, carry):
        cols = pl.ds(pl.multiple_of(i * LANES, LANES), LANES)
        from_cols = pl.ds(pl.multiple_of(WA + i * LANES, LANES), LANES)
        gb[y, z, :, cols] = jnp.concatenate(
            [masked(1, from_cols), masked(2, from_cols)], axis=0).astype(BF16)
        return carry

    pl.semaphore_wait(barrier, 38 - 2 * has_self)

    hops = []
    for r in range(1, 4):
        q = mod4(x + r)
        for h in range(2):
            src = na.at[y, :, pl.ds(pl.multiple_of(h * 512 + q * LANES, LANES), LANES)]
            hops.append(copy(src, hop.at[r, h], h_s.at[r, h], h_r.at[r, h], (z, y, 2 * q + c)))
    for k in hops:
        k.start()

    pieces = []

    def send_piece(i):
        r, h, dev = targets[i]
        same = target_self[i]
        if r:
            src = hop.at[4 - r, h]
            copy(src, src, h_s.at[4 - r, h], h_r.at[4 - r, h], (z, y, lax.rem(t + 1, 8))).wait_recv()
        else:
            src = na.at[y, :, pl.ds(pl.multiple_of(h * 512 + x * LANES, LANES), LANES)]
        dst = ao.at[x, z, y]
        far_copy = copy(src, dst, p_s.at[i], p_r.at[lax.rem(z, 2) * 4 + y], dev)
        near_copy = pltpu.make_async_copy(src, dst, p_l)

        @pl.when(same)
        def _():
            near_copy.start()

        @pl.when(jnp.logical_not(same))
        def _():
            far_copy.start()
        pieces.append((far_copy, same))

    rings = []

    class Ring:
        def __init__(self, at, axis, first, second):
            n = len(rings)
            rings.append(self)
            me = {"x": x, "y": y, "z": z}[axis]

            def dev(v):
                return {"x": (z, y, 2 * v + c), "y": (z, v, t), "z": (v, y, t)}[axis]

            up, down, far = mod4(me + 1), mod4(me + 3), mod4(me + 2)
            own, low, high, opp = at(me), at(down), at(up), at(far)
            self.go = [copy(own, own, ring_s.at[n, 0], ring_r.at[n, 0], dev(up)),
                       copy(own, own, ring_s.at[n, 1], ring_r.at[n, 1], dev(down))]
            self.got = [copy(low, low, ring_s.at[n, 0], ring_r.at[n, 0], dev(up)),
                        copy(high, high, ring_s.at[n, 1], ring_r.at[n, 1], dev(down))]
            self.pass_on = [
                copy(low.at[first], low.at[first], ring_s.at[n, 2], ring_r.at[n, 2], dev(up)),
                copy(high.at[second], high.at[second], ring_s.at[n, 3], ring_r.at[n, 3], dev(down))]
            self.got_far = [
                copy(opp.at[first], opp.at[first], ring_s.at[n, 2], ring_r.at[n, 2], dev(up)),
                copy(opp.at[second], opp.at[second], ring_s.at[n, 3], ring_r.at[n, 3], dev(down))]

        def start(self):
            for k in self.go:
                k.start()

        def forward(self):
            for k in range(2):
                self.got[k].wait_recv()
                self.pass_on[k].start()

        def finish(self):
            for k in self.got_far:
                k.wait_recv()

        def drain(self):
            for k in self.go + self.pass_on:
                k.wait_send()

    even = (pl.ds(0, 96),), (pl.ds(96, 80),)
    odd = (pl.ds(80, 96),), (pl.ds(0, 80),)
    equal = (pl.ds(0, 48),), (pl.ds(48, 48),)

    def az_ring(k):
        item = mod4(y + k)
        return Ring(lambda v: ga.at[v, item], "z", *(even if k in (0, 1) else odd))

    def by_ring(k):
        item = mod4(z + k)
        return Ring(lambda v: gb.at[v, item], "y", *(even if k in (0, 1) else odd))

    def rows_of(chunk):
        return pl.ds(pl.multiple_of(chunk * SEG, 8), SEG)

    r_na = Ring(lambda v: na.at[v], "y", *even)
    r_ca = Ring(lambda v: ca.at[v], "z", *equal)
    r_cg = Ring(lambda v: cg.at[v], "z", *equal)
    r_ay = Ring(lambda v: ga.at[z, v], "y", *odd)
    r_bz = Ring(lambda v: gb.at[y, v], "z", *odd)
    r_az = {k: az_ring(k) for k in (0, 3, 1, 2)}
    r_by = {k: by_ring(k) for k in (0, 3, 1, 2)}
    here = pl.ds(2 * c, 2)
    there = pl.ds(2 * (1 - c), 2)
    r_ao = Ring(lambda v: ao.at[v, here], "x", (pl.ds(0, 1),), (pl.ds(1, 1),))
    r_full = Ring(lambda v: full.at[rows_of(4 * c + v)], "x", (pl.ds(0, 48),), (pl.ds(48, 40),))

    r_na.start()
    r_ca.start()
    lax.fori_loop(0, WA // LANES, stage_a, 0)
    r_ay.start()
    lax.fori_loop(0, (WA + WB) // LANES, stage_clean, 0)
    r_cg.start()
    lax.fori_loop(0, WB // LANES, stage_b, 0)

    send_piece(0)
    send_piece(1)
    r_ca.forward()
    r_bz.start()
    r_na.forward()
    r_by[0].start()
    for i in range(2, 8):
        send_piece(i)
    r_cg.forward()
    r_az[0].start()
    r_ay.forward()

    for i, ((zs, ys), same) in enumerate(zip(sources, source_self)):
        dst = ao.at[x, zs, ys]
        far_copy = copy(dst, dst, p_s.at[i], p_r.at[i], (z, y, lax.rem(t + 1, 8)))
        near_copy = pltpu.make_async_copy(dst, dst, p_l)

        @pl.when(same)
        def _():
            near_copy.wait()

        @pl.when(jnp.logical_not(same))
        def _():
            far_copy.wait_recv()
    mine = ao.at[x, here]
    partner = (z, y, 2 * x + 1 - c)
    r_ao.start()
    core = [copy(mine, mine, k_s.at[0], k_r.at[0], partner)]
    core[0].start()

    def relay(r):
        block = ao.at[mod4(x + 4 - r), here]
        core.append(copy(block, block, k_s.at[r], k_r.at[r], partner))
        core[-1].start()

    contract = (((1,), (1,)), ((), ()))

    def gram(left, right):
        return lax.dot_general(left, right, contract, preferred_element_type=F32)

    r_na.finish()
    r_ca.finish()
    part_gram[...] = gram(na[...].reshape(4 * NOISE, 1024), ca[...].reshape(4 * CLEAN_ROWS, 1024))
    own_half = pl.ds(pl.multiple_of(c * 352, 8), 352)
    other_half = pl.ds(pl.multiple_of((1 - c) * 352, 8), 352)
    swap = copy(part_gram.at[other_half], d2, d_s.at[0], d_r.at[0], partner)
    swap.start()

    r_bz.forward()
    r_az[3].start()
    r_az[1].start()

    swap.wait_recv()
    sm[...] = part_gram[own_half] + d2[...]
    up, down, across = mod4(x + 1), mod4(x + 3), mod4(x + 2)
    dev_up, dev_down = (z, y, 2 * up + c), (z, y, 2 * down + c)
    first = pl.ds(pl.multiple_of(across * SEG, 8), 48)
    second = pl.ds(pl.multiple_of(across * SEG + 48, 8), 40)
    share = [copy(sm.at[first], near_a, m_s.at[0], m_r.at[0], dev_up),
             copy(sm.at[second], near_b, m_s.at[1], m_r.at[1], dev_down),
             copy(sm.at[rows_of(up)], x3.at[0], m_s.at[2], m_r.at[2], dev_up),
             copy(sm.at[rows_of(down)], x3.at[1], m_s.at[3], m_r.at[3], dev_down)]
    share[0].start()
    share[1].start()
    r_ao.forward()
    relay(1)
    relay(3)
    r_by[0].forward()
    r_by[3].start()
    r_by[1].start()
    share[0].wait_recv()
    sm[pl.ds(pl.multiple_of(up * SEG, 8), 48)] += near_a[...]
    share[2].start()
    share[1].wait_recv()
    sm[pl.ds(pl.multiple_of(down * SEG + 48, 8), 40)] += near_b[...]
    share[3].start()

    r_cg.finish()
    r_ay.finish()
    r_az[2].start()
    grad_gram[...] = gram(ga[z].reshape(4 * NOISE, WA), cg[:, :, :WA].reshape(4 * CLEAN_ROWS, WA))

    share[2].wait_recv()
    share[3].wait_recv()
    full[rows_of(4 * c + x)] = sm[rows_of(x)] + x3[0] + x3[1]
    r_full.start()
    r_az[0].forward()
    r_full.forward()
    r_ao.finish()
    relay(2)
    r_full.finish()
    give = copy(full.at[own_half], full.at[own_half], d_s.at[1], d_r.at[1], partner)
    give.start()

    r_bz.finish()
    r_by[2].start()
    r_by[0].finish()
    grad_gram[...] += gram(gb[:, z].reshape(4 * NOISE, WB), cg[:, :, WA:].reshape(4 * CLEAN_ROWS, WB))
    copy(full.at[other_half], full.at[other_half], d_s.at[1], d_r.at[1], partner).wait_recv()

    def row_dot(j):
        terms = [grad_gram[g * SEG:(g + 1) * SEG] * full[g * SEG:(g + 1) * SEG] for g in range(j, 8, 2)]
        rows_sum = jnp.sum(terms[0] + terms[1] + terms[2] + terms[3], axis=0, keepdims=True)
        return jnp.broadcast_to(jnp.sum(rows_sum, axis=1, keepdims=True), (8, LANES))

    place = lax.broadcasted_iota(jnp.int32, (8, LANES), 0)
    tile = jnp.where(place == 2 * z, row_dot(0), jnp.where(place == 2 * z + 1, row_dot(1), 0.0))

    sends = []

    def send_tile(buf, value, me, n, dev, base):
        buf[me] = value
        for r in range(1, n):
            out = copy(buf.at[me], buf.at[me], v_s.at[base + r], v_r.at[base + r], dev(r))
            out.start()
            sends.append(out)

    def sum_tiles(buf, me, n, base):
        for r in range(1, n):
            origin = buf.at[lax.rem(me + n - r, n)]
            copy(origin, origin, v_s.at[base + r], v_r.at[base + r], partner).wait_recv()
        return jnp.sum(buf[...], axis=0)

    send_tile(sv1, tile, t, 8, lambda r: (z, y, lax.rem(t + r, 8)), 0)

    for r in range(4):
        block = ao.at[mod4(x + 4 - r), there]
        copy(block, block, k_s.at[r], k_r.at[r], partner).wait_recv()

    def turn(k, carry):
        for q in range(4):
            span = pl.ds(q * LANES, LANES)
            ata[k, span, :] = ao[q, k].reshape(4 * NOISE, LANES).T
            atb[k, span, :] = ao[q, :, k].reshape(4 * NOISE, LANES).T
        return carry

    lax.fori_loop(0, 4, turn, 0)

    tile = sum_tiles(sv1, t, 8, 0)
    send_tile(sv2, tile, 4 * z + y, 16, cell, 8)
    r_az[3].forward()
    r_by[3].forward()
    tile = sum_tiles(sv2, 4 * z + y, 16, 8)
    weights = jnp.maximum(-tile, 0.0) / jnp.sum(jnp.abs(tile), axis=0, keepdims=True)
    wts[...] = weights
    for k in range(4):
        scale[k, :SEG] = jnp.broadcast_to(wts[2 * k:2 * k + 1, :], (SEG, LANES))
        scale[k, SEG:] = jnp.broadcast_to(wts[2 * k + 1:2 * k + 2, :], (SEG, LANES))
    lane = lax.broadcasted_iota(jnp.int32, (1, LANES), 1)
    wout_ref[...] = jnp.where(lane == 0, wts[pl.ds(2 * z, 1), :], wts[pl.ds(2 * z + 1, 1), :])[:, :2]

    def scaled(raw, s):
        full = jnp.concatenate([s, s], axis=1)
        return (raw.astype(F32) * full).astype(BF16)

    def product(at, pieces_of, width, base, first):
        def step(i, carry):
            cols = pl.ds(pl.multiple_of(i * 256, 256), 256)
            dest = pl.ds(pl.multiple_of(base + i * 256, 256), 256)
            right = jnp.concatenate([scaled(raw, s) for raw, s in pieces_of(cols)], axis=0)
            value = jnp.dot(at[...], right, preferred_element_type=F32)
            if first:
                out_ref[:, dest] = value
            else:
                out_ref[:, dest] += value
            return carry

        lax.fori_loop(0, width // 256, step, 0)

    def add_a(k, first=False):
        v = mod4(z + k)
        product(ata.at[v], lambda cols: [(ga[v, i, :, cols], scale[v]) for i in range(4)], WA, 0, first)

    def add_b(k, first=False):
        v = mod4(y + k)
        product(atb.at[v], lambda cols: [(gb[v, i, :, cols], scale[i]) for i in range(4)], WB, WA, first)

    add_a(0, True)
    r_az[1].forward()
    r_by[1].forward()
    add_b(0, True)
    r_az[2].forward()
    add_a(3)
    r_by[2].forward()
    add_a(1)
    add_b(3)
    add_b(1)
    for k in (0, 3, 1, 2):
        r_az[k].finish()
    add_a(2)
    for k in (3, 1, 2):
        r_by[k].finish()
    add_b(2)

    for far_copy, same in pieces:
        @pl.when(jnp.logical_not(same))
        def _():
            far_copy.wait_send()
    for ring in rings:
        ring.drain()
    for k in hops + core + [swap, give] + share + sends:
        k.wait_send()


def body(activations, cotangents, row_ids, row_counts):
    dma = pltpu.SemaphoreType.DMA
    vmem = pltpu.VMEM
    return pl.pallas_call(
        body_kernel,
        out_shape=(pltpu.VMEM((512, WA + WB), F32), pltpu.VMEM((1, 2), F32)),
        in_specs=[pl.BlockSpec(memory_space=pltpu.SMEM)] * 2 + [pl.BlockSpec(memory_space=pltpu.VMEM)] * 2,
        out_specs=(pl.BlockSpec(memory_space=pltpu.VMEM), pl.BlockSpec(memory_space=pltpu.VMEM)),
        scratch_shapes=[
            vmem((4, NOISE, 1024), BF16),
            vmem((4, CLEAN_ROWS, 1024), BF16),
            vmem((4, CLEAN_ROWS, WA + WB), BF16),
            vmem((4, 4, NOISE, WA), BF16),
            vmem((4, 4, NOISE, WB), BF16),
            vmem((4, 2, NOISE, LANES), BF16),
            vmem((4, 4, 4, NOISE, LANES), BF16),
            vmem((4, 512, 4 * NOISE), BF16),
            vmem((4, 512, 4 * NOISE), BF16),
            vmem((4 * NOISE, 4 * CLEAN_ROWS), F32),
            vmem((4 * NOISE, 4 * CLEAN_ROWS), F32),
            vmem((4 * NOISE, 4 * CLEAN_ROWS), F32),
            vmem((2 * NOISE, 4 * CLEAN_ROWS), F32),
            vmem((2 * NOISE, 4 * CLEAN_ROWS), F32),
            vmem((48, 4 * CLEAN_ROWS), F32),
            vmem((40, 4 * CLEAN_ROWS), F32),
            vmem((2, SEG, 4 * CLEAN_ROWS), F32),
            vmem((8, 8, LANES), F32),
            vmem((16, 8, LANES), F32),
            vmem((8, LANES), F32),
            vmem((4, NOISE, LANES), F32),
            dma((15, 4)), dma((15, 4)),
            dma((4, 2)), dma((4, 2)),
            dma((8,)), dma((8,)), dma,
            dma((4,)), dma((4,)),
            dma((2,)), dma((2,)),
            dma((4,)), dma((4,)),
            dma((24,)), dma((24,)),
        ],
        compiler_params=pltpu.CompilerParams(
            collective_id=0, has_side_effects=True, vmem_limit_bytes=60 * 1024 * 1024),
        cost_estimate=pl.CostEstimate(flops=8_000_000_000, bytes_accessed=8_000_000, transcendentals=0),
        name="reweight",
    )(row_ids, row_counts, activations, cotangents)


def solution(mesh):
    placed = (P("dp", "seq", "tensor"), P("dp", "seq", "tensor"), P("dp", None), P("dp", None))
    return jax.shard_map(
        body,
        mesh=mesh,
        in_specs=placed,
        out_specs=(P(("dp", "seq"), "tensor"), P("dp", None)),
        check_vma=False,
    )
```

```python
import jax
import jax.numpy as jnp
from jax import lax
from jax.experimental import pallas as pl
from jax.experimental.pallas import tpu as pltpu
from jax.sharding import PartitionSpec as P

MESH = pl.DeviceIdType.MESH
F32 = jnp.float32
BF16 = jnp.bfloat16

SEG = 88
NOISE = 176
CLEAN_ROWS = 96
WA = 768
WB = 1024
LANES = 128


def body_kernel(ids_ref, counts_ref, acts_ref, cot_ref, out_ref, wout_ref,
                na, ca, cg, ga, gb, raw, at, part_gram, grad_gram, full, d2, sm,
                near_a, near_b, x3, sv1, sv2, wts, scale,
                ring_s, ring_r, p_s, p_r, p_l, k_s, k_r,
                d_s, d_r, m_s, m_r, v_s, v_r):
    z = lax.axis_index("dp")
    y = lax.axis_index("seq")
    t = lax.axis_index("tensor")
    x = t // 2
    c = lax.rem(t, 2)

    def mod4(v):
        return lax.rem(v, 4)

    def copy(src, dst, s, r, dev):
        return pltpu.make_async_remote_copy(
            src_ref=src, dst_ref=dst, send_sem=s, recv_sem=r, device_id=dev, device_id_type=MESH)

    barrier = pltpu.get_barrier_semaphore()

    def greet(dev):
        pl.semaphore_signal(barrier, inc=1, device_id=dev, device_id_type=MESH)

    def cell(r):
        other = lax.rem(4 * z + y + r, 16)
        return other // 4, lax.rem(other, 4), t

    for r in range(1, 16):
        greet(cell(r))
    for r in range(1, 8):
        greet((z, y, lax.rem(t + r, 8)))

    targets = [(h, q, (x, 2 * c + h, 2 * q + z // 2)) for h in range(2) for q in range(4)]
    target_self = [(x == z) & (y == 2 * c + h) & (q == x) & (c == z // 2) for h, q, _ in targets]
    sources = [(2 * c + i // 4, i % 4) for i in range(8)]
    source_self = [(zs == z) & (ys == y) & (x == z) & (c == y // 2) for zs, ys in sources]
    for (_, _, dev), same in zip(targets, target_self):
        @pl.when(jnp.logical_not(same))
        def _():
            greet(dev)
    for (zs, ys), same in zip(sources, source_self):
        @pl.when(jnp.logical_not(same))
        def _():
            greet((zs, ys, 2 * z + y // 2))
    has_self = ((x == z) & (c == y // 2) & (c == z // 2)).astype(jnp.int32)

    rid = [ids_ref[0, j] for j in range(3)]
    live = [counts_ref[0, rid[j]] - y * SEG for j in range(3)]
    rows = lax.broadcasted_iota(jnp.int32, (SEG, LANES), 0)
    pad = jnp.zeros((CLEAN_ROWS - SEG, LANES), F32)

    def stage_acts(i, carry):
        cols = pl.ds(pl.multiple_of(i * LANES, LANES), LANES)
        part = [acts_ref[rid[j], :, cols].astype(F32) for j in range(3)]
        na[y, :, cols] = jnp.concatenate([part[1], part[2]], axis=0).astype(BF16)
        ca[z, :, cols] = jnp.concatenate([part[0], pad], axis=0).astype(BF16)
        return carry

    lax.fori_loop(0, 1024 // LANES, stage_acts, 0)

    def masked(j, cols):
        return jnp.where(rows < live[j], cot_ref[rid[j], :, cols].astype(F32), 0.0)

    def stage_clean(i, carry):
        cols = pl.ds(pl.multiple_of(i * LANES, LANES), LANES)
        cg[z, :, cols] = jnp.concatenate([masked(0, cols), pad], axis=0).astype(BF16)
        return carry

    def stage_a(i, carry):
        cols = pl.ds(pl.multiple_of(i * LANES, LANES), LANES)
        ga[z, y, :, cols] = jnp.concatenate([masked(1, cols), masked(2, cols)], axis=0).astype(BF16)
        return carry

    def stage_b(i, carry):
        cols = pl.ds(pl.multiple_of(i * LANES, LANES), LANES)
        from_cols = pl.ds(pl.multiple_of(WA + i * LANES, LANES), LANES)
        gb[y, z, :, cols] = jnp.concatenate(
            [masked(1, from_cols), masked(2, from_cols)], axis=0).astype(BF16)
        return carry

    pl.semaphore_wait(barrier, 38 - 2 * has_self)

    pieces = []
    for i, ((h, q, dev), same) in enumerate(zip(targets, target_self)):
        src = na.at[y, :, pl.ds(h * 512 + q * LANES, LANES)]
        dst = raw.at[lax.rem(z, 2), y]
        far_copy = copy(src, dst, p_s.at[i], p_r.at[lax.rem(z, 2) * 4 + y], dev)
        near_copy = pltpu.make_async_copy(src, dst, p_l)

        @pl.when(same)
        def _():
            near_copy.start()

        @pl.when(jnp.logical_not(same))
        def _():
            far_copy.start()
        pieces.append((far_copy, near_copy, same))

    rings = []

    class Ring:
        def __init__(self, at, axis, first, second):
            n = len(rings)
            rings.append(self)
            me = {"x": x, "y": y, "z": z}[axis]

            def dev(v):
                return {"x": (z, y, 2 * v + c), "y": (z, v, t), "z": (v, y, t)}[axis]

            up, down, far = mod4(me + 1), mod4(me + 3), mod4(me + 2)
            own, low, high, opp = at(me), at(down), at(up), at(far)
            self.go = [copy(own, own, ring_s.at[n, 0], ring_r.at[n, 0], dev(up)),
                       copy(own, own, ring_s.at[n, 1], ring_r.at[n, 1], dev(down))]
            self.got = [copy(low, low, ring_s.at[n, 0], ring_r.at[n, 0], dev(up)),
                        copy(high, high, ring_s.at[n, 1], ring_r.at[n, 1], dev(down))]
            self.pass_on = [
                copy(low.at[first], low.at[first], ring_s.at[n, 2], ring_r.at[n, 2], dev(up)),
                copy(high.at[second], high.at[second], ring_s.at[n, 3], ring_r.at[n, 3], dev(down))]
            self.got_far = [
                copy(opp.at[first], opp.at[first], ring_s.at[n, 2], ring_r.at[n, 2], dev(up)),
                copy(opp.at[second], opp.at[second], ring_s.at[n, 3], ring_r.at[n, 3], dev(down))]

        def start(self):
            for k in self.go:
                k.start()

        def forward(self):
            for k in range(2):
                self.got[k].wait_recv()
                self.pass_on[k].start()

        def finish(self):
            for k in self.got_far:
                k.wait_recv()

        def drain(self):
            for k in self.go + self.pass_on:
                k.wait_send()

    even = (pl.ds(0, 96),), (pl.ds(96, 80),)
    odd = (pl.ds(80, 96),), (pl.ds(0, 80),)
    equal = (pl.ds(0, 48),), (pl.ds(48, 48),)

    def az_ring(k):
        item = mod4(y + k)
        return Ring(lambda v: ga.at[v, item], "z", *(even if k in (0, 1) else odd))

    def by_ring(k):
        item = mod4(z + k)
        return Ring(lambda v: gb.at[v, item], "y", *(even if k in (0, 1) else odd))

    def rows_of(chunk):
        return pl.ds(pl.multiple_of(chunk * SEG, 8), SEG)

    r_na = Ring(lambda v: na.at[v], "y", *even)
    r_ca = Ring(lambda v: ca.at[v], "z", *equal)
    r_cg = Ring(lambda v: cg.at[v], "z", *equal)
    r_ay = Ring(lambda v: ga.at[z, v], "y", *odd)
    r_bz = Ring(lambda v: gb.at[y, v], "z", *odd)
    r_az = {k: az_ring(k) for k in (0, 3, 1, 2)}
    r_by = {k: by_ring(k) for k in (0, 3, 1, 2)}
    here = pl.ds(2 * c, 2)
    there = pl.ds(2 * (1 - c), 2)
    r_ao = Ring(lambda v: at.at[v, here], "x", (pl.ds(0, 1),), (pl.ds(1, 1),))
    r_full = Ring(lambda v: full.at[rows_of(4 * c + v)], "x", (pl.ds(0, 48),), (pl.ds(48, 40),))

    r_na.start()
    r_ca.start()
    lax.fori_loop(0, WA // LANES, stage_a, 0)
    r_ay.start()
    lax.fori_loop(0, (WA + WB) // LANES, stage_clean, 0)
    r_cg.start()
    lax.fori_loop(0, WB // LANES, stage_b, 0)

    r_ca.forward()
    r_bz.start()
    r_na.forward()
    r_by[0].start()
    for i, ((zs, ys), same) in enumerate(zip(sources, source_self)):
        dst = raw.at[i // 4, i % 4]
        far_copy = copy(dst, dst, p_s.at[i], p_r.at[i], (z, y, lax.rem(t + 1, 8)))
        near_copy = pltpu.make_async_copy(dst, dst, p_l)

        @pl.when(same)
        def _():
            near_copy.wait()

        @pl.when(jnp.logical_not(same))
        def _():
            far_copy.wait_recv()
    tail = jnp.zeros((256 - NOISE, LANES), F32)

    def turn(i, carry):
        piece = jnp.concatenate([raw[i // 4, lax.rem(i, 4)].astype(F32), tail], axis=0)
        at[x, 2 * c + i // 4, lax.rem(i, 4)] = piece.T.astype(BF16)
        return carry

    lax.fori_loop(0, 8, turn, 0)
    mine = at.at[x, here]
    partner = (z, y, 2 * x + 1 - c)
    r_ao.start()
    core = [copy(mine, mine, k_s.at[0], k_r.at[0], partner)]
    core[0].start()

    def relay(r):
        block = at.at[mod4(x + 4 - r), here]
        core.append(copy(block, block, k_s.at[r], k_r.at[r], partner))
        core[-1].start()

    r_cg.forward()
    r_az[0].start()
    r_ay.forward()

    contract = (((1,), (1,)), ((), ()))

    def gram(left, right):
        return lax.dot_general(left, right, contract, preferred_element_type=F32)

    r_na.finish()
    r_ca.finish()
    part_gram[...] = gram(na[...].reshape(4 * NOISE, 1024), ca[...].reshape(4 * CLEAN_ROWS, 1024))
    own_half = pl.ds(pl.multiple_of(c * 352, 8), 352)
    other_half = pl.ds(pl.multiple_of((1 - c) * 352, 8), 352)
    swap = copy(part_gram.at[other_half], d2, d_s.at[0], d_r.at[0], partner)
    swap.start()

    r_ao.forward()
    relay(1)
    relay(3)
    r_bz.forward()
    r_az[3].start()
    r_az[1].start()

    swap.wait_recv()
    sm[...] = part_gram[own_half] + d2[...]
    up, down, across = mod4(x + 1), mod4(x + 3), mod4(x + 2)
    dev_up, dev_down = (z, y, 2 * up + c), (z, y, 2 * down + c)
    first = pl.ds(pl.multiple_of(across * SEG, 8), 48)
    second = pl.ds(pl.multiple_of(across * SEG + 48, 8), 40)
    share = [copy(sm.at[first], near_a, m_s.at[0], m_r.at[0], dev_up),
             copy(sm.at[second], near_b, m_s.at[1], m_r.at[1], dev_down),
             copy(sm.at[rows_of(up)], x3.at[0], m_s.at[2], m_r.at[2], dev_up),
             copy(sm.at[rows_of(down)], x3.at[1], m_s.at[3], m_r.at[3], dev_down)]
    share[0].start()
    share[1].start()
    r_ao.finish()
    relay(2)
    r_by[0].forward()
    r_by[3].start()
    r_by[1].start()
    share[0].wait_recv()
    sm[pl.ds(pl.multiple_of(up * SEG, 8), 48)] += near_a[...]
    share[2].start()
    share[1].wait_recv()
    sm[pl.ds(pl.multiple_of(down * SEG + 48, 8), 40)] += near_b[...]
    share[3].start()

    r_cg.finish()
    r_ay.finish()
    r_az[2].start()
    grad_gram[...] = gram(ga[z].reshape(4 * NOISE, WA), cg[:, :, :WA].reshape(4 * CLEAN_ROWS, WA))

    share[2].wait_recv()
    share[3].wait_recv()
    full[rows_of(4 * c + x)] = sm[rows_of(x)] + x3[0] + x3[1]
    r_full.start()
    r_az[0].forward()
    r_full.forward()
    r_full.finish()
    give = copy(full.at[own_half], full.at[own_half], d_s.at[1], d_r.at[1], partner)
    give.start()

    r_bz.finish()
    r_by[2].start()
    r_by[0].finish()
    grad_gram[...] += gram(gb[:, z].reshape(4 * NOISE, WB), cg[:, :, WA:].reshape(4 * CLEAN_ROWS, WB))
    copy(full.at[other_half], full.at[other_half], d_s.at[1], d_r.at[1], partner).wait_recv()

    def row_dot(j):
        terms = [grad_gram[g * SEG:(g + 1) * SEG] * full[g * SEG:(g + 1) * SEG] for g in range(j, 8, 2)]
        rows_sum = jnp.sum(terms[0] + terms[1] + terms[2] + terms[3], axis=0, keepdims=True)
        return jnp.broadcast_to(jnp.sum(rows_sum, axis=1, keepdims=True), (8, LANES))

    place = lax.broadcasted_iota(jnp.int32, (8, LANES), 0)
    tile = jnp.where(place == 2 * z, row_dot(0), jnp.where(place == 2 * z + 1, row_dot(1), 0.0))

    sends = []

    def send_tile(buf, value, me, n, dev, base):
        buf[me] = value
        for r in range(1, n):
            out = copy(buf.at[me], buf.at[me], v_s.at[base + r], v_r.at[base + r], dev(r))
            out.start()
            sends.append(out)

    def sum_tiles(buf, me, n, base):
        for r in range(1, n):
            origin = buf.at[lax.rem(me + n - r, n)]
            copy(origin, origin, v_s.at[base + r], v_r.at[base + r], partner).wait_recv()
        return jnp.sum(buf[...], axis=0)

    send_tile(sv1, tile, t, 8, lambda r: (z, y, lax.rem(t + r, 8)), 0)

    for r in range(4):
        block = at.at[mod4(x + 4 - r), there]
        copy(block, block, k_s.at[r], k_r.at[r], partner).wait_recv()

    tile = sum_tiles(sv1, t, 8, 0)
    send_tile(sv2, tile, 4 * z + y, 16, cell, 8)
    r_az[3].forward()
    r_by[3].forward()
    tile = sum_tiles(sv2, 4 * z + y, 16, 8)
    weights = jnp.maximum(-tile, 0.0) / jnp.sum(jnp.abs(tile), axis=0, keepdims=True)
    wts[...] = weights
    for k in range(4):
        scale[k, :SEG] = jnp.broadcast_to(wts[2 * k:2 * k + 1, :], (SEG, LANES))
        scale[k, SEG:] = jnp.broadcast_to(wts[2 * k + 1:2 * k + 2, :], (SEG, LANES))
    lane = lax.broadcasted_iota(jnp.int32, (1, LANES), 1)
    wout_ref[...] = jnp.where(lane == 0, wts[pl.ds(2 * z, 1), :], wts[pl.ds(2 * z + 1, 1), :])[:, :2]

    gap = jnp.zeros((256 - NOISE, 256), BF16)

    def product(left_of, pieces_of, width, base, first):
        def step(i, carry):
            cols = pl.ds(pl.multiple_of(i * 256, 256), 256)
            dest = pl.ds(pl.multiple_of(base + i * 256, 256), 256)
            right = []
            for raw_rows, s in pieces_of(cols):
                full_scale = jnp.concatenate([s, s], axis=1)
                right += [(raw_rows.astype(F32) * full_scale).astype(BF16), gap]
            left = jnp.concatenate(
                [jnp.concatenate([left_of(q, k) for k in range(4)], axis=1) for q in range(4)], axis=0)
            value = jnp.dot(left, jnp.concatenate(right, axis=0), preferred_element_type=F32)
            if first:
                out_ref[:, dest] = value
            else:
                out_ref[:, dest] += value
            return carry

        lax.fori_loop(0, width // 256, step, 0)

    def add_a(k, first=False):
        v = mod4(z + k)
        product(lambda q, i: at[q, v, i], lambda cols: [(ga[v, i, :, cols], scale[v]) for i in range(4)],
                WA, 0, first)

    def add_b(k, first=False):
        v = mod4(y + k)
        product(lambda q, i: at[q, i, v], lambda cols: [(gb[v, i, :, cols], scale[i]) for i in range(4)],
                WB, WA, first)

    add_a(0, True)
    r_az[1].forward()
    r_by[1].forward()
    add_b(0, True)
    r_az[2].forward()
    add_a(3)
    r_by[2].forward()
    add_a(1)
    add_b(3)
    add_b(1)
    for k in (0, 3, 1, 2):
        r_az[k].finish()
    add_a(2)
    for k in (3, 1, 2):
        r_by[k].finish()
    add_b(2)

    for far_copy, _, same in pieces:
        @pl.when(jnp.logical_not(same))
        def _():
            far_copy.wait_send()
    for ring in rings:
        ring.drain()
    for k in core + [swap, give] + share + sends:
        k.wait_send()


def body(activations, cotangents, row_ids, row_counts):
    dma = pltpu.SemaphoreType.DMA
    vmem = pltpu.VMEM
    return pl.pallas_call(
        body_kernel,
        out_shape=(pltpu.VMEM((512, WA + WB), F32), pltpu.VMEM((1, 2), F32)),
        in_specs=[pl.BlockSpec(memory_space=pltpu.SMEM)] * 2 + [pl.BlockSpec(memory_space=pltpu.VMEM)] * 2,
        out_specs=(pl.BlockSpec(memory_space=pltpu.VMEM), pl.BlockSpec(memory_space=pltpu.VMEM)),
        scratch_shapes=[
            vmem((4, NOISE, 1024), BF16),
            vmem((4, CLEAN_ROWS, 1024), BF16),
            vmem((4, CLEAN_ROWS, WA + WB), BF16),
            vmem((4, 4, NOISE, WA), BF16),
            vmem((4, 4, NOISE, WB), BF16),
            vmem((2, 4, NOISE, LANES), BF16),
            vmem((4, 4, 4, LANES, 256), BF16),
            vmem((4 * NOISE, 4 * CLEAN_ROWS), F32),
            vmem((4 * NOISE, 4 * CLEAN_ROWS), F32),
            vmem((4 * NOISE, 4 * CLEAN_ROWS), F32),
            vmem((2 * NOISE, 4 * CLEAN_ROWS), F32),
            vmem((2 * NOISE, 4 * CLEAN_ROWS), F32),
            vmem((48, 4 * CLEAN_ROWS), F32),
            vmem((40, 4 * CLEAN_ROWS), F32),
            vmem((2, SEG, 4 * CLEAN_ROWS), F32),
            vmem((8, 8, LANES), F32),
            vmem((16, 8, LANES), F32),
            vmem((8, LANES), F32),
            vmem((4, NOISE, LANES), F32),
            dma((15, 4)), dma((15, 4)),
            dma((8,)), dma((8,)), dma,
            dma((4,)), dma((4,)),
            dma((2,)), dma((2,)),
            dma((4,)), dma((4,)),
            dma((24,)), dma((24,)),
        ],
        compiler_params=pltpu.CompilerParams(
            collective_id=0, has_side_effects=True, vmem_limit_bytes=60 * 1024 * 1024),
        cost_estimate=pl.CostEstimate(flops=8_000_000_000, bytes_accessed=8_000_000, transcendentals=0),
        name="reweight",
    )(row_ids, row_counts, activations, cotangents)


def solution(mesh):
    placed = (P("dp", "seq", "tensor"), P("dp", "seq", "tensor"), P("dp", None), P("dp", None))
    return jax.shard_map(
        body,
        mesh=mesh,
        in_specs=placed,
        out_specs=(P(("dp", "seq"), "tensor"), P("dp", None)),
        check_vma=False,
    )
```

```python
import jax
import jax.numpy as jnp
from jax import lax
from jax.experimental import pallas as pl
from jax.experimental.pallas import tpu as pltpu
from jax.sharding import PartitionSpec as P

MESH = pl.DeviceIdType.MESH
F32 = jnp.float32
BF16 = jnp.bfloat16

SEG = 88
NOISE = 176
CLEAN_ROWS = 96
WA = 768
WB = 1024
LANES = 128


def body_kernel(ids_ref, counts_ref, acts_ref, cot_ref, out_ref, wout_ref,
                na, ca, cg, ga, gb, ao, ata, atb, part_gram, grad_gram, full, d2, sm,
                near_a, near_b, x3, sv1, sv2, wts, scale,
                ring_s, ring_r, p_s, p_r, p_l, k_s, k_r,
                d_s, d_r, m_s, m_r, v_s, v_r):
    z = lax.axis_index("dp")
    y = lax.axis_index("seq")
    t = lax.axis_index("tensor")
    x = t // 2
    c = lax.rem(t, 2)

    def mod4(v):
        return lax.rem(v, 4)

    def copy(src, dst, s, r, dev):
        return pltpu.make_async_remote_copy(
            src_ref=src, dst_ref=dst, send_sem=s, recv_sem=r, device_id=dev, device_id_type=MESH)

    barrier = pltpu.get_barrier_semaphore()

    def greet(dev):
        pl.semaphore_signal(barrier, inc=1, device_id=dev, device_id_type=MESH)

    def cell(r):
        other = lax.rem(4 * z + y + r, 16)
        return other // 4, lax.rem(other, 4), t

    for r in range(1, 16):
        greet(cell(r))
    for r in range(1, 8):
        greet((z, y, lax.rem(t + r, 8)))

    targets = [(h, q, (x, 2 * c + h, 2 * q + z // 2)) for h in range(2) for q in range(4)]
    target_self = [(x == z) & (y == 2 * c + h) & (q == x) & (c == z // 2) for h, q, _ in targets]
    sources = [(2 * c + i // 4, i % 4) for i in range(8)]
    source_self = [(zs == z) & (ys == y) & (x == z) & (c == y // 2) for zs, ys in sources]
    for (_, _, dev), same in zip(targets, target_self):
        @pl.when(jnp.logical_not(same))
        def _():
            greet(dev)
    for (zs, ys), same in zip(sources, source_self):
        @pl.when(jnp.logical_not(same))
        def _():
            greet((zs, ys, 2 * z + y // 2))
    has_self = ((x == z) & (c == y // 2) & (c == z // 2)).astype(jnp.int32)

    rid = [ids_ref[0, j] for j in range(3)]
    live = [counts_ref[0, rid[j]] - y * SEG for j in range(3)]
    rows = lax.broadcasted_iota(jnp.int32, (SEG, LANES), 0)
    pad = jnp.zeros((CLEAN_ROWS - SEG, LANES), F32)

    def stage_acts(i, carry):
        cols = pl.ds(pl.multiple_of(i * LANES, LANES), LANES)
        part = [acts_ref[rid[j], :, cols].astype(F32) for j in range(3)]
        na[y, :, cols] = jnp.concatenate([part[1], part[2]], axis=0).astype(BF16)
        ca[z, :, cols] = jnp.concatenate([part[0], pad], axis=0).astype(BF16)
        return carry

    lax.fori_loop(0, 1024 // LANES, stage_acts, 0)

    def masked(j, cols):
        return jnp.where(rows < live[j], cot_ref[rid[j], :, cols].astype(F32), 0.0)

    def stage_clean(i, carry):
        cols = pl.ds(pl.multiple_of(i * LANES, LANES), LANES)
        cg[z, :, cols] = jnp.concatenate([masked(0, cols), pad], axis=0).astype(BF16)
        return carry

    def stage_a(i, carry):
        cols = pl.ds(pl.multiple_of(i * LANES, LANES), LANES)
        ga[z, y, :, cols] = jnp.concatenate([masked(1, cols), masked(2, cols)], axis=0).astype(BF16)
        return carry

    def stage_b(i, carry):
        cols = pl.ds(pl.multiple_of(i * LANES, LANES), LANES)
        from_cols = pl.ds(pl.multiple_of(WA + i * LANES, LANES), LANES)
        gb[y, z, :, cols] = jnp.concatenate(
            [masked(1, from_cols), masked(2, from_cols)], axis=0).astype(BF16)
        return carry

    pl.semaphore_wait(barrier, 38 - 2 * has_self)

    pieces = []
    for i, ((h, q, dev), same) in enumerate(zip(targets, target_self)):
        src = na.at[y, :, pl.ds(h * 512 + q * LANES, LANES)]
        dst = ao.at[q, z, y]
        far_copy = copy(src, dst, p_s.at[i], p_r.at[lax.rem(z, 2) * 4 + y], dev)
        near_copy = pltpu.make_async_copy(src, dst, p_l)

        @pl.when(same)
        def _():
            near_copy.start()

        @pl.when(jnp.logical_not(same))
        def _():
            far_copy.start()
        pieces.append((far_copy, near_copy, same))

    rings = []

    class Ring:
        def __init__(self, at, axis, first, second):
            n = len(rings)
            rings.append(self)
            me = {"x": x, "y": y, "z": z}[axis]

            def dev(v):
                return {"x": (z, y, 2 * v + c), "y": (z, v, t), "z": (v, y, t)}[axis]

            up, down, far = mod4(me + 1), mod4(me + 3), mod4(me + 2)
            own, low, high, opp = at(me), at(down), at(up), at(far)
            self.go = [copy(own, own, ring_s.at[n, 0], ring_r.at[n, 0], dev(up)),
                       copy(own, own, ring_s.at[n, 1], ring_r.at[n, 1], dev(down))]
            self.got = [copy(low, low, ring_s.at[n, 0], ring_r.at[n, 0], dev(up)),
                        copy(high, high, ring_s.at[n, 1], ring_r.at[n, 1], dev(down))]
            self.pass_on = [
                copy(low.at[first], low.at[first], ring_s.at[n, 2], ring_r.at[n, 2], dev(up)),
                copy(high.at[second], high.at[second], ring_s.at[n, 3], ring_r.at[n, 3], dev(down))]
            self.got_far = [
                copy(opp.at[first], opp.at[first], ring_s.at[n, 2], ring_r.at[n, 2], dev(up)),
                copy(opp.at[second], opp.at[second], ring_s.at[n, 3], ring_r.at[n, 3], dev(down))]

        def start(self):
            for k in self.go:
                k.start()

        def forward(self):
            for k in range(2):
                self.got[k].wait_recv()
                self.pass_on[k].start()

        def finish(self):
            for k in self.got_far:
                k.wait_recv()

        def drain(self):
            for k in self.go + self.pass_on:
                k.wait_send()

    even = (pl.ds(0, 96),), (pl.ds(96, 80),)
    odd = (pl.ds(80, 96),), (pl.ds(0, 80),)
    equal = (pl.ds(0, 48),), (pl.ds(48, 48),)

    def az_ring(k):
        item = mod4(y + k)
        return Ring(lambda v: ga.at[v, item], "z", *(even if k in (0, 1) else odd))

    def by_ring(k):
        item = mod4(z + k)
        return Ring(lambda v: gb.at[v, item], "y", *(even if k in (0, 1) else odd))

    def rows_of(chunk):
        return pl.ds(pl.multiple_of(chunk * SEG, 8), SEG)

    r_na = Ring(lambda v: na.at[v], "y", *even)
    r_ca = Ring(lambda v: ca.at[v], "z", *equal)
    r_cg = Ring(lambda v: cg.at[v], "z", *equal)
    r_ay = Ring(lambda v: ga.at[z, v], "y", *odd)
    r_bz = Ring(lambda v: gb.at[y, v], "z", *odd)
    r_az = {k: az_ring(k) for k in (0, 3, 1, 2)}
    r_by = {k: by_ring(k) for k in (0, 3, 1, 2)}
    here = pl.ds(2 * c, 2)
    there = pl.ds(2 * (1 - c), 2)
    r_ao = Ring(lambda v: ao.at[v, here], "x", (pl.ds(0, 1),), (pl.ds(1, 1),))
    r_full = Ring(lambda v: full.at[rows_of(4 * c + v)], "x", (pl.ds(0, 48),), (pl.ds(48, 40),))

    r_na.start()
    r_ca.start()
    lax.fori_loop(0, WA // LANES, stage_a, 0)
    r_ay.start()
    lax.fori_loop(0, (WA + WB) // LANES, stage_clean, 0)
    r_cg.start()
    lax.fori_loop(0, WB // LANES, stage_b, 0)

    r_ca.forward()
    r_bz.start()
    r_na.forward()
    r_by[0].start()
    for i, ((zs, ys), same) in enumerate(zip(sources, source_self)):
        dst = ao.at[x, zs, ys]
        far_copy = copy(dst, dst, p_s.at[i], p_r.at[i], (z, y, lax.rem(t + 1, 8)))
        near_copy = pltpu.make_async_copy(dst, dst, p_l)

        @pl.when(same)
        def _():
            near_copy.wait()

        @pl.when(jnp.logical_not(same))
        def _():
            far_copy.wait_recv()
    mine = ao.at[x, here]
    partner = (z, y, 2 * x + 1 - c)
    r_ao.start()
    core = [copy(mine, mine, k_s.at[0], k_r.at[0], partner)]
    core[0].start()

    def relay(r):
        block = ao.at[mod4(x + 4 - r), here]
        core.append(copy(block, block, k_s.at[r], k_r.at[r], partner))
        core[-1].start()

    r_cg.forward()
    r_az[0].start()
    r_ay.forward()
    r_ao.forward()
    relay(1)
    relay(3)

    contract = (((1,), (1,)), ((), ()))

    def gram(left, right):
        return lax.dot_general(left, right, contract, preferred_element_type=F32)

    r_na.finish()
    r_ca.finish()
    part_gram[...] = gram(na[...].reshape(4 * NOISE, 1024), ca[...].reshape(4 * CLEAN_ROWS, 1024))
    own_half = pl.ds(pl.multiple_of(c * 352, 8), 352)
    other_half = pl.ds(pl.multiple_of((1 - c) * 352, 8), 352)
    swap = copy(part_gram.at[other_half], d2, d_s.at[0], d_r.at[0], partner)
    swap.start()

    r_ao.finish()
    relay(2)
    r_bz.forward()
    r_az[3].start()
    r_az[1].start()

    def turn(k):
        def step(q, carry):
            span = pl.ds(pl.multiple_of(q * LANES, LANES), LANES)
            ata[k, span, :] = ao[q, k].reshape(4 * NOISE, LANES).T
            atb[k, span, :] = ao[q, :, k].reshape(4 * NOISE, LANES).T
            return carry

        lax.fori_loop(0, 4, step, 0)

    swap.wait_recv()
    sm[...] = part_gram[own_half] + d2[...]
    up, down, across = mod4(x + 1), mod4(x + 3), mod4(x + 2)
    dev_up, dev_down = (z, y, 2 * up + c), (z, y, 2 * down + c)
    first = pl.ds(pl.multiple_of(across * SEG, 8), 48)
    second = pl.ds(pl.multiple_of(across * SEG + 48, 8), 40)
    share = [copy(sm.at[first], near_a, m_s.at[0], m_r.at[0], dev_up),
             copy(sm.at[second], near_b, m_s.at[1], m_r.at[1], dev_down),
             copy(sm.at[rows_of(up)], x3.at[0], m_s.at[2], m_r.at[2], dev_up),
             copy(sm.at[rows_of(down)], x3.at[1], m_s.at[3], m_r.at[3], dev_down)]
    share[0].start()
    share[1].start()
    for r in range(4):
        block = ao.at[mod4(x + 4 - r), there]
        copy(block, block, k_s.at[r], k_r.at[r], partner).wait_recv()
    r_by[0].forward()
    r_by[3].start()
    r_by[1].start()
    turn(0)
    share[0].wait_recv()
    sm[pl.ds(pl.multiple_of(up * SEG, 8), 48)] += near_a[...]
    share[2].start()
    share[1].wait_recv()
    sm[pl.ds(pl.multiple_of(down * SEG + 48, 8), 40)] += near_b[...]
    share[3].start()
    turn(1)

    r_cg.finish()
    r_ay.finish()
    r_az[2].start()
    grad_gram[...] = gram(ga[z].reshape(4 * NOISE, WA), cg[:, :, :WA].reshape(4 * CLEAN_ROWS, WA))

    share[2].wait_recv()
    share[3].wait_recv()
    full[rows_of(4 * c + x)] = sm[rows_of(x)] + x3[0] + x3[1]
    r_full.start()
    r_az[0].forward()
    turn(2)
    r_full.forward()
    turn(3)
    r_full.finish()
    give = copy(full.at[own_half], full.at[own_half], d_s.at[1], d_r.at[1], partner)
    give.start()

    r_bz.finish()
    r_by[2].start()
    r_by[0].finish()
    grad_gram[...] += gram(gb[:, z].reshape(4 * NOISE, WB), cg[:, :, WA:].reshape(4 * CLEAN_ROWS, WB))
    copy(full.at[other_half], full.at[other_half], d_s.at[1], d_r.at[1], partner).wait_recv()

    def row_dot(j):
        terms = [grad_gram[g * SEG:(g + 1) * SEG] * full[g * SEG:(g + 1) * SEG] for g in range(j, 8, 2)]
        rows_sum = jnp.sum(terms[0] + terms[1] + terms[2] + terms[3], axis=0, keepdims=True)
        return jnp.broadcast_to(jnp.sum(rows_sum, axis=1, keepdims=True), (8, LANES))

    place = lax.broadcasted_iota(jnp.int32, (8, LANES), 0)
    tile = jnp.where(place == 2 * z, row_dot(0), jnp.where(place == 2 * z + 1, row_dot(1), 0.0))

    sends = []

    def send_tile(buf, value, me, n, dev, base):
        buf[me] = value
        for r in range(1, n):
            out = copy(buf.at[me], buf.at[me], v_s.at[base + r], v_r.at[base + r], dev(r))
            out.start()
            sends.append(out)

    def sum_tiles(buf, me, n, base):
        for r in range(1, n):
            origin = buf.at[lax.rem(me + n - r, n)]
            copy(origin, origin, v_s.at[base + r], v_r.at[base + r], partner).wait_recv()
        return jnp.sum(buf[...], axis=0)

    send_tile(sv1, tile, t, 8, lambda r: (z, y, lax.rem(t + r, 8)), 0)

    tile = sum_tiles(sv1, t, 8, 0)
    send_tile(sv2, tile, 4 * z + y, 16, cell, 8)
    r_az[3].forward()
    r_by[3].forward()
    tile = sum_tiles(sv2, 4 * z + y, 16, 8)
    weights = jnp.maximum(-tile, 0.0) / jnp.sum(jnp.abs(tile), axis=0, keepdims=True)
    wts[...] = weights
    for k in range(4):
        scale[k, :SEG] = jnp.broadcast_to(wts[2 * k:2 * k + 1, :], (SEG, LANES))
        scale[k, SEG:] = jnp.broadcast_to(wts[2 * k + 1:2 * k + 2, :], (SEG, LANES))
    lane = lax.broadcasted_iota(jnp.int32, (1, LANES), 1)
    wout_ref[...] = jnp.where(lane == 0, wts[pl.ds(2 * z, 1), :], wts[pl.ds(2 * z + 1, 1), :])[:, :2]

    def scaled(raw, s):
        full = jnp.concatenate([s] * (raw.shape[1] // LANES), axis=1)
        return (raw.astype(F32) * full).astype(BF16)

    def product(at, pieces_of, width, base, first, span):
        def step(i, carry):
            cols = pl.ds(pl.multiple_of(i * span, span), span)
            dest = pl.ds(pl.multiple_of(base + i * span, 256), span)
            right = jnp.concatenate([scaled(raw, s) for raw, s in pieces_of(cols)], axis=0)
            value = jnp.dot(at[...], right, preferred_element_type=F32)
            if first:
                out_ref[:, dest] = value
            else:
                out_ref[:, dest] += value
            return carry

        lax.fori_loop(0, width // span, step, 0)

    def add_a(k, first=False):
        v = mod4(z + k)
        product(ata.at[v], lambda cols: [(ga[v, i, :, cols], scale[v]) for i in range(4)], WA, 0, first, 768)

    def add_b(k, first=False):
        v = mod4(y + k)
        product(atb.at[v], lambda cols: [(gb[v, i, :, cols], scale[i]) for i in range(4)], WB, WA, first, 512)

    add_a(0, True)
    r_az[1].forward()
    r_by[1].forward()
    add_b(0, True)
    r_az[2].forward()
    add_a(3)
    r_by[2].forward()
    add_a(1)
    add_b(3)
    add_b(1)
    for k in (0, 3, 1, 2):
        r_az[k].finish()
    add_a(2)
    for k in (3, 1, 2):
        r_by[k].finish()
    add_b(2)

    for far_copy, _, same in pieces:
        @pl.when(jnp.logical_not(same))
        def _():
            far_copy.wait_send()
    for ring in rings:
        ring.drain()
    for k in core + [swap, give] + share + sends:
        k.wait_send()


def body(activations, cotangents, row_ids, row_counts):
    dma = pltpu.SemaphoreType.DMA
    vmem = pltpu.VMEM
    return pl.pallas_call(
        body_kernel,
        out_shape=(pltpu.VMEM((512, WA + WB), F32), pltpu.VMEM((1, 2), F32)),
        in_specs=[pl.BlockSpec(memory_space=pltpu.SMEM)] * 2 + [pl.BlockSpec(memory_space=pltpu.VMEM)] * 2,
        out_specs=(pl.BlockSpec(memory_space=pltpu.VMEM), pl.BlockSpec(memory_space=pltpu.VMEM)),
        scratch_shapes=[
            vmem((4, NOISE, 1024), BF16),
            vmem((4, CLEAN_ROWS, 1024), BF16),
            vmem((4, CLEAN_ROWS, WA + WB), BF16),
            vmem((4, 4, NOISE, WA), BF16),
            vmem((4, 4, NOISE, WB), BF16),
            vmem((4, 4, 4, NOISE, LANES), BF16),
            vmem((4, 512, 4 * NOISE), BF16),
            vmem((4, 512, 4 * NOISE), BF16),
            vmem((4 * NOISE, 4 * CLEAN_ROWS), F32),
            vmem((4 * NOISE, 4 * CLEAN_ROWS), F32),
            vmem((4 * NOISE, 4 * CLEAN_ROWS), F32),
            vmem((2 * NOISE, 4 * CLEAN_ROWS), F32),
            vmem((2 * NOISE, 4 * CLEAN_ROWS), F32),
            vmem((48, 4 * CLEAN_ROWS), F32),
            vmem((40, 4 * CLEAN_ROWS), F32),
            vmem((2, SEG, 4 * CLEAN_ROWS), F32),
            vmem((8, 8, LANES), F32),
            vmem((16, 8, LANES), F32),
            vmem((8, LANES), F32),
            vmem((4, NOISE, LANES), F32),
            dma((15, 4)), dma((15, 4)),
            dma((8,)), dma((8,)), dma,
            dma((4,)), dma((4,)),
            dma((2,)), dma((2,)),
            dma((4,)), dma((4,)),
            dma((24,)), dma((24,)),
        ],
        compiler_params=pltpu.CompilerParams(
            collective_id=0, has_side_effects=True, vmem_limit_bytes=60 * 1024 * 1024),
        cost_estimate=pl.CostEstimate(flops=8_000_000_000, bytes_accessed=8_000_000, transcendentals=0),
        name="reweight",
    )(row_ids, row_counts, activations, cotangents)


def solution(mesh):
    placed = (P("dp", "seq", "tensor"), P("dp", "seq", "tensor"), P("dp", None), P("dp", None))
    return jax.shard_map(
        body,
        mesh=mesh,
        in_specs=placed,
        out_specs=(P(("dp", "seq"), "tensor"), P("dp", None)),
        check_vma=False,
    )
```

```python
import jax
import jax.numpy as jnp
from jax import lax
from jax.experimental import pallas as pl
from jax.experimental.pallas import tpu as pltpu
from jax.sharding import PartitionSpec as P

MESH = pl.DeviceIdType.MESH
F32 = jnp.float32
BF16 = jnp.bfloat16

SEG = 88
NOISE = 176
CLEAN_ROWS = 96
WA = 768
WB = 1024
LANES = 128


def body_kernel(ids_ref, counts_ref, acts_ref, cot_ref, out_ref, wout_ref,
                na, ca, cg, ga, gb, ao, ata, atb, part_gram, grad_gram, full, d2, sm,
                near_a, near_b, x3, sv1, sv2, wts, scale,
                ring_s, ring_r, p_s, p_r, p_l, k_s, k_r,
                d_s, d_r, m_s, m_r, v_s, v_r):
    z = lax.axis_index("dp")
    y = lax.axis_index("seq")
    t = lax.axis_index("tensor")
    x = t // 2
    c = lax.rem(t, 2)

    def mod4(v):
        return lax.rem(v, 4)

    def copy(src, dst, s, r, dev):
        return pltpu.make_async_remote_copy(
            src_ref=src, dst_ref=dst, send_sem=s, recv_sem=r, device_id=dev, device_id_type=MESH)

    barrier = pltpu.get_barrier_semaphore()

    def greet(dev):
        pl.semaphore_signal(barrier, inc=1, device_id=dev, device_id_type=MESH)

    def cell(r):
        other = lax.rem(4 * z + y + r, 16)
        return other // 4, lax.rem(other, 4), t

    for r in range(1, 16):
        greet(cell(r))
    for r in range(1, 8):
        greet((z, y, lax.rem(t + r, 8)))

    targets = [(h, q, (x, 2 * c + h, 2 * q + z // 2)) for h in range(2) for q in range(4)]
    target_self = [(x == z) & (y == 2 * c + h) & (q == x) & (c == z // 2) for h, q, _ in targets]
    sources = [(2 * c + i // 4, i % 4) for i in range(8)]
    source_self = [(zs == z) & (ys == y) & (x == z) & (c == y // 2) for zs, ys in sources]
    for (_, _, dev), same in zip(targets, target_self):
        @pl.when(jnp.logical_not(same))
        def _():
            greet(dev)
    for (zs, ys), same in zip(sources, source_self):
        @pl.when(jnp.logical_not(same))
        def _():
            greet((zs, ys, 2 * z + y // 2))
    has_self = ((x == z) & (c == y // 2) & (c == z // 2)).astype(jnp.int32)

    rid = [ids_ref[0, j] for j in range(3)]
    live = [counts_ref[0, rid[j]] - y * SEG for j in range(3)]
    rows = lax.broadcasted_iota(jnp.int32, (SEG, LANES), 0)
    pad = jnp.zeros((CLEAN_ROWS - SEG, LANES), F32)

    def stage_acts(i, carry):
        cols = pl.ds(pl.multiple_of(i * LANES, LANES), LANES)
        part = [acts_ref[rid[j], :, cols].astype(F32) for j in range(3)]
        na[y, :, cols] = jnp.concatenate([part[1], part[2]], axis=0).astype(BF16)
        ca[z, :, cols] = jnp.concatenate([part[0], pad], axis=0).astype(BF16)
        return carry

    lax.fori_loop(0, 1024 // LANES, stage_acts, 0)

    def masked(j, cols):
        return jnp.where(rows < live[j], cot_ref[rid[j], :, cols].astype(F32), 0.0)

    def stage_clean(i, carry):
        cols = pl.ds(pl.multiple_of(i * LANES, LANES), LANES)
        cg[z, :, cols] = jnp.concatenate([masked(0, cols), pad], axis=0).astype(BF16)
        return carry

    def stage_a(i, carry):
        cols = pl.ds(pl.multiple_of(i * LANES, LANES), LANES)
        ga[z, y, :, cols] = jnp.concatenate([masked(1, cols), masked(2, cols)], axis=0).astype(BF16)
        return carry

    def stage_b(i, carry):
        cols = pl.ds(pl.multiple_of(i * LANES, LANES), LANES)
        from_cols = pl.ds(pl.multiple_of(WA + i * LANES, LANES), LANES)
        gb[y, z, :, cols] = jnp.concatenate(
            [masked(1, from_cols), masked(2, from_cols)], axis=0).astype(BF16)
        return carry

    pl.semaphore_wait(barrier, 38 - 2 * has_self)

    pieces = []
    for i, ((h, q, dev), same) in enumerate(zip(targets, target_self)):
        src = na.at[y, :, pl.ds(h * 512 + q * LANES, LANES)]
        dst = ao.at[q, z, y]
        far_copy = copy(src, dst, p_s.at[i], p_r.at[lax.rem(z, 2) * 4 + y], dev)
        near_copy = pltpu.make_async_copy(src, dst, p_l)

        @pl.when(same)
        def _():
            near_copy.start()

        @pl.when(jnp.logical_not(same))
        def _():
            far_copy.start()
        pieces.append((far_copy, near_copy, same))

    rings = []

    class Ring:
        def __init__(self, at, axis, first, second):
            n = len(rings)
            rings.append(self)
            me = {"x": x, "y": y, "z": z}[axis]

            def dev(v):
                return {"x": (z, y, 2 * v + c), "y": (z, v, t), "z": (v, y, t)}[axis]

            up, down, far = mod4(me + 1), mod4(me + 3), mod4(me + 2)
            own, low, high, opp = at(me), at(down), at(up), at(far)
            self.go = [copy(own, own, ring_s.at[n, 0], ring_r.at[n, 0], dev(up)),
                       copy(own, own, ring_s.at[n, 1], ring_r.at[n, 1], dev(down))]
            self.got = [copy(low, low, ring_s.at[n, 0], ring_r.at[n, 0], dev(up)),
                        copy(high, high, ring_s.at[n, 1], ring_r.at[n, 1], dev(down))]
            self.pass_on = [
                copy(low.at[first], low.at[first], ring_s.at[n, 2], ring_r.at[n, 2], dev(up)),
                copy(high.at[second], high.at[second], ring_s.at[n, 3], ring_r.at[n, 3], dev(down))]
            self.got_far = [
                copy(opp.at[first], opp.at[first], ring_s.at[n, 2], ring_r.at[n, 2], dev(up)),
                copy(opp.at[second], opp.at[second], ring_s.at[n, 3], ring_r.at[n, 3], dev(down))]

        def start(self):
            for k in self.go:
                k.start()

        def forward(self):
            for k in range(2):
                self.got[k].wait_recv()
                self.pass_on[k].start()

        def finish(self):
            for k in self.got_far:
                k.wait_recv()

        def drain(self):
            for k in self.go + self.pass_on:
                k.wait_send()

    even = (pl.ds(0, 96),), (pl.ds(96, 80),)
    odd = (pl.ds(80, 96),), (pl.ds(0, 80),)
    equal = (pl.ds(0, 48),), (pl.ds(48, 48),)

    def az_ring(k):
        item = mod4(y + k)
        return Ring(lambda v: ga.at[v, item], "z", *(even if k in (0, 1) else odd))

    def by_ring(k):
        item = mod4(z + k)
        return Ring(lambda v: gb.at[v, item], "y", *(even if k in (0, 1) else odd))

    def rows_of(chunk):
        return pl.ds(pl.multiple_of(chunk * SEG, 8), SEG)

    r_na = Ring(lambda v: na.at[v], "y", *even)
    r_ca = Ring(lambda v: ca.at[v], "z", *equal)
    r_cg = Ring(lambda v: cg.at[v], "z", *equal)
    r_ay = Ring(lambda v: ga.at[z, v], "y", *odd)
    r_bz = Ring(lambda v: gb.at[y, v], "z", *odd)
    r_az = {k: az_ring(k) for k in (0, 3, 1, 2)}
    r_by = {k: by_ring(k) for k in (0, 3, 1, 2)}
    here = pl.ds(2 * c, 2)
    there = pl.ds(2 * (1 - c), 2)
    r_ao = Ring(lambda v: ao.at[v, here], "x", (pl.ds(0, 1),), (pl.ds(1, 1),))
    r_full = Ring(lambda v: full.at[rows_of(4 * c + v)], "x", (pl.ds(0, 48),), (pl.ds(48, 40),))

    r_na.start()
    r_ca.start()
    lax.fori_loop(0, WA // LANES, stage_a, 0)
    r_ay.start()
    lax.fori_loop(0, (WA + WB) // LANES, stage_clean, 0)
    r_cg.start()
    lax.fori_loop(0, WB // LANES, stage_b, 0)

    r_ca.forward()
    r_bz.start()
    r_na.forward()
    r_by[0].start()
    for i, ((zs, ys), same) in enumerate(zip(sources, source_self)):
        dst = ao.at[x, zs, ys]
        far_copy = copy(dst, dst, p_s.at[i], p_r.at[i], (z, y, lax.rem(t + 1, 8)))
        near_copy = pltpu.make_async_copy(dst, dst, p_l)

        @pl.when(same)
        def _():
            near_copy.wait()

        @pl.when(jnp.logical_not(same))
        def _():
            far_copy.wait_recv()
    mine = ao.at[x, here]
    partner = (z, y, 2 * x + 1 - c)
    r_ao.start()
    core = [copy(mine, mine, k_s.at[0], k_r.at[0], partner)]
    core[0].start()

    def relay(r):
        block = ao.at[mod4(x + 4 - r), here]
        core.append(copy(block, block, k_s.at[r], k_r.at[r], partner))
        core[-1].start()

    r_cg.forward()
    r_az[0].start()
    r_ay.forward()
    r_ao.forward()
    relay(1)
    relay(3)

    contract = (((1,), (1,)), ((), ()))

    def gram(left, right):
        return lax.dot_general(left, right, contract, preferred_element_type=F32)

    r_na.finish()
    r_ca.finish()
    part_gram[...] = gram(na[...].reshape(4 * NOISE, 1024), ca[...].reshape(4 * CLEAN_ROWS, 1024))
    own_half = pl.ds(pl.multiple_of(c * 352, 8), 352)
    other_half = pl.ds(pl.multiple_of((1 - c) * 352, 8), 352)
    swap = copy(part_gram.at[other_half], d2, d_s.at[0], d_r.at[0], partner)
    swap.start()

    r_ao.finish()
    relay(2)
    r_bz.forward()
    r_az[3].start()

    def turn(k):
        def step(q, carry):
            span = pl.ds(pl.multiple_of(q * LANES, LANES), LANES)
            ata[k, span, :] = ao[q, k].reshape(4 * NOISE, LANES).T
            atb[k, span, :] = ao[q, :, k].reshape(4 * NOISE, LANES).T
            return carry

        lax.fori_loop(0, 4, step, 0)

    swap.wait_recv()
    sm[...] = part_gram[own_half] + d2[...]
    up, down, across = mod4(x + 1), mod4(x + 3), mod4(x + 2)
    dev_up, dev_down = (z, y, 2 * up + c), (z, y, 2 * down + c)
    first = pl.ds(pl.multiple_of(across * SEG, 8), 48)
    second = pl.ds(pl.multiple_of(across * SEG + 48, 8), 40)
    share = [copy(sm.at[first], near_a, m_s.at[0], m_r.at[0], dev_up),
             copy(sm.at[second], near_b, m_s.at[1], m_r.at[1], dev_down),
             copy(sm.at[rows_of(up)], x3.at[0], m_s.at[2], m_r.at[2], dev_up),
             copy(sm.at[rows_of(down)], x3.at[1], m_s.at[3], m_r.at[3], dev_down)]
    share[0].start()
    share[1].start()
    for r in range(4):
        block = ao.at[mod4(x + 4 - r), there]
        copy(block, block, k_s.at[r], k_r.at[r], partner).wait_recv()
    r_by[0].forward()
    r_by[3].start()
    turn(0)
    share[0].wait_recv()
    sm[pl.ds(pl.multiple_of(up * SEG, 8), 48)] += near_a[...]
    share[2].start()
    share[1].wait_recv()
    sm[pl.ds(pl.multiple_of(down * SEG + 48, 8), 40)] += near_b[...]
    share[3].start()
    turn(1)

    r_cg.finish()
    r_ay.finish()
    grad_gram[...] = gram(ga[z].reshape(4 * NOISE, WA), cg[:, :, :WA].reshape(4 * CLEAN_ROWS, WA))

    share[2].wait_recv()
    share[3].wait_recv()
    full[rows_of(4 * c + x)] = sm[rows_of(x)] + x3[0] + x3[1]
    r_full.start()
    r_az[0].forward()
    turn(2)
    r_full.forward()
    turn(3)
    r_full.finish()
    give = copy(full.at[own_half], full.at[own_half], d_s.at[1], d_r.at[1], partner)
    give.start()

    r_by[0].finish()
    grad_gram[...] += gram(gb[:, z].reshape(4 * NOISE, WB), cg[:, :, WA:].reshape(4 * CLEAN_ROWS, WB))
    copy(full.at[other_half], full.at[other_half], d_s.at[1], d_r.at[1], partner).wait_recv()

    def row_dot(j):
        terms = [grad_gram[g * SEG:(g + 1) * SEG] * full[g * SEG:(g + 1) * SEG] for g in range(j, 8, 2)]
        rows_sum = jnp.sum(terms[0] + terms[1] + terms[2] + terms[3], axis=0, keepdims=True)
        return jnp.broadcast_to(jnp.sum(rows_sum, axis=1, keepdims=True), (8, LANES))

    place = lax.broadcasted_iota(jnp.int32, (8, LANES), 0)
    tile = jnp.where(place == 2 * z, row_dot(0), jnp.where(place == 2 * z + 1, row_dot(1), 0.0))

    sends = []

    def send_tile(buf, value, me, n, dev, base):
        buf[me] = value
        for r in range(1, n):
            out = copy(buf.at[me], buf.at[me], v_s.at[base + r], v_r.at[base + r], dev(r))
            out.start()
            sends.append(out)

    def sum_tiles(buf, me, n, base):
        for r in range(1, n):
            origin = buf.at[lax.rem(me + n - r, n)]
            copy(origin, origin, v_s.at[base + r], v_r.at[base + r], partner).wait_recv()
        return jnp.sum(buf[...], axis=0)

    send_tile(sv1, tile, t, 8, lambda r: (z, y, lax.rem(t + r, 8)), 0)

    tile = sum_tiles(sv1, t, 8, 0)
    send_tile(sv2, tile, 4 * z + y, 16, cell, 8)
    r_by[1].start()
    r_az[1].start()
    r_az[2].start()
    r_bz.finish()
    r_by[2].start()
    r_az[3].forward()
    r_by[3].forward()
    tile = sum_tiles(sv2, 4 * z + y, 16, 8)
    weights = jnp.maximum(-tile, 0.0) / jnp.sum(jnp.abs(tile), axis=0, keepdims=True)
    wts[...] = weights
    for k in range(4):
        scale[k, :SEG] = jnp.broadcast_to(wts[2 * k:2 * k + 1, :], (SEG, LANES))
        scale[k, SEG:] = jnp.broadcast_to(wts[2 * k + 1:2 * k + 2, :], (SEG, LANES))
    lane = lax.broadcasted_iota(jnp.int32, (1, LANES), 1)
    wout_ref[...] = jnp.where(lane == 0, wts[pl.ds(2 * z, 1), :], wts[pl.ds(2 * z + 1, 1), :])[:, :2]

    def scaled(raw, s):
        full = jnp.concatenate([s] * (raw.shape[1] // LANES), axis=1)
        return (raw.astype(F32) * full).astype(BF16)

    def product(at, pieces_of, width, base, first, span):
        def step(i, carry):
            cols = pl.ds(pl.multiple_of(i * span, span), span)
            dest = pl.ds(pl.multiple_of(base + i * span, 256), span)
            right = jnp.concatenate([scaled(raw, s) for raw, s in pieces_of(cols)], axis=0)
            value = jnp.dot(at[...], right, preferred_element_type=F32)
            if first:
                out_ref[:, dest] = value
            else:
                out_ref[:, dest] += value
            return carry

        lax.fori_loop(0, width // span, step, 0)

    def add_a(k, first=False):
        v = mod4(z + k)
        product(ata.at[v], lambda cols: [(ga[v, i, :, cols], scale[v]) for i in range(4)], WA, 0, first, 768)

    def add_b(k, first=False):
        v = mod4(y + k)
        product(atb.at[v], lambda cols: [(gb[v, i, :, cols], scale[i]) for i in range(4)], WB, WA, first, 512)

    add_a(0, True)
    r_az[1].forward()
    r_by[1].forward()
    add_b(0, True)
    r_az[2].forward()
    add_a(3)
    r_by[2].forward()
    add_a(1)
    add_b(3)
    add_b(1)
    for k in (0, 3, 1, 2):
        r_az[k].finish()
    add_a(2)
    for k in (3, 1, 2):
        r_by[k].finish()
    add_b(2)

    for far_copy, _, same in pieces:
        @pl.when(jnp.logical_not(same))
        def _():
            far_copy.wait_send()
    for ring in rings:
        ring.drain()
    for k in core + [swap, give] + share + sends:
        k.wait_send()


def body(activations, cotangents, row_ids, row_counts):
    dma = pltpu.SemaphoreType.DMA
    vmem = pltpu.VMEM
    return pl.pallas_call(
        body_kernel,
        out_shape=(pltpu.VMEM((512, WA + WB), F32), pltpu.VMEM((1, 2), F32)),
        in_specs=[pl.BlockSpec(memory_space=pltpu.SMEM)] * 2 + [pl.BlockSpec(memory_space=pltpu.VMEM)] * 2,
        out_specs=(pl.BlockSpec(memory_space=pltpu.VMEM), pl.BlockSpec(memory_space=pltpu.VMEM)),
        scratch_shapes=[
            vmem((4, NOISE, 1024), BF16),
            vmem((4, CLEAN_ROWS, 1024), BF16),
            vmem((4, CLEAN_ROWS, WA + WB), BF16),
            vmem((4, 4, NOISE, WA), BF16),
            vmem((4, 4, NOISE, WB), BF16),
            vmem((4, 4, 4, NOISE, LANES), BF16),
            vmem((4, 512, 4 * NOISE), BF16),
            vmem((4, 512, 4 * NOISE), BF16),
            vmem((4 * NOISE, 4 * CLEAN_ROWS), F32),
            vmem((4 * NOISE, 4 * CLEAN_ROWS), F32),
            vmem((4 * NOISE, 4 * CLEAN_ROWS), F32),
            vmem((2 * NOISE, 4 * CLEAN_ROWS), F32),
            vmem((2 * NOISE, 4 * CLEAN_ROWS), F32),
            vmem((48, 4 * CLEAN_ROWS), F32),
            vmem((40, 4 * CLEAN_ROWS), F32),
            vmem((2, SEG, 4 * CLEAN_ROWS), F32),
            vmem((8, 8, LANES), F32),
            vmem((16, 8, LANES), F32),
            vmem((8, LANES), F32),
            vmem((4, NOISE, LANES), F32),
            dma((15, 4)), dma((15, 4)),
            dma((8,)), dma((8,)), dma,
            dma((4,)), dma((4,)),
            dma((2,)), dma((2,)),
            dma((4,)), dma((4,)),
            dma((24,)), dma((24,)),
        ],
        compiler_params=pltpu.CompilerParams(
            collective_id=0, has_side_effects=True, vmem_limit_bytes=60 * 1024 * 1024),
        cost_estimate=pl.CostEstimate(flops=8_000_000_000, bytes_accessed=8_000_000, transcendentals=0),
        name="reweight",
    )(row_ids, row_counts, activations, cotangents)


def solution(mesh):
    placed = (P("dp", "seq", "tensor"), P("dp", "seq", "tensor"), P("dp", None), P("dp", None))
    return jax.shard_map(
        body,
        mesh=mesh,
        in_specs=placed,
        out_specs=(P(("dp", "seq"), "tensor"), P("dp", None)),
        check_vma=False,
    )
```

```python
import jax
import jax.numpy as jnp
from jax import lax
from jax.experimental import pallas as pl
from jax.experimental.pallas import tpu as pltpu
from jax.sharding import PartitionSpec as P

MESH = pl.DeviceIdType.MESH
F32 = jnp.float32
BF16 = jnp.bfloat16

SEG = 88
NOISE = 176
CLEAN_ROWS = 96
WA = 768
WB = 1024
LANES = 128


def body_kernel(ids_ref, counts_ref, acts_ref, cot_ref, out_ref, wout_ref,
                na, ca, cg, ga, gb, ao, ata, atb, part_gram, grad_gram, full, d2, sm,
                near_a, near_b, x3, sv1, sv2, wts,
                ring_s, ring_r, p_s, p_r, p_l, k_s, k_r,
                d_s, d_r, m_s, m_r, v_s, v_r):
    z = lax.axis_index("dp")
    y = lax.axis_index("seq")
    t = lax.axis_index("tensor")
    x = t // 2
    c = lax.rem(t, 2)

    def mod4(v):
        return lax.rem(v, 4)

    def copy(src, dst, s, r, dev):
        return pltpu.make_async_remote_copy(
            src_ref=src, dst_ref=dst, send_sem=s, recv_sem=r, device_id=dev, device_id_type=MESH)

    barrier = pltpu.get_barrier_semaphore()

    def greet(dev):
        pl.semaphore_signal(barrier, inc=1, device_id=dev, device_id_type=MESH)

    def cell(r):
        other = lax.rem(4 * z + y + r, 16)
        return other // 4, lax.rem(other, 4), t

    for r in range(1, 16):
        greet(cell(r))
    for r in range(1, 8):
        greet((z, y, lax.rem(t + r, 8)))

    targets = [(h, q, (x, 2 * c + h, 2 * q + z // 2)) for h in range(2) for q in range(4)]
    target_self = [(x == z) & (y == 2 * c + h) & (q == x) & (c == z // 2) for h, q, _ in targets]
    sources = [(2 * c + i // 4, i % 4) for i in range(8)]
    source_self = [(zs == z) & (ys == y) & (x == z) & (c == y // 2) for zs, ys in sources]
    for (_, _, dev), same in zip(targets, target_self):
        @pl.when(jnp.logical_not(same))
        def _():
            greet(dev)
    for (zs, ys), same in zip(sources, source_self):
        @pl.when(jnp.logical_not(same))
        def _():
            greet((zs, ys, 2 * z + y // 2))
    has_self = ((x == z) & (c == y // 2) & (c == z // 2)).astype(jnp.int32)

    rid = [ids_ref[0, j] for j in range(3)]
    live = [counts_ref[0, rid[j]] - y * SEG for j in range(3)]
    rows = lax.broadcasted_iota(jnp.int32, (SEG, LANES), 0)
    pad = jnp.zeros((CLEAN_ROWS - SEG, LANES), F32)

    def stage_acts(i, carry):
        cols = pl.ds(pl.multiple_of(i * LANES, LANES), LANES)
        part = [acts_ref[rid[j], :, cols].astype(F32) for j in range(3)]
        na[y, :, cols] = jnp.concatenate([part[1], part[2]], axis=0).astype(BF16)
        ca[z, :, cols] = jnp.concatenate([part[0], pad], axis=0).astype(BF16)
        return carry

    lax.fori_loop(0, 1024 // LANES, stage_acts, 0)

    def masked(j, cols):
        return jnp.where(rows < live[j], cot_ref[rid[j], :, cols].astype(F32), 0.0)

    def stage_clean(i, carry):
        cols = pl.ds(pl.multiple_of(i * LANES, LANES), LANES)
        cg[z, :, cols] = jnp.concatenate([masked(0, cols), pad], axis=0).astype(BF16)
        return carry

    def stage_a(i, carry):
        cols = pl.ds(pl.multiple_of(i * LANES, LANES), LANES)
        ga[z, y, :, cols] = jnp.concatenate([masked(1, cols), masked(2, cols)], axis=0).astype(BF16)
        return carry

    def stage_b(i, carry):
        cols = pl.ds(pl.multiple_of(i * LANES, LANES), LANES)
        from_cols = pl.ds(pl.multiple_of(WA + i * LANES, LANES), LANES)
        gb[y, z, :, cols] = jnp.concatenate(
            [masked(1, from_cols), masked(2, from_cols)], axis=0).astype(BF16)
        return carry

    pl.semaphore_wait(barrier, 38 - 2 * has_self)

    pieces = []
    for i, ((h, q, dev), same) in enumerate(zip(targets, target_self)):
        src = na.at[y, :, pl.ds(h * 512 + q * LANES, LANES)]
        dst = ao.at[q, z, y]
        far_copy = copy(src, dst, p_s.at[i], p_r.at[lax.rem(z, 2) * 4 + y], dev)
        near_copy = pltpu.make_async_copy(src, dst, p_l)

        @pl.when(same)
        def _():
            near_copy.start()

        @pl.when(jnp.logical_not(same))
        def _():
            far_copy.start()
        pieces.append((far_copy, near_copy, same))

    rings = []

    class Ring:
        def __init__(self, at, axis, first, second):
            n = len(rings)
            rings.append(self)
            me = {"x": x, "y": y, "z": z}[axis]

            def dev(v):
                return {"x": (z, y, 2 * v + c), "y": (z, v, t), "z": (v, y, t)}[axis]

            up, down, far = mod4(me + 1), mod4(me + 3), mod4(me + 2)
            own, low, high, opp = at(me), at(down), at(up), at(far)
            self.go = [copy(own, own, ring_s.at[n, 0], ring_r.at[n, 0], dev(up)),
                       copy(own, own, ring_s.at[n, 1], ring_r.at[n, 1], dev(down))]
            self.got = [copy(low, low, ring_s.at[n, 0], ring_r.at[n, 0], dev(up)),
                        copy(high, high, ring_s.at[n, 1], ring_r.at[n, 1], dev(down))]
            self.pass_on = [
                copy(low.at[first], low.at[first], ring_s.at[n, 2], ring_r.at[n, 2], dev(up)),
                copy(high.at[second], high.at[second], ring_s.at[n, 3], ring_r.at[n, 3], dev(down))]
            self.got_far = [
                copy(opp.at[first], opp.at[first], ring_s.at[n, 2], ring_r.at[n, 2], dev(up)),
                copy(opp.at[second], opp.at[second], ring_s.at[n, 3], ring_r.at[n, 3], dev(down))]

        def start(self):
            for k in self.go:
                k.start()

        def forward(self):
            for k in range(2):
                self.got[k].wait_recv()
                self.pass_on[k].start()

        def finish(self):
            for k in self.got_far:
                k.wait_recv()

        def drain(self):
            for k in self.go + self.pass_on:
                k.wait_send()

    even = (pl.ds(0, 96),), (pl.ds(96, 80),)
    odd = (pl.ds(80, 96),), (pl.ds(0, 80),)
    equal = (pl.ds(0, 48),), (pl.ds(48, 48),)

    def az_ring(k):
        item = mod4(y + k)
        return Ring(lambda v: ga.at[v, item], "z", *(even if k in (0, 1) else odd))

    def by_ring(k):
        item = mod4(z + k)
        return Ring(lambda v: gb.at[v, item], "y", *(even if k in (0, 1) else odd))

    def rows_of(chunk):
        return pl.ds(pl.multiple_of(chunk * SEG, 8), SEG)

    r_na = Ring(lambda v: na.at[v], "y", *even)
    r_ca = Ring(lambda v: ca.at[v], "z", *equal)
    r_cg = Ring(lambda v: cg.at[v], "z", *equal)
    r_ay = Ring(lambda v: ga.at[z, v], "y", *odd)
    r_bz = Ring(lambda v: gb.at[y, v], "z", *odd)
    r_az = {k: az_ring(k) for k in (0, 3, 1, 2)}
    r_by = {k: by_ring(k) for k in (0, 3, 1, 2)}
    here = pl.ds(2 * c, 2)
    there = pl.ds(2 * (1 - c), 2)
    r_ao = Ring(lambda v: ao.at[v, here], "x", (pl.ds(0, 1),), (pl.ds(1, 1),))
    r_full = Ring(lambda v: full.at[rows_of(4 * c + v)], "x", (pl.ds(0, 48),), (pl.ds(48, 40),))

    r_na.start()
    r_ca.start()
    lax.fori_loop(0, WA // LANES, stage_a, 0)
    r_ay.start()
    lax.fori_loop(0, (WA + WB) // LANES, stage_clean, 0)
    r_cg.start()
    lax.fori_loop(0, WB // LANES, stage_b, 0)

    r_ca.forward()
    r_bz.start()
    r_na.forward()
    r_by[0].start()
    for i, ((zs, ys), same) in enumerate(zip(sources, source_self)):
        dst = ao.at[x, zs, ys]
        far_copy = copy(dst, dst, p_s.at[i], p_r.at[i], (z, y, lax.rem(t + 1, 8)))
        near_copy = pltpu.make_async_copy(dst, dst, p_l)

        @pl.when(same)
        def _():
            near_copy.wait()

        @pl.when(jnp.logical_not(same))
        def _():
            far_copy.wait_recv()
    partner = (z, y, 2 * x + 1 - c)
    r_ao.start()
    r_cg.forward()
    r_az[0].start()
    r_ay.forward()
    r_ao.forward()

    contract = (((1,), (1,)), ((), ()))

    def gram(left, right):
        return lax.dot_general(left, right, contract, preferred_element_type=F32)

    r_na.finish()
    r_ca.finish()
    part_gram[...] = gram(na[...].reshape(4 * NOISE, 1024), ca[...].reshape(4 * CLEAN_ROWS, 1024))
    own_half = pl.ds(pl.multiple_of(c * 352, 8), 352)
    other_half = pl.ds(pl.multiple_of((1 - c) * 352, 8), 352)
    swap = copy(part_gram.at[other_half], d2, d_s.at[0], d_r.at[0], partner)
    swap.start()

    r_ao.finish()
    r_bz.forward()
    r_az[3].start()
    r_az[1].start()

    def turn_a(k):
        def step(q, carry):
            span = pl.ds(pl.multiple_of(q * LANES, LANES), LANES)
            ata[2 * c + k, span, :] = ao[q, 2 * c + k].reshape(4 * NOISE, LANES).T
            return carry

        lax.fori_loop(0, 4, step, 0)

    gap = jnp.zeros((32, LANES), BF16)

    def turn_b(v):
        def step(q, carry):
            span = pl.ds(pl.multiple_of(q * LANES, LANES), LANES)
            tokens = jnp.concatenate([ao[q, 2 * c, v], ao[q, 2 * c + 1, v], gap], axis=0)
            atb[c, v, span, :] = tokens.T
            return carry

        lax.fori_loop(0, 4, step, 0)

    turned = [copy(ata.at[here], ata.at[here], k_s.at[0], k_r.at[0], partner),
              copy(atb.at[c], atb.at[c], k_s.at[1], k_r.at[1], partner)]
    turn_a(0)
    swap.wait_recv()
    sm[...] = part_gram[own_half] + d2[...]
    up, down, across = mod4(x + 1), mod4(x + 3), mod4(x + 2)
    dev_up, dev_down = (z, y, 2 * up + c), (z, y, 2 * down + c)
    first = pl.ds(pl.multiple_of(across * SEG, 8), 48)
    second = pl.ds(pl.multiple_of(across * SEG + 48, 8), 40)
    share = [copy(sm.at[first], near_a, m_s.at[0], m_r.at[0], dev_up),
             copy(sm.at[second], near_b, m_s.at[1], m_r.at[1], dev_down),
             copy(sm.at[rows_of(up)], x3.at[0], m_s.at[2], m_r.at[2], dev_up),
             copy(sm.at[rows_of(down)], x3.at[1], m_s.at[3], m_r.at[3], dev_down)]
    share[0].start()
    share[1].start()
    r_by[0].forward()
    r_by[3].start()
    r_by[1].start()
    turn_a(1)
    turned[0].start()
    share[0].wait_recv()
    sm[pl.ds(pl.multiple_of(up * SEG, 8), 48)] += near_a[...]
    share[2].start()
    share[1].wait_recv()
    sm[pl.ds(pl.multiple_of(down * SEG + 48, 8), 40)] += near_b[...]
    share[3].start()
    turn_b(0)

    r_cg.finish()
    r_ay.finish()
    r_az[2].start()
    grad_gram[...] = gram(ga[z].reshape(4 * NOISE, WA), cg[:, :, :WA].reshape(4 * CLEAN_ROWS, WA))

    share[2].wait_recv()
    share[3].wait_recv()
    full[rows_of(4 * c + x)] = sm[rows_of(x)] + x3[0] + x3[1]
    r_full.start()
    r_az[0].forward()
    turn_b(1)
    r_full.forward()
    turn_b(2)
    r_full.finish()
    give = copy(full.at[own_half], full.at[own_half], d_s.at[1], d_r.at[1], partner)
    give.start()
    turn_b(3)
    turned[1].start()

    r_bz.finish()
    r_by[2].start()
    r_by[0].finish()
    grad_gram[...] += gram(gb[:, z].reshape(4 * NOISE, WB), cg[:, :, WA:].reshape(4 * CLEAN_ROWS, WB))
    copy(full.at[other_half], full.at[other_half], d_s.at[1], d_r.at[1], partner).wait_recv()

    def row_dot(j):
        terms = [grad_gram[g * SEG:(g + 1) * SEG] * full[g * SEG:(g + 1) * SEG] for g in range(j, 8, 2)]
        rows_sum = jnp.sum(terms[0] + terms[1] + terms[2] + terms[3], axis=0, keepdims=True)
        return jnp.broadcast_to(jnp.sum(rows_sum, axis=1, keepdims=True), (8, LANES))

    place = lax.broadcasted_iota(jnp.int32, (8, LANES), 0)
    tile = jnp.where(place == 2 * z, row_dot(0), jnp.where(place == 2 * z + 1, row_dot(1), 0.0))

    sends = []

    def send_tile(buf, value, me, n, dev, base):
        buf[me] = value
        for r in range(1, n):
            out = copy(buf.at[me], buf.at[me], v_s.at[base + r], v_r.at[base + r], dev(r))
            out.start()
            sends.append(out)

    def sum_tiles(buf, me, n, base):
        for r in range(1, n):
            origin = buf.at[lax.rem(me + n - r, n)]
            copy(origin, origin, v_s.at[base + r], v_r.at[base + r], partner).wait_recv()
        return jnp.sum(buf[...], axis=0)

    send_tile(sv1, tile, t, 8, lambda r: (z, y, lax.rem(t + r, 8)), 0)

    tile = sum_tiles(sv1, t, 8, 0)
    send_tile(sv2, tile, 4 * z + y, 16, cell, 8)
    r_az[3].forward()
    r_by[3].forward()
    tile = sum_tiles(sv2, 4 * z + y, 16, 8)
    weights = jnp.maximum(-tile, 0.0) / jnp.sum(jnp.abs(tile), axis=0, keepdims=True)
    wts[...] = weights
    lane = lax.broadcasted_iota(jnp.int32, (1, LANES), 1)
    wout_ref[...] = jnp.where(lane == 0, wts[pl.ds(2 * z, 1), :], wts[pl.ds(2 * z + 1, 1), :])[:, :2]

    copy(ata.at[there], ata.at[there], k_s.at[0], k_r.at[0], partner).wait_recv()
    copy(atb.at[1 - c], atb.at[1 - c], k_s.at[1], k_r.at[1], partner).wait_recv()

    def scaled(rows_in, k):
        width = rows_in.shape[1]

        def part(j):
            row = wts[pl.ds(2 * k + j, 1), :]
            factor = jnp.broadcast_to(jnp.concatenate([row] * (width // LANES), axis=1), (SEG, width))
            return rows_in[j * SEG:(j + 1) * SEG] * factor

        return jnp.concatenate([part(0), part(1)], axis=0).astype(BF16)

    def product(left_of, right_of, width, base, first, span):
        def step(i, carry):
            cols = pl.ds(pl.multiple_of(i * span, span), span)
            dest = pl.ds(pl.multiple_of(base + i * span, 256), span)
            value = jnp.dot(left_of(), right_of(cols), preferred_element_type=F32)
            if first:
                out_ref[:, dest] = value
            else:
                out_ref[:, dest] += value
            return carry

        lax.fori_loop(0, width // span, step, 0)

    def add_a(k, first=False):
        v = mod4(z + k)

        def right_of(cols):
            return jnp.concatenate([scaled(ga[v, i, :, cols].astype(F32), v) for i in range(4)], axis=0)

        product(lambda: ata[v], right_of, WA, 0, first, 768)

    def add_b(k, first=False):
        v = mod4(y + k)

        def right_of(cols):
            parts = [scaled(gb[v, i, :, cols].astype(F32), i) for i in range(4)]
            empty = jnp.zeros((32, 512), BF16)
            return jnp.concatenate([parts[0], parts[1], empty, parts[2], parts[3], empty], axis=0)

        product(lambda: jnp.concatenate([atb[0, v], atb[1, v]], axis=1), right_of, WB, WA, first, 512)

    add_a(0, True)
    r_az[1].forward()
    r_by[1].forward()
    add_b(0, True)
    r_az[2].forward()
    add_a(3)
    r_by[2].forward()
    add_a(1)
    add_b(3)
    add_b(1)
    for k in (0, 3, 1, 2):
        r_az[k].finish()
    add_a(2)
    for k in (3, 1, 2):
        r_by[k].finish()
    add_b(2)

    for far_copy, _, same in pieces:
        @pl.when(jnp.logical_not(same))
        def _():
            far_copy.wait_send()
    for ring in rings:
        ring.drain()
    for k in turned + [swap, give] + share + sends:
        k.wait_send()


def body(activations, cotangents, row_ids, row_counts):
    dma = pltpu.SemaphoreType.DMA
    vmem = pltpu.VMEM
    return pl.pallas_call(
        body_kernel,
        out_shape=(pltpu.VMEM((512, WA + WB), F32), pltpu.VMEM((1, 2), F32)),
        in_specs=[pl.BlockSpec(memory_space=pltpu.SMEM)] * 2 + [pl.BlockSpec(memory_space=pltpu.VMEM)] * 2,
        out_specs=(pl.BlockSpec(memory_space=pltpu.VMEM), pl.BlockSpec(memory_space=pltpu.VMEM)),
        scratch_shapes=[
            vmem((4, NOISE, 1024), BF16),
            vmem((4, CLEAN_ROWS, 1024), BF16),
            vmem((4, CLEAN_ROWS, WA + WB), BF16),
            vmem((4, 4, NOISE, WA), BF16),
            vmem((4, 4, NOISE, WB), BF16),
            vmem((4, 4, 4, NOISE, LANES), BF16),
            vmem((4, 512, 4 * NOISE), BF16),
            vmem((2, 4, 512, 384), BF16),
            vmem((4 * NOISE, 4 * CLEAN_ROWS), F32),
            vmem((4 * NOISE, 4 * CLEAN_ROWS), F32),
            vmem((4 * NOISE, 4 * CLEAN_ROWS), F32),
            vmem((2 * NOISE, 4 * CLEAN_ROWS), F32),
            vmem((2 * NOISE, 4 * CLEAN_ROWS), F32),
            vmem((48, 4 * CLEAN_ROWS), F32),
            vmem((40, 4 * CLEAN_ROWS), F32),
            vmem((2, SEG, 4 * CLEAN_ROWS), F32),
            vmem((8, 8, LANES), F32),
            vmem((16, 8, LANES), F32),
            vmem((8, LANES), F32),
            dma((15, 4)), dma((15, 4)),
            dma((8,)), dma((8,)), dma,
            dma((2,)), dma((2,)),
            dma((2,)), dma((2,)),
            dma((4,)), dma((4,)),
            dma((24,)), dma((24,)),
        ],
        compiler_params=pltpu.CompilerParams(
            collective_id=0, has_side_effects=True, vmem_limit_bytes=60 * 1024 * 1024),
        cost_estimate=pl.CostEstimate(flops=8_000_000_000, bytes_accessed=8_000_000, transcendentals=0),
        name="reweight",
    )(row_ids, row_counts, activations, cotangents)


def solution(mesh):
    placed = (P("dp", "seq", "tensor"), P("dp", "seq", "tensor"), P("dp", None), P("dp", None))
    return jax.shard_map(
        body,
        mesh=mesh,
        in_specs=placed,
        out_specs=(P(("dp", "seq"), "tensor"), P("dp", None)),
        check_vma=False,
    )
```

```python
import jax
import jax.numpy as jnp
from jax import lax
from jax.experimental import pallas as pl
from jax.experimental.pallas import tpu as pltpu
from jax.sharding import PartitionSpec as P

MESH = pl.DeviceIdType.MESH
F32 = jnp.float32
BF16 = jnp.bfloat16

SEG = 88
NOISE = 176
CLEAN_ROWS = 96
WA = 768
WB = 1024
LANES = 128


def body_kernel(ids_ref, counts_ref, acts_ref, cot_ref, out_ref, wout_ref,
                na, ca, cg, ga, gb, ao, ata, atb, part_gram, grad_gram, full, d2, sm,
                near_a, near_b, x3, sv1, sv2, wts,
                ring_s, ring_r, p_s, p_r, p_l, k_s, k_r,
                d_s, d_r, m_s, m_r, v_s, v_r):
    z = lax.axis_index("dp")
    y = lax.axis_index("seq")
    t = lax.axis_index("tensor")
    x = t // 2
    c = lax.rem(t, 2)

    def mod4(v):
        return lax.rem(v, 4)

    def copy(src, dst, s, r, dev):
        return pltpu.make_async_remote_copy(
            src_ref=src, dst_ref=dst, send_sem=s, recv_sem=r, device_id=dev, device_id_type=MESH)

    barrier = pltpu.get_barrier_semaphore()

    def greet(dev):
        pl.semaphore_signal(barrier, inc=1, device_id=dev, device_id_type=MESH)

    def cell(r):
        other = lax.rem(4 * z + y + r, 16)
        return other // 4, lax.rem(other, 4), t

    for r in range(1, 16):
        greet(cell(r))
    for r in range(1, 8):
        greet((z, y, lax.rem(t + r, 8)))

    targets = [(h, q, (x, 2 * c + h, 2 * q + z // 2)) for h in range(2) for q in range(4)]
    target_self = [(x == z) & (y == 2 * c + h) & (q == x) & (c == z // 2) for h, q, _ in targets]
    sources = [(2 * c + i // 4, i % 4) for i in range(8)]
    source_self = [(zs == z) & (ys == y) & (x == z) & (c == y // 2) for zs, ys in sources]
    for (_, _, dev), same in zip(targets, target_self):
        @pl.when(jnp.logical_not(same))
        def _():
            greet(dev)
    for (zs, ys), same in zip(sources, source_self):
        @pl.when(jnp.logical_not(same))
        def _():
            greet((zs, ys, 2 * z + y // 2))
    has_self = ((x == z) & (c == y // 2) & (c == z // 2)).astype(jnp.int32)

    rid = [ids_ref[0, j] for j in range(3)]
    live = [counts_ref[0, rid[j]] - y * SEG for j in range(3)]
    rows = lax.broadcasted_iota(jnp.int32, (SEG, LANES), 0)
    pad = jnp.zeros((CLEAN_ROWS - SEG, LANES), F32)

    def stage_acts(i, carry):
        cols = pl.ds(pl.multiple_of(i * LANES, LANES), LANES)
        part = [acts_ref[rid[j], :, cols].astype(F32) for j in range(3)]
        na[y, :, cols] = jnp.concatenate([part[1], part[2]], axis=0).astype(BF16)
        ca[z, :, cols] = jnp.concatenate([part[0], pad], axis=0).astype(BF16)
        return carry

    lax.fori_loop(0, 1024 // LANES, stage_acts, 0)

    def masked(j, cols):
        return jnp.where(rows < live[j], cot_ref[rid[j], :, cols].astype(F32), 0.0)

    def stage_clean(i, carry):
        cols = pl.ds(pl.multiple_of(i * LANES, LANES), LANES)
        cg[z, :, cols] = jnp.concatenate([masked(0, cols), pad], axis=0).astype(BF16)
        return carry

    def stage_a(i, carry):
        cols = pl.ds(pl.multiple_of(i * LANES, LANES), LANES)
        ga[z, y, :, cols] = jnp.concatenate([masked(1, cols), masked(2, cols)], axis=0).astype(BF16)
        return carry

    def stage_b(i, carry):
        cols = pl.ds(pl.multiple_of(i * LANES, LANES), LANES)
        from_cols = pl.ds(pl.multiple_of(WA + i * LANES, LANES), LANES)
        gb[y, z, :, cols] = jnp.concatenate(
            [masked(1, from_cols), masked(2, from_cols)], axis=0).astype(BF16)
        return carry

    pl.semaphore_wait(barrier, 38 - 2 * has_self)

    pieces = []
    for i, ((h, q, dev), same) in enumerate(zip(targets, target_self)):
        src = na.at[y, :, pl.ds(h * 512 + q * LANES, LANES)]
        dst = ao.at[q, z, y]
        far_copy = copy(src, dst, p_s.at[i], p_r.at[lax.rem(z, 2) * 4 + y], dev)
        near_copy = pltpu.make_async_copy(src, dst, p_l)

        @pl.when(same)
        def _():
            near_copy.start()

        @pl.when(jnp.logical_not(same))
        def _():
            far_copy.start()
        pieces.append((far_copy, near_copy, same))

    rings = []

    class Ring:
        def __init__(self, at, axis, first, second):
            n = len(rings)
            rings.append(self)
            me = {"x": x, "y": y, "z": z}[axis]

            def dev(v):
                return {"x": (z, y, 2 * v + c), "y": (z, v, t), "z": (v, y, t)}[axis]

            up, down, far = mod4(me + 1), mod4(me + 3), mod4(me + 2)
            own, low, high, opp = at(me), at(down), at(up), at(far)
            self.go = [copy(own, own, ring_s.at[n, 0], ring_r.at[n, 0], dev(up)),
                       copy(own, own, ring_s.at[n, 1], ring_r.at[n, 1], dev(down))]
            self.got = [copy(low, low, ring_s.at[n, 0], ring_r.at[n, 0], dev(up)),
                        copy(high, high, ring_s.at[n, 1], ring_r.at[n, 1], dev(down))]
            self.pass_on = [
                copy(low.at[first], low.at[first], ring_s.at[n, 2], ring_r.at[n, 2], dev(up)),
                copy(high.at[second], high.at[second], ring_s.at[n, 3], ring_r.at[n, 3], dev(down))]
            self.got_far = [
                copy(opp.at[first], opp.at[first], ring_s.at[n, 2], ring_r.at[n, 2], dev(up)),
                copy(opp.at[second], opp.at[second], ring_s.at[n, 3], ring_r.at[n, 3], dev(down))]

        def start(self):
            for k in self.go:
                k.start()

        def forward(self):
            for k in range(2):
                self.got[k].wait_recv()
                self.pass_on[k].start()

        def finish(self):
            for k in self.got_far:
                k.wait_recv()

        def drain(self):
            for k in self.go + self.pass_on:
                k.wait_send()

    even = (pl.ds(0, 96),), (pl.ds(96, 80),)
    odd = (pl.ds(80, 96),), (pl.ds(0, 80),)
    equal = (pl.ds(0, 48),), (pl.ds(48, 48),)

    def az_ring(k):
        item = mod4(y + k)
        return Ring(lambda v: ga.at[v, item], "z", *(even if k in (0, 1) else odd))

    def by_ring(k):
        item = mod4(z + k)
        return Ring(lambda v: gb.at[v, item], "y", *(even if k in (0, 1) else odd))

    def rows_of(chunk):
        return pl.ds(pl.multiple_of(chunk * SEG, 8), SEG)

    r_na = Ring(lambda v: na.at[v], "y", *even)
    r_ca = Ring(lambda v: ca.at[v], "z", *equal)
    r_cg = Ring(lambda v: cg.at[v], "z", *equal)
    r_ay = Ring(lambda v: ga.at[z, v], "y", *odd)
    r_bz = Ring(lambda v: gb.at[y, v], "z", *odd)
    r_az = {k: az_ring(k) for k in (0, 3, 1, 2)}
    r_by = {k: by_ring(k) for k in (0, 3, 1, 2)}
    here = pl.ds(2 * c, 2)
    there = pl.ds(2 * (1 - c), 2)
    r_ao = Ring(lambda v: ao.at[v, here], "x", (pl.ds(0, 1),), (pl.ds(1, 1),))
    r_full = Ring(lambda v: full.at[rows_of(4 * c + v)], "x", (pl.ds(0, 48),), (pl.ds(48, 40),))

    r_na.start()
    r_ca.start()
    lax.fori_loop(0, WA // LANES, stage_a, 0)
    r_ay.start()
    lax.fori_loop(0, (WA + WB) // LANES, stage_clean, 0)
    r_cg.start()
    lax.fori_loop(0, WB // LANES, stage_b, 0)

    r_ca.forward()
    r_bz.start()
    r_na.forward()
    r_by[0].start()
    partner = (z, y, 2 * x + 1 - c)
    r_cg.forward()
    r_az[0].start()
    r_ay.forward()

    contract = (((1,), (1,)), ((), ()))

    def gram(left, right):
        return lax.dot_general(left, right, contract, preferred_element_type=F32)

    r_na.finish()
    r_ca.finish()
    part_gram[...] = gram(na[...].reshape(4 * NOISE, 1024), ca[...].reshape(4 * CLEAN_ROWS, 1024))
    own_half = pl.ds(pl.multiple_of(c * 352, 8), 352)
    other_half = pl.ds(pl.multiple_of((1 - c) * 352, 8), 352)
    swap = copy(part_gram.at[other_half], d2, d_s.at[0], d_r.at[0], partner)
    swap.start()

    r_bz.forward()
    r_az[3].start()
    r_az[1].start()
    for i, ((zs, ys), same) in enumerate(zip(sources, source_self)):
        dst = ao.at[x, zs, ys]
        far_copy = copy(dst, dst, p_s.at[i], p_r.at[i], (z, y, lax.rem(t + 1, 8)))
        near_copy = pltpu.make_async_copy(dst, dst, p_l)

        @pl.when(same)
        def _():
            near_copy.wait()

        @pl.when(jnp.logical_not(same))
        def _():
            far_copy.wait_recv()
    r_ao.start()

    def turn_a(k):
        def step(q, carry):
            span = pl.ds(pl.multiple_of(q * LANES, LANES), LANES)
            ata[2 * c + k, span, :] = ao[q, 2 * c + k].reshape(4 * NOISE, LANES).T
            return carry

        lax.fori_loop(0, 4, step, 0)

    gap = jnp.zeros((32, LANES), BF16)

    def turn_b(v):
        def step(q, carry):
            span = pl.ds(pl.multiple_of(q * LANES, LANES), LANES)
            tokens = jnp.concatenate([ao[q, 2 * c, v], ao[q, 2 * c + 1, v], gap], axis=0)
            atb[c, v, span, :] = tokens.T
            return carry

        lax.fori_loop(0, 4, step, 0)

    turned = [copy(ata.at[here], ata.at[here], k_s.at[0], k_r.at[0], partner),
              copy(atb.at[c], atb.at[c], k_s.at[1], k_r.at[1], partner)]
    swap.wait_recv()
    sm[...] = part_gram[own_half] + d2[...]
    up, down, across = mod4(x + 1), mod4(x + 3), mod4(x + 2)
    dev_up, dev_down = (z, y, 2 * up + c), (z, y, 2 * down + c)
    first = pl.ds(pl.multiple_of(across * SEG, 8), 48)
    second = pl.ds(pl.multiple_of(across * SEG + 48, 8), 40)
    share = [copy(sm.at[first], near_a, m_s.at[0], m_r.at[0], dev_up),
             copy(sm.at[second], near_b, m_s.at[1], m_r.at[1], dev_down),
             copy(sm.at[rows_of(up)], x3.at[0], m_s.at[2], m_r.at[2], dev_up),
             copy(sm.at[rows_of(down)], x3.at[1], m_s.at[3], m_r.at[3], dev_down)]
    share[0].start()
    share[1].start()
    r_by[0].forward()
    r_by[3].start()
    r_by[1].start()
    share[0].wait_recv()
    sm[pl.ds(pl.multiple_of(up * SEG, 8), 48)] += near_a[...]
    share[2].start()
    share[1].wait_recv()
    sm[pl.ds(pl.multiple_of(down * SEG + 48, 8), 40)] += near_b[...]
    share[3].start()
    r_ao.forward()

    r_cg.finish()
    r_ay.finish()
    r_az[2].start()
    grad_gram[...] = gram(ga[z].reshape(4 * NOISE, WA), cg[:, :, :WA].reshape(4 * CLEAN_ROWS, WA))

    share[2].wait_recv()
    share[3].wait_recv()
    full[rows_of(4 * c + x)] = sm[rows_of(x)] + x3[0] + x3[1]
    r_full.start()
    r_az[0].forward()
    r_full.forward()
    r_ao.finish()
    turn_a(0)
    r_full.finish()
    give = copy(full.at[own_half], full.at[own_half], d_s.at[1], d_r.at[1], partner)
    give.start()
    turn_a(1)
    turned[0].start()

    r_bz.finish()
    r_by[2].start()
    r_by[0].finish()
    grad_gram[...] += gram(gb[:, z].reshape(4 * NOISE, WB), cg[:, :, WA:].reshape(4 * CLEAN_ROWS, WB))
    copy(full.at[other_half], full.at[other_half], d_s.at[1], d_r.at[1], partner).wait_recv()

    def row_dot(j):
        terms = [grad_gram[g * SEG:(g + 1) * SEG] * full[g * SEG:(g + 1) * SEG] for g in range(j, 8, 2)]
        rows_sum = jnp.sum(terms[0] + terms[1] + terms[2] + terms[3], axis=0, keepdims=True)
        return jnp.broadcast_to(jnp.sum(rows_sum, axis=1, keepdims=True), (8, LANES))

    place = lax.broadcasted_iota(jnp.int32, (8, LANES), 0)
    tile = jnp.where(place == 2 * z, row_dot(0), jnp.where(place == 2 * z + 1, row_dot(1), 0.0))

    sends = []

    def send_tile(buf, value, me, n, dev, base):
        buf[me] = value
        for r in range(1, n):
            out = copy(buf.at[me], buf.at[me], v_s.at[base + r], v_r.at[base + r], dev(r))
            out.start()
            sends.append(out)

    def sum_tiles(buf, me, n, base):
        for r in range(1, n):
            origin = buf.at[lax.rem(me + n - r, n)]
            copy(origin, origin, v_s.at[base + r], v_r.at[base + r], partner).wait_recv()
        return jnp.sum(buf[...], axis=0)

    send_tile(sv1, tile, t, 8, lambda r: (z, y, lax.rem(t + r, 8)), 0)

    for v in range(4):
        turn_b(v)
    turned[1].start()
    tile = sum_tiles(sv1, t, 8, 0)
    send_tile(sv2, tile, 4 * z + y, 16, cell, 8)
    r_az[3].forward()
    r_by[3].forward()
    tile = sum_tiles(sv2, 4 * z + y, 16, 8)
    weights = jnp.maximum(-tile, 0.0) / jnp.sum(jnp.abs(tile), axis=0, keepdims=True)
    wts[...] = weights
    lane = lax.broadcasted_iota(jnp.int32, (1, LANES), 1)
    wout_ref[...] = jnp.where(lane == 0, wts[pl.ds(2 * z, 1), :], wts[pl.ds(2 * z + 1, 1), :])[:, :2]

    copy(ata.at[there], ata.at[there], k_s.at[0], k_r.at[0], partner).wait_recv()
    copy(atb.at[1 - c], atb.at[1 - c], k_s.at[1], k_r.at[1], partner).wait_recv()

    def scaled(rows_in, k):
        width = rows_in.shape[1]

        def part(j):
            row = wts[pl.ds(2 * k + j, 1), :]
            factor = jnp.broadcast_to(jnp.concatenate([row] * (width // LANES), axis=1), (SEG, width))
            return rows_in[j * SEG:(j + 1) * SEG] * factor

        return jnp.concatenate([part(0), part(1)], axis=0).astype(BF16)

    def product(left_of, right_of, width, base, first, span):
        def step(i, carry):
            cols = pl.ds(pl.multiple_of(i * span, span), span)
            dest = pl.ds(pl.multiple_of(base + i * span, 256), span)
            value = jnp.dot(left_of(), right_of(cols), preferred_element_type=F32)
            if first:
                out_ref[:, dest] = value
            else:
                out_ref[:, dest] += value
            return carry

        lax.fori_loop(0, width // span, step, 0)

    def add_a(k, first=False):
        v = mod4(z + k)

        def right_of(cols):
            return jnp.concatenate([scaled(ga[v, i, :, cols].astype(F32), v) for i in range(4)], axis=0)

        product(lambda: ata[v], right_of, WA, 0, first, 768)

    def add_b(k, first=False):
        v = mod4(y + k)

        def right_of(cols):
            parts = [scaled(gb[v, i, :, cols].astype(F32), i) for i in range(4)]
            empty = jnp.zeros((32, 512), BF16)
            return jnp.concatenate([parts[0], parts[1], empty, parts[2], parts[3], empty], axis=0)

        product(lambda: jnp.concatenate([atb[0, v], atb[1, v]], axis=1), right_of, WB, WA, first, 512)

    add_a(0, True)
    r_az[1].forward()
    r_by[1].forward()
    add_b(0, True)
    r_az[2].forward()
    add_a(3)
    r_by[2].forward()
    add_a(1)
    add_b(3)
    add_b(1)
    for k in (0, 3, 1, 2):
        r_az[k].finish()
    add_a(2)
    for k in (3, 1, 2):
        r_by[k].finish()
    add_b(2)

    for far_copy, _, same in pieces:
        @pl.when(jnp.logical_not(same))
        def _():
            far_copy.wait_send()
    for ring in rings:
        ring.drain()
    for k in turned + [swap, give] + share + sends:
        k.wait_send()


def body(activations, cotangents, row_ids, row_counts):
    dma = pltpu.SemaphoreType.DMA
    vmem = pltpu.VMEM
    return pl.pallas_call(
        body_kernel,
        out_shape=(pltpu.VMEM((512, WA + WB), F32), pltpu.VMEM((1, 2), F32)),
        in_specs=[pl.BlockSpec(memory_space=pltpu.SMEM)] * 2 + [pl.BlockSpec(memory_space=pltpu.VMEM)] * 2,
        out_specs=(pl.BlockSpec(memory_space=pltpu.VMEM), pl.BlockSpec(memory_space=pltpu.VMEM)),
        scratch_shapes=[
            vmem((4, NOISE, 1024), BF16),
            vmem((4, CLEAN_ROWS, 1024), BF16),
            vmem((4, CLEAN_ROWS, WA + WB), BF16),
            vmem((4, 4, NOISE, WA), BF16),
            vmem((4, 4, NOISE, WB), BF16),
            vmem((4, 4, 4, NOISE, LANES), BF16),
            vmem((4, 512, 4 * NOISE), BF16),
            vmem((2, 4, 512, 384), BF16),
            vmem((4 * NOISE, 4 * CLEAN_ROWS), F32),
            vmem((4 * NOISE, 4 * CLEAN_ROWS), F32),
            vmem((4 * NOISE, 4 * CLEAN_ROWS), F32),
            vmem((2 * NOISE, 4 * CLEAN_ROWS), F32),
            vmem((2 * NOISE, 4 * CLEAN_ROWS), F32),
            vmem((48, 4 * CLEAN_ROWS), F32),
            vmem((40, 4 * CLEAN_ROWS), F32),
            vmem((2, SEG, 4 * CLEAN_ROWS), F32),
            vmem((8, 8, LANES), F32),
            vmem((16, 8, LANES), F32),
            vmem((8, LANES), F32),
            dma((15, 4)), dma((15, 4)),
            dma((8,)), dma((8,)), dma,
            dma((2,)), dma((2,)),
            dma((2,)), dma((2,)),
            dma((4,)), dma((4,)),
            dma((24,)), dma((24,)),
        ],
        compiler_params=pltpu.CompilerParams(
            collective_id=0, has_side_effects=True, vmem_limit_bytes=60 * 1024 * 1024),
        cost_estimate=pl.CostEstimate(flops=8_000_000_000, bytes_accessed=8_000_000, transcendentals=0),
        name="reweight",
    )(row_ids, row_counts, activations, cotangents)


def solution(mesh):
    placed = (P("dp", "seq", "tensor"), P("dp", "seq", "tensor"), P("dp", None), P("dp", None))
    return jax.shard_map(
        body,
        mesh=mesh,
        in_specs=placed,
        out_specs=(P(("dp", "seq"), "tensor"), P("dp", None)),
        check_vma=False,
    )
```

```python
import jax
import jax.numpy as jnp
from jax import lax
from jax.experimental import pallas as pl
from jax.experimental.pallas import tpu as pltpu
from jax.sharding import PartitionSpec as P

MESH = pl.DeviceIdType.MESH
F32 = jnp.float32
BF16 = jnp.bfloat16

SEG = 88
NOISE = 176
CLEAN_ROWS = 96
WA = 768
WB = 1024
LANES = 128


def body_kernel(ids_ref, counts_ref, acts_ref, cot_ref, out_ref, wout_ref,
                na, ca, cg, ga, gb, hop, ao, ata, atb, part_gram, grad_gram, full, d2, sm,
                near_a, near_b, x3, sv1, sv2, wts,
                ring_s, ring_r, h_s, h_r, p_s, p_r, p_l, k_s, k_r,
                d_s, d_r, m_s, m_r, v_s, v_r):
    z = lax.axis_index("dp")
    y = lax.axis_index("seq")
    t = lax.axis_index("tensor")
    x = t // 2
    c = lax.rem(t, 2)

    def mod4(v):
        return lax.rem(v, 4)

    def copy(src, dst, s, r, dev):
        return pltpu.make_async_remote_copy(
            src_ref=src, dst_ref=dst, send_sem=s, recv_sem=r, device_id=dev, device_id_type=MESH)

    barrier = pltpu.get_barrier_semaphore()

    def greet(dev):
        pl.semaphore_signal(barrier, inc=1, device_id=dev, device_id_type=MESH)

    def cell(r):
        other = lax.rem(4 * z + y + r, 16)
        return other // 4, lax.rem(other, 4), t

    for r in range(1, 16):
        greet(cell(r))
    for r in range(1, 8):
        greet((z, y, lax.rem(t + r, 8)))

    targets = [(r, h, (mod4(x + r), 2 * c + h, 2 * x + z // 2)) for r in range(4) for h in range(2)]
    target_self = [(dev[0] == z) & (dev[1] == y) & (c == z // 2) for _, _, dev in targets]
    sources = [(2 * c + i // 4, i % 4) for i in range(8)]
    source_self = [(zs == z) & (ys == y) & (c == y // 2) for zs, ys in sources]
    for (_, _, dev), same in zip(targets, target_self):
        @pl.when(jnp.logical_not(same))
        def _():
            greet(dev)
    for (zs, ys), same in zip(sources, source_self):
        @pl.when(jnp.logical_not(same))
        def _():
            greet((zs, ys, 2 * x + y // 2))
    has_self = ((c == y // 2) & (c == z // 2)).astype(jnp.int32)

    rid = [ids_ref[0, j] for j in range(3)]
    live = [counts_ref[0, rid[j]] - y * SEG for j in range(3)]
    rows = lax.broadcasted_iota(jnp.int32, (SEG, LANES), 0)
    pad = jnp.zeros((CLEAN_ROWS - SEG, LANES), F32)

    def stage_acts(i, carry):
        cols = pl.ds(pl.multiple_of(i * LANES, LANES), LANES)
        part = [acts_ref[rid[j], :, cols].astype(F32) for j in range(3)]
        na[y, :, cols] = jnp.concatenate([part[1], part[2]], axis=0).astype(BF16)
        ca[z, :, cols] = jnp.concatenate([part[0], pad], axis=0).astype(BF16)
        return carry

    lax.fori_loop(0, 1024 // LANES, stage_acts, 0)

    def masked(j, cols):
        return jnp.where(rows < live[j], cot_ref[rid[j], :, cols].astype(F32), 0.0)

    def stage_clean(i, carry):
        cols = pl.ds(pl.multiple_of(i * LANES, LANES), LANES)
        cg[z, :, cols] = jnp.concatenate([masked(0, cols), pad], axis=0).astype(BF16)
        return carry

    def stage_a(i, carry):
        cols = pl.ds(pl.multiple_of(i * LANES, LANES), LANES)
        ga[z, y, :, cols] = jnp.concatenate([masked(1, cols), masked(2, cols)], axis=0).astype(BF16)
        return carry

    def stage_b(i, carry):
        cols = pl.ds(pl.multiple_of(i * LANES, LANES), LANES)
        from_cols = pl.ds(pl.multiple_of(WA + i * LANES, LANES), LANES)
        gb[y, z, :, cols] = jnp.concatenate(
            [masked(1, from_cols), masked(2, from_cols)], axis=0).astype(BF16)
        return carry

    pl.semaphore_wait(barrier, 38 - 2 * has_self)

    hops = []
    for r in range(1, 4):
        q = mod4(x + r)
        for h in range(2):
            src = na.at[y, :, pl.ds(pl.multiple_of(h * 512 + q * LANES, LANES), LANES)]
            hops.append(copy(src, hop.at[r, h], h_s.at[r, h], h_r.at[r, h], (z, y, 2 * q + c)))
    for k in hops:
        k.start()

    pieces = []

    def send_piece(i):
        r, h, dev = targets[i]
        same = target_self[i]
        if r:
            src = hop.at[4 - r, h]
            copy(src, src, h_s.at[4 - r, h], h_r.at[4 - r, h], (z, y, lax.rem(t + 1, 8))).wait_recv()
        else:
            src = na.at[y, :, pl.ds(pl.multiple_of(h * 512 + x * LANES, LANES), LANES)]
        dst = ao.at[x, z, y]
        far_copy = copy(src, dst, p_s.at[i], p_r.at[lax.rem(z, 2) * 4 + y], dev)
        near_copy = pltpu.make_async_copy(src, dst, p_l)

        @pl.when(same)
        def _():
            near_copy.start()

        @pl.when(jnp.logical_not(same))
        def _():
            far_copy.start()
        pieces.append((far_copy, same))

    rings = []

    class Ring:
        def __init__(self, at, axis, first, second):
            n = len(rings)
            rings.append(self)
            me = {"x": x, "y": y, "z": z}[axis]

            def dev(v):
                return {"x": (z, y, 2 * v + c), "y": (z, v, t), "z": (v, y, t)}[axis]

            up, down, far = mod4(me + 1), mod4(me + 3), mod4(me + 2)
            own, low, high, opp = at(me), at(down), at(up), at(far)
            self.go = [copy(own, own, ring_s.at[n, 0], ring_r.at[n, 0], dev(up)),
                       copy(own, own, ring_s.at[n, 1], ring_r.at[n, 1], dev(down))]
            self.got = [copy(low, low, ring_s.at[n, 0], ring_r.at[n, 0], dev(up)),
                        copy(high, high, ring_s.at[n, 1], ring_r.at[n, 1], dev(down))]
            self.pass_on = [
                copy(low.at[first], low.at[first], ring_s.at[n, 2], ring_r.at[n, 2], dev(up)),
                copy(high.at[second], high.at[second], ring_s.at[n, 3], ring_r.at[n, 3], dev(down))]
            self.got_far = [
                copy(opp.at[first], opp.at[first], ring_s.at[n, 2], ring_r.at[n, 2], dev(up)),
                copy(opp.at[second], opp.at[second], ring_s.at[n, 3], ring_r.at[n, 3], dev(down))]

        def start(self):
            for k in self.go:
                k.start()

        def forward(self):
            for k in range(2):
                self.got[k].wait_recv()
                self.pass_on[k].start()

        def finish(self):
            for k in self.got_far:
                k.wait_recv()

        def drain(self):
            for k in self.go + self.pass_on:
                k.wait_send()

    even = (pl.ds(0, 96),), (pl.ds(96, 80),)
    odd = (pl.ds(80, 96),), (pl.ds(0, 80),)
    equal = (pl.ds(0, 48),), (pl.ds(48, 48),)

    def az_ring(k):
        item = mod4(y + k)
        return Ring(lambda v: ga.at[v, item], "z", *(even if k in (0, 1) else odd))

    def by_ring(k):
        item = mod4(z + k)
        return Ring(lambda v: gb.at[v, item], "y", *(even if k in (0, 1) else odd))

    def rows_of(chunk):
        return pl.ds(pl.multiple_of(chunk * SEG, 8), SEG)

    r_na = Ring(lambda v: na.at[v], "y", *even)
    r_ca = Ring(lambda v: ca.at[v], "z", *equal)
    r_cg = Ring(lambda v: cg.at[v], "z", *equal)
    r_ay = Ring(lambda v: ga.at[z, v], "y", *odd)
    r_bz = Ring(lambda v: gb.at[y, v], "z", *odd)
    r_az = {k: az_ring(k) for k in (0, 3, 1, 2)}
    r_by = {k: by_ring(k) for k in (0, 3, 1, 2)}
    here = pl.ds(2 * c, 2)
    there = pl.ds(2 * (1 - c), 2)
    r_ao = Ring(lambda v: ao.at[v, here], "x", (pl.ds(0, 1),), (pl.ds(1, 1),))
    r_full = Ring(lambda v: full.at[rows_of(4 * c + v)], "x", (pl.ds(0, 48),), (pl.ds(48, 40),))

    r_na.start()
    r_ca.start()
    lax.fori_loop(0, WA // LANES, stage_a, 0)
    lax.fori_loop(0, (WA + WB) // LANES, stage_clean, 0)
    lax.fori_loop(0, WB // LANES, stage_b, 0)
    for i in range(8):
        send_piece(i)
    r_ay.start()
    r_cg.start()

    r_ca.forward()
    r_bz.start()
    r_na.forward()
    r_by[0].start()
    partner = (z, y, 2 * x + 1 - c)
    r_cg.forward()
    r_az[0].start()
    r_ay.forward()

    contract = (((1,), (1,)), ((), ()))

    def gram(left, right):
        return lax.dot_general(left, right, contract, preferred_element_type=F32)

    r_na.finish()
    r_ca.finish()
    part_gram[...] = gram(na[...].reshape(4 * NOISE, 1024), ca[...].reshape(4 * CLEAN_ROWS, 1024))
    own_half = pl.ds(pl.multiple_of(c * 352, 8), 352)
    other_half = pl.ds(pl.multiple_of((1 - c) * 352, 8), 352)
    swap = copy(part_gram.at[other_half], d2, d_s.at[0], d_r.at[0], partner)
    swap.start()

    r_bz.forward()
    r_az[3].start()
    r_az[1].start()
    for i, ((zs, ys), same) in enumerate(zip(sources, source_self)):
        dst = ao.at[x, zs, ys]
        far_copy = copy(dst, dst, p_s.at[i], p_r.at[i], (z, y, lax.rem(t + 1, 8)))
        near_copy = pltpu.make_async_copy(dst, dst, p_l)

        @pl.when(same)
        def _():
            near_copy.wait()

        @pl.when(jnp.logical_not(same))
        def _():
            far_copy.wait_recv()
    r_ao.start()

    def turn_a(k):
        def step(q, carry):
            span = pl.ds(pl.multiple_of(q * LANES, LANES), LANES)
            ata[2 * c + k, span, :] = ao[q, 2 * c + k].reshape(4 * NOISE, LANES).T
            return carry

        lax.fori_loop(0, 4, step, 0)

    gap = jnp.zeros((32, LANES), BF16)

    def turn_b(v):
        def step(q, carry):
            span = pl.ds(pl.multiple_of(q * LANES, LANES), LANES)
            tokens = jnp.concatenate([ao[q, 2 * c, v], ao[q, 2 * c + 1, v], gap], axis=0)
            atb[c, v, span, :] = tokens.T
            return carry

        lax.fori_loop(0, 4, step, 0)

    turned = [copy(ata.at[here], ata.at[here], k_s.at[0], k_r.at[0], partner),
              copy(atb.at[c], atb.at[c], k_s.at[1], k_r.at[1], partner)]
    swap.wait_recv()
    sm[...] = part_gram[own_half] + d2[...]
    up, down, across = mod4(x + 1), mod4(x + 3), mod4(x + 2)
    dev_up, dev_down = (z, y, 2 * up + c), (z, y, 2 * down + c)
    first = pl.ds(pl.multiple_of(across * SEG, 8), 48)
    second = pl.ds(pl.multiple_of(across * SEG + 48, 8), 40)
    share = [copy(sm.at[first], near_a, m_s.at[0], m_r.at[0], dev_up),
             copy(sm.at[second], near_b, m_s.at[1], m_r.at[1], dev_down),
             copy(sm.at[rows_of(up)], x3.at[0], m_s.at[2], m_r.at[2], dev_up),
             copy(sm.at[rows_of(down)], x3.at[1], m_s.at[3], m_r.at[3], dev_down)]
    share[0].start()
    share[1].start()
    r_by[0].forward()
    r_by[3].start()
    r_by[1].start()
    share[0].wait_recv()
    sm[pl.ds(pl.multiple_of(up * SEG, 8), 48)] += near_a[...]
    share[2].start()
    share[1].wait_recv()
    sm[pl.ds(pl.multiple_of(down * SEG + 48, 8), 40)] += near_b[...]
    share[3].start()
    r_ao.forward()

    r_cg.finish()
    r_ay.finish()
    r_az[2].start()
    grad_gram[...] = gram(ga[z].reshape(4 * NOISE, WA), cg[:, :, :WA].reshape(4 * CLEAN_ROWS, WA))

    share[2].wait_recv()
    share[3].wait_recv()
    full[rows_of(4 * c + x)] = sm[rows_of(x)] + x3[0] + x3[1]
    r_full.start()
    r_az[0].forward()
    r_full.forward()
    r_ao.finish()
    turn_a(0)
    r_full.finish()
    give = copy(full.at[own_half], full.at[own_half], d_s.at[1], d_r.at[1], partner)
    give.start()
    turn_a(1)
    turned[0].start()

    r_bz.finish()
    r_by[2].start()
    r_by[0].finish()
    grad_gram[...] += gram(gb[:, z].reshape(4 * NOISE, WB), cg[:, :, WA:].reshape(4 * CLEAN_ROWS, WB))
    copy(full.at[other_half], full.at[other_half], d_s.at[1], d_r.at[1], partner).wait_recv()

    def row_dot(j):
        terms = [grad_gram[g * SEG:(g + 1) * SEG] * full[g * SEG:(g + 1) * SEG] for g in range(j, 8, 2)]
        rows_sum = jnp.sum(terms[0] + terms[1] + terms[2] + terms[3], axis=0, keepdims=True)
        return jnp.broadcast_to(jnp.sum(rows_sum, axis=1, keepdims=True), (8, LANES))

    place = lax.broadcasted_iota(jnp.int32, (8, LANES), 0)
    tile = jnp.where(place == 2 * z, row_dot(0), jnp.where(place == 2 * z + 1, row_dot(1), 0.0))

    sends = []

    def send_tile(buf, value, me, n, dev, base):
        buf[me] = value
        for r in range(1, n):
            out = copy(buf.at[me], buf.at[me], v_s.at[base + r], v_r.at[base + r], dev(r))
            out.start()
            sends.append(out)

    def sum_tiles(buf, me, n, base):
        for r in range(1, n):
            origin = buf.at[lax.rem(me + n - r, n)]
            copy(origin, origin, v_s.at[base + r], v_r.at[base + r], partner).wait_recv()
        return jnp.sum(buf[...], axis=0)

    send_tile(sv1, tile, t, 8, lambda r: (z, y, lax.rem(t + r, 8)), 0)

    for v in range(4):
        turn_b(v)
    turned[1].start()
    tile = sum_tiles(sv1, t, 8, 0)
    send_tile(sv2, tile, 4 * z + y, 16, cell, 8)
    r_az[3].forward()
    r_by[3].forward()
    tile = sum_tiles(sv2, 4 * z + y, 16, 8)
    weights = jnp.maximum(-tile, 0.0) / jnp.sum(jnp.abs(tile), axis=0, keepdims=True)
    wts[...] = weights
    lane = lax.broadcasted_iota(jnp.int32, (1, LANES), 1)
    wout_ref[...] = jnp.where(lane == 0, wts[pl.ds(2 * z, 1), :], wts[pl.ds(2 * z + 1, 1), :])[:, :2]

    copy(ata.at[there], ata.at[there], k_s.at[0], k_r.at[0], partner).wait_recv()
    copy(atb.at[1 - c], atb.at[1 - c], k_s.at[1], k_r.at[1], partner).wait_recv()

    def scaled(rows_in, k):
        width = rows_in.shape[1]

        def part(j):
            row = wts[pl.ds(2 * k + j, 1), :]
            factor = jnp.broadcast_to(jnp.concatenate([row] * (width // LANES), axis=1), (SEG, width))
            return rows_in[j * SEG:(j + 1) * SEG] * factor

        return jnp.concatenate([part(0), part(1)], axis=0).astype(BF16)

    def product(left_of, right_of, width, base, first, span):
        def step(i, carry):
            cols = pl.ds(pl.multiple_of(i * span, span), span)
            dest = pl.ds(pl.multiple_of(base + i * span, 256), span)
            value = jnp.dot(left_of(), right_of(cols), preferred_element_type=F32)
            if first:
                out_ref[:, dest] = value
            else:
                out_ref[:, dest] += value
            return carry

        lax.fori_loop(0, width // span, step, 0)

    def add_a(k, first=False):
        v = mod4(z + k)

        def right_of(cols):
            return jnp.concatenate([scaled(ga[v, i, :, cols].astype(F32), v) for i in range(4)], axis=0)

        product(lambda: ata[v], right_of, WA, 0, first, 768)

    def add_b(k, first=False):
        v = mod4(y + k)

        def right_of(cols):
            parts = [scaled(gb[v, i, :, cols].astype(F32), i) for i in range(4)]
            empty = jnp.zeros((32, 512), BF16)
            return jnp.concatenate([parts[0], parts[1], empty, parts[2], parts[3], empty], axis=0)

        product(lambda: jnp.concatenate([atb[0, v], atb[1, v]], axis=1), right_of, WB, WA, first, 512)

    add_a(0, True)
    r_az[1].forward()
    r_by[1].forward()
    add_b(0, True)
    r_az[2].forward()
    add_a(3)
    r_by[2].forward()
    add_a(1)
    add_b(3)
    add_b(1)
    for k in (0, 3, 1, 2):
        r_az[k].finish()
    add_a(2)
    for k in (3, 1, 2):
        r_by[k].finish()
    add_b(2)

    for far_copy, same in pieces:
        @pl.when(jnp.logical_not(same))
        def _():
            far_copy.wait_send()
    for ring in rings:
        ring.drain()
    for k in hops + turned + [swap, give] + share + sends:
        k.wait_send()


def body(activations, cotangents, row_ids, row_counts):
    dma = pltpu.SemaphoreType.DMA
    vmem = pltpu.VMEM
    return pl.pallas_call(
        body_kernel,
        out_shape=(pltpu.VMEM((512, WA + WB), F32), pltpu.VMEM((1, 2), F32)),
        in_specs=[pl.BlockSpec(memory_space=pltpu.SMEM)] * 2 + [pl.BlockSpec(memory_space=pltpu.VMEM)] * 2,
        out_specs=(pl.BlockSpec(memory_space=pltpu.VMEM), pl.BlockSpec(memory_space=pltpu.VMEM)),
        scratch_shapes=[
            vmem((4, NOISE, 1024), BF16),
            vmem((4, CLEAN_ROWS, 1024), BF16),
            vmem((4, CLEAN_ROWS, WA + WB), BF16),
            vmem((4, 4, NOISE, WA), BF16),
            vmem((4, 4, NOISE, WB), BF16),
            vmem((4, 2, NOISE, LANES), BF16),
            vmem((4, 4, 4, NOISE, LANES), BF16),
            vmem((4, 512, 4 * NOISE), BF16),
            vmem((2, 4, 512, 384), BF16),
            vmem((4 * NOISE, 4 * CLEAN_ROWS), F32),
            vmem((4 * NOISE, 4 * CLEAN_ROWS), F32),
            vmem((4 * NOISE, 4 * CLEAN_ROWS), F32),
            vmem((2 * NOISE, 4 * CLEAN_ROWS), F32),
            vmem((2 * NOISE, 4 * CLEAN_ROWS), F32),
            vmem((48, 4 * CLEAN_ROWS), F32),
            vmem((40, 4 * CLEAN_ROWS), F32),
            vmem((2, SEG, 4 * CLEAN_ROWS), F32),
            vmem((8, 8, LANES), F32),
            vmem((16, 8, LANES), F32),
            vmem((8, LANES), F32),
            dma((15, 4)), dma((15, 4)),
            dma((4, 2)), dma((4, 2)),
            dma((8,)), dma((8,)), dma,
            dma((2,)), dma((2,)),
            dma((2,)), dma((2,)),
            dma((4,)), dma((4,)),
            dma((24,)), dma((24,)),
        ],
        compiler_params=pltpu.CompilerParams(
            collective_id=0, has_side_effects=True, vmem_limit_bytes=60 * 1024 * 1024),
        cost_estimate=pl.CostEstimate(flops=8_000_000_000, bytes_accessed=8_000_000, transcendentals=0),
        name="reweight",
    )(row_ids, row_counts, activations, cotangents)


def solution(mesh):
    placed = (P("dp", "seq", "tensor"), P("dp", "seq", "tensor"), P("dp", None), P("dp", None))
    return jax.shard_map(
        body,
        mesh=mesh,
        in_specs=placed,
        out_specs=(P(("dp", "seq"), "tensor"), P("dp", None)),
        check_vma=False,
    )
```

```python
import jax
import jax.numpy as jnp
from jax import lax
from jax.experimental import pallas as pl
from jax.experimental.pallas import tpu as pltpu
from jax.sharding import PartitionSpec as P

MESH = pl.DeviceIdType.MESH
F32 = jnp.float32
BF16 = jnp.bfloat16

SEG = 88
NOISE = 176
CLEAN_ROWS = 96
WA = 768
WB = 1024
LANES = 128


def body_kernel(ids_ref, counts_ref, acts_ref, cot_ref, out_ref, wout_ref,
                na, ca, cg, ga, gb, ao, ata, atb, part_gram, grad_gram, full, d2, sm,
                near_a, near_b, x3, sv1, sv2, wts,
                ring_s, ring_r, p_s, p_r, p_l, k_s, k_r,
                d_s, d_r, m_s, m_r, v_s, v_r):
    z = lax.axis_index("dp")
    y = lax.axis_index("seq")
    t = lax.axis_index("tensor")
    x = t // 2
    c = lax.rem(t, 2)

    def mod4(v):
        return lax.rem(v, 4)

    def copy(src, dst, s, r, dev):
        return pltpu.make_async_remote_copy(
            src_ref=src, dst_ref=dst, send_sem=s, recv_sem=r, device_id=dev, device_id_type=MESH)

    barrier = pltpu.get_barrier_semaphore()

    def greet(dev):
        pl.semaphore_signal(barrier, inc=1, device_id=dev, device_id_type=MESH)

    def cell(r):
        other = lax.rem(4 * z + y + r, 16)
        return other // 4, lax.rem(other, 4), t

    for r in range(1, 16):
        greet(cell(r))
    for r in range(1, 8):
        greet((z, y, lax.rem(t + r, 8)))

    targets = [(h, q, (x, 2 * c + h, 2 * q + z // 2)) for h in range(2) for q in range(4)]
    target_self = [(x == z) & (y == 2 * c + h) & (q == x) & (c == z // 2) for h, q, _ in targets]
    sources = [(2 * c + i // 4, i % 4) for i in range(8)]
    source_self = [(zs == z) & (ys == y) & (x == z) & (c == y // 2) for zs, ys in sources]
    for (_, _, dev), same in zip(targets, target_self):
        @pl.when(jnp.logical_not(same))
        def _():
            greet(dev)
    for (zs, ys), same in zip(sources, source_self):
        @pl.when(jnp.logical_not(same))
        def _():
            greet((zs, ys, 2 * z + y // 2))
    has_self = ((x == z) & (c == y // 2) & (c == z // 2)).astype(jnp.int32)

    rid = [ids_ref[0, j] for j in range(3)]
    live = [counts_ref[0, rid[j]] - y * SEG for j in range(3)]
    rows = lax.broadcasted_iota(jnp.int32, (SEG, LANES), 0)
    pad = jnp.zeros((CLEAN_ROWS - SEG, LANES), F32)

    def stage_acts(i, carry):
        cols = pl.ds(pl.multiple_of(i * LANES, LANES), LANES)
        part = [acts_ref[rid[j], :, cols].astype(F32) for j in range(3)]
        na[y, :, cols] = jnp.concatenate([part[1], part[2]], axis=0).astype(BF16)
        ca[z, :, cols] = jnp.concatenate([part[0], pad], axis=0).astype(BF16)
        return carry

    lax.fori_loop(0, 1024 // LANES, stage_acts, 0)

    def masked(j, cols):
        return jnp.where(rows < live[j], cot_ref[rid[j], :, cols].astype(F32), 0.0)

    def stage_clean(i, carry):
        cols = pl.ds(pl.multiple_of(i * LANES, LANES), LANES)
        cg[z, :, cols] = jnp.concatenate([masked(0, cols), pad], axis=0).astype(BF16)
        return carry

    def stage_a(i, carry):
        cols = pl.ds(pl.multiple_of(i * LANES, LANES), LANES)
        ga[z, y, :, cols] = jnp.concatenate([masked(1, cols), masked(2, cols)], axis=0).astype(BF16)
        return carry

    def stage_b(i, carry):
        cols = pl.ds(pl.multiple_of(i * LANES, LANES), LANES)
        from_cols = pl.ds(pl.multiple_of(WA + i * LANES, LANES), LANES)
        gb[y, z, :, cols] = jnp.concatenate(
            [masked(1, from_cols), masked(2, from_cols)], axis=0).astype(BF16)
        return carry

    pl.semaphore_wait(barrier, 38 - 2 * has_self)

    pieces = []
    for i, ((h, q, dev), same) in enumerate(zip(targets, target_self)):
        src = na.at[y, :, pl.ds(h * 512 + q * LANES, LANES)]
        dst = ao.at[q, z, y]
        far_copy = copy(src, dst, p_s.at[i], p_r.at[lax.rem(z, 2) * 4 + y], dev)
        near_copy = pltpu.make_async_copy(src, dst, p_l)

        @pl.when(same)
        def _():
            near_copy.start()

        @pl.when(jnp.logical_not(same))
        def _():
            far_copy.start()
        pieces.append((far_copy, near_copy, same))

    rings = []

    class Ring:
        def __init__(self, at, axis, first, second):
            n = len(rings)
            rings.append(self)
            me = {"x": x, "y": y, "z": z}[axis]

            def dev(v):
                return {"x": (z, y, 2 * v + c), "y": (z, v, t), "z": (v, y, t)}[axis]

            up, down, far = mod4(me + 1), mod4(me + 3), mod4(me + 2)
            own, low, high, opp = at(me), at(down), at(up), at(far)
            self.go = [copy(own, own, ring_s.at[n, 0], ring_r.at[n, 0], dev(up)),
                       copy(own, own, ring_s.at[n, 1], ring_r.at[n, 1], dev(down))]
            self.got = [copy(low, low, ring_s.at[n, 0], ring_r.at[n, 0], dev(up)),
                        copy(high, high, ring_s.at[n, 1], ring_r.at[n, 1], dev(down))]
            self.pass_on = [
                copy(low.at[first], low.at[first], ring_s.at[n, 2], ring_r.at[n, 2], dev(up)),
                copy(high.at[second], high.at[second], ring_s.at[n, 3], ring_r.at[n, 3], dev(down))]
            self.got_far = [
                copy(opp.at[first], opp.at[first], ring_s.at[n, 2], ring_r.at[n, 2], dev(up)),
                copy(opp.at[second], opp.at[second], ring_s.at[n, 3], ring_r.at[n, 3], dev(down))]

        def start(self):
            for k in self.go:
                k.start()

        def forward(self):
            for k in range(2):
                self.got[k].wait_recv()
                self.pass_on[k].start()

        def finish(self):
            for k in self.got_far:
                k.wait_recv()

        def drain(self):
            for k in self.go + self.pass_on:
                k.wait_send()

    even = (pl.ds(0, 96),), (pl.ds(96, 80),)
    odd = (pl.ds(80, 96),), (pl.ds(0, 80),)
    equal = (pl.ds(0, 48),), (pl.ds(48, 48),)

    def az_ring(k):
        item = mod4(y + k)
        return Ring(lambda v: ga.at[v, item], "z", *odd)

    def by_ring(k):
        item = mod4(z + k)
        return Ring(lambda v: gb.at[v, item], "y", *odd)

    def rows_of(chunk):
        return pl.ds(pl.multiple_of(chunk * SEG, 8), SEG)

    r_na = Ring(lambda v: na.at[v], "y", *odd)
    r_ca = Ring(lambda v: ca.at[v], "z", *equal)
    r_cg = Ring(lambda v: cg.at[v], "z", *equal)
    r_ay = Ring(lambda v: ga.at[z, v], "y", *odd)
    r_bz = Ring(lambda v: gb.at[y, v], "z", *odd)
    r_az = {k: az_ring(k) for k in (0, 3, 1, 2)}
    r_by = {k: by_ring(k) for k in (0, 3, 1, 2)}
    here = pl.ds(2 * c, 2)
    there = pl.ds(2 * (1 - c), 2)
    r_ao = Ring(lambda v: ao.at[v, here], "x", (pl.ds(0, 1),), (pl.ds(1, 1),))
    r_full = Ring(lambda v: full.at[rows_of(4 * c + v)], "x", (pl.ds(0, 48),), (pl.ds(48, 40),))

    r_na.start()
    r_ca.start()
    lax.fori_loop(0, WA // LANES, stage_a, 0)
    r_ay.start()
    lax.fori_loop(0, (WA + WB) // LANES, stage_clean, 0)
    r_cg.start()
    lax.fori_loop(0, WB // LANES, stage_b, 0)

    r_ca.forward()
    r_bz.start()
    r_na.forward()
    r_by[0].start()
    for i, ((zs, ys), same) in enumerate(zip(sources, source_self)):
        dst = ao.at[x, zs, ys]
        far_copy = copy(dst, dst, p_s.at[i], p_r.at[i], (z, y, lax.rem(t + 1, 8)))
        near_copy = pltpu.make_async_copy(dst, dst, p_l)

        @pl.when(same)
        def _():
            near_copy.wait()

        @pl.when(jnp.logical_not(same))
        def _():
            far_copy.wait_recv()
    partner = (z, y, 2 * x + 1 - c)
    r_ao.start()
    r_cg.forward()
    r_az[0].start()
    r_ay.forward()
    r_ao.forward()

    contract = (((1,), (1,)), ((), ()))

    def gram(left, right):
        return lax.dot_general(left, right, contract, preferred_element_type=F32)

    r_na.finish()
    r_ca.finish()
    part_gram[...] = gram(na[...].reshape(4 * NOISE, 1024), ca[...].reshape(4 * CLEAN_ROWS, 1024))
    own_half = pl.ds(pl.multiple_of(c * 352, 8), 352)
    other_half = pl.ds(pl.multiple_of((1 - c) * 352, 8), 352)
    swap = copy(part_gram.at[other_half], d2, d_s.at[0], d_r.at[0], partner)
    swap.start()

    r_ao.finish()
    r_bz.forward()
    r_az[3].start()
    r_az[1].start()

    def turn_a(k):
        def step(q, carry):
            span = pl.ds(pl.multiple_of(q * LANES, LANES), LANES)
            ata[2 * c + k, span, :] = ao[q, 2 * c + k].reshape(4 * NOISE, LANES).T
            return carry

        lax.fori_loop(0, 4, step, 0)

    gap = jnp.zeros((32, LANES), BF16)

    def turn_b(v):
        def step(q, carry):
            span = pl.ds(pl.multiple_of(q * LANES, LANES), LANES)
            tokens = jnp.concatenate([ao[q, 2 * c, v], ao[q, 2 * c + 1, v], gap], axis=0)
            atb[c, v, span, :] = tokens.T
            return carry

        lax.fori_loop(0, 4, step, 0)

    turned = [copy(ata.at[here], ata.at[here], k_s.at[0], k_r.at[0], partner),
              copy(atb.at[c], atb.at[c], k_s.at[1], k_r.at[1], partner)]
    turn_a(0)
    swap.wait_recv()
    sm[...] = part_gram[own_half] + d2[...]
    up, down, across = mod4(x + 1), mod4(x + 3), mod4(x + 2)
    dev_up, dev_down = (z, y, 2 * up + c), (z, y, 2 * down + c)
    first = pl.ds(pl.multiple_of(across * SEG, 8), 48)
    second = pl.ds(pl.multiple_of(across * SEG + 48, 8), 40)
    share = [copy(sm.at[first], near_a, m_s.at[0], m_r.at[0], dev_up),
             copy(sm.at[second], near_b, m_s.at[1], m_r.at[1], dev_down),
             copy(sm.at[rows_of(up)], x3.at[0], m_s.at[2], m_r.at[2], dev_up),
             copy(sm.at[rows_of(down)], x3.at[1], m_s.at[3], m_r.at[3], dev_down)]
    share[0].start()
    share[1].start()
    r_by[0].forward()
    r_by[3].start()
    r_by[1].start()
    turn_a(1)
    turned[0].start()
    share[0].wait_recv()
    sm[pl.ds(pl.multiple_of(up * SEG, 8), 48)] += near_a[...]
    share[2].start()
    share[1].wait_recv()
    sm[pl.ds(pl.multiple_of(down * SEG + 48, 8), 40)] += near_b[...]
    share[3].start()
    turn_b(0)

    r_cg.finish()
    r_ay.finish()
    r_az[2].start()
    grad_gram[...] = gram(ga[z].reshape(4 * NOISE, WA), cg[:, :, :WA].reshape(4 * CLEAN_ROWS, WA))

    share[2].wait_recv()
    share[3].wait_recv()
    full[rows_of(4 * c + x)] = sm[rows_of(x)] + x3[0] + x3[1]
    r_full.start()
    r_az[0].forward()
    turn_b(1)
    r_full.forward()
    turn_b(2)
    r_full.finish()
    give = copy(full.at[own_half], full.at[own_half], d_s.at[1], d_r.at[1], partner)
    give.start()
    turn_b(3)
    turned[1].start()

    r_bz.finish()
    r_by[2].start()
    r_by[0].finish()
    grad_gram[...] += gram(gb[:, z].reshape(4 * NOISE, WB), cg[:, :, WA:].reshape(4 * CLEAN_ROWS, WB))
    copy(full.at[other_half], full.at[other_half], d_s.at[1], d_r.at[1], partner).wait_recv()

    def row_dot(j):
        terms = [grad_gram[g * SEG:(g + 1) * SEG] * full[g * SEG:(g + 1) * SEG] for g in range(j, 8, 2)]
        rows_sum = jnp.sum(terms[0] + terms[1] + terms[2] + terms[3], axis=0, keepdims=True)
        return jnp.broadcast_to(jnp.sum(rows_sum, axis=1, keepdims=True), (8, LANES))

    place = lax.broadcasted_iota(jnp.int32, (8, LANES), 0)
    tile = jnp.where(place == 2 * z, row_dot(0), jnp.where(place == 2 * z + 1, row_dot(1), 0.0))

    sends = []

    def send_tile(buf, value, me, n, dev, base):
        buf[me] = value
        for r in range(1, n):
            out = copy(buf.at[me], buf.at[me], v_s.at[base + r], v_r.at[base + r], dev(r))
            out.start()
            sends.append(out)

    def sum_tiles(buf, me, n, base):
        for r in range(1, n):
            origin = buf.at[lax.rem(me + n - r, n)]
            copy(origin, origin, v_s.at[base + r], v_r.at[base + r], partner).wait_recv()
        return jnp.sum(buf[...], axis=0)

    send_tile(sv1, tile, t, 8, lambda r: (z, y, lax.rem(t + r, 8)), 0)

    tile = sum_tiles(sv1, t, 8, 0)
    send_tile(sv2, tile, 4 * z + y, 16, cell, 8)
    r_az[3].forward()
    r_by[3].forward()
    tile = sum_tiles(sv2, 4 * z + y, 16, 8)
    weights = jnp.maximum(-tile, 0.0) / jnp.sum(jnp.abs(tile), axis=0, keepdims=True)
    wts[...] = weights
    lane = lax.broadcasted_iota(jnp.int32, (1, LANES), 1)
    wout_ref[...] = jnp.where(lane == 0, wts[pl.ds(2 * z, 1), :], wts[pl.ds(2 * z + 1, 1), :])[:, :2]

    copy(ata.at[there], ata.at[there], k_s.at[0], k_r.at[0], partner).wait_recv()
    copy(atb.at[1 - c], atb.at[1 - c], k_s.at[1], k_r.at[1], partner).wait_recv()

    def scaled(rows_in, k):
        width = rows_in.shape[1]

        def part(j):
            row = wts[pl.ds(2 * k + j, 1), :]
            factor = jnp.broadcast_to(jnp.concatenate([row] * (width // LANES), axis=1), (SEG, width))
            return rows_in[j * SEG:(j + 1) * SEG] * factor

        return jnp.concatenate([part(0), part(1)], axis=0).astype(BF16)

    def product(left_of, right_of, width, base, first, span):
        def step(i, carry):
            cols = pl.ds(pl.multiple_of(i * span, span), span)
            dest = pl.ds(pl.multiple_of(base + i * span, 256), span)
            value = jnp.dot(left_of(), right_of(cols), preferred_element_type=F32)
            if first:
                out_ref[:, dest] = value
            else:
                out_ref[:, dest] += value
            return carry

        lax.fori_loop(0, width // span, step, 0)

    def add_a(k, first=False):
        v = mod4(z + k)

        def right_of(cols):
            return jnp.concatenate([scaled(ga[v, i, :, cols].astype(F32), v) for i in range(4)], axis=0)

        product(lambda: ata[v], right_of, WA, 0, first, 768)

    def add_b(k, first=False):
        v = mod4(y + k)

        def right_of(cols):
            parts = [scaled(gb[v, i, :, cols].astype(F32), i) for i in range(4)]
            empty = jnp.zeros((32, 512), BF16)
            return jnp.concatenate([parts[0], parts[1], empty, parts[2], parts[3], empty], axis=0)

        product(lambda: jnp.concatenate([atb[0, v], atb[1, v]], axis=1), right_of, WB, WA, first, 512)

    add_a(0, True)
    r_az[1].forward()
    r_by[1].forward()
    add_b(0, True)
    r_az[2].forward()
    add_a(3)
    r_by[2].forward()
    add_a(1)
    add_b(3)
    add_b(1)
    for k in (0, 3, 1, 2):
        r_az[k].finish()
    add_a(2)
    for k in (3, 1, 2):
        r_by[k].finish()
    add_b(2)

    for far_copy, _, same in pieces:
        @pl.when(jnp.logical_not(same))
        def _():
            far_copy.wait_send()
    for ring in rings:
        ring.drain()
    for k in turned + [swap, give] + share + sends:
        k.wait_send()


def body(activations, cotangents, row_ids, row_counts):
    dma = pltpu.SemaphoreType.DMA
    vmem = pltpu.VMEM
    return pl.pallas_call(
        body_kernel,
        out_shape=(pltpu.VMEM((512, WA + WB), F32), pltpu.VMEM((1, 2), F32)),
        in_specs=[pl.BlockSpec(memory_space=pltpu.SMEM)] * 2 + [pl.BlockSpec(memory_space=pltpu.VMEM)] * 2,
        out_specs=(pl.BlockSpec(memory_space=pltpu.VMEM), pl.BlockSpec(memory_space=pltpu.VMEM)),
        scratch_shapes=[
            vmem((4, NOISE, 1024), BF16),
            vmem((4, CLEAN_ROWS, 1024), BF16),
            vmem((4, CLEAN_ROWS, WA + WB), BF16),
            vmem((4, 4, NOISE, WA), BF16),
            vmem((4, 4, NOISE, WB), BF16),
            vmem((4, 4, 4, NOISE, LANES), BF16),
            vmem((4, 512, 4 * NOISE), BF16),
            vmem((2, 4, 512, 384), BF16),
            vmem((4 * NOISE, 4 * CLEAN_ROWS), F32),
            vmem((4 * NOISE, 4 * CLEAN_ROWS), F32),
            vmem((4 * NOISE, 4 * CLEAN_ROWS), F32),
            vmem((2 * NOISE, 4 * CLEAN_ROWS), F32),
            vmem((2 * NOISE, 4 * CLEAN_ROWS), F32),
            vmem((48, 4 * CLEAN_ROWS), F32),
            vmem((40, 4 * CLEAN_ROWS), F32),
            vmem((2, SEG, 4 * CLEAN_ROWS), F32),
            vmem((8, 8, LANES), F32),
            vmem((16, 8, LANES), F32),
            vmem((8, LANES), F32),
            dma((15, 4)), dma((15, 4)),
            dma((8,)), dma((8,)), dma,
            dma((2,)), dma((2,)),
            dma((2,)), dma((2,)),
            dma((4,)), dma((4,)),
            dma((24,)), dma((24,)),
        ],
        compiler_params=pltpu.CompilerParams(
            collective_id=0, has_side_effects=True, vmem_limit_bytes=60 * 1024 * 1024),
        cost_estimate=pl.CostEstimate(flops=8_000_000_000, bytes_accessed=8_000_000, transcendentals=0),
        name="reweight",
    )(row_ids, row_counts, activations, cotangents)


def solution(mesh):
    placed = (P("dp", "seq", "tensor"), P("dp", "seq", "tensor"), P("dp", None), P("dp", None))
    return jax.shard_map(
        body,
        mesh=mesh,
        in_specs=placed,
        out_specs=(P(("dp", "seq"), "tensor"), P("dp", None)),
        check_vma=False,
    )
```

```python
import jax
import jax.numpy as jnp
from jax import lax
from jax.experimental import pallas as pl
from jax.experimental.pallas import tpu as pltpu
from jax.sharding import PartitionSpec as P

MESH = pl.DeviceIdType.MESH
F32 = jnp.float32
BF16 = jnp.bfloat16

SEG = 88
NOISE = 176
CLEAN_ROWS = 96
WA = 768
WB = 1024
LANES = 128


def body_kernel(ids_ref, counts_ref, acts_ref, cot_ref, out_ref, wout_ref,
                na, ca, cg, ga, gb, ao, ata, atb, part_gram, grad_gram, full, d2, sm,
                near_a, near_b, x3, sv1, sv2, wts,
                ring_s, ring_r, p_s, p_r, p_l, k_s, k_r,
                d_s, d_r, m_s, m_r, v_s, v_r):
    z = lax.axis_index("dp")
    y = lax.axis_index("seq")
    t = lax.axis_index("tensor")
    x = t // 2
    c = lax.rem(t, 2)

    def mod4(v):
        return lax.rem(v, 4)

    def copy(src, dst, s, r, dev):
        return pltpu.make_async_remote_copy(
            src_ref=src, dst_ref=dst, send_sem=s, recv_sem=r, device_id=dev, device_id_type=MESH)

    barrier = pltpu.get_barrier_semaphore()

    def greet(dev):
        pl.semaphore_signal(barrier, inc=1, device_id=dev, device_id_type=MESH)

    def cell(r):
        other = lax.rem(4 * z + y + r, 16)
        return other // 4, lax.rem(other, 4), t

    for r in range(1, 16):
        greet(cell(r))
    for r in range(1, 8):
        greet((z, y, lax.rem(t + r, 8)))

    targets = [(h, q, (x, 2 * c + h, 2 * q + z // 2)) for h in range(2) for q in range(4)]
    target_self = [(x == z) & (y == 2 * c + h) & (q == x) & (c == z // 2) for h, q, _ in targets]
    sources = [(2 * c + i // 4, i % 4) for i in range(8)]
    source_self = [(zs == z) & (ys == y) & (x == z) & (c == y // 2) for zs, ys in sources]
    for (_, _, dev), same in zip(targets, target_self):
        @pl.when(jnp.logical_not(same))
        def _():
            greet(dev)
    for (zs, ys), same in zip(sources, source_self):
        @pl.when(jnp.logical_not(same))
        def _():
            greet((zs, ys, 2 * z + y // 2))
    has_self = ((x == z) & (c == y // 2) & (c == z // 2)).astype(jnp.int32)

    rid = [ids_ref[0, j] for j in range(3)]
    live = [counts_ref[0, rid[j]] - y * SEG for j in range(3)]
    rows = lax.broadcasted_iota(jnp.int32, (SEG, LANES), 0)
    pad = jnp.zeros((CLEAN_ROWS - SEG, LANES), F32)

    def stage_acts(i, carry):
        cols = pl.ds(pl.multiple_of(i * LANES, LANES), LANES)
        part = [acts_ref[rid[j], :, cols].astype(F32) for j in range(3)]
        na[y, :, cols] = jnp.concatenate([part[1], part[2]], axis=0).astype(BF16)
        ca[z, :, cols] = jnp.concatenate([part[0], pad], axis=0).astype(BF16)
        return carry

    lax.fori_loop(0, 1024 // LANES, stage_acts, 0)

    def masked(j, cols):
        return jnp.where(rows < live[j], cot_ref[rid[j], :, cols].astype(F32), 0.0)

    def stage_clean(i, carry):
        cols = pl.ds(pl.multiple_of(i * LANES, LANES), LANES)
        cg[z, :, cols] = jnp.concatenate([masked(0, cols), pad], axis=0).astype(BF16)
        return carry

    def stage_a(i, carry):
        cols = pl.ds(pl.multiple_of(i * LANES, LANES), LANES)
        ga[z, y, :, cols] = jnp.concatenate([masked(1, cols), masked(2, cols)], axis=0).astype(BF16)
        return carry

    def stage_b(i, carry):
        cols = pl.ds(pl.multiple_of(i * LANES, LANES), LANES)
        from_cols = pl.ds(pl.multiple_of(WA + i * LANES, LANES), LANES)
        gb[y, z, :, cols] = jnp.concatenate(
            [masked(1, from_cols), masked(2, from_cols)], axis=0).astype(BF16)
        return carry

    pl.semaphore_wait(barrier, 38 - 2 * has_self)

    pieces = []
    for i, ((h, q, dev), same) in enumerate(zip(targets, target_self)):
        src = na.at[y, :, pl.ds(h * 512 + q * LANES, LANES)]
        dst = ao.at[q, z, y]
        far_copy = copy(src, dst, p_s.at[i], p_r.at[lax.rem(z, 2) * 4 + y], dev)
        near_copy = pltpu.make_async_copy(src, dst, p_l)

        @pl.when(same)
        def _():
            near_copy.start()

        @pl.when(jnp.logical_not(same))
        def _():
            far_copy.start()
        pieces.append((far_copy, near_copy, same))

    rings = []

    class Ring:
        def __init__(self, at, axis, first, second):
            n = len(rings)
            rings.append(self)
            me = {"x": x, "y": y, "z": z}[axis]

            def dev(v):
                return {"x": (z, y, 2 * v + c), "y": (z, v, t), "z": (v, y, t)}[axis]

            up, down, far = mod4(me + 1), mod4(me + 3), mod4(me + 2)
            own, low, high, opp = at(me), at(down), at(up), at(far)
            self.go = [copy(own, own, ring_s.at[n, 0], ring_r.at[n, 0], dev(up)),
                       copy(own, own, ring_s.at[n, 1], ring_r.at[n, 1], dev(down))]
            self.got = [copy(low, low, ring_s.at[n, 0], ring_r.at[n, 0], dev(up)),
                        copy(high, high, ring_s.at[n, 1], ring_r.at[n, 1], dev(down))]
            self.pass_on = [
                copy(low.at[first], low.at[first], ring_s.at[n, 2], ring_r.at[n, 2], dev(up)),
                copy(high.at[second], high.at[second], ring_s.at[n, 3], ring_r.at[n, 3], dev(down))]
            self.got_far = [
                copy(opp.at[first], opp.at[first], ring_s.at[n, 2], ring_r.at[n, 2], dev(up)),
                copy(opp.at[second], opp.at[second], ring_s.at[n, 3], ring_r.at[n, 3], dev(down))]

        def start(self):
            for k in self.go:
                k.start()

        def forward(self):
            for k in range(2):
                self.got[k].wait_recv()
                self.pass_on[k].start()

        def finish(self):
            for k in self.got_far:
                k.wait_recv()

        def drain(self):
            for k in self.go + self.pass_on:
                k.wait_send()

    uneven = (pl.ds(0, 80),), (pl.ds(80, 96),)
    equal = (pl.ds(0, 48),), (pl.ds(48, 48),)

    def az_ring(k):
        item = mod4(y + k)
        return Ring(lambda v: ga.at[v, item], "z", *uneven)

    def by_ring(k):
        item = mod4(z + k)
        return Ring(lambda v: gb.at[v, item], "y", *uneven)

    def rows_of(chunk):
        return pl.ds(pl.multiple_of(chunk * SEG, 8), SEG)

    r_na = Ring(lambda v: na.at[v], "y", *uneven)
    r_ca = Ring(lambda v: ca.at[v], "z", *equal)
    r_cg = Ring(lambda v: cg.at[v], "z", *equal)
    r_ay = Ring(lambda v: ga.at[z, v], "y", *uneven)
    r_bz = Ring(lambda v: gb.at[y, v], "z", *uneven)
    r_az = {k: az_ring(k) for k in (0, 3, 1, 2)}
    r_by = {k: by_ring(k) for k in (0, 3, 1, 2)}
    here = pl.ds(2 * c, 2)
    there = pl.ds(2 * (1 - c), 2)
    r_ao = Ring(lambda v: ao.at[v, here], "x", (pl.ds(0, 1),), (pl.ds(1, 1),))
    r_full = Ring(lambda v: full.at[rows_of(4 * c + v)], "x", (pl.ds(0, 48),), (pl.ds(48, 40),))

    r_na.start()
    r_ca.start()
    lax.fori_loop(0, WA // LANES, stage_a, 0)
    r_ay.start()
    lax.fori_loop(0, (WA + WB) // LANES, stage_clean, 0)
    r_cg.start()
    lax.fori_loop(0, WB // LANES, stage_b, 0)

    r_ca.forward()
    r_bz.start()
    r_na.forward()
    r_by[0].start()
    for i, ((zs, ys), same) in enumerate(zip(sources, source_self)):
        dst = ao.at[x, zs, ys]
        far_copy = copy(dst, dst, p_s.at[i], p_r.at[i], (z, y, lax.rem(t + 1, 8)))
        near_copy = pltpu.make_async_copy(dst, dst, p_l)

        @pl.when(same)
        def _():
            near_copy.wait()

        @pl.when(jnp.logical_not(same))
        def _():
            far_copy.wait_recv()
    partner = (z, y, 2 * x + 1 - c)
    r_ao.start()
    r_cg.forward()
    r_az[0].start()
    r_ay.forward()
    r_ao.forward()

    contract = (((1,), (1,)), ((), ()))

    def gram(left, right):
        return lax.dot_general(left, right, contract, preferred_element_type=F32)

    r_na.finish()
    r_ca.finish()
    part_gram[...] = gram(na[...].reshape(4 * NOISE, 1024), ca[...].reshape(4 * CLEAN_ROWS, 1024))
    own_half = pl.ds(pl.multiple_of(c * 352, 8), 352)
    other_half = pl.ds(pl.multiple_of((1 - c) * 352, 8), 352)
    swap = copy(part_gram.at[other_half], d2, d_s.at[0], d_r.at[0], partner)
    swap.start()

    r_ao.finish()
    r_bz.forward()
    r_az[3].start()
    r_az[1].start()

    def turn_a(k):
        def step(q, carry):
            span = pl.ds(pl.multiple_of(q * LANES, LANES), LANES)
            ata[2 * c + k, span, :] = ao[q, 2 * c + k].reshape(4 * NOISE, LANES).T
            return carry

        lax.fori_loop(0, 4, step, 0)

    gap = jnp.zeros((32, LANES), BF16)

    def turn_b(v):
        def step(q, carry):
            span = pl.ds(pl.multiple_of(q * LANES, LANES), LANES)
            tokens = jnp.concatenate([ao[q, 2 * c, v], ao[q, 2 * c + 1, v], gap], axis=0)
            atb[c, v, span, :] = tokens.T
            return carry

        lax.fori_loop(0, 4, step, 0)

    turned = [copy(ata.at[here], ata.at[here], k_s.at[0], k_r.at[0], partner),
              copy(atb.at[c], atb.at[c], k_s.at[1], k_r.at[1], partner)]
    turn_a(0)
    swap.wait_recv()
    sm[...] = part_gram[own_half] + d2[...]
    up, down, across = mod4(x + 1), mod4(x + 3), mod4(x + 2)
    dev_up, dev_down = (z, y, 2 * up + c), (z, y, 2 * down + c)
    first = pl.ds(pl.multiple_of(across * SEG, 8), 48)
    second = pl.ds(pl.multiple_of(across * SEG + 48, 8), 40)
    share = [copy(sm.at[first], near_a, m_s.at[0], m_r.at[0], dev_up),
             copy(sm.at[second], near_b, m_s.at[1], m_r.at[1], dev_down),
             copy(sm.at[rows_of(up)], x3.at[0], m_s.at[2], m_r.at[2], dev_up),
             copy(sm.at[rows_of(down)], x3.at[1], m_s.at[3], m_r.at[3], dev_down)]
    share[0].start()
    share[1].start()
    r_by[0].forward()
    r_by[3].start()
    r_by[1].start()
    turn_a(1)
    turned[0].start()
    share[0].wait_recv()
    sm[pl.ds(pl.multiple_of(up * SEG, 8), 48)] += near_a[...]
    share[2].start()
    share[1].wait_recv()
    sm[pl.ds(pl.multiple_of(down * SEG + 48, 8), 40)] += near_b[...]
    share[3].start()
    turn_b(0)

    r_cg.finish()
    r_ay.finish()
    r_az[2].start()
    grad_gram[...] = gram(ga[z].reshape(4 * NOISE, WA), cg[:, :, :WA].reshape(4 * CLEAN_ROWS, WA))

    share[2].wait_recv()
    share[3].wait_recv()
    full[rows_of(4 * c + x)] = sm[rows_of(x)] + x3[0] + x3[1]
    r_full.start()
    r_az[0].forward()
    turn_b(1)
    r_full.forward()
    turn_b(2)
    r_full.finish()
    give = copy(full.at[own_half], full.at[own_half], d_s.at[1], d_r.at[1], partner)
    give.start()
    turn_b(3)
    turned[1].start()

    r_bz.finish()
    r_by[2].start()
    r_by[0].finish()
    grad_gram[...] += gram(gb[:, z].reshape(4 * NOISE, WB), cg[:, :, WA:].reshape(4 * CLEAN_ROWS, WB))
    copy(full.at[other_half], full.at[other_half], d_s.at[1], d_r.at[1], partner).wait_recv()

    def row_dot(j):
        terms = [grad_gram[g * SEG:(g + 1) * SEG] * full[g * SEG:(g + 1) * SEG] for g in range(j, 8, 2)]
        rows_sum = jnp.sum(terms[0] + terms[1] + terms[2] + terms[3], axis=0, keepdims=True)
        return jnp.broadcast_to(jnp.sum(rows_sum, axis=1, keepdims=True), (8, LANES))

    place = lax.broadcasted_iota(jnp.int32, (8, LANES), 0)
    tile = jnp.where(place == 2 * z, row_dot(0), jnp.where(place == 2 * z + 1, row_dot(1), 0.0))

    sends = []

    def send_tile(buf, value, me, n, dev, base):
        buf[me] = value
        for r in range(1, n):
            out = copy(buf.at[me], buf.at[me], v_s.at[base + r], v_r.at[base + r], dev(r))
            out.start()
            sends.append(out)

    def sum_tiles(buf, me, n, base):
        for r in range(1, n):
            origin = buf.at[lax.rem(me + n - r, n)]
            copy(origin, origin, v_s.at[base + r], v_r.at[base + r], partner).wait_recv()
        return jnp.sum(buf[...], axis=0)

    send_tile(sv1, tile, t, 8, lambda r: (z, y, lax.rem(t + r, 8)), 0)

    tile = sum_tiles(sv1, t, 8, 0)
    send_tile(sv2, tile, 4 * z + y, 16, cell, 8)
    r_az[3].forward()
    r_by[3].forward()
    tile = sum_tiles(sv2, 4 * z + y, 16, 8)
    weights = jnp.maximum(-tile, 0.0) / jnp.sum(jnp.abs(tile), axis=0, keepdims=True)
    wts[...] = weights
    lane = lax.broadcasted_iota(jnp.int32, (1, LANES), 1)
    wout_ref[...] = jnp.where(lane == 0, wts[pl.ds(2 * z, 1), :], wts[pl.ds(2 * z + 1, 1), :])[:, :2]

    copy(ata.at[there], ata.at[there], k_s.at[0], k_r.at[0], partner).wait_recv()
    copy(atb.at[1 - c], atb.at[1 - c], k_s.at[1], k_r.at[1], partner).wait_recv()

    def scaled(rows_in, k):
        width = rows_in.shape[1]

        def part(j):
            row = wts[pl.ds(2 * k + j, 1), :]
            factor = jnp.broadcast_to(jnp.concatenate([row] * (width // LANES), axis=1), (SEG, width))
            return rows_in[j * SEG:(j + 1) * SEG] * factor

        return jnp.concatenate([part(0), part(1)], axis=0).astype(BF16)

    def product(left_of, right_of, width, base, first, span):
        def step(i, carry):
            cols = pl.ds(pl.multiple_of(i * span, span), span)
            dest = pl.ds(pl.multiple_of(base + i * span, 256), span)
            value = jnp.dot(left_of(), right_of(cols), preferred_element_type=F32)
            if first:
                out_ref[:, dest] = value
            else:
                out_ref[:, dest] += value
            return carry

        lax.fori_loop(0, width // span, step, 0)

    def add_a(k, first=False):
        v = mod4(z + k)

        def right_of(cols):
            return jnp.concatenate([scaled(ga[v, i, :, cols].astype(F32), v) for i in range(4)], axis=0)

        product(lambda: ata[v], right_of, WA, 0, first, 768)

    def add_b(k, first=False):
        v = mod4(y + k)

        def right_of(cols):
            parts = [scaled(gb[v, i, :, cols].astype(F32), i) for i in range(4)]
            empty = jnp.zeros((32, 512), BF16)
            return jnp.concatenate([parts[0], parts[1], empty, parts[2], parts[3], empty], axis=0)

        product(lambda: jnp.concatenate([atb[0, v], atb[1, v]], axis=1), right_of, WB, WA, first, 512)

    add_a(0, True)
    r_az[1].forward()
    r_by[1].forward()
    add_b(0, True)
    r_az[2].forward()
    add_a(3)
    r_by[2].forward()
    add_a(1)
    add_b(3)
    add_b(1)
    for k in (0, 3, 1, 2):
        r_az[k].finish()
    add_a(2)
    for k in (3, 1, 2):
        r_by[k].finish()
    add_b(2)

    for far_copy, _, same in pieces:
        @pl.when(jnp.logical_not(same))
        def _():
            far_copy.wait_send()
    for ring in rings:
        ring.drain()
    for k in turned + [swap, give] + share + sends:
        k.wait_send()


def body(activations, cotangents, row_ids, row_counts):
    dma = pltpu.SemaphoreType.DMA
    vmem = pltpu.VMEM
    return pl.pallas_call(
        body_kernel,
        out_shape=(pltpu.VMEM((512, WA + WB), F32), pltpu.VMEM((1, 2), F32)),
        in_specs=[pl.BlockSpec(memory_space=pltpu.SMEM)] * 2 + [pl.BlockSpec(memory_space=pltpu.VMEM)] * 2,
        out_specs=(pl.BlockSpec(memory_space=pltpu.VMEM), pl.BlockSpec(memory_space=pltpu.VMEM)),
        scratch_shapes=[
            vmem((4, NOISE, 1024), BF16),
            vmem((4, CLEAN_ROWS, 1024), BF16),
            vmem((4, CLEAN_ROWS, WA + WB), BF16),
            vmem((4, 4, NOISE, WA), BF16),
            vmem((4, 4, NOISE, WB), BF16),
            vmem((4, 4, 4, NOISE, LANES), BF16),
            vmem((4, 512, 4 * NOISE), BF16),
            vmem((2, 4, 512, 384), BF16),
            vmem((4 * NOISE, 4 * CLEAN_ROWS), F32),
            vmem((4 * NOISE, 4 * CLEAN_ROWS), F32),
            vmem((4 * NOISE, 4 * CLEAN_ROWS), F32),
            vmem((2 * NOISE, 4 * CLEAN_ROWS), F32),
            vmem((2 * NOISE, 4 * CLEAN_ROWS), F32),
            vmem((48, 4 * CLEAN_ROWS), F32),
            vmem((40, 4 * CLEAN_ROWS), F32),
            vmem((2, SEG, 4 * CLEAN_ROWS), F32),
            vmem((8, 8, LANES), F32),
            vmem((16, 8, LANES), F32),
            vmem((8, LANES), F32),
            dma((15, 4)), dma((15, 4)),
            dma((8,)), dma((8,)), dma,
            dma((2,)), dma((2,)),
            dma((2,)), dma((2,)),
            dma((4,)), dma((4,)),
            dma((24,)), dma((24,)),
        ],
        compiler_params=pltpu.CompilerParams(
            collective_id=0, has_side_effects=True, vmem_limit_bytes=60 * 1024 * 1024),
        cost_estimate=pl.CostEstimate(flops=8_000_000_000, bytes_accessed=8_000_000, transcendentals=0),
        name="reweight",
    )(row_ids, row_counts, activations, cotangents)


def solution(mesh):
    placed = (P("dp", "seq", "tensor"), P("dp", "seq", "tensor"), P("dp", None), P("dp", None))
    return jax.shard_map(
        body,
        mesh=mesh,
        in_specs=placed,
        out_specs=(P(("dp", "seq"), "tensor"), P("dp", None)),
        check_vma=False,
    )
```

```python
import jax
import jax.numpy as jnp
from jax import lax
from jax.experimental import pallas as pl
from jax.experimental.pallas import tpu as pltpu
from jax.sharding import PartitionSpec as P

MESH = pl.DeviceIdType.MESH
F32 = jnp.float32
BF16 = jnp.bfloat16

SEG = 88
NOISE = 176
CLEAN_ROWS = 96
WA = 768
WB = 1024
LANES = 128


def body_kernel(ids_ref, counts_ref, acts_ref, cot_ref, out_ref, wout_ref,
                na, ca, cg, ga, gb, ao, ata, atb, part_gram, grad_gram, full, d2, sm,
                near_a, near_b, x3, sv1, sv2, wts,
                ring_s, ring_r, p_s, p_r, p_l, k_s, k_r,
                d_s, d_r, m_s, m_r, v_s, v_r):
    z = lax.axis_index("dp")
    y = lax.axis_index("seq")
    t = lax.axis_index("tensor")
    x = t // 2
    c = lax.rem(t, 2)

    def mod4(v):
        return lax.rem(v, 4)

    def copy(src, dst, s, r, dev):
        return pltpu.make_async_remote_copy(
            src_ref=src, dst_ref=dst, send_sem=s, recv_sem=r, device_id=dev, device_id_type=MESH)

    barrier = pltpu.get_barrier_semaphore()

    def greet(dev):
        pl.semaphore_signal(barrier, inc=1, device_id=dev, device_id_type=MESH)

    def cell(r):
        other = lax.rem(4 * z + y + r, 16)
        return other // 4, lax.rem(other, 4), t

    for r in range(1, 16):
        greet(cell(r))
    for r in range(1, 8):
        greet((z, y, lax.rem(t + r, 8)))

    targets = [(h, q, (x, 2 * c + h, 2 * q + z // 2)) for h in range(2) for q in range(4)]
    target_self = [(x == z) & (y == 2 * c + h) & (q == x) & (c == z // 2) for h, q, _ in targets]
    sources = [(2 * c + i // 4, i % 4) for i in range(8)]
    source_self = [(zs == z) & (ys == y) & (x == z) & (c == y // 2) for zs, ys in sources]
    for (_, _, dev), same in zip(targets, target_self):
        @pl.when(jnp.logical_not(same))
        def _():
            greet(dev)
    for (zs, ys), same in zip(sources, source_self):
        @pl.when(jnp.logical_not(same))
        def _():
            greet((zs, ys, 2 * z + y // 2))
    has_self = ((x == z) & (c == y // 2) & (c == z // 2)).astype(jnp.int32)

    rid = [ids_ref[0, j] for j in range(3)]
    live = [counts_ref[0, rid[j]] - y * SEG for j in range(3)]
    rows = lax.broadcasted_iota(jnp.int32, (SEG, LANES), 0)
    pad = jnp.zeros((CLEAN_ROWS - SEG, LANES), F32)

    def stage_acts(i, carry):
        cols = pl.ds(pl.multiple_of(i * LANES, LANES), LANES)
        part = [acts_ref[rid[j], :, cols].astype(F32) for j in range(3)]
        na[y, :, cols] = jnp.concatenate([part[1], part[2]], axis=0).astype(BF16)
        ca[z, :, cols] = jnp.concatenate([part[0], pad], axis=0).astype(BF16)
        return carry

    lax.fori_loop(0, 1024 // LANES, stage_acts, 0)

    def masked(j, cols):
        return jnp.where(rows < live[j], cot_ref[rid[j], :, cols].astype(F32), 0.0)

    def stage_clean(i, carry):
        cols = pl.ds(pl.multiple_of(i * LANES, LANES), LANES)
        cg[z, :, cols] = jnp.concatenate([masked(0, cols), pad], axis=0).astype(BF16)
        return carry

    def stage_a(i, carry):
        cols = pl.ds(pl.multiple_of(i * LANES, LANES), LANES)
        ga[z, y, :, cols] = jnp.concatenate([masked(1, cols), masked(2, cols)], axis=0).astype(BF16)
        return carry

    def stage_b(i, carry):
        cols = pl.ds(pl.multiple_of(i * LANES, LANES), LANES)
        from_cols = pl.ds(pl.multiple_of(WA + i * LANES, LANES), LANES)
        gb[y, z, :, cols] = jnp.concatenate(
            [masked(1, from_cols), masked(2, from_cols)], axis=0).astype(BF16)
        return carry

    pl.semaphore_wait(barrier, 38 - 2 * has_self)

    pieces = []
    for i, ((h, q, dev), same) in enumerate(zip(targets, target_self)):
        src = na.at[y, :, pl.ds(h * 512 + q * LANES, LANES)]
        dst = ao.at[q, z, y]
        far_copy = copy(src, dst, p_s.at[i], p_r.at[lax.rem(z, 2) * 4 + y], dev)
        near_copy = pltpu.make_async_copy(src, dst, p_l)

        @pl.when(same)
        def _():
            near_copy.start()

        @pl.when(jnp.logical_not(same))
        def _():
            far_copy.start()
        pieces.append((far_copy, near_copy, same))

    rings = []

    class Ring:
        def __init__(self, at, axis, first, second):
            n = len(rings)
            rings.append(self)
            me = {"x": x, "y": y, "z": z}[axis]

            def dev(v):
                return {"x": (z, y, 2 * v + c), "y": (z, v, t), "z": (v, y, t)}[axis]

            up, down, far = mod4(me + 1), mod4(me + 3), mod4(me + 2)
            own, low, high, opp = at(me), at(down), at(up), at(far)
            self.go = [copy(own, own, ring_s.at[n, 0], ring_r.at[n, 0], dev(up)),
                       copy(own, own, ring_s.at[n, 1], ring_r.at[n, 1], dev(down))]
            self.got = [copy(low, low, ring_s.at[n, 0], ring_r.at[n, 0], dev(up)),
                        copy(high, high, ring_s.at[n, 1], ring_r.at[n, 1], dev(down))]
            self.pass_on = [
                copy(low.at[first], low.at[first], ring_s.at[n, 2], ring_r.at[n, 2], dev(up)),
                copy(high.at[second], high.at[second], ring_s.at[n, 3], ring_r.at[n, 3], dev(down))]
            self.got_far = [
                copy(opp.at[first], opp.at[first], ring_s.at[n, 2], ring_r.at[n, 2], dev(up)),
                copy(opp.at[second], opp.at[second], ring_s.at[n, 3], ring_r.at[n, 3], dev(down))]

        def start(self):
            for k in self.go:
                k.start()

        def forward(self):
            for k in range(2):
                self.got[k].wait_recv()
                self.pass_on[k].start()

        def finish(self):
            for k in self.got_far:
                k.wait_recv()

        def drain(self):
            for k in self.go + self.pass_on:
                k.wait_send()

    even = (pl.ds(0, 96),), (pl.ds(96, 80),)
    odd = (pl.ds(80, 96),), (pl.ds(0, 80),)
    equal = (pl.ds(0, 48),), (pl.ds(48, 48),)

    def az_ring(k):
        item = mod4(y + k)
        return Ring(lambda v: ga.at[v, item], "z", *(even if k in (0, 1) else odd))

    def by_ring(k):
        item = mod4(z + k)
        return Ring(lambda v: gb.at[v, item], "y", *(even if k in (0, 1) else odd))

    def rows_of(chunk):
        return pl.ds(pl.multiple_of(chunk * SEG, 8), SEG)

    r_na = Ring(lambda v: na.at[v], "y", *even)
    r_ca = Ring(lambda v: ca.at[v], "z", *equal)
    r_cg = Ring(lambda v: cg.at[v], "z", *equal)
    r_ay = Ring(lambda v: ga.at[z, v], "y", *odd)
    r_bz = Ring(lambda v: gb.at[y, v], "z", *odd)
    r_az = {k: az_ring(k) for k in (0, 3, 1, 2)}
    r_by = {k: by_ring(k) for k in (0, 3, 1, 2)}
    here = pl.ds(2 * c, 2)
    there = pl.ds(2 * (1 - c), 2)
    r_ao = Ring(lambda v: ao.at[v, here], "x", (pl.ds(0, 1),), (pl.ds(1, 1),))
    r_full = Ring(lambda v: full.at[rows_of(4 * c + v)], "x", (pl.ds(0, 48),), (pl.ds(48, 40),))

    r_na.start()
    r_ca.start()
    lax.fori_loop(0, (WA + WB) // LANES, stage_clean, 0)
    r_cg.start()
    lax.fori_loop(0, WA // LANES, stage_a, 0)
    lax.fori_loop(0, WB // LANES, stage_b, 0)

    r_ca.forward()
    r_na.forward()
    r_ay.start()
    r_by[0].start()
    for i, ((zs, ys), same) in enumerate(zip(sources, source_self)):
        dst = ao.at[x, zs, ys]
        far_copy = copy(dst, dst, p_s.at[i], p_r.at[i], (z, y, lax.rem(t + 1, 8)))
        near_copy = pltpu.make_async_copy(dst, dst, p_l)

        @pl.when(same)
        def _():
            near_copy.wait()

        @pl.when(jnp.logical_not(same))
        def _():
            far_copy.wait_recv()
    partner = (z, y, 2 * x + 1 - c)
    r_ao.start()
    r_cg.forward()
    r_bz.start()
    r_az[0].start()

    contract = (((1,), (1,)), ((), ()))

    def gram(left, right):
        return lax.dot_general(left, right, contract, preferred_element_type=F32)

    r_na.finish()
    r_ca.finish()
    part_gram[...] = gram(na[...].reshape(4 * NOISE, 1024), ca[...].reshape(4 * CLEAN_ROWS, 1024))
    own_half = pl.ds(pl.multiple_of(c * 352, 8), 352)
    other_half = pl.ds(pl.multiple_of((1 - c) * 352, 8), 352)
    swap = copy(part_gram.at[other_half], d2, d_s.at[0], d_r.at[0], partner)
    swap.start()
    r_ay.forward()


    def turn_a(k):
        def step(q, carry):
            span = pl.ds(pl.multiple_of(q * LANES, LANES), LANES)
            ata[2 * c + k, span, :] = ao[q, 2 * c + k].reshape(4 * NOISE, LANES).T
            return carry

        lax.fori_loop(0, 4, step, 0)

    gap = jnp.zeros((32, LANES), BF16)

    def turn_b(v):
        def step(q, carry):
            span = pl.ds(pl.multiple_of(q * LANES, LANES), LANES)
            tokens = jnp.concatenate([ao[q, 2 * c, v], ao[q, 2 * c + 1, v], gap], axis=0)
            atb[c, v, span, :] = tokens.T
            return carry

        lax.fori_loop(0, 4, step, 0)

    turned = [copy(ata.at[here], ata.at[here], k_s.at[0], k_r.at[0], partner),
              copy(atb.at[c], atb.at[c], k_s.at[1], k_r.at[1], partner)]
    swap.wait_recv()
    sm[...] = part_gram[own_half] + d2[...]
    up, down, across = mod4(x + 1), mod4(x + 3), mod4(x + 2)
    dev_up, dev_down = (z, y, 2 * up + c), (z, y, 2 * down + c)
    first = pl.ds(pl.multiple_of(across * SEG, 8), 48)
    second = pl.ds(pl.multiple_of(across * SEG + 48, 8), 40)
    share = [copy(sm.at[first], near_a, m_s.at[0], m_r.at[0], dev_up),
             copy(sm.at[second], near_b, m_s.at[1], m_r.at[1], dev_down),
             copy(sm.at[rows_of(up)], x3.at[0], m_s.at[2], m_r.at[2], dev_up),
             copy(sm.at[rows_of(down)], x3.at[1], m_s.at[3], m_r.at[3], dev_down)]
    share[0].start()
    share[1].start()
    r_ao.forward()
    share[0].wait_recv()
    sm[pl.ds(pl.multiple_of(up * SEG, 8), 48)] += near_a[...]
    share[2].start()
    share[1].wait_recv()
    sm[pl.ds(pl.multiple_of(down * SEG + 48, 8), 40)] += near_b[...]
    share[3].start()
    r_bz.forward()

    share[2].wait_recv()
    share[3].wait_recv()
    full[rows_of(4 * c + x)] = sm[rows_of(x)] + x3[0] + x3[1]
    r_full.start()
    r_by[0].forward()
    r_by[3].start()
    r_az[3].start()
    r_full.forward()
    r_full.finish()
    give = copy(full.at[own_half], full.at[own_half], d_s.at[1], d_r.at[1], partner)
    give.start()
    r_cg.finish()
    r_ay.finish()
    grad_gram[...] = gram(ga[z].reshape(4 * NOISE, WA), cg[:, :, :WA].reshape(4 * CLEAN_ROWS, WA))
    r_ao.finish()
    turn_a(0)
    turn_a(1)
    turned[0].start()

    r_by[0].finish()
    grad_gram[...] += gram(gb[:, z].reshape(4 * NOISE, WB), cg[:, :, WA:].reshape(4 * CLEAN_ROWS, WB))
    copy(full.at[other_half], full.at[other_half], d_s.at[1], d_r.at[1], partner).wait_recv()

    def row_dot(j):
        terms = [grad_gram[g * SEG:(g + 1) * SEG] * full[g * SEG:(g + 1) * SEG] for g in range(j, 8, 2)]
        rows_sum = jnp.sum(terms[0] + terms[1] + terms[2] + terms[3], axis=0, keepdims=True)
        return jnp.broadcast_to(jnp.sum(rows_sum, axis=1, keepdims=True), (8, LANES))

    place = lax.broadcasted_iota(jnp.int32, (8, LANES), 0)
    tile = jnp.where(place == 2 * z, row_dot(0), jnp.where(place == 2 * z + 1, row_dot(1), 0.0))

    sends = []

    def send_tile(buf, value, me, n, dev, base):
        buf[me] = value
        for r in range(1, n):
            out = copy(buf.at[me], buf.at[me], v_s.at[base + r], v_r.at[base + r], dev(r))
            out.start()
            sends.append(out)

    def sum_tiles(buf, me, n, base):
        for r in range(1, n):
            origin = buf.at[lax.rem(me + n - r, n)]
            copy(origin, origin, v_s.at[base + r], v_r.at[base + r], partner).wait_recv()
        return jnp.sum(buf[...], axis=0)

    send_tile(sv1, tile, t, 8, lambda r: (z, y, lax.rem(t + r, 8)), 0)

    r_az[0].forward()
    tile = sum_tiles(sv1, t, 8, 0)
    send_tile(sv2, tile, 4 * z + y, 16, cell, 8)
    r_by[1].start()
    r_az[1].start()
    r_az[2].start()
    r_bz.finish()
    r_by[2].start()
    for v in range(4):
        turn_b(v)
    turned[1].start()
    r_az[3].forward()
    r_by[3].forward()
    tile = sum_tiles(sv2, 4 * z + y, 16, 8)
    weights = jnp.maximum(-tile, 0.0) / jnp.sum(jnp.abs(tile), axis=0, keepdims=True)
    wts[...] = weights
    lane = lax.broadcasted_iota(jnp.int32, (1, LANES), 1)
    wout_ref[...] = jnp.where(lane == 0, wts[pl.ds(2 * z, 1), :], wts[pl.ds(2 * z + 1, 1), :])[:, :2]

    copy(ata.at[there], ata.at[there], k_s.at[0], k_r.at[0], partner).wait_recv()
    copy(atb.at[1 - c], atb.at[1 - c], k_s.at[1], k_r.at[1], partner).wait_recv()

    def scaled(rows_in, k):
        width = rows_in.shape[1]

        def part(j):
            row = wts[pl.ds(2 * k + j, 1), :]
            factor = jnp.broadcast_to(jnp.concatenate([row] * (width // LANES), axis=1), (SEG, width))
            return rows_in[j * SEG:(j + 1) * SEG] * factor

        return jnp.concatenate([part(0), part(1)], axis=0).astype(BF16)

    def product(left_of, right_of, width, base, first, span):
        def step(i, carry):
            cols = pl.ds(pl.multiple_of(i * span, span), span)
            dest = pl.ds(pl.multiple_of(base + i * span, 256), span)
            value = jnp.dot(left_of(), right_of(cols), preferred_element_type=F32)
            if first:
                out_ref[:, dest] = value
            else:
                out_ref[:, dest] += value
            return carry

        lax.fori_loop(0, width // span, step, 0)

    def add_a(k, first=False):
        v = mod4(z + k)

        def right_of(cols):
            return jnp.concatenate([scaled(ga[v, i, :, cols].astype(F32), v) for i in range(4)], axis=0)

        product(lambda: ata[v], right_of, WA, 0, first, 768)

    def add_b(k, first=False):
        v = mod4(y + k)

        def right_of(cols):
            parts = [scaled(gb[v, i, :, cols].astype(F32), i) for i in range(4)]
            empty = jnp.zeros((32, 512), BF16)
            return jnp.concatenate([parts[0], parts[1], empty, parts[2], parts[3], empty], axis=0)

        product(lambda: jnp.concatenate([atb[0, v], atb[1, v]], axis=1), right_of, WB, WA, first, 512)

    add_a(0, True)
    r_az[1].forward()
    r_by[1].forward()
    add_b(0, True)
    r_az[2].forward()
    add_a(3)
    r_by[2].forward()
    add_a(1)
    add_b(3)
    add_b(1)
    for k in (0, 3, 1, 2):
        r_az[k].finish()
    add_a(2)
    for k in (3, 1, 2):
        r_by[k].finish()
    add_b(2)

    for far_copy, _, same in pieces:
        @pl.when(jnp.logical_not(same))
        def _():
            far_copy.wait_send()
    for ring in rings:
        ring.drain()
    for k in turned + [swap, give] + share + sends:
        k.wait_send()


def body(activations, cotangents, row_ids, row_counts):
    dma = pltpu.SemaphoreType.DMA
    vmem = pltpu.VMEM
    return pl.pallas_call(
        body_kernel,
        out_shape=(pltpu.VMEM((512, WA + WB), F32), pltpu.VMEM((1, 2), F32)),
        in_specs=[pl.BlockSpec(memory_space=pltpu.SMEM)] * 2 + [pl.BlockSpec(memory_space=pltpu.VMEM)] * 2,
        out_specs=(pl.BlockSpec(memory_space=pltpu.VMEM), pl.BlockSpec(memory_space=pltpu.VMEM)),
        scratch_shapes=[
            vmem((4, NOISE, 1024), BF16),
            vmem((4, CLEAN_ROWS, 1024), BF16),
            vmem((4, CLEAN_ROWS, WA + WB), BF16),
            vmem((4, 4, NOISE, WA), BF16),
            vmem((4, 4, NOISE, WB), BF16),
            vmem((4, 4, 4, NOISE, LANES), BF16),
            vmem((4, 512, 4 * NOISE), BF16),
            vmem((2, 4, 512, 384), BF16),
            vmem((4 * NOISE, 4 * CLEAN_ROWS), F32),
            vmem((4 * NOISE, 4 * CLEAN_ROWS), F32),
            vmem((4 * NOISE, 4 * CLEAN_ROWS), F32),
            vmem((2 * NOISE, 4 * CLEAN_ROWS), F32),
            vmem((2 * NOISE, 4 * CLEAN_ROWS), F32),
            vmem((48, 4 * CLEAN_ROWS), F32),
            vmem((40, 4 * CLEAN_ROWS), F32),
            vmem((2, SEG, 4 * CLEAN_ROWS), F32),
            vmem((8, 8, LANES), F32),
            vmem((16, 8, LANES), F32),
            vmem((8, LANES), F32),
            dma((15, 4)), dma((15, 4)),
            dma((8,)), dma((8,)), dma,
            dma((2,)), dma((2,)),
            dma((2,)), dma((2,)),
            dma((4,)), dma((4,)),
            dma((24,)), dma((24,)),
        ],
        compiler_params=pltpu.CompilerParams(
            collective_id=0, has_side_effects=True, vmem_limit_bytes=60 * 1024 * 1024),
        cost_estimate=pl.CostEstimate(flops=8_000_000_000, bytes_accessed=8_000_000, transcendentals=0),
        name="reweight",
    )(row_ids, row_counts, activations, cotangents)


def solution(mesh):
    placed = (P("dp", "seq", "tensor"), P("dp", "seq", "tensor"), P("dp", None), P("dp", None))
    return jax.shard_map(
        body,
        mesh=mesh,
        in_specs=placed,
        out_specs=(P(("dp", "seq"), "tensor"), P("dp", None)),
        check_vma=False,
    )
```

```python
import jax
import jax.numpy as jnp
from jax import lax
from jax.experimental import pallas as pl
from jax.experimental.pallas import tpu as pltpu
from jax.sharding import PartitionSpec as P

MESH = pl.DeviceIdType.MESH
F32 = jnp.float32
BF16 = jnp.bfloat16

SEG = 88
NOISE = 176
CLEAN_ROWS = 88
HALF = 896
WA = 768
WB = 1024
LANES = 128


def body_kernel(ids_ref, counts_ref, acts_ref, cot_ref, out_ref, wout_ref,
                na, ca, cg, left, right, ga, gb, ao, ata, atb, part_gram, grad_gram, full, d2, sm,
                near_a, near_b, x3, sv1, sv2, wts,
                ring_s, ring_r, p_s, p_r, p_l, k_s, k_r,
                d_s, d_r, m_s, m_r, v_s, v_r):
    z = lax.axis_index("dp")
    y = lax.axis_index("seq")
    t = lax.axis_index("tensor")
    x = t // 2
    c = lax.rem(t, 2)

    def mod4(v):
        return lax.rem(v, 4)

    def copy(src, dst, s, r, dev):
        return pltpu.make_async_remote_copy(
            src_ref=src, dst_ref=dst, send_sem=s, recv_sem=r, device_id=dev, device_id_type=MESH)

    barrier = pltpu.get_barrier_semaphore()

    def greet(dev):
        pl.semaphore_signal(barrier, inc=1, device_id=dev, device_id_type=MESH)

    def cell(r):
        other = lax.rem(4 * z + y + r, 16)
        return other // 4, lax.rem(other, 4), t

    for r in range(1, 16):
        greet(cell(r))
    for r in range(1, 8):
        greet((z, y, lax.rem(t + r, 8)))

    active = c == y // 2
    targets = [(x, y, 2 * q + z // 2) for q in range(4)]
    target_self = [active & (x == z) & (q == x) & (c == z // 2) for q in range(4)]
    sources = [(2 * c + i // 4, i % 4) for i in range(8)]
    source_self = [(zs == z) & (x == z) & active for zs, _ in sources]
    for dev, same in zip(targets, target_self):
        @pl.when(active & jnp.logical_not(same))
        def _():
            greet(dev)
    for i in (0, 4):
        @pl.when(jnp.logical_not(source_self[i]))
        def _():
            greet((sources[i][0], y, 2 * z + y // 2))
    sends_here = active.astype(jnp.int32)
    has_self = (active & (x == z) & (c == z // 2)).astype(jnp.int32)

    rid = [ids_ref[0, j] for j in range(3)]
    live = [counts_ref[0, rid[j]] - y * SEG for j in range(3)]
    rows = lax.broadcasted_iota(jnp.int32, (SEG, LANES), 0)

    def block_of(i, base=0):
        return pl.ds(pl.multiple_of(base + i * LANES, LANES), LANES)

    def stage_acts(i, carry):
        cols = block_of(i)
        part = [acts_ref[rid[j], :, cols].astype(F32) for j in (1, 2)]
        na[y, :, cols] = jnp.concatenate(part, axis=0).astype(BF16)
        return carry

    def stage_clean_acts(i, carry):
        part = [acts_ref[rid[0], :, block_of(i, base)].astype(F32) for base in (0, 512)]
        ca[z, :, block_of(i)] = jnp.concatenate(part, axis=0).astype(BF16)
        return carry

    lax.fori_loop(0, 1024 // LANES, stage_acts, 0)
    lax.fori_loop(0, 512 // LANES, stage_clean_acts, 0)

    def masked(j, cols):
        return jnp.where(rows < live[j], cot_ref[rid[j], :, cols].astype(F32), 0.0)

    def stage_clean(i, carry):
        part = [masked(0, block_of(i, base)) for base in (0, HALF)]
        cg[z, :, block_of(i)] = jnp.concatenate(part, axis=0).astype(BF16)
        return carry

    def stage_a(i, carry):
        cols = pl.ds(pl.multiple_of(i * LANES, LANES), LANES)
        ga[z, y, :, cols] = jnp.concatenate([masked(1, cols), masked(2, cols)], axis=0).astype(BF16)
        return carry

    def stage_b(i, carry):
        cols = pl.ds(pl.multiple_of(i * LANES, LANES), LANES)
        from_cols = pl.ds(pl.multiple_of(WA + i * LANES, LANES), LANES)
        gb[y, z, :, cols] = jnp.concatenate(
            [masked(1, from_cols), masked(2, from_cols)], axis=0).astype(BF16)
        return carry

    pl.semaphore_wait(barrier, 24 + 4 * sends_here - 2 * has_self)

    pieces = []

    def send_cell(k):
        ys = mod4(y + k)
        for q in range(4):
            start = lax.rem(y, 2) * 512 + q * LANES
            src = na.at[ys, :, pl.ds(pl.multiple_of(start, LANES), LANES)]
            dst = ao.at[q, z, ys]
            same = target_self[q]
            goes = active & jnp.logical_not(same)
            far_copy = copy(src, dst, p_s.at[k, q], p_r.at[lax.rem(z, 2) * 4 + ys], targets[q])
            near_copy = pltpu.make_async_copy(src, dst, p_l.at[ys])

            @pl.when(same)
            def _():
                near_copy.start()

            @pl.when(goes)
            def _():
                far_copy.start()
            pieces.append((far_copy, goes))

    def wait_pieces():
        for i, ((zs, ys), same) in enumerate(zip(sources, source_self)):
            dst = ao.at[x, zs, ys]
            far_copy = copy(dst, dst, p_s.at[0, 0], p_r.at[i], (z, y, lax.rem(t + 1, 8)))
            near_copy = pltpu.make_async_copy(dst, dst, p_l.at[ys])

            @pl.when(same)
            def _():
                near_copy.wait()

            @pl.when(jnp.logical_not(same))
            def _():
                far_copy.wait_recv()

    rings = []

    class Ring:
        def __init__(self, at, axis, first, second):
            n = len(rings)
            rings.append(self)
            me = {"x": x, "y": y, "z": z}[axis]

            def dev(v):
                return {"x": (z, y, 2 * v + c), "y": (z, v, t), "z": (v, y, t)}[axis]

            up, down, far = mod4(me + 1), mod4(me + 3), mod4(me + 2)
            own, low, high, opp = at(me), at(down), at(up), at(far)
            self.go = [copy(own, own, ring_s.at[n, 0], ring_r.at[n, 0], dev(up)),
                       copy(own, own, ring_s.at[n, 1], ring_r.at[n, 1], dev(down))]
            self.got = [copy(low, low, ring_s.at[n, 0], ring_r.at[n, 0], dev(up)),
                        copy(high, high, ring_s.at[n, 1], ring_r.at[n, 1], dev(down))]
            self.pass_on = [
                copy(low.at[first], low.at[first], ring_s.at[n, 2], ring_r.at[n, 2], dev(up)),
                copy(high.at[second], high.at[second], ring_s.at[n, 3], ring_r.at[n, 3], dev(down))]
            self.got_far = [
                copy(opp.at[first], opp.at[first], ring_s.at[n, 2], ring_r.at[n, 2], dev(up)),
                copy(opp.at[second], opp.at[second], ring_s.at[n, 3], ring_r.at[n, 3], dev(down))]

        def start(self):
            for k in self.go:
                k.start()

        def forward(self):
            for k in range(2):
                self.got[k].wait_recv()
                self.pass_on[k].start()

        def finish(self):
            for k in self.got_far:
                k.wait_recv()

        def drain(self):
            for k in self.go + self.pass_on:
                k.wait_send()

    more_up = (pl.ds(0, 96),), (pl.ds(96, 80),)
    more_down = (pl.ds(0, 80),), (pl.ds(80, 96),)

    def az_ring(k):
        item = mod4(y + k)
        return Ring(lambda v: ga.at[v, item], "z", *(more_up if k in (0, 1) else more_down))

    def by_ring(k):
        item = mod4(z + k)
        return Ring(lambda v: gb.at[v, item], "y", *(more_up if k in (0, 1) else more_down))

    def rows_of(chunk):
        return pl.ds(pl.multiple_of(chunk * SEG, 8), SEG)

    r_na = Ring(lambda v: na.at[v], "y", *more_up)
    r_ca = Ring(lambda v: ca.at[v], "z", *more_up)
    r_cg = Ring(lambda v: cg.at[v], "z", *more_down)
    r_ay = Ring(lambda v: ga.at[z, v], "y", *more_down)
    r_bz = Ring(lambda v: gb.at[y, v], "z", *more_down)
    r_az = {k: az_ring(k) for k in (0, 3, 1, 2)}
    r_by = {k: by_ring(k) for k in (0, 3, 1, 2)}
    here = pl.ds(2 * c, 2)
    there = pl.ds(2 * (1 - c), 2)
    r_ao = Ring(lambda v: ao.at[v, here], "x", (pl.ds(0, 1),), (pl.ds(1, 1),))
    r_full = Ring(lambda v: full.at[rows_of(4 * c + v)], "x", (pl.ds(0, 48),), (pl.ds(48, 40),))

    r_na.start()
    r_ca.start()
    send_cell(0)
    lax.fori_loop(0, WA // LANES, stage_a, 0)
    lax.fori_loop(0, HALF // LANES, stage_clean, 0)
    r_cg.start()
    lax.fori_loop(0, WB // LANES, stage_b, 0)

    partner = (z, y, 2 * x + 1 - c)
    r_ca.forward()
    r_na.forward()
    r_ay.start()
    r_by[0].start()
    r_bz.start()
    send_cell(3)
    send_cell(1)

    def gram(left, right):
        return lax.dot_general(left, right, (((1,), (1,)), ((), ())), preferred_element_type=F32)

    def unpack(ref, half):
        part = [ref[v].astype(F32)[half * SEG:(half + 1) * SEG] for v in range(4)]
        return jnp.concatenate(part, axis=0).astype(BF16)

    r_na.finish()
    r_ca.finish()
    part_gram[...] = gram(na[:, :, :512].reshape(4 * NOISE, 512), unpack(ca, 0)) + gram(
        na[:, :, 512:].reshape(4 * NOISE, 512), unpack(ca, 1))
    own_half = pl.ds(pl.multiple_of(c * 352, 8), 352)
    other_half = pl.ds(pl.multiple_of((1 - c) * 352, 8), 352)
    swap = copy(part_gram.at[other_half], d2, d_s.at[0], d_r.at[0], partner)
    swap.start()
    send_cell(2)

    def turn_a(k):
        def step(q, carry):
            span = pl.ds(pl.multiple_of(q * LANES, LANES), LANES)
            ata[2 * c + k, span, :] = ao[q, 2 * c + k].reshape(4 * NOISE, LANES).T
            return carry

        lax.fori_loop(0, 4, step, 0)

    gap = jnp.zeros((32, LANES), BF16)

    def turn_b(v):
        def step(q, carry):
            span = pl.ds(pl.multiple_of(q * LANES, LANES), LANES)
            tokens = jnp.concatenate([ao[q, 2 * c, v], ao[q, 2 * c + 1, v], gap], axis=0)
            atb[c, v, span, :] = tokens.T
            return carry

        lax.fori_loop(0, 4, step, 0)

    turned = [copy(ata.at[here], ata.at[here], k_s.at[0], k_r.at[0], partner),
              copy(atb.at[c], atb.at[c], k_s.at[1], k_r.at[1], partner)]

    swap.wait_recv()
    sm[...] = part_gram[own_half] + d2[...]
    up, down, across = mod4(x + 1), mod4(x + 3), mod4(x + 2)
    dev_up, dev_down = (z, y, 2 * up + c), (z, y, 2 * down + c)
    first = pl.ds(pl.multiple_of(across * SEG, 8), 48)
    second = pl.ds(pl.multiple_of(across * SEG + 48, 8), 40)
    share = [copy(sm.at[first], near_a, m_s.at[0], m_r.at[0], dev_up),
             copy(sm.at[second], near_b, m_s.at[1], m_r.at[1], dev_down),
             copy(sm.at[rows_of(up)], x3.at[0], m_s.at[2], m_r.at[2], dev_up),
             copy(sm.at[rows_of(down)], x3.at[1], m_s.at[3], m_r.at[3], dev_down)]
    share[0].start()
    share[1].start()
    r_ay.forward()
    r_cg.forward()
    share[0].wait_recv()
    sm[pl.ds(pl.multiple_of(up * SEG, 8), 48)] += near_a[...]
    share[2].start()
    share[1].wait_recv()
    sm[pl.ds(pl.multiple_of(down * SEG + 48, 8), 40)] += near_b[...]
    share[3].start()
    r_bz.forward()
    r_az[0].start()
    r_az[3].start()
    wait_pieces()
    r_ao.start()
    r_by[0].forward()
    r_by[3].start()
    r_by[1].start()
    r_az[1].start()

    share[2].wait_recv()
    share[3].wait_recv()
    full[rows_of(4 * c + x)] = sm[rows_of(x)] + x3[0] + x3[1]
    r_full.start()
    r_cg.finish()
    r_ay.finish()
    r_az[2].start()
    r_full.forward()
    left[...] = unpack(cg, 0)
    right[...] = unpack(cg, 1)
    grad_gram[...] = gram(ga[z].reshape(4 * NOISE, WA), left[:, :WA])
    r_ao.forward()
    r_full.finish()
    give = copy(full.at[own_half], full.at[own_half], d_s.at[1], d_r.at[1], partner)
    give.start()
    r_bz.finish()
    r_by[2].start()

    r_by[0].finish()
    grad_gram[...] += gram(gb[:, z, :, :HALF - WA].reshape(4 * NOISE, HALF - WA), left[:, WA:]) + gram(
        gb[:, z, :, HALF - WA:].reshape(4 * NOISE, HALF), right[...])
    copy(full.at[other_half], full.at[other_half], d_s.at[1], d_r.at[1], partner).wait_recv()

    def row_dot(j):
        terms = [grad_gram[g * SEG:(g + 1) * SEG] * full[g * SEG:(g + 1) * SEG] for g in range(j, 8, 2)]
        rows_sum = jnp.sum(terms[0] + terms[1] + terms[2] + terms[3], axis=0, keepdims=True)
        return jnp.broadcast_to(jnp.sum(rows_sum, axis=1, keepdims=True), (8, LANES))

    place = lax.broadcasted_iota(jnp.int32, (8, LANES), 0)
    tile = jnp.where(place == 2 * z, row_dot(0), jnp.where(place == 2 * z + 1, row_dot(1), 0.0))

    sends = []

    def send_tile(buf, value, me, n, dev, base):
        buf[me] = value
        for r in range(1, n):
            out = copy(buf.at[me], buf.at[me], v_s.at[base + r], v_r.at[base + r], dev(r))
            out.start()
            sends.append(out)

    def sum_tiles(buf, me, n, base):
        for r in range(1, n):
            origin = buf.at[lax.rem(me + n - r, n)]
            copy(origin, origin, v_s.at[base + r], v_r.at[base + r], partner).wait_recv()
        return jnp.sum(buf[...], axis=0)

    send_tile(sv1, tile, t, 8, lambda r: (z, y, lax.rem(t + r, 8)), 0)

    r_ao.finish()
    turn_a(0)
    turn_a(1)
    turned[0].start()
    tile = sum_tiles(sv1, t, 8, 0)
    send_tile(sv2, tile, 4 * z + y, 16, cell, 8)
    r_az[0].forward()
    for v in range(4):
        turn_b(v)
    turned[1].start()
    r_az[3].forward()
    r_by[3].forward()
    r_az[1].forward()
    r_by[1].forward()
    tile = sum_tiles(sv2, 4 * z + y, 16, 8)
    weights = jnp.maximum(-tile, 0.0) / jnp.sum(jnp.abs(tile), axis=0, keepdims=True)
    wts[...] = weights
    lane = lax.broadcasted_iota(jnp.int32, (1, LANES), 1)
    wout_ref[...] = jnp.where(lane == 0, wts[pl.ds(2 * z, 1), :], wts[pl.ds(2 * z + 1, 1), :])[:, :2]

    copy(ata.at[there], ata.at[there], k_s.at[0], k_r.at[0], partner).wait_recv()
    copy(atb.at[1 - c], atb.at[1 - c], k_s.at[1], k_r.at[1], partner).wait_recv()

    def scaled(rows_in, k):
        width = rows_in.shape[1]

        def part(j):
            row = wts[pl.ds(2 * k + j, 1), :]
            factor = jnp.broadcast_to(jnp.concatenate([row] * (width // LANES), axis=1), (SEG, width))
            return rows_in[j * SEG:(j + 1) * SEG] * factor

        return jnp.concatenate([part(0), part(1)], axis=0).astype(BF16)

    def product(left_of, right_of, width, base, first, span):
        def step(i, carry):
            cols = pl.ds(pl.multiple_of(i * span, span), span)
            dest = pl.ds(pl.multiple_of(base + i * span, 256), span)
            value = jnp.dot(left_of(), right_of(cols), preferred_element_type=F32)
            if first:
                out_ref[:, dest] = value
            else:
                out_ref[:, dest] += value
            return carry

        lax.fori_loop(0, width // span, step, 0)

    def add_a(k, first=False):
        v = mod4(z + k)

        def right_of(cols):
            return jnp.concatenate([scaled(ga[v, i, :, cols].astype(F32), v) for i in range(4)], axis=0)

        product(lambda: ata[v], right_of, WA, 0, first, 768)

    def add_b(k, first=False):
        v = mod4(y + k)

        def right_of(cols):
            parts = [scaled(gb[v, i, :, cols].astype(F32), i) for i in range(4)]
            empty = jnp.zeros((32, 512), BF16)
            return jnp.concatenate([parts[0], parts[1], empty, parts[2], parts[3], empty], axis=0)

        product(lambda: jnp.concatenate([atb[0, v], atb[1, v]], axis=1), right_of, WB, WA, first, 512)

    add_a(0, True)
    add_b(0, True)
    r_az[2].forward()
    r_by[2].forward()
    add_a(3)
    add_a(1)
    add_b(3)
    add_b(1)
    for k in (0, 3, 1, 2):
        r_az[k].finish()
    add_a(2)
    for k in (3, 1, 2):
        r_by[k].finish()
    add_b(2)

    for far_copy, goes in pieces:
        @pl.when(goes)
        def _():
            far_copy.wait_send()
    for ring in rings:
        ring.drain()
    for k in turned + [swap, give] + share + sends:
        k.wait_send()


def body(activations, cotangents, row_ids, row_counts):
    dma = pltpu.SemaphoreType.DMA
    vmem = pltpu.VMEM
    return pl.pallas_call(
        body_kernel,
        out_shape=(pltpu.VMEM((512, WA + WB), F32), pltpu.VMEM((1, 2), F32)),
        in_specs=[pl.BlockSpec(memory_space=pltpu.SMEM)] * 2 + [pl.BlockSpec(memory_space=pltpu.VMEM)] * 2,
        out_specs=(pl.BlockSpec(memory_space=pltpu.VMEM), pl.BlockSpec(memory_space=pltpu.VMEM)),
        scratch_shapes=[
            vmem((4, NOISE, 1024), BF16),
            vmem((4, NOISE, 512), BF16),
            vmem((4, NOISE, HALF), BF16),
            vmem((4 * SEG, HALF), BF16),
            vmem((4 * SEG, HALF), BF16),
            vmem((4, 4, NOISE, WA), BF16),
            vmem((4, 4, NOISE, WB), BF16),
            vmem((4, 4, 4, NOISE, LANES), BF16),
            vmem((4, 512, 4 * NOISE), BF16),
            vmem((2, 4, 512, 384), BF16),
            vmem((4 * NOISE, 4 * CLEAN_ROWS), F32),
            vmem((4 * NOISE, 4 * CLEAN_ROWS), F32),
            vmem((4 * NOISE, 4 * CLEAN_ROWS), F32),
            vmem((2 * NOISE, 4 * CLEAN_ROWS), F32),
            vmem((2 * NOISE, 4 * CLEAN_ROWS), F32),
            vmem((48, 4 * CLEAN_ROWS), F32),
            vmem((40, 4 * CLEAN_ROWS), F32),
            vmem((2, SEG, 4 * CLEAN_ROWS), F32),
            vmem((8, 8, LANES), F32),
            vmem((16, 8, LANES), F32),
            vmem((8, LANES), F32),
            dma((15, 4)), dma((15, 4)),
            dma((4, 4)), dma((8,)), dma((4,)),
            dma((2,)), dma((2,)),
            dma((2,)), dma((2,)),
            dma((4,)), dma((4,)),
            dma((24,)), dma((24,)),
        ],
        compiler_params=pltpu.CompilerParams(
            collective_id=0, has_side_effects=True, vmem_limit_bytes=60 * 1024 * 1024),
        cost_estimate=pl.CostEstimate(flops=8_000_000_000, bytes_accessed=8_000_000, transcendentals=0),
        name="reweight",
    )(row_ids, row_counts, activations, cotangents)


def solution(mesh):
    placed = (P("dp", "seq", "tensor"), P("dp", "seq", "tensor"), P("dp", None), P("dp", None))
    return jax.shard_map(
        body,
        mesh=mesh,
        in_specs=placed,
        out_specs=(P(("dp", "seq"), "tensor"), P("dp", None)),
        check_vma=False,
    )
```

```python
import jax
import jax.numpy as jnp
from jax import lax
from jax.experimental import pallas as pl
from jax.experimental.pallas import tpu as pltpu
from jax.sharding import PartitionSpec as P

MESH = pl.DeviceIdType.MESH
F32 = jnp.float32
BF16 = jnp.bfloat16

SEG = 88
NOISE = 176
CLEAN_ROWS = 88
HALF = 896
WA = 768
WB = 1024
LANES = 128


def body_kernel(ids_ref, counts_ref, acts_ref, cot_ref, out_ref, wout_ref,
                na, ca, cg, left, right, ga, gb, ao, ata, atb, part_gram, grad_gram, full, d2, sm,
                near_a, near_b, x3, sv1, sv2, wts,
                ring_s, ring_r, p_s, p_r, p_l, k_s, k_r,
                d_s, d_r, m_s, m_r, v_s, v_r):
    z = lax.axis_index("dp")
    y = lax.axis_index("seq")
    t = lax.axis_index("tensor")
    x = t // 2
    c = lax.rem(t, 2)

    def mod4(v):
        return lax.rem(v, 4)

    def copy(src, dst, s, r, dev):
        return pltpu.make_async_remote_copy(
            src_ref=src, dst_ref=dst, send_sem=s, recv_sem=r, device_id=dev, device_id_type=MESH)

    barrier = pltpu.get_barrier_semaphore()

    def greet(dev):
        pl.semaphore_signal(barrier, inc=1, device_id=dev, device_id_type=MESH)

    def cell(r):
        other = lax.rem(4 * z + y + r, 16)
        return other // 4, lax.rem(other, 4), t

    for r in range(1, 16):
        greet(cell(r))
    for r in range(1, 8):
        greet((z, y, lax.rem(t + r, 8)))

    active = c == y // 2
    targets = [(x, y, 2 * q + z // 2) for q in range(4)]
    target_self = [active & (x == z) & (q == x) & (c == z // 2) for q in range(4)]
    sources = [(2 * c + i // 4, i % 4) for i in range(8)]
    source_self = [(zs == z) & (x == z) & active for zs, _ in sources]
    for dev, same in zip(targets, target_self):
        @pl.when(active & jnp.logical_not(same))
        def _():
            greet(dev)
    for i in (0, 4):
        @pl.when(jnp.logical_not(source_self[i]))
        def _():
            greet((sources[i][0], y, 2 * z + y // 2))
    sends_here = active.astype(jnp.int32)
    has_self = (active & (x == z) & (c == z // 2)).astype(jnp.int32)

    rid = [ids_ref[0, j] for j in range(3)]
    live = [counts_ref[0, rid[j]] - y * SEG for j in range(3)]
    rows = lax.broadcasted_iota(jnp.int32, (SEG, LANES), 0)

    def block_of(i, base=0):
        return pl.ds(pl.multiple_of(base + i * LANES, LANES), LANES)

    def stage_acts(i, carry):
        cols = block_of(i)
        part = [acts_ref[rid[j], :, cols].astype(F32) for j in (1, 2)]
        na[y, :, cols] = jnp.concatenate(part, axis=0).astype(BF16)
        return carry

    def stage_clean_acts(i, carry):
        part = [acts_ref[rid[0], :, block_of(i, base)].astype(F32) for base in (0, 512)]
        ca[z, :, block_of(i)] = jnp.concatenate(part, axis=0).astype(BF16)
        return carry

    lax.fori_loop(0, 1024 // LANES, stage_acts, 0)
    lax.fori_loop(0, 512 // LANES, stage_clean_acts, 0)

    def masked(j, cols):
        return jnp.where(rows < live[j], cot_ref[rid[j], :, cols].astype(F32), 0.0)

    def stage_clean(i, carry):
        part = [masked(0, block_of(i, base)) for base in (0, HALF)]
        cg[z, :, block_of(i)] = jnp.concatenate(part, axis=0).astype(BF16)
        return carry

    def stage_a(i, carry):
        cols = pl.ds(pl.multiple_of(i * LANES, LANES), LANES)
        ga[z, y, :, cols] = jnp.concatenate([masked(1, cols), masked(2, cols)], axis=0).astype(BF16)
        return carry

    def stage_b(i, carry):
        cols = pl.ds(pl.multiple_of(i * LANES, LANES), LANES)
        from_cols = pl.ds(pl.multiple_of(WA + i * LANES, LANES), LANES)
        gb[y, z, :, cols] = jnp.concatenate(
            [masked(1, from_cols), masked(2, from_cols)], axis=0).astype(BF16)
        return carry

    pl.semaphore_wait(barrier, 24 + 4 * sends_here - 2 * has_self)

    pieces = []

    def send_cell(k):
        ys = mod4(y + k)
        for q in range(4):
            start = lax.rem(y, 2) * 512 + q * LANES
            src = na.at[ys, :, pl.ds(pl.multiple_of(start, LANES), LANES)]
            dst = ao.at[q, z, ys]
            same = target_self[q]
            goes = active & jnp.logical_not(same)
            far_copy = copy(src, dst, p_s.at[k, q], p_r.at[lax.rem(z, 2) * 4 + ys], targets[q])
            near_copy = pltpu.make_async_copy(src, dst, p_l.at[ys])

            @pl.when(same)
            def _():
                near_copy.start()

            @pl.when(goes)
            def _():
                far_copy.start()
            pieces.append((far_copy, goes))

    def wait_pieces():
        for i, ((zs, ys), same) in enumerate(zip(sources, source_self)):
            dst = ao.at[x, zs, ys]
            far_copy = copy(dst, dst, p_s.at[0, 0], p_r.at[i], (z, y, lax.rem(t + 1, 8)))
            near_copy = pltpu.make_async_copy(dst, dst, p_l.at[ys])

            @pl.when(same)
            def _():
                near_copy.wait()

            @pl.when(jnp.logical_not(same))
            def _():
                far_copy.wait_recv()

    rings = []

    class Ring:
        def __init__(self, at, axis, first, second):
            n = len(rings)
            rings.append(self)
            me = {"x": x, "y": y, "z": z}[axis]

            def dev(v):
                return {"x": (z, y, 2 * v + c), "y": (z, v, t), "z": (v, y, t)}[axis]

            up, down, far = mod4(me + 1), mod4(me + 3), mod4(me + 2)
            own, low, high, opp = at(me), at(down), at(up), at(far)
            self.go = [copy(own, own, ring_s.at[n, 0], ring_r.at[n, 0], dev(up)),
                       copy(own, own, ring_s.at[n, 1], ring_r.at[n, 1], dev(down))]
            self.got = [copy(low, low, ring_s.at[n, 0], ring_r.at[n, 0], dev(up)),
                        copy(high, high, ring_s.at[n, 1], ring_r.at[n, 1], dev(down))]
            self.pass_on = [
                copy(low.at[first], low.at[first], ring_s.at[n, 2], ring_r.at[n, 2], dev(up)),
                copy(high.at[second], high.at[second], ring_s.at[n, 3], ring_r.at[n, 3], dev(down))]
            self.got_far = [
                copy(opp.at[first], opp.at[first], ring_s.at[n, 2], ring_r.at[n, 2], dev(up)),
                copy(opp.at[second], opp.at[second], ring_s.at[n, 3], ring_r.at[n, 3], dev(down))]

        def start(self):
            for k in self.go:
                k.start()

        def forward(self):
            for k in range(2):
                self.got[k].wait_recv()
                self.pass_on[k].start()

        def finish(self):
            for k in self.got_far:
                k.wait_recv()

        def drain(self):
            for k in self.go + self.pass_on:
                k.wait_send()

    more_up = (pl.ds(0, 96),), (pl.ds(96, 80),)
    more_down = (pl.ds(0, 80),), (pl.ds(80, 96),)

    def az_ring(k):
        item = mod4(y + k)
        return Ring(lambda v: ga.at[v, item], "z", *(more_up if k in (0, 1) else more_down))

    def by_ring(k):
        item = mod4(z + k)
        return Ring(lambda v: gb.at[v, item], "y", *(more_up if k in (0, 1) else more_down))

    def rows_of(chunk):
        return pl.ds(pl.multiple_of(chunk * SEG, 8), SEG)

    r_na = [Ring(lambda v, h=h: na.at[v, :, pl.ds(h * 512, 512)], "y", *(more_up, more_down)[h]) for h in range(2)]
    r_ca = Ring(lambda v: ca.at[v], "z", *more_up)
    r_cg = Ring(lambda v: cg.at[v], "z", *more_down)
    r_ay = Ring(lambda v: ga.at[z, v], "y", *more_down)
    r_bz = Ring(lambda v: gb.at[y, v], "z", *more_down)
    r_az = {k: az_ring(k) for k in (0, 3, 1, 2)}
    r_by = {k: by_ring(k) for k in (0, 3, 1, 2)}
    here = pl.ds(2 * c, 2)
    there = pl.ds(2 * (1 - c), 2)
    r_ao = Ring(lambda v: ao.at[v, here], "x", (pl.ds(0, 1),), (pl.ds(1, 1),))
    r_full = Ring(lambda v: full.at[rows_of(4 * c + v)], "x", (pl.ds(0, 48),), (pl.ds(48, 40),))

    for ring in r_na:
        ring.start()
    r_ca.start()
    send_cell(0)
    lax.fori_loop(0, WA // LANES, stage_a, 0)
    lax.fori_loop(0, HALF // LANES, stage_clean, 0)
    r_cg.start()
    lax.fori_loop(0, WB // LANES, stage_b, 0)

    partner = (z, y, 2 * x + 1 - c)
    r_ca.forward()
    for ring in r_na:
        ring.forward()
    r_ay.start()
    r_by[0].start()
    r_bz.start()
    send_cell(3)
    send_cell(1)

    def gram(left, right):
        return lax.dot_general(left, right, (((1,), (1,)), ((), ())), preferred_element_type=F32)

    def unpack(ref, half):
        part = [ref[v].astype(F32)[half * SEG:(half + 1) * SEG] for v in range(4)]
        return jnp.concatenate(part, axis=0).astype(BF16)

    for ring in r_na:
        ring.finish()
    r_ca.finish()
    part_gram[...] = gram(na[:, :, :512].reshape(4 * NOISE, 512), unpack(ca, 0)) + gram(
        na[:, :, 512:].reshape(4 * NOISE, 512), unpack(ca, 1))
    own_half = pl.ds(pl.multiple_of(c * 352, 8), 352)
    other_half = pl.ds(pl.multiple_of((1 - c) * 352, 8), 352)
    swap = copy(part_gram.at[other_half], d2, d_s.at[0], d_r.at[0], partner)
    swap.start()
    send_cell(2)

    def turn_a(k):
        def step(q, carry):
            span = pl.ds(pl.multiple_of(q * LANES, LANES), LANES)
            ata[2 * c + k, span, :] = ao[q, 2 * c + k].reshape(4 * NOISE, LANES).T
            return carry

        lax.fori_loop(0, 4, step, 0)

    gap = jnp.zeros((32, LANES), BF16)

    def turn_b(v):
        def step(q, carry):
            span = pl.ds(pl.multiple_of(q * LANES, LANES), LANES)
            tokens = jnp.concatenate([ao[q, 2 * c, v], ao[q, 2 * c + 1, v], gap], axis=0)
            atb[c, v, span, :] = tokens.T
            return carry

        lax.fori_loop(0, 4, step, 0)

    turned = [copy(ata.at[here], ata.at[here], k_s.at[0], k_r.at[0], partner),
              copy(atb.at[c], atb.at[c], k_s.at[1], k_r.at[1], partner)]

    swap.wait_recv()
    sm[...] = part_gram[own_half] + d2[...]
    up, down, across = mod4(x + 1), mod4(x + 3), mod4(x + 2)
    dev_up, dev_down = (z, y, 2 * up + c), (z, y, 2 * down + c)
    first = pl.ds(pl.multiple_of(across * SEG, 8), 48)
    second = pl.ds(pl.multiple_of(across * SEG + 48, 8), 40)
    share = [copy(sm.at[first], near_a, m_s.at[0], m_r.at[0], dev_up),
             copy(sm.at[second], near_b, m_s.at[1], m_r.at[1], dev_down),
             copy(sm.at[rows_of(up)], x3.at[0], m_s.at[2], m_r.at[2], dev_up),
             copy(sm.at[rows_of(down)], x3.at[1], m_s.at[3], m_r.at[3], dev_down)]
    share[0].start()
    share[1].start()
    r_ay.forward()
    r_cg.forward()
    share[0].wait_recv()
    sm[pl.ds(pl.multiple_of(up * SEG, 8), 48)] += near_a[...]
    share[2].start()
    share[1].wait_recv()
    sm[pl.ds(pl.multiple_of(down * SEG + 48, 8), 40)] += near_b[...]
    share[3].start()
    r_bz.forward()
    r_az[0].start()
    r_az[3].start()
    wait_pieces()
    r_ao.start()
    r_by[0].forward()
    r_by[3].start()
    r_by[1].start()
    r_az[1].start()

    share[2].wait_recv()
    share[3].wait_recv()
    full[rows_of(4 * c + x)] = sm[rows_of(x)] + x3[0] + x3[1]
    r_full.start()
    r_cg.finish()
    r_ay.finish()
    r_az[2].start()
    r_full.forward()
    left[...] = unpack(cg, 0)
    right[...] = unpack(cg, 1)
    grad_gram[...] = gram(ga[z].reshape(4 * NOISE, WA), left[:, :WA])
    r_ao.forward()
    r_full.finish()
    give = copy(full.at[own_half], full.at[own_half], d_s.at[1], d_r.at[1], partner)
    give.start()
    r_bz.finish()
    r_by[2].start()

    r_by[0].finish()
    grad_gram[...] += gram(gb[:, z, :, :HALF - WA].reshape(4 * NOISE, HALF - WA), left[:, WA:]) + gram(
        gb[:, z, :, HALF - WA:].reshape(4 * NOISE, HALF), right[...])
    copy(full.at[other_half], full.at[other_half], d_s.at[1], d_r.at[1], partner).wait_recv()

    def row_dot(j):
        terms = [grad_gram[g * SEG:(g + 1) * SEG] * full[g * SEG:(g + 1) * SEG] for g in range(j, 8, 2)]
        rows_sum = jnp.sum(terms[0] + terms[1] + terms[2] + terms[3], axis=0, keepdims=True)
        return jnp.broadcast_to(jnp.sum(rows_sum, axis=1, keepdims=True), (8, LANES))

    place = lax.broadcasted_iota(jnp.int32, (8, LANES), 0)
    tile = jnp.where(place == 2 * z, row_dot(0), jnp.where(place == 2 * z + 1, row_dot(1), 0.0))

    sends = []

    def send_tile(buf, value, me, n, dev, base):
        buf[me] = value
        for r in range(1, n):
            out = copy(buf.at[me], buf.at[me], v_s.at[base + r], v_r.at[base + r], dev(r))
            out.start()
            sends.append(out)

    def sum_tiles(buf, me, n, base):
        for r in range(1, n):
            origin = buf.at[lax.rem(me + n - r, n)]
            copy(origin, origin, v_s.at[base + r], v_r.at[base + r], partner).wait_recv()
        return jnp.sum(buf[...], axis=0)

    send_tile(sv1, tile, t, 8, lambda r: (z, y, lax.rem(t + r, 8)), 0)

    r_ao.finish()
    turn_a(0)
    turn_a(1)
    turned[0].start()
    tile = sum_tiles(sv1, t, 8, 0)
    send_tile(sv2, tile, 4 * z + y, 16, cell, 8)
    r_az[0].forward()
    for v in range(4):
        turn_b(v)
    turned[1].start()
    r_az[3].forward()
    r_by[3].forward()
    r_az[1].forward()
    r_by[1].forward()
    tile = sum_tiles(sv2, 4 * z + y, 16, 8)
    weights = jnp.maximum(-tile, 0.0) / jnp.sum(jnp.abs(tile), axis=0, keepdims=True)
    wts[...] = weights
    lane = lax.broadcasted_iota(jnp.int32, (1, LANES), 1)
    wout_ref[...] = jnp.where(lane == 0, wts[pl.ds(2 * z, 1), :], wts[pl.ds(2 * z + 1, 1), :])[:, :2]

    copy(ata.at[there], ata.at[there], k_s.at[0], k_r.at[0], partner).wait_recv()
    copy(atb.at[1 - c], atb.at[1 - c], k_s.at[1], k_r.at[1], partner).wait_recv()

    def scaled(rows_in, k):
        width = rows_in.shape[1]

        def part(j):
            row = wts[pl.ds(2 * k + j, 1), :]
            factor = jnp.broadcast_to(jnp.concatenate([row] * (width // LANES), axis=1), (SEG, width))
            return rows_in[j * SEG:(j + 1) * SEG] * factor

        return jnp.concatenate([part(0), part(1)], axis=0).astype(BF16)

    def product(left_of, right_of, width, base, first, span):
        def step(i, carry):
            cols = pl.ds(pl.multiple_of(i * span, span), span)
            dest = pl.ds(pl.multiple_of(base + i * span, 256), span)
            value = jnp.dot(left_of(), right_of(cols), preferred_element_type=F32)
            if first:
                out_ref[:, dest] = value
            else:
                out_ref[:, dest] += value
            return carry

        lax.fori_loop(0, width // span, step, 0)

    def add_a(k, first=False):
        v = mod4(z + k)

        def right_of(cols):
            return jnp.concatenate([scaled(ga[v, i, :, cols].astype(F32), v) for i in range(4)], axis=0)

        product(lambda: ata[v], right_of, WA, 0, first, 768)

    def add_b(k, first=False):
        v = mod4(y + k)

        def right_of(cols):
            parts = [scaled(gb[v, i, :, cols].astype(F32), i) for i in range(4)]
            empty = jnp.zeros((32, 512), BF16)
            return jnp.concatenate([parts[0], parts[1], empty, parts[2], parts[3], empty], axis=0)

        product(lambda: jnp.concatenate([atb[0, v], atb[1, v]], axis=1), right_of, WB, WA, first, 512)

    add_a(0, True)
    add_b(0, True)
    r_az[2].forward()
    r_by[2].forward()
    add_a(3)
    add_a(1)
    add_b(3)
    add_b(1)
    for k in (0, 3, 1, 2):
        r_az[k].finish()
    add_a(2)
    for k in (3, 1, 2):
        r_by[k].finish()
    add_b(2)

    for far_copy, goes in pieces:
        @pl.when(goes)
        def _():
            far_copy.wait_send()
    for ring in rings:
        ring.drain()
    for k in turned + [swap, give] + share + sends:
        k.wait_send()


def store_kernel(held_ref, weights_ref, out_ref, wout_ref, sems):
    copies = [pltpu.make_async_copy(held_ref, out_ref, sems.at[0]),
              pltpu.make_async_copy(weights_ref, wout_ref, sems.at[1])]
    for k in copies:
        k.start()
    for k in copies:
        k.wait()


def body(activations, cotangents, row_ids, row_counts):
    dma = pltpu.SemaphoreType.DMA
    vmem = pltpu.VMEM
    held, weights = pl.pallas_call(
        body_kernel,
        out_shape=(pltpu.VMEM((512, WA + WB), F32), pltpu.VMEM((1, 2), F32)),
        in_specs=[pl.BlockSpec(memory_space=pltpu.SMEM)] * 2 + [pl.BlockSpec(memory_space=pltpu.VMEM)] * 2,
        out_specs=(pl.BlockSpec(memory_space=pltpu.VMEM), pl.BlockSpec(memory_space=pltpu.VMEM)),
        scratch_shapes=[
            vmem((4, NOISE, 1024), BF16),
            vmem((4, NOISE, 512), BF16),
            vmem((4, NOISE, HALF), BF16),
            vmem((4 * SEG, HALF), BF16),
            vmem((4 * SEG, HALF), BF16),
            vmem((4, 4, NOISE, WA), BF16),
            vmem((4, 4, NOISE, WB), BF16),
            vmem((4, 4, 4, NOISE, LANES), BF16),
            vmem((4, 512, 4 * NOISE), BF16),
            vmem((2, 4, 512, 384), BF16),
            vmem((4 * NOISE, 4 * CLEAN_ROWS), F32),
            vmem((4 * NOISE, 4 * CLEAN_ROWS), F32),
            vmem((4 * NOISE, 4 * CLEAN_ROWS), F32),
            vmem((2 * NOISE, 4 * CLEAN_ROWS), F32),
            vmem((2 * NOISE, 4 * CLEAN_ROWS), F32),
            vmem((48, 4 * CLEAN_ROWS), F32),
            vmem((40, 4 * CLEAN_ROWS), F32),
            vmem((2, SEG, 4 * CLEAN_ROWS), F32),
            vmem((8, 8, LANES), F32),
            vmem((16, 8, LANES), F32),
            vmem((8, LANES), F32),
            dma((16, 4)), dma((16, 4)),
            dma((4, 4)), dma((8,)), dma((4,)),
            dma((2,)), dma((2,)),
            dma((2,)), dma((2,)),
            dma((4,)), dma((4,)),
            dma((24,)), dma((24,)),
        ],
        compiler_params=pltpu.CompilerParams(
            collective_id=0, has_side_effects=True, vmem_limit_bytes=60 * 1024 * 1024),
        cost_estimate=pl.CostEstimate(flops=8_000_000_000, bytes_accessed=8_000_000, transcendentals=0),
        name="reweight",
    )(row_ids, row_counts, activations, cotangents)
    return pl.pallas_call(
        store_kernel,
        out_shape=(jax.ShapeDtypeStruct((512, WA + WB), F32), jax.ShapeDtypeStruct((1, 2), F32)),
        in_specs=[pl.BlockSpec(memory_space=pltpu.VMEM)] * 2,
        out_specs=(pl.BlockSpec(memory_space=pl.ANY), pl.BlockSpec(memory_space=pl.ANY)),
        scratch_shapes=[dma((2,))],
        name="store",
    )(held, weights)


def solution(mesh):
    placed = (P("dp", "seq", "tensor"), P("dp", "seq", "tensor"), P("dp", None), P("dp", None))
    return jax.shard_map(
        body,
        mesh=mesh,
        in_specs=placed,
        out_specs=(P(("dp", "seq"), "tensor"), P("dp", None)),
        check_vma=False,
    )
```

```python
import jax
import jax.numpy as jnp
from jax import lax
from jax.experimental import pallas as pl
from jax.experimental.pallas import tpu as pltpu
from jax.sharding import PartitionSpec as P

MESH = pl.DeviceIdType.MESH
F32 = jnp.float32
BF16 = jnp.bfloat16

SEG = 88
NOISE = 176
CLEAN_ROWS = 88
HALF = 896
WA = 768
WB = 1024
LANES = 128


def body_kernel(ids_ref, counts_ref, acts_ref, cot_ref, out_ref, wout_ref,
                na, ca, cg, left, right, ga, gb, ao, ata, atb, part_gram, grad_gram, full, d2, sm,
                near_a, near_b, x3, sv1, sv2, wts,
                ring_s, ring_r, p_s, p_r, p_l, k_s, k_r,
                d_s, d_r, m_s, m_r, v_s, v_r):
    z = lax.axis_index("dp")
    y = lax.axis_index("seq")
    t = lax.axis_index("tensor")
    x = t // 2
    c = lax.rem(t, 2)

    def mod4(v):
        return lax.rem(v, 4)

    def copy(src, dst, s, r, dev):
        return pltpu.make_async_remote_copy(
            src_ref=src, dst_ref=dst, send_sem=s, recv_sem=r, device_id=dev, device_id_type=MESH)

    barrier = pltpu.get_barrier_semaphore()

    def greet(dev):
        pl.semaphore_signal(barrier, inc=1, device_id=dev, device_id_type=MESH)

    def cell(r):
        other = lax.rem(4 * z + y + r, 16)
        return other // 4, lax.rem(other, 4), t

    for r in range(1, 16):
        greet(cell(r))
    for r in range(1, 8):
        greet((z, y, lax.rem(t + r, 8)))

    active = c == y // 2
    targets = [(x, y, 2 * q + z // 2) for q in range(4)]
    target_self = [active & (x == z) & (q == x) & (c == z // 2) for q in range(4)]
    sources = [(2 * c + i // 4, i % 4) for i in range(8)]
    source_self = [(zs == z) & (x == z) & active for zs, _ in sources]
    for dev, same in zip(targets, target_self):
        @pl.when(active & jnp.logical_not(same))
        def _():
            greet(dev)
    for i in (0, 4):
        @pl.when(jnp.logical_not(source_self[i]))
        def _():
            greet((sources[i][0], y, 2 * z + y // 2))
    sends_here = active.astype(jnp.int32)
    has_self = (active & (x == z) & (c == z // 2)).astype(jnp.int32)

    rid = [ids_ref[0, j] for j in range(3)]
    live = [counts_ref[0, rid[j]] - y * SEG for j in range(3)]
    rows = lax.broadcasted_iota(jnp.int32, (SEG, LANES), 0)

    def block_of(i, base=0):
        return pl.ds(pl.multiple_of(base + i * LANES, LANES), LANES)

    def stage_acts(i, carry):
        cols = block_of(i)
        part = [acts_ref[rid[j], :, cols].astype(F32) for j in (1, 2)]
        na[y, :, cols] = jnp.concatenate(part, axis=0).astype(BF16)
        return carry

    def stage_clean_acts(i, carry):
        part = [acts_ref[rid[0], :, block_of(i, base)].astype(F32) for base in (0, 512)]
        ca[z, :, block_of(i)] = jnp.concatenate(part, axis=0).astype(BF16)
        return carry

    lax.fori_loop(0, 1024 // LANES, stage_acts, 0)
    lax.fori_loop(0, 512 // LANES, stage_clean_acts, 0)

    def masked(j, cols):
        return jnp.where(rows < live[j], cot_ref[rid[j], :, cols].astype(F32), 0.0)

    def stage_clean(i, carry):
        part = [masked(0, block_of(i, base)) for base in (0, HALF)]
        cg[z, :, block_of(i)] = jnp.concatenate(part, axis=0).astype(BF16)
        return carry

    def stage_a(i, carry):
        cols = pl.ds(pl.multiple_of(i * LANES, LANES), LANES)
        ga[z, y, :, cols] = jnp.concatenate([masked(1, cols), masked(2, cols)], axis=0).astype(BF16)
        return carry

    def stage_b(i, carry):
        cols = pl.ds(pl.multiple_of(i * LANES, LANES), LANES)
        from_cols = pl.ds(pl.multiple_of(WA + i * LANES, LANES), LANES)
        gb[y, z, :, cols] = jnp.concatenate(
            [masked(1, from_cols), masked(2, from_cols)], axis=0).astype(BF16)
        return carry

    pl.semaphore_wait(barrier, 24 + 4 * sends_here - 2 * has_self)

    pieces = []

    def send_cell(k):
        ys = mod4(y + k)
        for q in range(4):
            start = lax.rem(y, 2) * 512 + q * LANES
            src = na.at[ys, :, pl.ds(pl.multiple_of(start, LANES), LANES)]
            dst = ao.at[q, z, ys]
            same = target_self[q]
            goes = active & jnp.logical_not(same)
            far_copy = copy(src, dst, p_s.at[k, q], p_r.at[lax.rem(z, 2) * 4 + ys], targets[q])
            near_copy = pltpu.make_async_copy(src, dst, p_l.at[ys])

            @pl.when(same)
            def _():
                near_copy.start()

            @pl.when(goes)
            def _():
                far_copy.start()
            pieces.append((far_copy, goes))

    def wait_pieces():
        for i, ((zs, ys), same) in enumerate(zip(sources, source_self)):
            dst = ao.at[x, zs, ys]
            far_copy = copy(dst, dst, p_s.at[0, 0], p_r.at[i], (z, y, lax.rem(t + 1, 8)))
            near_copy = pltpu.make_async_copy(dst, dst, p_l.at[ys])

            @pl.when(same)
            def _():
                near_copy.wait()

            @pl.when(jnp.logical_not(same))
            def _():
                far_copy.wait_recv()

    rings = []

    class Ring:
        def __init__(self, at, axis, first, second):
            n = len(rings)
            rings.append(self)
            me = {"x": x, "y": y, "z": z}[axis]

            def dev(v):
                return {"x": (z, y, 2 * v + c), "y": (z, v, t), "z": (v, y, t)}[axis]

            up, down, far = mod4(me + 1), mod4(me + 3), mod4(me + 2)
            own, low, high, opp = at(me), at(down), at(up), at(far)
            self.go = [copy(own, own, ring_s.at[n, 0], ring_r.at[n, 0], dev(up)),
                       copy(own, own, ring_s.at[n, 1], ring_r.at[n, 1], dev(down))]
            self.got = [copy(low, low, ring_s.at[n, 0], ring_r.at[n, 0], dev(up)),
                        copy(high, high, ring_s.at[n, 1], ring_r.at[n, 1], dev(down))]
            self.pass_on = [
                copy(low.at[first], low.at[first], ring_s.at[n, 2], ring_r.at[n, 2], dev(up)),
                copy(high.at[second], high.at[second], ring_s.at[n, 3], ring_r.at[n, 3], dev(down))]
            self.got_far = [
                copy(opp.at[first], opp.at[first], ring_s.at[n, 2], ring_r.at[n, 2], dev(up)),
                copy(opp.at[second], opp.at[second], ring_s.at[n, 3], ring_r.at[n, 3], dev(down))]

        def start(self):
            for k in self.go:
                k.start()

        def forward(self):
            for k in range(2):
                self.got[k].wait_recv()
                self.pass_on[k].start()

        def finish(self):
            for k in self.got_far:
                k.wait_recv()

        def drain(self):
            for k in self.go + self.pass_on:
                k.wait_send()

    more_up = (pl.ds(0, 96),), (pl.ds(96, 80),)
    more_down = (pl.ds(0, 80),), (pl.ds(80, 96),)

    def az_ring(k):
        item = mod4(y + k)
        return Ring(lambda v: ga.at[v, item], "z", *(more_up if k in (0, 1) else more_down))

    def by_ring(k):
        item = mod4(z + k)
        return Ring(lambda v: gb.at[v, item], "y", *(more_up if k in (0, 1) else more_down))

    def rows_of(chunk):
        return pl.ds(pl.multiple_of(chunk * SEG, 8), SEG)

    r_na = [Ring(lambda v, h=h: na.at[v, :, pl.ds(h * 512, 512)], "y", *(more_up, more_down)[h]) for h in range(2)]
    r_ca = Ring(lambda v: ca.at[v], "z", *more_up)
    r_cg = Ring(lambda v: cg.at[v], "z", *more_down)
    r_ay = Ring(lambda v: ga.at[z, v], "y", *more_down)
    r_bz = Ring(lambda v: gb.at[y, v], "z", *more_down)
    r_az = {k: az_ring(k) for k in (0, 3, 1, 2)}
    r_by = {k: by_ring(k) for k in (0, 3, 1, 2)}
    here = pl.ds(2 * c, 2)
    there = pl.ds(2 * (1 - c), 2)
    r_ao = Ring(lambda v: ao.at[v, here], "x", (pl.ds(0, 1),), (pl.ds(1, 1),))
    r_full = Ring(lambda v: full.at[rows_of(4 * c + v)], "x", (pl.ds(0, 48),), (pl.ds(48, 40),))

    for ring in r_na:
        ring.start()
    r_ca.start()
    send_cell(0)
    lax.fori_loop(0, WA // LANES, stage_a, 0)
    lax.fori_loop(0, HALF // LANES, stage_clean, 0)
    r_cg.start()
    lax.fori_loop(0, WB // LANES, stage_b, 0)

    partner = (z, y, 2 * x + 1 - c)
    r_ca.forward()
    for ring in r_na:
        ring.forward()
    r_ay.start()
    r_by[0].start()
    r_bz.start()
    send_cell(3)
    send_cell(1)

    def gram(left, right):
        return lax.dot_general(left, right, (((1,), (1,)), ((), ())), preferred_element_type=F32)

    def unpack(ref, half):
        part = [ref[v].astype(F32)[half * SEG:(half + 1) * SEG] for v in range(4)]
        return jnp.concatenate(part, axis=0).astype(BF16)

    for ring in r_na:
        ring.finish()
    r_ca.finish()
    part_gram[...] = gram(na[:, :, :512].reshape(4 * NOISE, 512), unpack(ca, 0)) + gram(
        na[:, :, 512:].reshape(4 * NOISE, 512), unpack(ca, 1))
    own_half = pl.ds(pl.multiple_of(c * 352, 8), 352)
    other_half = pl.ds(pl.multiple_of((1 - c) * 352, 8), 352)
    swap = copy(part_gram.at[other_half], d2, d_s.at[0], d_r.at[0], partner)
    swap.start()
    send_cell(2)

    gap = jnp.zeros((32, LANES), BF16)

    def turn_a(k):
        def step(q, carry):
            span = pl.ds(pl.multiple_of(q * LANES, LANES), LANES)
            for g in range(2):
                cells = [ao[q, 2 * c + k, 2 * g], ao[q, 2 * c + k, 2 * g + 1], gap]
                ata[2 * c + k, g, span, :] = jnp.concatenate(cells, axis=0).T
            return carry

        lax.fori_loop(0, 4, step, 0)

    def turn_b(v):
        def step(q, carry):
            span = pl.ds(pl.multiple_of(q * LANES, LANES), LANES)
            tokens = jnp.concatenate([ao[q, 2 * c, v], ao[q, 2 * c + 1, v], gap], axis=0)
            atb[c, v, span, :] = tokens.T
            return carry

        lax.fori_loop(0, 4, step, 0)

    turned = [copy(ata.at[here], ata.at[here], k_s.at[0], k_r.at[0], partner),
              copy(atb.at[c], atb.at[c], k_s.at[1], k_r.at[1], partner)]

    swap.wait_recv()
    sm[...] = part_gram[own_half] + d2[...]
    up, down, across = mod4(x + 1), mod4(x + 3), mod4(x + 2)
    dev_up, dev_down = (z, y, 2 * up + c), (z, y, 2 * down + c)
    first = pl.ds(pl.multiple_of(across * SEG, 8), 48)
    second = pl.ds(pl.multiple_of(across * SEG + 48, 8), 40)
    share = [copy(sm.at[first], near_a, m_s.at[0], m_r.at[0], dev_up),
             copy(sm.at[second], near_b, m_s.at[1], m_r.at[1], dev_down),
             copy(sm.at[rows_of(up)], x3.at[0], m_s.at[2], m_r.at[2], dev_up),
             copy(sm.at[rows_of(down)], x3.at[1], m_s.at[3], m_r.at[3], dev_down)]
    share[0].start()
    share[1].start()
    r_ay.forward()
    r_cg.forward()
    share[0].wait_recv()
    sm[pl.ds(pl.multiple_of(up * SEG, 8), 48)] += near_a[...]
    share[2].start()
    share[1].wait_recv()
    sm[pl.ds(pl.multiple_of(down * SEG + 48, 8), 40)] += near_b[...]
    share[3].start()
    r_bz.forward()
    r_az[0].start()
    r_az[3].start()
    wait_pieces()
    r_ao.start()
    r_by[0].forward()
    r_by[3].start()
    r_by[1].start()
    r_az[1].start()

    share[2].wait_recv()
    share[3].wait_recv()
    full[rows_of(4 * c + x)] = sm[rows_of(x)] + x3[0] + x3[1]
    r_full.start()
    r_cg.finish()
    r_ay.finish()
    r_az[2].start()
    r_full.forward()
    left[...] = unpack(cg, 0)
    right[...] = unpack(cg, 1)
    grad_gram[...] = gram(ga[z].reshape(4 * NOISE, WA), left[:, :WA])
    r_ao.forward()
    r_full.finish()
    give = copy(full.at[own_half], full.at[own_half], d_s.at[1], d_r.at[1], partner)
    give.start()
    r_bz.finish()
    r_by[2].start()

    r_by[0].finish()
    grad_gram[...] += gram(gb[:, z, :, :HALF - WA].reshape(4 * NOISE, HALF - WA), left[:, WA:]) + gram(
        gb[:, z, :, HALF - WA:].reshape(4 * NOISE, HALF), right[...])
    copy(full.at[other_half], full.at[other_half], d_s.at[1], d_r.at[1], partner).wait_recv()

    def row_dot(j):
        terms = [grad_gram[g * SEG:(g + 1) * SEG] * full[g * SEG:(g + 1) * SEG] for g in range(j, 8, 2)]
        rows_sum = jnp.sum(terms[0] + terms[1] + terms[2] + terms[3], axis=0, keepdims=True)
        return jnp.broadcast_to(jnp.sum(rows_sum, axis=1, keepdims=True), (8, LANES))

    place = lax.broadcasted_iota(jnp.int32, (8, LANES), 0)
    tile = jnp.where(place == 2 * z, row_dot(0), jnp.where(place == 2 * z + 1, row_dot(1), 0.0))

    sends = []

    def send_tile(buf, value, me, n, dev, base):
        buf[me] = value
        for r in range(1, n):
            out = copy(buf.at[me], buf.at[me], v_s.at[base + r], v_r.at[base + r], dev(r))
            out.start()
            sends.append(out)

    def sum_tiles(buf, me, n, base):
        for r in range(1, n):
            origin = buf.at[lax.rem(me + n - r, n)]
            copy(origin, origin, v_s.at[base + r], v_r.at[base + r], partner).wait_recv()
        return jnp.sum(buf[...], axis=0)

    send_tile(sv1, tile, t, 8, lambda r: (z, y, lax.rem(t + r, 8)), 0)

    r_ao.finish()
    turn_a(0)
    turn_a(1)
    turned[0].start()
    tile = sum_tiles(sv1, t, 8, 0)
    send_tile(sv2, tile, 4 * z + y, 16, cell, 8)
    r_az[0].forward()
    for v in range(4):
        turn_b(v)
    turned[1].start()
    r_az[3].forward()
    r_by[3].forward()
    r_az[1].forward()
    r_by[1].forward()
    tile = sum_tiles(sv2, 4 * z + y, 16, 8)
    weights = jnp.maximum(-tile, 0.0) / jnp.sum(jnp.abs(tile), axis=0, keepdims=True)
    wts[...] = weights
    lane = lax.broadcasted_iota(jnp.int32, (1, LANES), 1)
    wout_ref[...] = jnp.where(lane == 0, wts[pl.ds(2 * z, 1), :], wts[pl.ds(2 * z + 1, 1), :])[:, :2]

    copy(ata.at[there], ata.at[there], k_s.at[0], k_r.at[0], partner).wait_recv()
    copy(atb.at[1 - c], atb.at[1 - c], k_s.at[1], k_r.at[1], partner).wait_recv()

    def scaled(rows_in, k):
        width = rows_in.shape[1]

        def part(j):
            row = wts[pl.ds(2 * k + j, 1), :]
            factor = jnp.broadcast_to(jnp.concatenate([row] * (width // LANES), axis=1), (SEG, width))
            return rows_in[j * SEG:(j + 1) * SEG] * factor

        return jnp.concatenate([part(0), part(1)], axis=0).astype(BF16)

    def product(lefts, rights, width, base, span, first=False):
        empty = jnp.zeros((32, span), BF16)

        def step(i, carry):
            cols = pl.ds(pl.multiple_of(i * span, span), span)
            dest = pl.ds(pl.multiple_of(base + i * span, 256), span)
            right = []
            for two in rights:
                right += [scaled(rows_in[cell_at + (slice(None), cols)].astype(F32), k)
                          for rows_in, cell_at, k in two] + [empty]
            left_side = jnp.concatenate([ref[at] for ref, at in lefts], axis=1)
            value = jnp.dot(left_side, jnp.concatenate(right, axis=0), preferred_element_type=F32)
            if first:
                out_ref[:, dest] = value
            else:
                out_ref[:, dest] += value
            return carry

        lax.fori_loop(0, width // span, step, 0)

    def add_a(k, first=False, parts=(0, 1)):
        v = mod4(z + k)
        product([(ata, (v, g)) for g in parts],
                [[(ga, (v, 2 * g + j), v) for j in range(2)] for g in parts], WA, 0, 768, first)

    def add_b(k, first=False, parts=(0, 1)):
        v = mod4(y + k)
        product([(atb, (g, v)) for g in parts],
                [[(gb, (v, 2 * g + j), 2 * g + j) for j in range(2)] for g in parts], WB, WA, 512, first)

    add_a(0, True)
    add_b(0, True)
    r_az[2].forward()
    r_by[2].forward()
    add_a(3)
    add_a(1)
    add_b(3)
    add_b(1)
    for k in (0, 3, 1):
        r_az[k].finish()
    add_a(2, parts=(y // 2,))
    for k in (3, 1):
        r_by[k].finish()
    add_b(2, parts=(z // 2,))
    r_az[2].finish()
    add_a(2, parts=(1 - y // 2,))
    r_by[2].finish()
    add_b(2, parts=(1 - z // 2,))

    for far_copy, goes in pieces:
        @pl.when(goes)
        def _():
            far_copy.wait_send()
    for ring in rings:
        ring.drain()
    for k in turned + [swap, give] + share + sends:
        k.wait_send()


def body(activations, cotangents, row_ids, row_counts):
    dma = pltpu.SemaphoreType.DMA
    vmem = pltpu.VMEM
    return pl.pallas_call(
        body_kernel,
        out_shape=(pltpu.VMEM((512, WA + WB), F32), pltpu.VMEM((1, 2), F32)),
        in_specs=[pl.BlockSpec(memory_space=pltpu.SMEM)] * 2 + [pl.BlockSpec(memory_space=pltpu.VMEM)] * 2,
        out_specs=(pl.BlockSpec(memory_space=pltpu.VMEM), pl.BlockSpec(memory_space=pltpu.VMEM)),
        scratch_shapes=[
            vmem((4, NOISE, 1024), BF16),
            vmem((4, NOISE, 512), BF16),
            vmem((4, NOISE, HALF), BF16),
            vmem((4 * SEG, HALF), BF16),
            vmem((4 * SEG, HALF), BF16),
            vmem((4, 4, NOISE, WA), BF16),
            vmem((4, 4, NOISE, WB), BF16),
            vmem((4, 4, 4, NOISE, LANES), BF16),
            vmem((4, 2, 512, 384), BF16),
            vmem((2, 4, 512, 384), BF16),
            vmem((4 * NOISE, 4 * CLEAN_ROWS), F32),
            vmem((4 * NOISE, 4 * CLEAN_ROWS), F32),
            vmem((4 * NOISE, 4 * CLEAN_ROWS), F32),
            vmem((2 * NOISE, 4 * CLEAN_ROWS), F32),
            vmem((2 * NOISE, 4 * CLEAN_ROWS), F32),
            vmem((48, 4 * CLEAN_ROWS), F32),
            vmem((40, 4 * CLEAN_ROWS), F32),
            vmem((2, SEG, 4 * CLEAN_ROWS), F32),
            vmem((8, 8, LANES), F32),
            vmem((16, 8, LANES), F32),
            vmem((8, LANES), F32),
            dma((16, 4)), dma((16, 4)),
            dma((4, 4)), dma((8,)), dma((4,)),
            dma((2,)), dma((2,)),
            dma((2,)), dma((2,)),
            dma((4,)), dma((4,)),
            dma((24,)), dma((24,)),
        ],
        compiler_params=pltpu.CompilerParams(
            collective_id=0, has_side_effects=True, vmem_limit_bytes=60 * 1024 * 1024),
        cost_estimate=pl.CostEstimate(flops=8_000_000_000, bytes_accessed=8_000_000, transcendentals=0),
        name="reweight",
    )(row_ids, row_counts, activations, cotangents)


def solution(mesh):
    placed = (P("dp", "seq", "tensor"), P("dp", "seq", "tensor"), P("dp", None), P("dp", None))
    return jax.shard_map(
        body,
        mesh=mesh,
        in_specs=placed,
        out_specs=(P(("dp", "seq"), "tensor"), P("dp", None)),
        check_vma=False,
    )
```

```python
import jax
import jax.numpy as jnp
from jax import lax
from jax.experimental import pallas as pl
from jax.experimental.pallas import tpu as pltpu
from jax.sharding import PartitionSpec as P

MESH = pl.DeviceIdType.MESH
F32 = jnp.float32
BF16 = jnp.bfloat16

SEG = 88
NOISE = 176
CLEAN_ROWS = 88
HALF = 896
WA = 768
WB = 1024
LANES = 128


def body_kernel(ids_ref, counts_ref, acts_ref, cot_ref, out_ref, wout_ref,
                na, ca, cg, left, right, ga, gb, ao, ata, atb, part_gram, grad_gram, full, d2, sm,
                near_a, near_b, x3, sv1, sv2, wts,
                ring_s, ring_r, p_s, p_r, p_l, k_s, k_r,
                d_s, d_r, m_s, m_r, v_s, v_r):
    z = lax.axis_index("dp")
    y = lax.axis_index("seq")
    t = lax.axis_index("tensor")
    x = t // 2
    c = lax.rem(t, 2)

    def mod4(v):
        return lax.rem(v, 4)

    def copy(src, dst, s, r, dev):
        return pltpu.make_async_remote_copy(
            src_ref=src, dst_ref=dst, send_sem=s, recv_sem=r, device_id=dev, device_id_type=MESH)

    barrier = pltpu.get_barrier_semaphore()

    def greet(dev):
        pl.semaphore_signal(barrier, inc=1, device_id=dev, device_id_type=MESH)

    def cell(r):
        other = lax.rem(4 * z + y + r, 16)
        return other // 4, lax.rem(other, 4), t

    for r in range(1, 16):
        greet(cell(r))
    for r in range(1, 8):
        greet((z, y, lax.rem(t + r, 8)))

    active = c == y // 2
    targets = [(x, y, 2 * q + z // 2) for q in range(4)]
    target_self = [active & (x == z) & (q == x) & (c == z // 2) for q in range(4)]
    sources = [(2 * c + i // 4, i % 4) for i in range(8)]
    source_self = [(zs == z) & (x == z) & active for zs, _ in sources]
    for dev, same in zip(targets, target_self):
        @pl.when(active & jnp.logical_not(same))
        def _():
            greet(dev)
    for i in (0, 4):
        @pl.when(jnp.logical_not(source_self[i]))
        def _():
            greet((sources[i][0], y, 2 * z + y // 2))
    sends_here = active.astype(jnp.int32)
    has_self = (active & (x == z) & (c == z // 2)).astype(jnp.int32)

    rid = [ids_ref[0, j] for j in range(3)]
    live = [counts_ref[0, rid[j]] - y * SEG for j in range(3)]
    rows = lax.broadcasted_iota(jnp.int32, (SEG, LANES), 0)

    def block_of(i, base=0):
        return pl.ds(pl.multiple_of(base + i * LANES, LANES), LANES)

    def stage_acts(i, carry):
        cols = block_of(i)
        part = [acts_ref[rid[j], :, cols].astype(F32) for j in (1, 2)]
        na[y, :, cols] = jnp.concatenate(part, axis=0).astype(BF16)
        return carry

    def stage_clean_acts(i, carry):
        part = [acts_ref[rid[0], :, block_of(i, base)].astype(F32) for base in (0, 512)]
        ca[z, :, block_of(i)] = jnp.concatenate(part, axis=0).astype(BF16)
        return carry

    lax.fori_loop(0, 1024 // LANES, stage_acts, 0)
    lax.fori_loop(0, 512 // LANES, stage_clean_acts, 0)

    def masked(j, cols):
        return jnp.where(rows < live[j], cot_ref[rid[j], :, cols].astype(F32), 0.0)

    def stage_clean(i, carry):
        part = [masked(0, block_of(i, base)) for base in (0, HALF)]
        cg[z, :, block_of(i)] = jnp.concatenate(part, axis=0).astype(BF16)
        return carry

    def stage_a(i, carry):
        cols = pl.ds(pl.multiple_of(i * LANES, LANES), LANES)
        ga[z, y, :, cols] = jnp.concatenate([masked(1, cols), masked(2, cols)], axis=0).astype(BF16)
        return carry

    def stage_b(i, carry):
        cols = pl.ds(pl.multiple_of(i * LANES, LANES), LANES)
        from_cols = pl.ds(pl.multiple_of(WA + i * LANES, LANES), LANES)
        gb[y, z, :, cols] = jnp.concatenate(
            [masked(1, from_cols), masked(2, from_cols)], axis=0).astype(BF16)
        return carry

    pl.semaphore_wait(barrier, 24 + 4 * sends_here - 2 * has_self)

    pieces = []

    def send_cell(k):
        ys = mod4(y + k)
        for q in range(4):
            start = lax.rem(y, 2) * 512 + q * LANES
            src = na.at[ys, :, pl.ds(pl.multiple_of(start, LANES), LANES)]
            dst = ao.at[q, z, ys]
            same = target_self[q]
            goes = active & jnp.logical_not(same)
            far_copy = copy(src, dst, p_s.at[k, q], p_r.at[lax.rem(z, 2) * 4 + ys], targets[q])
            near_copy = pltpu.make_async_copy(src, dst, p_l.at[ys])

            @pl.when(same)
            def _():
                near_copy.start()

            @pl.when(goes)
            def _():
                far_copy.start()
            pieces.append((far_copy, goes))

    def wait_pieces():
        for i, ((zs, ys), same) in enumerate(zip(sources, source_self)):
            dst = ao.at[x, zs, ys]
            far_copy = copy(dst, dst, p_s.at[0, 0], p_r.at[i], (z, y, lax.rem(t + 1, 8)))
            near_copy = pltpu.make_async_copy(dst, dst, p_l.at[ys])

            @pl.when(same)
            def _():
                near_copy.wait()

            @pl.when(jnp.logical_not(same))
            def _():
                far_copy.wait_recv()

    rings = []

    class Ring:
        def __init__(self, at, axis, first, second):
            n = len(rings)
            rings.append(self)
            me = {"x": x, "y": y, "z": z}[axis]

            def dev(v):
                return {"x": (z, y, 2 * v + c), "y": (z, v, t), "z": (v, y, t)}[axis]

            up, down, far = mod4(me + 1), mod4(me + 3), mod4(me + 2)
            own, low, high, opp = at(me), at(down), at(up), at(far)
            self.go = [copy(own, own, ring_s.at[n, 0], ring_r.at[n, 0], dev(up)),
                       copy(own, own, ring_s.at[n, 1], ring_r.at[n, 1], dev(down))]
            self.got = [copy(low, low, ring_s.at[n, 0], ring_r.at[n, 0], dev(up)),
                        copy(high, high, ring_s.at[n, 1], ring_r.at[n, 1], dev(down))]
            self.pass_on = [
                copy(low.at[first], low.at[first], ring_s.at[n, 2], ring_r.at[n, 2], dev(up)),
                copy(high.at[second], high.at[second], ring_s.at[n, 3], ring_r.at[n, 3], dev(down))]
            self.got_far = [
                copy(opp.at[first], opp.at[first], ring_s.at[n, 2], ring_r.at[n, 2], dev(up)),
                copy(opp.at[second], opp.at[second], ring_s.at[n, 3], ring_r.at[n, 3], dev(down))]

        def start(self):
            for k in self.go:
                k.start()

        def forward(self):
            for k in range(2):
                self.got[k].wait_recv()
                self.pass_on[k].start()

        def finish(self):
            for k in self.got_far:
                k.wait_recv()

        def drain(self):
            for k in self.go + self.pass_on:
                k.wait_send()

    more_up = (pl.ds(0, 96),), (pl.ds(96, 80),)
    more_down = (pl.ds(0, 80),), (pl.ds(80, 96),)

    def az_ring(k):
        item = mod4(y + k)
        return Ring(lambda v: ga.at[v, item], "z", *(more_up if k in (0, 1) else more_down))

    def by_ring(k):
        item = mod4(z + k)
        return Ring(lambda v: gb.at[v, item], "y", *(more_up if k in (0, 1) else more_down))

    def rows_of(chunk):
        return pl.ds(pl.multiple_of(chunk * SEG, 8), SEG)

    r_na = [Ring(lambda v, h=h: na.at[v, :, pl.ds(h * 512, 512)], "y", *(more_up, more_down)[h]) for h in range(2)]
    r_ca = Ring(lambda v: ca.at[v], "z", *more_up)
    r_cg = Ring(lambda v: cg.at[v], "z", *more_down)
    r_ay = Ring(lambda v: ga.at[z, v], "y", *more_down)
    r_bz = Ring(lambda v: gb.at[y, v], "z", *more_down)
    r_az = {k: az_ring(k) for k in (0, 3, 1, 2)}
    r_by = {k: by_ring(k) for k in (0, 3, 1, 2)}
    here = pl.ds(2 * c, 2)
    there = pl.ds(2 * (1 - c), 2)
    r_ao = Ring(lambda v: ao.at[v, here], "x", (pl.ds(0, 1),), (pl.ds(1, 1),))
    r_full = Ring(lambda v: full.at[rows_of(4 * c + v)], "x", (pl.ds(0, 48),), (pl.ds(48, 40),))

    for ring in r_na:
        ring.start()
    r_ca.start()
    send_cell(0)
    lax.fori_loop(0, WA // LANES, stage_a, 0)
    lax.fori_loop(0, HALF // LANES, stage_clean, 0)
    r_cg.start()
    lax.fori_loop(0, WB // LANES, stage_b, 0)

    partner = (z, y, 2 * x + 1 - c)
    r_ca.forward()
    for ring in r_na:
        ring.forward()
    r_ay.start()
    r_by[0].start()
    r_bz.start()
    send_cell(3)
    send_cell(1)

    def gram(left, right):
        return lax.dot_general(left, right, (((1,), (1,)), ((), ())), preferred_element_type=F32)

    def unpack(ref, half):
        part = [ref[v].astype(F32)[half * SEG:(half + 1) * SEG] for v in range(4)]
        return jnp.concatenate(part, axis=0).astype(BF16)

    for ring in r_na:
        ring.finish()
    r_ca.finish()
    part_gram[...] = gram(na[:, :, :512].reshape(4 * NOISE, 512), unpack(ca, 0)) + gram(
        na[:, :, 512:].reshape(4 * NOISE, 512), unpack(ca, 1))
    own_half = pl.ds(pl.multiple_of(c * 352, 8), 352)
    other_half = pl.ds(pl.multiple_of((1 - c) * 352, 8), 352)
    swap = copy(part_gram.at[other_half], d2, d_s.at[0], d_r.at[0], partner)
    swap.start()
    send_cell(2)

    gap = jnp.zeros((32, LANES), BF16)

    def turn_a(k):
        def step(q, carry):
            span = pl.ds(pl.multiple_of(q * LANES, LANES), LANES)
            for g in range(2):
                cells = [ao[q, 2 * c + k, 2 * g], ao[q, 2 * c + k, 2 * g + 1], gap]
                ata[2 * c + k, g, span, :] = jnp.concatenate(cells, axis=0).T
            return carry

        lax.fori_loop(0, 4, step, 0)

    def turn_b(v):
        def step(q, carry):
            span = pl.ds(pl.multiple_of(q * LANES, LANES), LANES)
            tokens = jnp.concatenate([ao[q, 2 * c, v], ao[q, 2 * c + 1, v], gap], axis=0)
            atb[c, v, span, :] = tokens.T
            return carry

        lax.fori_loop(0, 4, step, 0)

    turned = [copy(ata.at[here], ata.at[here], k_s.at[0], k_r.at[0], partner),
              copy(atb.at[c], atb.at[c], k_s.at[1], k_r.at[1], partner)]

    swap.wait_recv()
    sm[...] = part_gram[own_half] + d2[...]
    up, down, across = mod4(x + 1), mod4(x + 3), mod4(x + 2)
    dev_up, dev_down = (z, y, 2 * up + c), (z, y, 2 * down + c)
    first = pl.ds(pl.multiple_of(across * SEG, 8), 48)
    second = pl.ds(pl.multiple_of(across * SEG + 48, 8), 40)
    share = [copy(sm.at[first], near_a, m_s.at[0], m_r.at[0], dev_up),
             copy(sm.at[second], near_b, m_s.at[1], m_r.at[1], dev_down),
             copy(sm.at[rows_of(up)], x3.at[0], m_s.at[2], m_r.at[2], dev_up),
             copy(sm.at[rows_of(down)], x3.at[1], m_s.at[3], m_r.at[3], dev_down)]
    share[0].start()
    share[1].start()
    r_ay.forward()
    r_cg.forward()
    share[0].wait_recv()
    sm[pl.ds(pl.multiple_of(up * SEG, 8), 48)] += near_a[...]
    share[2].start()
    share[1].wait_recv()
    sm[pl.ds(pl.multiple_of(down * SEG + 48, 8), 40)] += near_b[...]
    share[3].start()
    r_bz.forward()
    r_az[0].start()
    r_az[3].start()
    wait_pieces()
    r_ao.start()
    r_by[0].forward()
    r_by[3].start()
    r_by[1].start()
    r_az[1].start()

    share[2].wait_recv()
    share[3].wait_recv()
    full[rows_of(4 * c + x)] = sm[rows_of(x)] + x3[0] + x3[1]
    r_full.start()
    r_cg.finish()
    r_ay.finish()
    r_az[2].start()
    r_full.forward()
    left[...] = unpack(cg, 0)
    right[...] = unpack(cg, 1)
    grad_gram[...] = gram(ga[z].reshape(4 * NOISE, WA), left[:, :WA])
    r_ao.forward()
    r_full.finish()
    give = copy(full.at[own_half], full.at[own_half], d_s.at[1], d_r.at[1], partner)
    give.start()
    r_bz.finish()
    r_by[2].start()

    r_by[0].finish()
    grad_gram[...] += gram(gb[:, z, :, :HALF - WA].reshape(4 * NOISE, HALF - WA), left[:, WA:]) + gram(
        gb[:, z, :, HALF - WA:].reshape(4 * NOISE, HALF), right[...])
    copy(full.at[other_half], full.at[other_half], d_s.at[1], d_r.at[1], partner).wait_recv()

    def row_dot(j):
        terms = [grad_gram[g * SEG:(g + 1) * SEG] * full[g * SEG:(g + 1) * SEG] for g in range(j, 8, 2)]
        rows_sum = jnp.sum(terms[0] + terms[1] + terms[2] + terms[3], axis=0, keepdims=True)
        return jnp.broadcast_to(jnp.sum(rows_sum, axis=1, keepdims=True), (8, LANES))

    place = lax.broadcasted_iota(jnp.int32, (8, LANES), 0)
    tile = jnp.where(place == 2 * z, row_dot(0), jnp.where(place == 2 * z + 1, row_dot(1), 0.0))

    sends = []

    def send_tile(buf, value, me, n, dev, base):
        buf[me] = value
        for r in range(1, n):
            out = copy(buf.at[me], buf.at[me], v_s.at[base + r], v_r.at[base + r], dev(r))
            out.start()
            sends.append(out)

    def sum_tiles(buf, me, n, base):
        for r in range(1, n):
            origin = buf.at[lax.rem(me + n - r, n)]
            copy(origin, origin, v_s.at[base + r], v_r.at[base + r], partner).wait_recv()
        return jnp.sum(buf[...], axis=0)

    send_tile(sv1, tile, t, 8, lambda r: (z, y, lax.rem(t + r, 8)), 0)

    r_ao.finish()
    turn_a(0)
    turn_a(1)
    turned[0].start()
    tile = sum_tiles(sv1, t, 8, 0)
    send_tile(sv2, tile, 4 * z + y, 16, cell, 8)
    r_az[0].forward()
    for v in range(4):
        turn_b(v)
    turned[1].start()
    r_az[3].forward()
    r_by[3].forward()
    r_az[1].forward()
    r_by[1].forward()
    tile = sum_tiles(sv2, 4 * z + y, 16, 8)
    weights = jnp.maximum(-tile, 0.0) / jnp.sum(jnp.abs(tile), axis=0, keepdims=True)
    wts[...] = weights
    lane = lax.broadcasted_iota(jnp.int32, (1, LANES), 1)
    wout_ref[...] = jnp.where(lane == 0, wts[pl.ds(2 * z, 1), :], wts[pl.ds(2 * z + 1, 1), :])[:, :2]

    copy(ata.at[there], ata.at[there], k_s.at[0], k_r.at[0], partner).wait_recv()
    copy(atb.at[1 - c], atb.at[1 - c], k_s.at[1], k_r.at[1], partner).wait_recv()

    def scaled(rows_in, k):
        width = rows_in.shape[1]

        def part(j):
            row = wts[pl.ds(2 * k + j, 1), :]
            factor = jnp.broadcast_to(jnp.concatenate([row] * (width // LANES), axis=1), (SEG, width))
            return rows_in[j * SEG:(j + 1) * SEG] * factor

        return jnp.concatenate([part(0), part(1)], axis=0).astype(BF16)

    def product(lefts, rights, width, base, span, first=False):
        empty = jnp.zeros((32, span), BF16)

        def step(i, carry):
            cols = pl.ds(pl.multiple_of(i * span, span), span)
            dest = pl.ds(pl.multiple_of(base + i * span, 256), span)
            right = []
            for two in rights:
                right += [scaled(rows_in[cell_at + (slice(None), cols)].astype(F32), k)
                          for rows_in, cell_at, k in two] + [empty]
            left_side = jnp.concatenate([ref[at] for ref, at in lefts], axis=1)
            value = jnp.dot(left_side, jnp.concatenate(right, axis=0), preferred_element_type=F32)
            if first:
                out_ref[:, dest] = value
            else:
                out_ref[:, dest] += value
            return carry

        lax.fori_loop(0, width // span, step, 0, unroll=True)

    def add_a(k, first=False, parts=(0, 1)):
        v = mod4(z + k)
        product([(ata, (v, g)) for g in parts],
                [[(ga, (v, 2 * g + j), v) for j in range(2)] for g in parts], WA, 0, 256, first)

    def add_b(k, first=False, parts=(0, 1)):
        v = mod4(y + k)
        product([(atb, (g, v)) for g in parts],
                [[(gb, (v, 2 * g + j), 2 * g + j) for j in range(2)] for g in parts], WB, WA, 256, first)

    add_a(0, True)
    add_b(0, True)
    r_az[2].forward()
    r_by[2].forward()
    add_a(3)
    add_a(1)
    add_b(3)
    add_b(1)
    for k in (0, 3, 1):
        r_az[k].finish()
    add_a(2, parts=(y // 2,))
    for k in (3, 1):
        r_by[k].finish()
    add_b(2, parts=(z // 2,))
    r_az[2].finish()
    add_a(2, parts=(1 - y // 2,))
    r_by[2].finish()
    add_b(2, parts=(1 - z // 2,))

    for far_copy, goes in pieces:
        @pl.when(goes)
        def _():
            far_copy.wait_send()
    for ring in rings:
        ring.drain()
    for k in turned + [swap, give] + share + sends:
        k.wait_send()


def body(activations, cotangents, row_ids, row_counts):
    dma = pltpu.SemaphoreType.DMA
    vmem = pltpu.VMEM
    return pl.pallas_call(
        body_kernel,
        out_shape=(pltpu.VMEM((512, WA + WB), F32), pltpu.VMEM((1, 2), F32)),
        in_specs=[pl.BlockSpec(memory_space=pltpu.SMEM)] * 2 + [pl.BlockSpec(memory_space=pltpu.VMEM)] * 2,
        out_specs=(pl.BlockSpec(memory_space=pltpu.VMEM), pl.BlockSpec(memory_space=pltpu.VMEM)),
        scratch_shapes=[
            vmem((4, NOISE, 1024), BF16),
            vmem((4, NOISE, 512), BF16),
            vmem((4, NOISE, HALF), BF16),
            vmem((4 * SEG, HALF), BF16),
            vmem((4 * SEG, HALF), BF16),
            vmem((4, 4, NOISE, WA), BF16),
            vmem((4, 4, NOISE, WB), BF16),
            vmem((4, 4, 4, NOISE, LANES), BF16),
            vmem((4, 2, 512, 384), BF16),
            vmem((2, 4, 512, 384), BF16),
            vmem((4 * NOISE, 4 * CLEAN_ROWS), F32),
            vmem((4 * NOISE, 4 * CLEAN_ROWS), F32),
            vmem((4 * NOISE, 4 * CLEAN_ROWS), F32),
            vmem((2 * NOISE, 4 * CLEAN_ROWS), F32),
            vmem((2 * NOISE, 4 * CLEAN_ROWS), F32),
            vmem((48, 4 * CLEAN_ROWS), F32),
            vmem((40, 4 * CLEAN_ROWS), F32),
            vmem((2, SEG, 4 * CLEAN_ROWS), F32),
            vmem((8, 8, LANES), F32),
            vmem((16, 8, LANES), F32),
            vmem((8, LANES), F32),
            dma((16, 4)), dma((16, 4)),
            dma((4, 4)), dma((8,)), dma((4,)),
            dma((2,)), dma((2,)),
            dma((2,)), dma((2,)),
            dma((4,)), dma((4,)),
            dma((24,)), dma((24,)),
        ],
        compiler_params=pltpu.CompilerParams(
            collective_id=0, has_side_effects=True, vmem_limit_bytes=60 * 1024 * 1024),
        cost_estimate=pl.CostEstimate(flops=8_000_000_000, bytes_accessed=8_000_000, transcendentals=0),
        name="reweight",
    )(row_ids, row_counts, activations, cotangents)


def solution(mesh):
    placed = (P("dp", "seq", "tensor"), P("dp", "seq", "tensor"), P("dp", None), P("dp", None))
    return jax.shard_map(
        body,
        mesh=mesh,
        in_specs=placed,
        out_specs=(P(("dp", "seq"), "tensor"), P("dp", None)),
        check_vma=False,
    )
```

```python
import jax
import jax.numpy as jnp
from jax import lax
from jax.experimental import pallas as pl
from jax.experimental.pallas import tpu as pltpu
from jax.sharding import PartitionSpec as P

MESH = pl.DeviceIdType.MESH
F32 = jnp.float32
BF16 = jnp.bfloat16

SEG = 88
NOISE = 176
CLEAN_ROWS = 88
HALF = 896
WA = 768
WB = 1024
LANES = 128


def body_kernel(ids_ref, counts_ref, acts_ref, cot_ref, out_ref, wout_ref,
                na, ca, cg, left, right, ga, gb, ao, ata, atb, part_gram, grad_gram, full, d2, sm,
                near_a, near_b, x3, sv1, sv2, wts,
                ring_s, ring_r, p_s, p_r, p_l, k_s, k_r,
                d_s, d_r, m_s, m_r, v_s, v_r):
    z = lax.axis_index("dp")
    y = lax.axis_index("seq")
    t = lax.axis_index("tensor")
    x = t // 2
    c = lax.rem(t, 2)

    def mod4(v):
        return lax.rem(v, 4)

    def copy(src, dst, s, r, dev):
        return pltpu.make_async_remote_copy(
            src_ref=src, dst_ref=dst, send_sem=s, recv_sem=r, device_id=dev, device_id_type=MESH)

    barrier = pltpu.get_barrier_semaphore()

    def greet(dev):
        pl.semaphore_signal(barrier, inc=1, device_id=dev, device_id_type=MESH)

    def cell(r):
        other = lax.rem(4 * z + y + r, 16)
        return other // 4, lax.rem(other, 4), t

    for r in range(1, 16):
        greet(cell(r))
    for r in range(1, 8):
        greet((z, y, lax.rem(t + r, 8)))

    active = c == y // 2
    targets = [(x, y, 2 * q + z // 2) for q in range(4)]
    target_self = [active & (x == z) & (q == x) & (c == z // 2) for q in range(4)]
    sources = [(2 * c + i // 4, i % 4) for i in range(8)]
    source_self = [(zs == z) & (x == z) & active for zs, _ in sources]
    for dev, same in zip(targets, target_self):
        @pl.when(active & jnp.logical_not(same))
        def _():
            greet(dev)
    for i in (0, 4):
        @pl.when(jnp.logical_not(source_self[i]))
        def _():
            greet((sources[i][0], y, 2 * z + y // 2))
    sends_here = active.astype(jnp.int32)
    has_self = (active & (x == z) & (c == z // 2)).astype(jnp.int32)

    rid = [ids_ref[0, j] for j in range(3)]
    live = [counts_ref[0, rid[j]] - y * SEG for j in range(3)]
    rows = lax.broadcasted_iota(jnp.int32, (SEG, LANES), 0)

    def block_of(i, base=0):
        return pl.ds(pl.multiple_of(base + i * LANES, LANES), LANES)

    def stage_acts(i, carry):
        cols = block_of(i)
        part = [acts_ref[rid[j], :, cols].astype(F32) for j in (1, 2)]
        na[y, :, cols] = jnp.concatenate(part, axis=0).astype(BF16)
        return carry

    def stage_clean_acts(i, carry):
        part = [acts_ref[rid[0], :, block_of(i, base)].astype(F32) for base in (0, 512)]
        ca[z, :, block_of(i)] = jnp.concatenate(part, axis=0).astype(BF16)
        return carry

    lax.fori_loop(0, 1024 // LANES, stage_acts, 0)
    lax.fori_loop(0, 512 // LANES, stage_clean_acts, 0)

    def masked(j, cols):
        return jnp.where(rows < live[j], cot_ref[rid[j], :, cols].astype(F32), 0.0)

    def stage_clean(i, carry):
        part = [masked(0, block_of(i, base)) for base in (0, HALF)]
        cg[z, :, block_of(i)] = jnp.concatenate(part, axis=0).astype(BF16)
        return carry

    def stage_a(i, carry):
        cols = pl.ds(pl.multiple_of(i * LANES, LANES), LANES)
        ga[z, y, :, cols] = jnp.concatenate([masked(1, cols), masked(2, cols)], axis=0).astype(BF16)
        return carry

    def stage_b(i, carry):
        cols = pl.ds(pl.multiple_of(i * LANES, LANES), LANES)
        from_cols = pl.ds(pl.multiple_of(WA + i * LANES, LANES), LANES)
        gb[y, z, :, cols] = jnp.concatenate(
            [masked(1, from_cols), masked(2, from_cols)], axis=0).astype(BF16)
        return carry

    pl.semaphore_wait(barrier, 24 + 4 * sends_here - 2 * has_self)

    pieces = []

    def send_cell(k):
        ys = mod4(y + k)
        for q in range(4):
            start = lax.rem(y, 2) * 512 + q * LANES
            src = na.at[ys, :, pl.ds(pl.multiple_of(start, LANES), LANES)]
            dst = ao.at[q, z, ys]
            same = target_self[q]
            goes = active & jnp.logical_not(same)
            far_copy = copy(src, dst, p_s.at[k, q], p_r.at[lax.rem(z, 2) * 4 + ys], targets[q])
            near_copy = pltpu.make_async_copy(src, dst, p_l.at[ys])

            @pl.when(same)
            def _():
                near_copy.start()

            @pl.when(goes)
            def _():
                far_copy.start()
            pieces.append((far_copy, goes))

    def wait_pieces(k):
        ys = mod4(y + k)
        for j in range(2):
            dst = ao.at[x, 2 * c + j, ys]
            same = active & (x == z) & (2 * c + j == z)
            far_copy = copy(dst, dst, p_s.at[0, 0], p_r.at[4 * j + ys], (z, y, lax.rem(t + 1, 8)))
            near_copy = pltpu.make_async_copy(dst, dst, p_l.at[ys])

            @pl.when(same)
            def _():
                near_copy.wait()

            @pl.when(jnp.logical_not(same))
            def _():
                far_copy.wait_recv()

    rings = []

    class Ring:
        def __init__(self, at, axis, first, second):
            n = len(rings)
            rings.append(self)
            me = {"x": x, "y": y, "z": z}[axis]

            def dev(v):
                return {"x": (z, y, 2 * v + c), "y": (z, v, t), "z": (v, y, t)}[axis]

            up, down, far = mod4(me + 1), mod4(me + 3), mod4(me + 2)
            own, low, high, opp = at(me), at(down), at(up), at(far)
            self.go = [copy(own, own, ring_s.at[n, 0], ring_r.at[n, 0], dev(up)),
                       copy(own, own, ring_s.at[n, 1], ring_r.at[n, 1], dev(down))]
            self.got = [copy(low, low, ring_s.at[n, 0], ring_r.at[n, 0], dev(up)),
                        copy(high, high, ring_s.at[n, 1], ring_r.at[n, 1], dev(down))]
            self.pass_on = [
                copy(low.at[first], low.at[first], ring_s.at[n, 2], ring_r.at[n, 2], dev(up)),
                copy(high.at[second], high.at[second], ring_s.at[n, 3], ring_r.at[n, 3], dev(down))]
            self.got_far = [
                copy(opp.at[first], opp.at[first], ring_s.at[n, 2], ring_r.at[n, 2], dev(up)),
                copy(opp.at[second], opp.at[second], ring_s.at[n, 3], ring_r.at[n, 3], dev(down))]

        def start(self):
            for k in self.go:
                k.start()

        def forward(self):
            for k in range(2):
                self.got[k].wait_recv()
                self.pass_on[k].start()

        def finish(self):
            for k in self.got_far:
                k.wait_recv()

        def drain(self):
            for k in self.go + self.pass_on:
                k.wait_send()

    more_up = (pl.ds(0, 96),), (pl.ds(96, 80),)
    more_down = (pl.ds(0, 80),), (pl.ds(80, 96),)

    def az_ring(k):
        item = mod4(y + k)
        return Ring(lambda v: ga.at[v, item], "z", *(more_up if k in (0, 1) else more_down))

    def by_ring(k):
        item = mod4(z + k)
        return Ring(lambda v: gb.at[v, item], "y", *(more_up if k in (0, 1) else more_down))

    def rows_of(chunk):
        return pl.ds(pl.multiple_of(chunk * SEG, 8), SEG)

    r_na = [Ring(lambda v, h=h: na.at[v, :, pl.ds(h * 512, 512)], "y", *(more_up, more_down)[h]) for h in range(2)]
    r_ca = Ring(lambda v: ca.at[v], "z", *more_up)
    r_cg = Ring(lambda v: cg.at[v], "z", *more_down)
    r_ay = Ring(lambda v: ga.at[z, v], "y", *more_down)
    r_bz = Ring(lambda v: gb.at[y, v], "z", *more_down)
    r_az = {k: az_ring(k) for k in (0, 3, 1, 2)}
    r_by = {k: by_ring(k) for k in (0, 3, 1, 2)}
    here = pl.ds(2 * c, 2)
    there = pl.ds(2 * (1 - c), 2)

    def ao_ring(k):
        return Ring(lambda v: ao.at[v, here, mod4(y + k)], "x", (pl.ds(0, 1),), (pl.ds(1, 1),))

    r_ao = {k: ao_ring(k) for k in (0, 3, 1, 2)}
    r_full = Ring(lambda v: full.at[rows_of(4 * c + v)], "x", (pl.ds(0, 48),), (pl.ds(48, 40),))

    for ring in r_na:
        ring.start()
    r_ca.start()
    send_cell(0)
    lax.fori_loop(0, WA // LANES, stage_a, 0)
    lax.fori_loop(0, HALF // LANES, stage_clean, 0)
    r_cg.start()
    lax.fori_loop(0, WB // LANES, stage_b, 0)

    partner = (z, y, 2 * x + 1 - c)
    r_ca.forward()
    for ring in r_na:
        ring.forward()
    r_ay.start()
    r_by[0].start()
    send_cell(3)
    send_cell(1)
    r_bz.start()
    wait_pieces(0)
    r_ao[0].start()

    def gram(left, right):
        return lax.dot_general(left, right, (((1,), (1,)), ((), ())), preferred_element_type=F32)

    def unpack(ref, half):
        part = [ref[v].astype(F32)[half * SEG:(half + 1) * SEG] for v in range(4)]
        return jnp.concatenate(part, axis=0).astype(BF16)

    for ring in r_na:
        ring.finish()
    r_ca.finish()
    part_gram[...] = gram(na[:, :, :512].reshape(4 * NOISE, 512), unpack(ca, 0)) + gram(
        na[:, :, 512:].reshape(4 * NOISE, 512), unpack(ca, 1))
    own_half = pl.ds(pl.multiple_of(c * 352, 8), 352)
    other_half = pl.ds(pl.multiple_of((1 - c) * 352, 8), 352)
    swap = copy(part_gram.at[other_half], d2, d_s.at[0], d_r.at[0], partner)
    swap.start()
    send_cell(2)
    r_ao[0].forward()
    for k in (3, 1):
        wait_pieces(k)
        r_ao[k].start()

    gap = jnp.zeros((32, LANES), BF16)

    def turn_a(k):
        def step(q, carry):
            span = pl.ds(pl.multiple_of(q * LANES, LANES), LANES)
            for g in range(2):
                cells = [ao[q, 2 * c + k, 2 * g], ao[q, 2 * c + k, 2 * g + 1], gap]
                ata[2 * c + k, g, span, :] = jnp.concatenate(cells, axis=0).T
            return carry

        lax.fori_loop(0, 4, step, 0)

    def turn_b(v):
        def step(q, carry):
            span = pl.ds(pl.multiple_of(q * LANES, LANES), LANES)
            tokens = jnp.concatenate([ao[q, 2 * c, v], ao[q, 2 * c + 1, v], gap], axis=0)
            atb[c, v, span, :] = tokens.T
            return carry

        lax.fori_loop(0, 4, step, 0)

    turned = [copy(ata.at[here], ata.at[here], k_s.at[0], k_r.at[0], partner),
              copy(atb.at[c], atb.at[c], k_s.at[1], k_r.at[1], partner)]

    swap.wait_recv()
    sm[...] = part_gram[own_half] + d2[...]
    up, down, across = mod4(x + 1), mod4(x + 3), mod4(x + 2)
    dev_up, dev_down = (z, y, 2 * up + c), (z, y, 2 * down + c)
    first = pl.ds(pl.multiple_of(across * SEG, 8), 48)
    second = pl.ds(pl.multiple_of(across * SEG + 48, 8), 40)
    share = [copy(sm.at[first], near_a, m_s.at[0], m_r.at[0], dev_up),
             copy(sm.at[second], near_b, m_s.at[1], m_r.at[1], dev_down),
             copy(sm.at[rows_of(up)], x3.at[0], m_s.at[2], m_r.at[2], dev_up),
             copy(sm.at[rows_of(down)], x3.at[1], m_s.at[3], m_r.at[3], dev_down)]
    share[0].start()
    share[1].start()
    r_ay.forward()
    r_cg.forward()
    share[0].wait_recv()
    sm[pl.ds(pl.multiple_of(up * SEG, 8), 48)] += near_a[...]
    share[2].start()
    share[1].wait_recv()
    sm[pl.ds(pl.multiple_of(down * SEG + 48, 8), 40)] += near_b[...]
    share[3].start()
    r_bz.forward()
    r_az[0].start()
    r_az[3].start()
    r_ao[3].forward()
    r_ao[1].forward()
    r_by[0].forward()
    r_by[3].start()
    r_by[1].start()
    r_az[1].start()

    share[2].wait_recv()
    share[3].wait_recv()
    full[rows_of(4 * c + x)] = sm[rows_of(x)] + x3[0] + x3[1]
    r_full.start()
    r_cg.finish()
    r_ay.finish()
    r_az[2].start()
    r_full.forward()
    wait_pieces(2)
    r_ao[2].start()
    left[...] = unpack(cg, 0)
    right[...] = unpack(cg, 1)
    grad_gram[...] = gram(ga[z].reshape(4 * NOISE, WA), left[:, :WA])
    r_full.finish()
    give = copy(full.at[own_half], full.at[own_half], d_s.at[1], d_r.at[1], partner)
    give.start()
    r_ao[2].forward()
    r_bz.finish()
    r_by[2].start()

    r_by[0].finish()
    grad_gram[...] += gram(gb[:, z, :, :HALF - WA].reshape(4 * NOISE, HALF - WA), left[:, WA:]) + gram(
        gb[:, z, :, HALF - WA:].reshape(4 * NOISE, HALF), right[...])
    copy(full.at[other_half], full.at[other_half], d_s.at[1], d_r.at[1], partner).wait_recv()

    def row_dot(j):
        terms = [grad_gram[g * SEG:(g + 1) * SEG] * full[g * SEG:(g + 1) * SEG] for g in range(j, 8, 2)]
        rows_sum = jnp.sum(terms[0] + terms[1] + terms[2] + terms[3], axis=0, keepdims=True)
        return jnp.broadcast_to(jnp.sum(rows_sum, axis=1, keepdims=True), (8, LANES))

    place = lax.broadcasted_iota(jnp.int32, (8, LANES), 0)
    tile = jnp.where(place == 2 * z, row_dot(0), jnp.where(place == 2 * z + 1, row_dot(1), 0.0))

    sends = []

    def send_tile(buf, value, me, n, dev, base):
        buf[me] = value
        for r in range(1, n):
            out = copy(buf.at[me], buf.at[me], v_s.at[base + r], v_r.at[base + r], dev(r))
            out.start()
            sends.append(out)

    def sum_tiles(buf, me, n, base):
        for r in range(1, n):
            origin = buf.at[lax.rem(me + n - r, n)]
            copy(origin, origin, v_s.at[base + r], v_r.at[base + r], partner).wait_recv()
        return jnp.sum(buf[...], axis=0)

    send_tile(sv1, tile, t, 8, lambda r: (z, y, lax.rem(t + r, 8)), 0)

    for k in (0, 3, 1, 2):
        r_ao[k].finish()
    turn_a(0)
    turn_a(1)
    turned[0].start()
    tile = sum_tiles(sv1, t, 8, 0)
    send_tile(sv2, tile, 4 * z + y, 16, cell, 8)
    r_az[0].forward()
    for v in range(4):
        turn_b(v)
    turned[1].start()
    r_az[3].forward()
    r_by[3].forward()
    r_az[1].forward()
    r_by[1].forward()
    tile = sum_tiles(sv2, 4 * z + y, 16, 8)
    weights = jnp.maximum(-tile, 0.0) / jnp.sum(jnp.abs(tile), axis=0, keepdims=True)
    wts[...] = weights
    lane = lax.broadcasted_iota(jnp.int32, (1, LANES), 1)
    wout_ref[...] = jnp.where(lane == 0, wts[pl.ds(2 * z, 1), :], wts[pl.ds(2 * z + 1, 1), :])[:, :2]

    copy(ata.at[there], ata.at[there], k_s.at[0], k_r.at[0], partner).wait_recv()
    copy(atb.at[1 - c], atb.at[1 - c], k_s.at[1], k_r.at[1], partner).wait_recv()

    def scaled(rows_in, k):
        width = rows_in.shape[1]

        def part(j):
            row = wts[pl.ds(2 * k + j, 1), :]
            factor = jnp.broadcast_to(jnp.concatenate([row] * (width // LANES), axis=1), (SEG, width))
            return rows_in[j * SEG:(j + 1) * SEG] * factor

        return jnp.concatenate([part(0), part(1)], axis=0).astype(BF16)

    def product(lefts, rights, width, base, span, first=False):
        empty = jnp.zeros((32, span), BF16)

        def step(i, carry):
            cols = pl.ds(pl.multiple_of(i * span, span), span)
            dest = pl.ds(pl.multiple_of(base + i * span, 256), span)
            right = []
            for two in rights:
                right += [scaled(rows_in[cell_at + (slice(None), cols)].astype(F32), k)
                          for rows_in, cell_at, k in two] + [empty]
            left_side = jnp.concatenate([ref[at] for ref, at in lefts], axis=1)
            value = jnp.dot(left_side, jnp.concatenate(right, axis=0), preferred_element_type=F32)
            if first:
                out_ref[:, dest] = value
            else:
                out_ref[:, dest] += value
            return carry

        lax.fori_loop(0, width // span, step, 0, unroll=True)

    def add_a(k, first=False, parts=(0, 1)):
        v = mod4(z + k)
        product([(ata, (v, g)) for g in parts],
                [[(ga, (v, 2 * g + j), v) for j in range(2)] for g in parts], WA, 0, 256, first)

    def add_b(k, first=False, parts=(0, 1)):
        v = mod4(y + k)
        product([(atb, (g, v)) for g in parts],
                [[(gb, (v, 2 * g + j), 2 * g + j) for j in range(2)] for g in parts], WB, WA, 256, first)

    add_a(0, True)
    add_b(0, True)
    r_az[2].forward()
    r_by[2].forward()
    add_a(3)
    add_a(1)
    add_b(3)
    add_b(1)
    for k in (0, 3, 1):
        r_az[k].finish()
    add_a(2, parts=(y // 2,))
    for k in (3, 1):
        r_by[k].finish()
    add_b(2, parts=(z // 2,))
    r_az[2].finish()
    add_a(2, parts=(1 - y // 2,))
    r_by[2].finish()
    add_b(2, parts=(1 - z // 2,))

    for far_copy, goes in pieces:
        @pl.when(goes)
        def _():
            far_copy.wait_send()
    for ring in rings:
        ring.drain()
    for k in turned + [swap, give] + share + sends:
        k.wait_send()


def body(activations, cotangents, row_ids, row_counts):
    dma = pltpu.SemaphoreType.DMA
    vmem = pltpu.VMEM
    return pl.pallas_call(
        body_kernel,
        out_shape=(pltpu.VMEM((512, WA + WB), F32), pltpu.VMEM((1, 2), F32)),
        in_specs=[pl.BlockSpec(memory_space=pltpu.SMEM)] * 2 + [pl.BlockSpec(memory_space=pltpu.VMEM)] * 2,
        out_specs=(pl.BlockSpec(memory_space=pltpu.VMEM), pl.BlockSpec(memory_space=pltpu.VMEM)),
        scratch_shapes=[
            vmem((4, NOISE, 1024), BF16),
            vmem((4, NOISE, 512), BF16),
            vmem((4, NOISE, HALF), BF16),
            vmem((4 * SEG, HALF), BF16),
            vmem((4 * SEG, HALF), BF16),
            vmem((4, 4, NOISE, WA), BF16),
            vmem((4, 4, NOISE, WB), BF16),
            vmem((4, 4, 4, NOISE, LANES), BF16),
            vmem((4, 2, 512, 384), BF16),
            vmem((2, 4, 512, 384), BF16),
            vmem((4 * NOISE, 4 * CLEAN_ROWS), F32),
            vmem((4 * NOISE, 4 * CLEAN_ROWS), F32),
            vmem((4 * NOISE, 4 * CLEAN_ROWS), F32),
            vmem((2 * NOISE, 4 * CLEAN_ROWS), F32),
            vmem((2 * NOISE, 4 * CLEAN_ROWS), F32),
            vmem((48, 4 * CLEAN_ROWS), F32),
            vmem((40, 4 * CLEAN_ROWS), F32),
            vmem((2, SEG, 4 * CLEAN_ROWS), F32),
            vmem((8, 8, LANES), F32),
            vmem((16, 8, LANES), F32),
            vmem((8, LANES), F32),
            dma((19, 4)), dma((19, 4)),
            dma((4, 4)), dma((8,)), dma((4,)),
            dma((2,)), dma((2,)),
            dma((2,)), dma((2,)),
            dma((4,)), dma((4,)),
            dma((24,)), dma((24,)),
        ],
        compiler_params=pltpu.CompilerParams(
            collective_id=0, has_side_effects=True, vmem_limit_bytes=60 * 1024 * 1024),
        cost_estimate=pl.CostEstimate(flops=8_000_000_000, bytes_accessed=8_000_000, transcendentals=0),
        name="reweight",
    )(row_ids, row_counts, activations, cotangents)


def solution(mesh):
    placed = (P("dp", "seq", "tensor"), P("dp", "seq", "tensor"), P("dp", None), P("dp", None))
    return jax.shard_map(
        body,
        mesh=mesh,
        in_specs=placed,
        out_specs=(P(("dp", "seq"), "tensor"), P("dp", None)),
        check_vma=False,
    )
```

```python
import jax
import jax.numpy as jnp
from jax import lax
from jax.experimental import pallas as pl
from jax.experimental.pallas import tpu as pltpu
from jax.sharding import PartitionSpec as P

MESH = pl.DeviceIdType.MESH
F32 = jnp.float32
BF16 = jnp.bfloat16

SEG = 88
NOISE = 176
CLEAN_ROWS = 88
HALF = 896
WA = 768
WB = 1024
LANES = 128


def body_kernel(ids_ref, counts_ref, acts_ref, cot_ref, out_ref, wout_ref,
                na, ca, cg, left, right, ga, gb, ao, ata, atb, part_gram, grad_gram, full, d2, sm,
                near_a, near_b, x3, sv1, sv2, wts,
                ring_s, ring_r, p_s, p_r, p_l, k_s, k_r,
                d_s, d_r, m_s, m_r, v_s, v_r):
    z = lax.axis_index("dp")
    y = lax.axis_index("seq")
    t = lax.axis_index("tensor")
    x = t // 2
    c = lax.rem(t, 2)

    def mod4(v):
        return lax.rem(v, 4)

    def copy(src, dst, s, r, dev):
        return pltpu.make_async_remote_copy(
            src_ref=src, dst_ref=dst, send_sem=s, recv_sem=r, device_id=dev, device_id_type=MESH)

    barrier = pltpu.get_barrier_semaphore()

    def greet(dev):
        pl.semaphore_signal(barrier, inc=1, device_id=dev, device_id_type=MESH)

    def cell(r):
        other = lax.rem(4 * z + y + r, 16)
        return other // 4, lax.rem(other, 4), t

    for r in range(1, 16):
        greet(cell(r))
    for r in range(1, 8):
        greet((z, y, lax.rem(t + r, 8)))

    active = c == y // 2
    targets = [(x, y, 2 * q + z // 2) for q in range(4)]
    target_self = [active & (x == z) & (q == x) & (c == z // 2) for q in range(4)]
    sources = [(2 * c + i // 4, i % 4) for i in range(8)]
    source_self = [(zs == z) & (x == z) & active for zs, _ in sources]
    for dev, same in zip(targets, target_self):
        @pl.when(active & jnp.logical_not(same))
        def _():
            greet(dev)
    for i in (0, 4):
        @pl.when(jnp.logical_not(source_self[i]))
        def _():
            greet((sources[i][0], y, 2 * z + y // 2))
    sends_here = active.astype(jnp.int32)
    has_self = (active & (x == z) & (c == z // 2)).astype(jnp.int32)

    rid = [ids_ref[0, j] for j in range(3)]
    live = [counts_ref[0, rid[j]] - y * SEG for j in range(3)]
    rows = lax.broadcasted_iota(jnp.int32, (SEG, LANES), 0)

    def block_of(i, base=0):
        return pl.ds(pl.multiple_of(base + i * LANES, LANES), LANES)

    def stage_acts(i, carry):
        cols = block_of(i)
        part = [acts_ref[rid[j], :, cols].astype(F32) for j in (1, 2)]
        na[y, :, cols] = jnp.concatenate(part, axis=0).astype(BF16)
        return carry

    def stage_clean_acts(i, carry):
        part = [acts_ref[rid[0], :, block_of(i, base)].astype(F32) for base in (0, 512)]
        ca[z, :, block_of(i)] = jnp.concatenate(part, axis=0).astype(BF16)
        return carry

    lax.fori_loop(0, 1024 // LANES, stage_acts, 0)
    lax.fori_loop(0, 512 // LANES, stage_clean_acts, 0)

    def masked(j, cols):
        return jnp.where(rows < live[j], cot_ref[rid[j], :, cols].astype(F32), 0.0)

    def stage_clean(i, carry):
        part = [masked(0, block_of(i, base)) for base in (0, HALF)]
        cg[z, :, block_of(i)] = jnp.concatenate(part, axis=0).astype(BF16)
        return carry

    def stage_a(i, carry):
        cols = pl.ds(pl.multiple_of(i * LANES, LANES), LANES)
        ga[z, y, :, cols] = jnp.concatenate([masked(1, cols), masked(2, cols)], axis=0).astype(BF16)
        return carry

    def stage_b(i, carry):
        cols = pl.ds(pl.multiple_of(i * LANES, LANES), LANES)
        from_cols = pl.ds(pl.multiple_of(WA + i * LANES, LANES), LANES)
        gb[y, z, :, cols] = jnp.concatenate(
            [masked(1, from_cols), masked(2, from_cols)], axis=0).astype(BF16)
        return carry

    pl.semaphore_wait(barrier, 24 + 4 * sends_here - 2 * has_self)

    pieces = []

    def send_cell(k):
        ys = mod4(y + k)
        for q in range(4):
            start = lax.rem(y, 2) * 512 + q * LANES
            src = na.at[ys, :, pl.ds(pl.multiple_of(start, LANES), LANES)]
            dst = ao.at[q, z, ys]
            same = target_self[q]
            goes = active & jnp.logical_not(same)
            far_copy = copy(src, dst, p_s.at[k, q], p_r.at[lax.rem(z, 2) * 4 + ys], targets[q])
            near_copy = pltpu.make_async_copy(src, dst, p_l.at[ys])

            @pl.when(same)
            def _():
                near_copy.start()

            @pl.when(goes)
            def _():
                far_copy.start()
            pieces.append((far_copy, goes))

    def wait_pieces(k):
        ys = mod4(y + k)
        for j in range(2):
            dst = ao.at[x, 2 * c + j, ys]
            same = active & (x == z) & (2 * c + j == z)
            far_copy = copy(dst, dst, p_s.at[0, 0], p_r.at[4 * j + ys], (z, y, lax.rem(t + 1, 8)))
            near_copy = pltpu.make_async_copy(dst, dst, p_l.at[ys])

            @pl.when(same)
            def _():
                near_copy.wait()

            @pl.when(jnp.logical_not(same))
            def _():
                far_copy.wait_recv()

    rings = []

    class Ring:
        def __init__(self, at, axis, first, second):
            n = len(rings)
            rings.append(self)
            me = {"x": x, "y": y, "z": z}[axis]

            def dev(v):
                return {"x": (z, y, 2 * v + c), "y": (z, v, t), "z": (v, y, t)}[axis]

            up, down, far = mod4(me + 1), mod4(me + 3), mod4(me + 2)
            own, low, high, opp = at(me), at(down), at(up), at(far)
            self.go = [copy(own, own, ring_s.at[n, 0], ring_r.at[n, 0], dev(up)),
                       copy(own, own, ring_s.at[n, 1], ring_r.at[n, 1], dev(down))]
            self.got = [copy(low, low, ring_s.at[n, 0], ring_r.at[n, 0], dev(up)),
                        copy(high, high, ring_s.at[n, 1], ring_r.at[n, 1], dev(down))]
            self.pass_on = [
                copy(low.at[first], low.at[first], ring_s.at[n, 2], ring_r.at[n, 2], dev(up)),
                copy(high.at[second], high.at[second], ring_s.at[n, 3], ring_r.at[n, 3], dev(down))]
            self.got_far = [
                copy(opp.at[first], opp.at[first], ring_s.at[n, 2], ring_r.at[n, 2], dev(up)),
                copy(opp.at[second], opp.at[second], ring_s.at[n, 3], ring_r.at[n, 3], dev(down))]

        def start(self):
            for k in self.go:
                k.start()

        def forward(self):
            for k in range(2):
                self.got[k].wait_recv()
                self.pass_on[k].start()

        def finish(self):
            for k in self.got_far:
                k.wait_recv()

        def drain(self):
            for k in self.go + self.pass_on:
                k.wait_send()

    more_up = (pl.ds(0, 96),), (pl.ds(96, 80),)
    more_down = (pl.ds(0, 80),), (pl.ds(80, 96),)

    def az_ring(k):
        item = mod4(y + k)
        return Ring(lambda v: ga.at[v, item], "z", *(more_up if k in (0, 1) else more_down))

    def by_ring(k):
        item = mod4(z + k)
        return Ring(lambda v: gb.at[v, item], "y", *(more_up if k in (0, 1) else more_down))

    def rows_of(chunk):
        return pl.ds(pl.multiple_of(chunk * SEG, 8), SEG)

    r_na = [Ring(lambda v, h=h: na.at[v, :, pl.ds(h * 512, 512)], "y", *(more_up, more_down)[h]) for h in range(2)]
    r_ca = Ring(lambda v: ca.at[v], "z", *more_up)
    r_cg = Ring(lambda v: cg.at[v], "z", *more_down)
    r_ay = Ring(lambda v: ga.at[z, v], "y", *more_down)
    r_bz = Ring(lambda v: gb.at[y, v], "z", *more_down)
    r_az = {k: az_ring(k) for k in (0, 3, 1, 2)}
    r_by = {k: by_ring(k) for k in (0, 3, 1, 2)}
    here = pl.ds(2 * c, 2)
    there = pl.ds(2 * (1 - c), 2)

    def ao_ring(k):
        return Ring(lambda v: ao.at[v, here, mod4(y + k)], "x", (pl.ds(0, 1),), (pl.ds(1, 1),))

    r_ao = {k: ao_ring(k) for k in (0, 3, 1, 2)}
    r_full = Ring(lambda v: full.at[rows_of(4 * c + v)], "x", (pl.ds(0, 48),), (pl.ds(48, 40),))

    for ring in r_na:
        ring.start()
    r_ca.start()
    send_cell(0)
    lax.fori_loop(0, WA // LANES, stage_a, 0)
    lax.fori_loop(0, HALF // LANES, stage_clean, 0)
    r_cg.start()
    lax.fori_loop(0, WB // LANES, stage_b, 0)

    partner = (z, y, 2 * x + 1 - c)
    r_ca.forward()
    for ring in r_na:
        ring.forward()
    r_ay.start()
    r_by[0].start()
    send_cell(3)
    send_cell(1)
    r_bz.start()
    wait_pieces(0)
    r_ao[0].start()

    def gram(left, right):
        return lax.dot_general(left, right, (((1,), (1,)), ((), ())), preferred_element_type=F32)

    def unpack(ref, half):
        part = [ref[v].astype(F32)[half * SEG:(half + 1) * SEG] for v in range(4)]
        return jnp.concatenate(part, axis=0).astype(BF16)

    for ring in r_na:
        ring.finish()
    r_ca.finish()
    part_gram[...] = gram(na[:, :, :512].reshape(4 * NOISE, 512), unpack(ca, 0)) + gram(
        na[:, :, 512:].reshape(4 * NOISE, 512), unpack(ca, 1))
    own_half = pl.ds(pl.multiple_of(c * 352, 8), 352)
    other_half = pl.ds(pl.multiple_of((1 - c) * 352, 8), 352)
    swap = copy(part_gram.at[other_half], d2, d_s.at[0], d_r.at[0], partner)
    swap.start()
    send_cell(2)
    r_ao[0].forward()
    for k in (3, 1):
        wait_pieces(k)
        r_ao[k].start()

    gap = jnp.zeros((32, LANES), BF16)

    def turn_a(k):
        def step(q, carry):
            span = pl.ds(pl.multiple_of(q * LANES, LANES), LANES)
            for g in range(2):
                cells = [ao[q, 2 * c + k, 2 * g], ao[q, 2 * c + k, 2 * g + 1], gap]
                ata[2 * c + k, g, span, :] = jnp.concatenate(cells, axis=0).T
            return carry

        lax.fori_loop(0, 4, step, 0)

    def turn_b(v):
        def step(q, carry):
            span = pl.ds(pl.multiple_of(q * LANES, LANES), LANES)
            tokens = jnp.concatenate([ao[q, 2 * c, v], ao[q, 2 * c + 1, v], gap], axis=0)
            atb[c, v, span, :] = tokens.T
            return carry

        lax.fori_loop(0, 4, step, 0)

    turned = [copy(ata.at[here], ata.at[here], k_s.at[0], k_r.at[0], partner),
              copy(atb.at[c], atb.at[c], k_s.at[1], k_r.at[1], partner)]

    swap.wait_recv()
    sm[...] = part_gram[own_half] + d2[...]
    up, down, across = mod4(x + 1), mod4(x + 3), mod4(x + 2)
    dev_up, dev_down = (z, y, 2 * up + c), (z, y, 2 * down + c)
    first = pl.ds(pl.multiple_of(across * SEG, 8), 48)
    second = pl.ds(pl.multiple_of(across * SEG + 48, 8), 40)
    share = [copy(sm.at[first], near_a, m_s.at[0], m_r.at[0], dev_up),
             copy(sm.at[second], near_b, m_s.at[1], m_r.at[1], dev_down),
             copy(sm.at[rows_of(up)], x3.at[0], m_s.at[2], m_r.at[2], dev_up),
             copy(sm.at[rows_of(down)], x3.at[1], m_s.at[3], m_r.at[3], dev_down)]
    share[0].start()
    share[1].start()
    r_ay.forward()
    r_cg.forward()
    share[0].wait_recv()
    sm[pl.ds(pl.multiple_of(up * SEG, 8), 48)] += near_a[...]
    share[2].start()
    share[1].wait_recv()
    sm[pl.ds(pl.multiple_of(down * SEG + 48, 8), 40)] += near_b[...]
    share[3].start()
    r_bz.forward()
    r_az[0].start()
    r_az[3].start()
    r_ao[3].forward()
    r_ao[1].forward()
    r_by[0].forward()
    r_by[3].start()
    r_by[1].start()
    r_az[1].start()

    share[2].wait_recv()
    share[3].wait_recv()
    full[rows_of(4 * c + x)] = sm[rows_of(x)] + x3[0] + x3[1]
    r_full.start()
    r_cg.finish()
    r_ay.finish()
    r_az[2].start()
    r_full.forward()
    wait_pieces(2)
    r_ao[2].start()
    left[...] = unpack(cg, 0)
    right[...] = unpack(cg, 1)
    grad_gram[...] = gram(ga[z].reshape(4 * NOISE, WA), left[:, :WA])
    r_full.finish()
    give = copy(full.at[own_half], full.at[own_half], d_s.at[1], d_r.at[1], partner)
    give.start()
    r_ao[2].forward()
    r_bz.finish()
    r_by[2].start()

    r_by[0].finish()
    grad_gram[...] += gram(gb[:, z, :, :HALF - WA].reshape(4 * NOISE, HALF - WA), left[:, WA:]) + gram(
        gb[:, z, :, HALF - WA:].reshape(4 * NOISE, HALF), right[...])
    copy(full.at[other_half], full.at[other_half], d_s.at[1], d_r.at[1], partner).wait_recv()

    def row_dot(j):
        terms = [grad_gram[g * SEG:(g + 1) * SEG] * full[g * SEG:(g + 1) * SEG] for g in range(j, 8, 2)]
        rows_sum = jnp.sum(terms[0] + terms[1] + terms[2] + terms[3], axis=0, keepdims=True)
        return jnp.broadcast_to(jnp.sum(rows_sum, axis=1, keepdims=True), (8, LANES))

    place = lax.broadcasted_iota(jnp.int32, (8, LANES), 0)
    tile = jnp.where(place == 2 * z, row_dot(0), jnp.where(place == 2 * z + 1, row_dot(1), 0.0))

    sends = []

    def send_tile(buf, value, me, n, dev, base):
        buf[me] = value
        for r in range(1, n):
            out = copy(buf.at[me], buf.at[me], v_s.at[base + r], v_r.at[base + r], dev(r))
            out.start()
            sends.append(out)

    def sum_tiles(buf, me, n, base):
        for r in range(1, n):
            origin = buf.at[lax.rem(me + n - r, n)]
            copy(origin, origin, v_s.at[base + r], v_r.at[base + r], partner).wait_recv()
        return jnp.sum(buf[...], axis=0)

    send_tile(sv1, tile, t, 8, lambda r: (z, y, lax.rem(t + r, 8)), 0)

    tile = sum_tiles(sv1, t, 8, 0)
    send_tile(sv2, tile, 4 * z + y, 16, cell, 8)
    r_az[0].forward()
    for k in (0, 3, 1, 2):
        r_ao[k].finish()
    turn_a(0)
    turn_a(1)
    turned[0].start()
    for v in range(4):
        turn_b(v)
    turned[1].start()
    r_az[3].forward()
    r_by[3].forward()
    tile = sum_tiles(sv2, 4 * z + y, 16, 8)
    weights = jnp.maximum(-tile, 0.0) / jnp.sum(jnp.abs(tile), axis=0, keepdims=True)
    wts[...] = weights
    lane = lax.broadcasted_iota(jnp.int32, (1, LANES), 1)
    wout_ref[...] = jnp.where(lane == 0, wts[pl.ds(2 * z, 1), :], wts[pl.ds(2 * z + 1, 1), :])[:, :2]


    def scaled(rows_in, k):
        width = rows_in.shape[1]

        def part(j):
            row = wts[pl.ds(2 * k + j, 1), :]
            factor = jnp.broadcast_to(jnp.concatenate([row] * (width // LANES), axis=1), (SEG, width))
            return rows_in[j * SEG:(j + 1) * SEG] * factor

        return jnp.concatenate([part(0), part(1)], axis=0).astype(BF16)

    def product(lefts, rights, width, base, span, first=False):
        empty = jnp.zeros((32, span), BF16)

        def step(i, carry):
            cols = pl.ds(pl.multiple_of(i * span, span), span)
            dest = pl.ds(pl.multiple_of(base + i * span, 256), span)
            right = []
            for two in rights:
                right += [scaled(rows_in[cell_at + (slice(None), cols)].astype(F32), k)
                          for rows_in, cell_at, k in two] + [empty]
            left_side = jnp.concatenate([ref[at] for ref, at in lefts], axis=1)
            value = jnp.dot(left_side, jnp.concatenate(right, axis=0), preferred_element_type=F32)
            if first:
                out_ref[:, dest] = value
            else:
                out_ref[:, dest] += value
            return carry

        lax.fori_loop(0, width // span, step, 0, unroll=True)

    def add_a(k, first=False, parts=(0, 1)):
        v = mod4(z + k)
        product([(ata, (v, g)) for g in parts],
                [[(ga, (v, 2 * g + j), v) for j in range(2)] for g in parts], WA, 0, 256, first)

    def add_b(k, first=False, parts=(0, 1)):
        v = mod4(y + k)
        product([(atb, (g, v)) for g in parts],
                [[(gb, (v, 2 * g + j), 2 * g + j) for j in range(2)] for g in parts], WB, WA, 256, first)

    copy(ata.at[there], ata.at[there], k_s.at[0], k_r.at[0], partner).wait_recv()
    add_a(0, True)
    r_az[1].forward()
    r_by[1].forward()
    copy(atb.at[1 - c], atb.at[1 - c], k_s.at[1], k_r.at[1], partner).wait_recv()
    add_b(0, True)
    r_az[2].forward()
    add_a(3)
    r_by[2].forward()
    add_a(1)
    add_b(3)
    add_b(1)
    for k in (0, 3, 1):
        r_az[k].finish()
    add_a(2, parts=(y // 2,))
    for k in (3, 1):
        r_by[k].finish()
    add_b(2, parts=(z // 2,))
    r_az[2].finish()
    add_a(2, parts=(1 - y // 2,))
    r_by[2].finish()
    add_b(2, parts=(1 - z // 2,))

    for far_copy, goes in pieces:
        @pl.when(goes)
        def _():
            far_copy.wait_send()
    for ring in rings:
        ring.drain()
    for k in turned + [swap, give] + share + sends:
        k.wait_send()


def body(activations, cotangents, row_ids, row_counts):
    dma = pltpu.SemaphoreType.DMA
    vmem = pltpu.VMEM
    return pl.pallas_call(
        body_kernel,
        out_shape=(pltpu.VMEM((512, WA + WB), F32), pltpu.VMEM((1, 2), F32)),
        in_specs=[pl.BlockSpec(memory_space=pltpu.SMEM)] * 2 + [pl.BlockSpec(memory_space=pltpu.VMEM)] * 2,
        out_specs=(pl.BlockSpec(memory_space=pltpu.VMEM), pl.BlockSpec(memory_space=pltpu.VMEM)),
        scratch_shapes=[
            vmem((4, NOISE, 1024), BF16),
            vmem((4, NOISE, 512), BF16),
            vmem((4, NOISE, HALF), BF16),
            vmem((4 * SEG, HALF), BF16),
            vmem((4 * SEG, HALF), BF16),
            vmem((4, 4, NOISE, WA), BF16),
            vmem((4, 4, NOISE, WB), BF16),
            vmem((4, 4, 4, NOISE, LANES), BF16),
            vmem((4, 2, 512, 384), BF16),
            vmem((2, 4, 512, 384), BF16),
            vmem((4 * NOISE, 4 * CLEAN_ROWS), F32),
            vmem((4 * NOISE, 4 * CLEAN_ROWS), F32),
            vmem((4 * NOISE, 4 * CLEAN_ROWS), F32),
            vmem((2 * NOISE, 4 * CLEAN_ROWS), F32),
            vmem((2 * NOISE, 4 * CLEAN_ROWS), F32),
            vmem((48, 4 * CLEAN_ROWS), F32),
            vmem((40, 4 * CLEAN_ROWS), F32),
            vmem((2, SEG, 4 * CLEAN_ROWS), F32),
            vmem((8, 8, LANES), F32),
            vmem((16, 8, LANES), F32),
            vmem((8, LANES), F32),
            dma((19, 4)), dma((19, 4)),
            dma((4, 4)), dma((8,)), dma((4,)),
            dma((2,)), dma((2,)),
            dma((2,)), dma((2,)),
            dma((4,)), dma((4,)),
            dma((24,)), dma((24,)),
        ],
        compiler_params=pltpu.CompilerParams(
            collective_id=0, has_side_effects=True, vmem_limit_bytes=60 * 1024 * 1024),
        cost_estimate=pl.CostEstimate(flops=8_000_000_000, bytes_accessed=8_000_000, transcendentals=0),
        name="reweight",
    )(row_ids, row_counts, activations, cotangents)


def solution(mesh):
    placed = (P("dp", "seq", "tensor"), P("dp", "seq", "tensor"), P("dp", None), P("dp", None))
    return jax.shard_map(
        body,
        mesh=mesh,
        in_specs=placed,
        out_specs=(P(("dp", "seq"), "tensor"), P("dp", None)),
        check_vma=False,
    )
```

```python
import jax
import jax.numpy as jnp
from jax import lax
from jax.experimental import pallas as pl
from jax.experimental.pallas import tpu as pltpu
from jax.sharding import PartitionSpec as P

MESH = pl.DeviceIdType.MESH
F32 = jnp.float32
BF16 = jnp.bfloat16

SEG = 88
NOISE = 176
CLEAN_ROWS = 88
HALF = 896
WA = 768
WB = 1024
LANES = 128


def body_kernel(ids_ref, counts_ref, acts_ref, cot_ref, out_ref, wout_ref,
                na, ca, cg, left, right, ga, gb, ao, ata, atb, part_gram, grad_gram, full, d2, sm,
                near_a, near_b, x3, sv1, sv2, wts,
                ring_s, ring_r, p_s, p_r, p_l, k_s, k_r,
                d_s, d_r, m_s, m_r, v_s, v_r):
    z = lax.axis_index("dp")
    y = lax.axis_index("seq")
    t = lax.axis_index("tensor")
    x = t // 2
    c = lax.rem(t, 2)

    def mod4(v):
        return lax.rem(v, 4)

    def copy(src, dst, s, r, dev):
        return pltpu.make_async_remote_copy(
            src_ref=src, dst_ref=dst, send_sem=s, recv_sem=r, device_id=dev, device_id_type=MESH)

    barrier = pltpu.get_barrier_semaphore()

    def greet(dev):
        pl.semaphore_signal(barrier, inc=1, device_id=dev, device_id_type=MESH)

    def cell(r):
        other = lax.rem(4 * z + y + r, 16)
        return other // 4, lax.rem(other, 4), t

    for r in range(1, 16):
        greet(cell(r))
    for r in range(1, 8):
        greet((z, y, lax.rem(t + r, 8)))

    active = c == y // 2
    targets = [(x, y, 2 * q + z // 2) for q in range(4)]
    target_self = [active & (x == z) & (q == x) & (c == z // 2) for q in range(4)]
    sources = [(2 * c + i // 4, i % 4) for i in range(8)]
    source_self = [(zs == z) & (x == z) & active for zs, _ in sources]
    for dev, same in zip(targets, target_self):
        @pl.when(active & jnp.logical_not(same))
        def _():
            greet(dev)
    for i in (0, 4):
        @pl.when(jnp.logical_not(source_self[i]))
        def _():
            greet((sources[i][0], y, 2 * z + y // 2))
    sends_here = active.astype(jnp.int32)
    has_self = (active & (x == z) & (c == z // 2)).astype(jnp.int32)

    rid = [ids_ref[0, j] for j in range(3)]
    live = [counts_ref[0, rid[j]] - y * SEG for j in range(3)]
    rows = lax.broadcasted_iota(jnp.int32, (SEG, LANES), 0)

    def block_of(i, base=0):
        return pl.ds(pl.multiple_of(base + i * LANES, LANES), LANES)

    def stage_acts(i, carry):
        cols = block_of(i)
        part = [acts_ref[rid[j], :, cols].astype(F32) for j in (1, 2)]
        na[y, :, cols] = jnp.concatenate(part, axis=0).astype(BF16)
        return carry

    def stage_clean_acts(i, carry):
        part = [acts_ref[rid[0], :, block_of(i, base)].astype(F32) for base in (0, 512)]
        ca[z, :, block_of(i)] = jnp.concatenate(part, axis=0).astype(BF16)
        return carry

    lax.fori_loop(0, 1024 // LANES, stage_acts, 0)
    lax.fori_loop(0, 512 // LANES, stage_clean_acts, 0)

    def masked(j, cols):
        return jnp.where(rows < live[j], cot_ref[rid[j], :, cols].astype(F32), 0.0)

    def stage_clean(i, carry):
        part = [masked(0, block_of(i, base)) for base in (0, HALF)]
        cg[z, :, block_of(i)] = jnp.concatenate(part, axis=0).astype(BF16)
        return carry

    def stage_a(i, carry):
        cols = pl.ds(pl.multiple_of(i * LANES, LANES), LANES)
        ga[z, y, :, cols] = jnp.concatenate([masked(1, cols), masked(2, cols)], axis=0).astype(BF16)
        return carry

    def stage_b(i, carry):
        cols = pl.ds(pl.multiple_of(i * LANES, LANES), LANES)
        from_cols = pl.ds(pl.multiple_of(WA + i * LANES, LANES), LANES)
        gb[y, z, :, cols] = jnp.concatenate(
            [masked(1, from_cols), masked(2, from_cols)], axis=0).astype(BF16)
        return carry

    pl.semaphore_wait(barrier, 24 + 4 * sends_here - 2 * has_self)

    pieces = []

    def send_cell(k):
        ys = mod4(y + k)
        for q in range(4):
            start = lax.rem(y, 2) * 512 + q * LANES
            src = na.at[ys, :, pl.ds(pl.multiple_of(start, LANES), LANES)]
            dst = ao.at[q, z, ys]
            same = target_self[q]
            goes = active & jnp.logical_not(same)
            far_copy = copy(src, dst, p_s.at[k, q], p_r.at[lax.rem(z, 2) * 4 + ys], targets[q])
            near_copy = pltpu.make_async_copy(src, dst, p_l.at[ys])

            @pl.when(same)
            def _():
                near_copy.start()

            @pl.when(goes)
            def _():
                far_copy.start()
            pieces.append((far_copy, goes))

    def wait_pieces():
        for i, ((zs, ys), same) in enumerate(zip(sources, source_self)):
            dst = ao.at[x, zs, ys]
            far_copy = copy(dst, dst, p_s.at[0, 0], p_r.at[i], (z, y, lax.rem(t + 1, 8)))
            near_copy = pltpu.make_async_copy(dst, dst, p_l.at[ys])

            @pl.when(same)
            def _():
                near_copy.wait()

            @pl.when(jnp.logical_not(same))
            def _():
                far_copy.wait_recv()

    rings = []

    class Ring:
        def __init__(self, at, axis, first, second):
            n = len(rings)
            rings.append(self)
            me = {"x": x, "y": y, "z": z}[axis]

            def dev(v):
                return {"x": (z, y, 2 * v + c), "y": (z, v, t), "z": (v, y, t)}[axis]

            up, down, far = mod4(me + 1), mod4(me + 3), mod4(me + 2)
            own, low, high, opp = at(me), at(down), at(up), at(far)
            self.go = [copy(own, own, ring_s.at[n, 0], ring_r.at[n, 0], dev(up)),
                       copy(own, own, ring_s.at[n, 1], ring_r.at[n, 1], dev(down))]
            self.got = [copy(low, low, ring_s.at[n, 0], ring_r.at[n, 0], dev(up)),
                        copy(high, high, ring_s.at[n, 1], ring_r.at[n, 1], dev(down))]
            self.pass_on = [
                copy(low.at[first], low.at[first], ring_s.at[n, 2], ring_r.at[n, 2], dev(up)),
                copy(high.at[second], high.at[second], ring_s.at[n, 3], ring_r.at[n, 3], dev(down))]
            self.got_far = [
                copy(opp.at[first], opp.at[first], ring_s.at[n, 2], ring_r.at[n, 2], dev(up)),
                copy(opp.at[second], opp.at[second], ring_s.at[n, 3], ring_r.at[n, 3], dev(down))]

        def start(self):
            for k in self.go:
                k.start()

        def forward(self):
            for k in range(2):
                self.got[k].wait_recv()
                self.pass_on[k].start()

        def finish(self):
            for k in self.got_far:
                k.wait_recv()

        def drain(self):
            for k in self.go + self.pass_on:
                k.wait_send()

    more_up = (pl.ds(0, 96),), (pl.ds(96, 80),)
    more_down = (pl.ds(0, 80),), (pl.ds(80, 96),)

    def az_ring(k):
        item = mod4(y + k)
        return Ring(lambda v: ga.at[v, item], "z", *(more_up if k in (0, 1) else more_down))

    def by_ring(k):
        item = mod4(z + k)
        return Ring(lambda v: gb.at[v, item], "y", *(more_up if k in (0, 1) else more_down))

    def rows_of(chunk):
        return pl.ds(pl.multiple_of(chunk * SEG, 8), SEG)

    r_na = [Ring(lambda v, h=h: na.at[v, :, pl.ds(h * 512, 512)], "y", *(more_up, more_down)[h]) for h in range(2)]
    r_ca = Ring(lambda v: ca.at[v], "z", *more_up)
    r_cg = Ring(lambda v: cg.at[v], "z", *more_down)
    r_ay = Ring(lambda v: ga.at[z, v], "y", *more_down)
    r_bz = Ring(lambda v: gb.at[y, v], "z", *more_down)
    r_az = {k: az_ring(k) for k in (0, 3, 1, 2)}
    r_by = {k: by_ring(k) for k in (0, 3, 1, 2)}
    here = pl.ds(2 * c, 2)
    there = pl.ds(2 * (1 - c), 2)
    r_ao = Ring(lambda v: ao.at[v, here], "x", (pl.ds(0, 1),), (pl.ds(1, 1),))
    r_full = Ring(lambda v: full.at[rows_of(4 * c + v)], "x", (pl.ds(0, 48),), (pl.ds(48, 40),))

    for ring in r_na:
        ring.start()
    r_ca.start()
    send_cell(0)
    lax.fori_loop(0, WA // LANES, stage_a, 0)
    lax.fori_loop(0, HALF // LANES, stage_clean, 0)
    r_cg.start()
    lax.fori_loop(0, WB // LANES, stage_b, 0)

    partner = (z, y, 2 * x + 1 - c)
    r_ca.forward()
    for ring in r_na:
        ring.forward()
    r_ay.start()
    r_by[0].start()
    r_bz.start()
    send_cell(3)
    send_cell(1)

    def gram(left, right):
        return lax.dot_general(left, right, (((1,), (1,)), ((), ())), preferred_element_type=F32)

    def unpack(ref, half):
        part = [ref[v].astype(F32)[half * SEG:(half + 1) * SEG] for v in range(4)]
        return jnp.concatenate(part, axis=0).astype(BF16)

    for ring in r_na:
        ring.finish()
    r_ca.finish()
    part_gram[...] = gram(na[:, :, :512].reshape(4 * NOISE, 512), unpack(ca, 0)) + gram(
        na[:, :, 512:].reshape(4 * NOISE, 512), unpack(ca, 1))
    own_half = pl.ds(pl.multiple_of(c * 352, 8), 352)
    other_half = pl.ds(pl.multiple_of((1 - c) * 352, 8), 352)
    swap = copy(part_gram.at[other_half], d2, d_s.at[0], d_r.at[0], partner)
    swap.start()
    send_cell(2)
    r_az[0].start()

    gap = jnp.zeros((32, LANES), BF16)

    def turn_a(k):
        def step(q, carry):
            span = pl.ds(pl.multiple_of(q * LANES, LANES), LANES)
            for g in range(2):
                cells = [ao[q, 2 * c + k, 2 * g], ao[q, 2 * c + k, 2 * g + 1], gap]
                ata[2 * c + k, g, span, :] = jnp.concatenate(cells, axis=0).T
            return carry

        lax.fori_loop(0, 4, step, 0)

    def turn_b(v):
        def step(q, carry):
            span = pl.ds(pl.multiple_of(q * LANES, LANES), LANES)
            tokens = jnp.concatenate([ao[q, 2 * c, v], ao[q, 2 * c + 1, v], gap], axis=0)
            atb[c, v, span, :] = tokens.T
            return carry

        lax.fori_loop(0, 4, step, 0)

    turned = [copy(ata.at[here], ata.at[here], k_s.at[0], k_r.at[0], partner),
              copy(atb.at[c], atb.at[c], k_s.at[1], k_r.at[1], partner)]

    swap.wait_recv()
    sm[...] = part_gram[own_half] + d2[...]
    up, down, across = mod4(x + 1), mod4(x + 3), mod4(x + 2)
    dev_up, dev_down = (z, y, 2 * up + c), (z, y, 2 * down + c)
    first = pl.ds(pl.multiple_of(across * SEG, 8), 48)
    second = pl.ds(pl.multiple_of(across * SEG + 48, 8), 40)
    share = [copy(sm.at[first], near_a, m_s.at[0], m_r.at[0], dev_up),
             copy(sm.at[second], near_b, m_s.at[1], m_r.at[1], dev_down),
             copy(sm.at[rows_of(up)], x3.at[0], m_s.at[2], m_r.at[2], dev_up),
             copy(sm.at[rows_of(down)], x3.at[1], m_s.at[3], m_r.at[3], dev_down)]
    share[0].start()
    share[1].start()
    r_ay.forward()
    r_cg.forward()
    share[0].wait_recv()
    sm[pl.ds(pl.multiple_of(up * SEG, 8), 48)] += near_a[...]
    share[2].start()
    share[1].wait_recv()
    sm[pl.ds(pl.multiple_of(down * SEG + 48, 8), 40)] += near_b[...]
    share[3].start()
    r_bz.forward()
    r_az[3].start()
    wait_pieces()
    r_ao.start()
    r_by[0].forward()
    r_by[3].start()
    r_by[1].start()
    r_az[1].start()

    share[2].wait_recv()
    share[3].wait_recv()
    full[rows_of(4 * c + x)] = sm[rows_of(x)] + x3[0] + x3[1]
    r_full.start()
    r_cg.finish()
    r_ay.finish()
    r_az[2].start()
    r_full.forward()
    left[...] = unpack(cg, 0)
    right[...] = unpack(cg, 1)
    grad_gram[...] = gram(ga[z].reshape(4 * NOISE, WA), left[:, :WA])
    r_ao.forward()
    r_full.finish()
    give = copy(full.at[own_half], full.at[own_half], d_s.at[1], d_r.at[1], partner)
    give.start()
    r_bz.finish()
    r_by[2].start()

    r_by[0].finish()
    grad_gram[...] += gram(gb[:, z, :, :HALF - WA].reshape(4 * NOISE, HALF - WA), left[:, WA:]) + gram(
        gb[:, z, :, HALF - WA:].reshape(4 * NOISE, HALF), right[...])
    copy(full.at[other_half], full.at[other_half], d_s.at[1], d_r.at[1], partner).wait_recv()

    def row_dot(j):
        terms = [grad_gram[g * SEG:(g + 1) * SEG] * full[g * SEG:(g + 1) * SEG] for g in range(j, 8, 2)]
        rows_sum = jnp.sum(terms[0] + terms[1] + terms[2] + terms[3], axis=0, keepdims=True)
        return jnp.broadcast_to(jnp.sum(rows_sum, axis=1, keepdims=True), (8, LANES))

    place = lax.broadcasted_iota(jnp.int32, (8, LANES), 0)
    tile = jnp.where(place == 2 * z, row_dot(0), jnp.where(place == 2 * z + 1, row_dot(1), 0.0))

    sends = []

    def send_tile(buf, value, me, n, dev, base):
        buf[me] = value
        for r in range(1, n):
            out = copy(buf.at[me], buf.at[me], v_s.at[base + r], v_r.at[base + r], dev(r))
            out.start()
            sends.append(out)

    def sum_tiles(buf, me, n, base):
        for r in range(1, n):
            origin = buf.at[lax.rem(me + n - r, n)]
            copy(origin, origin, v_s.at[base + r], v_r.at[base + r], partner).wait_recv()
        return jnp.sum(buf[...], axis=0)

    send_tile(sv1, tile, t, 8, lambda r: (z, y, lax.rem(t + r, 8)), 0)

    r_ao.finish()
    turn_a(0)
    turn_a(1)
    turned[0].start()
    tile = sum_tiles(sv1, t, 8, 0)
    send_tile(sv2, tile, 4 * z + y, 16, cell, 8)
    r_az[0].forward()
    for v in range(4):
        turn_b(v)
    turned[1].start()
    r_az[3].forward()
    r_by[3].forward()
    r_az[1].forward()
    r_by[1].forward()
    tile = sum_tiles(sv2, 4 * z + y, 16, 8)
    weights = jnp.maximum(-tile, 0.0) / jnp.sum(jnp.abs(tile), axis=0, keepdims=True)
    wts[...] = weights
    lane = lax.broadcasted_iota(jnp.int32, (1, LANES), 1)
    wout_ref[...] = jnp.where(lane == 0, wts[pl.ds(2 * z, 1), :], wts[pl.ds(2 * z + 1, 1), :])[:, :2]

    copy(ata.at[there], ata.at[there], k_s.at[0], k_r.at[0], partner).wait_recv()
    copy(atb.at[1 - c], atb.at[1 - c], k_s.at[1], k_r.at[1], partner).wait_recv()

    def scaled(rows_in, k):
        width = rows_in.shape[1]

        def part(j):
            row = wts[pl.ds(2 * k + j, 1), :]
            factor = jnp.broadcast_to(jnp.concatenate([row] * (width // LANES), axis=1), (SEG, width))
            return rows_in[j * SEG:(j + 1) * SEG] * factor

        return jnp.concatenate([part(0), part(1)], axis=0).astype(BF16)

    def product(lefts, rights, width, base, span, first=False):
        empty = jnp.zeros((32, span), BF16)

        def step(i, carry):
            cols = pl.ds(pl.multiple_of(i * span, span), span)
            dest = pl.ds(pl.multiple_of(base + i * span, 256), span)
            right = []
            for two in rights:
                right += [scaled(rows_in[cell_at + (slice(None), cols)].astype(F32), k)
                          for rows_in, cell_at, k in two] + [empty]
            left_side = jnp.concatenate([ref[at] for ref, at in lefts], axis=1)
            value = jnp.dot(left_side, jnp.concatenate(right, axis=0), preferred_element_type=F32)
            if first:
                out_ref[:, dest] = value
            else:
                out_ref[:, dest] += value
            return carry

        lax.fori_loop(0, width // span, step, 0)

    def add_a(k, first=False, parts=(0, 1)):
        v = mod4(z + k)
        product([(ata, (v, g)) for g in parts],
                [[(ga, (v, 2 * g + j), v) for j in range(2)] for g in parts], WA, 0, 768, first)

    def add_b(k, first=False, parts=(0, 1)):
        v = mod4(y + k)
        product([(atb, (g, v)) for g in parts],
                [[(gb, (v, 2 * g + j), 2 * g + j) for j in range(2)] for g in parts], WB, WA, 512, first)

    add_a(0, True)
    add_b(0, True)
    r_az[2].forward()
    r_by[2].forward()
    add_a(3)
    add_a(1)
    add_b(3)
    add_b(1)
    for k in (0, 3, 1):
        r_az[k].finish()
    add_a(2, parts=(y // 2,))
    for k in (3, 1):
        r_by[k].finish()
    add_b(2, parts=(z // 2,))
    r_az[2].finish()
    add_a(2, parts=(1 - y // 2,))
    r_by[2].finish()
    add_b(2, parts=(1 - z // 2,))

    for far_copy, goes in pieces:
        @pl.when(goes)
        def _():
            far_copy.wait_send()
    for ring in rings:
        ring.drain()
    for k in turned + [swap, give] + share + sends:
        k.wait_send()


def body(activations, cotangents, row_ids, row_counts):
    dma = pltpu.SemaphoreType.DMA
    vmem = pltpu.VMEM
    return pl.pallas_call(
        body_kernel,
        out_shape=(pltpu.VMEM((512, WA + WB), F32), pltpu.VMEM((1, 2), F32)),
        in_specs=[pl.BlockSpec(memory_space=pltpu.SMEM)] * 2 + [pl.BlockSpec(memory_space=pltpu.VMEM)] * 2,
        out_specs=(pl.BlockSpec(memory_space=pltpu.VMEM), pl.BlockSpec(memory_space=pltpu.VMEM)),
        scratch_shapes=[
            vmem((4, NOISE, 1024), BF16),
            vmem((4, NOISE, 512), BF16),
            vmem((4, NOISE, HALF), BF16),
            vmem((4 * SEG, HALF), BF16),
            vmem((4 * SEG, HALF), BF16),
            vmem((4, 4, NOISE, WA), BF16),
            vmem((4, 4, NOISE, WB), BF16),
            vmem((4, 4, 4, NOISE, LANES), BF16),
            vmem((4, 2, 512, 384), BF16),
            vmem((2, 4, 512, 384), BF16),
            vmem((4 * NOISE, 4 * CLEAN_ROWS), F32),
            vmem((4 * NOISE, 4 * CLEAN_ROWS), F32),
            vmem((4 * NOISE, 4 * CLEAN_ROWS), F32),
            vmem((2 * NOISE, 4 * CLEAN_ROWS), F32),
            vmem((2 * NOISE, 4 * CLEAN_ROWS), F32),
            vmem((48, 4 * CLEAN_ROWS), F32),
            vmem((40, 4 * CLEAN_ROWS), F32),
            vmem((2, SEG, 4 * CLEAN_ROWS), F32),
            vmem((8, 8, LANES), F32),
            vmem((16, 8, LANES), F32),
            vmem((8, LANES), F32),
            dma((16, 4)), dma((16, 4)),
            dma((4, 4)), dma((8,)), dma((4,)),
            dma((2,)), dma((2,)),
            dma((2,)), dma((2,)),
            dma((4,)), dma((4,)),
            dma((24,)), dma((24,)),
        ],
        compiler_params=pltpu.CompilerParams(
            collective_id=0, has_side_effects=True, vmem_limit_bytes=60 * 1024 * 1024),
        cost_estimate=pl.CostEstimate(flops=8_000_000_000, bytes_accessed=8_000_000, transcendentals=0),
        name="reweight",
    )(row_ids, row_counts, activations, cotangents)


def solution(mesh):
    placed = (P("dp", "seq", "tensor"), P("dp", "seq", "tensor"), P("dp", None), P("dp", None))
    return jax.shard_map(
        body,
        mesh=mesh,
        in_specs=placed,
        out_specs=(P(("dp", "seq"), "tensor"), P("dp", None)),
        check_vma=False,
    )
```
